32 devices in a mesh: rows: 8 (over z, y), cols: 4 (over x, core).
Axes of the slice: x: 2, y: 2, z: 4, core: 2. Of those that a mesh axis runs over, the one named last changes fastest.
Arguments:
- activations: bfloat16 [128, 64, 384], P('rows', 'cols'), may hold values from -6 to 6
- grad_out: bfloat16 [128, 64, 384], P('rows', 'cols'), may hold values from -6 to 6
- kernels: float32 [2, 7, 7, 384], replicated, may hold values from -0.875 to 0.875
- norm_gains: float32 [2, 384], replicated, may hold values from 0.5 to 1.5
- norm_shifts: float32 [2, 384], replicated, may hold values from -3 to 3
- w_in: bfloat16 [2, 384, 1536], replicated, may hold values from -0.3125 to 0.3125
- b_in: float32 [2, 1536], replicated, may hold values from -3 to 3
- w_out: bfloat16 [2, 384, 1536], replicated, may hold values from -0.15625 to 0.15625
Outputs:
- grad_in: bfloat16 [128, 64, 384], P('rows', 'cols')
- grad_kernels: float32 [2, 7, 7, 384], replicated
- grad_gains: float32 [2, 384], replicated
- grad_shifts: float32 [2, 384], replicated
- grad_b_in: float32 [2, 1536], replicated
- grad_w_in: float32 [2, 384, 1536], P(None, None, ('rows', 'cols'))
- grad_w_out: float32 [2, 384, 1536], P(None, None, ('rows', 'cols'))
The draws below stay inside these ranges and needn't reach their ends.
All inputs are finite; a program needn't handle non-finite values.
Results may differ from the reference program's by a relative error of at most 0.017.
Values may be sent and summed in bfloat16 or wider, within the bound.
No kernel may reach another device: no remote copies, remote signals or barrier semaphores. Data moves between devices by JAX's collectives and lax.ppermute only.
A program may use at most 128 MiB of HBM per device.

```python
import math
import jax
import jax.numpy as jnp
from jax import lax

C = 384
HID = 1536
LAYERS = 2
NR = 128
NC = 64


def shard_levels(rng, dims, shards, smallest, top_value):
    def one(dim, shards_of):
        heights = jax.random.uniform(jax.random.fold_in(jax.random.fold_in(rng, 6), dim), (shards_of,), jnp.float32, smallest / len(shards), top_value / len(shards))
        return jnp.repeat(jnp.exp(heights), dims[dim] // shards_of).reshape((-1,) + (1,) * (len(dims) - dim - 1))

    factor_of = one(*shards[0])
    for cut in shards[1:]:
        factor_of = factor_of * one(*cut)
    return factor_of


def normal_values(rng, dims, scale, most, cuts=(), held_as=jnp.bfloat16):
    entries = jax.random.normal(rng, dims, jnp.float32) * scale
    if len(cuts) > 0:
        entries = shard_levels(rng, dims, cuts, -0.22, 0.18) * entries
    return jnp.clip(entries, min=-most, max=most).astype(held_as)


def setup_inputs(seed: int = 0) -> dict:
    key_of = jax.random.split(jax.random.key(seed), 9)
    return {
        "activations": normal_values(key_of[0], (NR, NC, C), 1.0, 6.0, ((0, 8), (1, 4))),
        "grad_out": normal_values(key_of[1], (NR, NC, C), 1.0, 6.0, ((0, 8), (1, 4))),
        "kernels": normal_values(key_of[2], (LAYERS, 7, 7, C), 49 ** -0.5, 0.875, (), jnp.float32),
        "norm_gains": jnp.clip(1.0 + 0.1 * jax.random.normal(key_of[3], (LAYERS, C), jnp.float32), 0.5, 1.5),
        "norm_shifts": normal_values(key_of[4], (LAYERS, C), 0.5, 3.0, (), jnp.float32),
        "w_in": normal_values(key_of[5], (LAYERS, C, HID), C ** -0.5, 0.3125),
        "b_in": normal_values(key_of[6], (LAYERS, HID), 0.5, 3.0, (), jnp.float32),
        "w_out": normal_values(key_of[7], (LAYERS, C, HID), HID ** -0.5, 0.15625),
    }


EPSILON = 1e-06
ROOT_HALF = 0.7071067811865476
INV_ROOT_TAU = 0.3989422804014327

def gelu_parts(pre_act):
    normal_cdf = 0.5 * (1.0 + lax.erf(pre_act * ROOT_HALF))
    density = jnp.exp(-0.5 * pre_act * pre_act) * INV_ROOT_TAU
    return (pre_act * normal_cdf, normal_cdf + pre_act * density)

def conv_from(padded, kernel, out_rows, out_cols):
    running = jnp.zeros((out_rows, out_cols, padded.shape[2]), jnp.float32)
    for row_off in range(7):
        for col_off in range(7):
            running = running + kernel[row_off, col_off] * padded[row_off:row_off + out_rows, col_off:col_off + out_cols]
    return running

def conv_back(padded_grad, kernel, out_rows, out_cols):
    running = jnp.zeros((out_rows, out_cols, padded_grad.shape[2]), jnp.float32)
    for row_off in range(7):
        for col_off in range(7):
            running = running + kernel[row_off, col_off] * padded_grad[6 - row_off:6 - row_off + out_rows, 6 - col_off:6 - col_off + out_cols]
    return running

def kernel_grad(grad_z, padded_in):
    out_rows, out_cols = (grad_z.shape[0], grad_z.shape[1])
    kernel_taps = []
    for row_off in range(7):
        for col_off in range(7):
            kernel_taps.append(lax.optimization_barrier(jnp.sum(grad_z * padded_in[row_off:row_off + out_rows, col_off:col_off + out_cols], axis=(0, 1))))
    return jnp.stack(kernel_taps).reshape(7, 7, grad_z.shape[2])

def norm_fwd(source, gain, shift):
    center = source - lax.optimization_barrier(jnp.mean(source, axis=-1, keepdims=True))
    inv_std = lax.rsqrt(lax.optimization_barrier(jnp.mean(center * center, axis=-1, keepdims=True)) + EPSILON)
    norm_hat = center * inv_std
    return (norm_hat, inv_std, (norm_hat * gain + shift).astype(jnp.bfloat16))

def norm_back(grad_n, norm_hat, inv_std, gain):
    scaled = grad_n * gain
    return inv_std * (scaled - lax.optimization_barrier(jnp.mean(scaled, axis=-1, keepdims=True)) - norm_hat * lax.optimization_barrier(jnp.mean(scaled * norm_hat, axis=-1, keepdims=True)))

def mlp_out(normed, weight_in, bias_in, weight_out, block_len):
    channels = normed.shape[1]

    def one_block(normed_block):
        pre_act = jnp.dot(normed_block, weight_in, preferred_element_type=jnp.float32) + bias_in
        act_b = gelu_parts(pre_act)[0].astype(jnp.bfloat16)
        return lax.dot_general(act_b, weight_out, (((1,), (1,)), ((), ())), preferred_element_type=jnp.float32)
    return lax.map(one_block, normed.reshape(-1, block_len, channels)).reshape(-1, channels)

def mlp_back(normed, grad_b, weight_in, bias_in, weight_out, block_len):
    channels = normed.shape[1]
    hidden = weight_in.shape[1]

    def one_block(running, block_pair):
        normed_block, grad_block = block_pair
        pre_act = jnp.dot(normed_block, weight_in, preferred_element_type=jnp.float32) + bias_in
        activation, gelu_slope = gelu_parts(pre_act)
        act_b = activation.astype(jnp.bfloat16)
        grad_wo = lax.dot_general(grad_block, act_b, (((0,), (0,)), ((), ())), preferred_element_type=jnp.float32)
        grad_pre = jnp.dot(grad_block, weight_out, preferred_element_type=jnp.float32) * gelu_slope
        grad_preb = grad_pre.astype(jnp.bfloat16)
        grad_wi = lax.dot_general(normed_block, grad_preb, (((0,), (0,)), ((), ())), preferred_element_type=jnp.float32)
        grad_n = lax.dot_general(grad_preb, weight_in, (((1,), (1,)), ((), ())), preferred_element_type=jnp.float32)
        return ((running[0] + grad_wi, running[1] + grad_wo, running[2] + lax.optimization_barrier(jnp.sum(grad_pre, axis=0))), grad_n)
    initial = (jnp.zeros((channels, hidden), jnp.float32), jnp.zeros((channels, hidden), jnp.float32), jnp.zeros((hidden,), jnp.float32))
    totals, grad_n = lax.scan(one_block, initial, (normed.reshape(-1, block_len, channels), grad_b.reshape(-1, block_len, channels)))
    return (totals, grad_n.reshape(-1, channels))

def layer_back(grad_b, normed, norm_hat, inv_std, padded_in, layer, kernels, norm_gains, w_in, b_in, w_out, block_len):
    image_rows, image_cols, channels = grad_b.shape
    totals, grad_n = mlp_back(normed.reshape(-1, channels), grad_b.reshape(-1, channels), w_in[layer], b_in[layer], w_out[layer], block_len)
    grad_n = grad_n.reshape(grad_b.shape)
    grad_gain = lax.optimization_barrier(jnp.sum(grad_n * norm_hat, axis=(0, 1)))
    grad_shift = lax.optimization_barrier(jnp.sum(grad_n, axis=(0, 1)))
    grad_z = norm_back(grad_n, norm_hat, inv_std, norm_gains[layer]).astype(jnp.bfloat16).astype(jnp.float32)
    kernel_taps = kernel_grad(grad_z, padded_in)
    spread = conv_back(jnp.pad(grad_z, ((3, 3), (3, 3), (0, 0))), kernels[layer], image_rows, image_cols)
    return (spread, kernel_taps, grad_gain, grad_shift, totals)

def reference(activations, grad_out, kernels, norm_gains, norm_shifts, w_in, b_in, w_out):
    image_rows, image_cols, channels = activations.shape
    pixels = image_rows * image_cols
    grad_scale = 1.0 / math.sqrt(pixels)
    block_len = math.gcd(pixels, 4096)
    inputs = activations.astype(jnp.float32)
    padded_in = jnp.pad(inputs, ((3, 3), (3, 3), (0, 0)))
    conv_one = conv_from(padded_in, kernels[0], image_rows, image_cols)
    hat_one, inv_one, normed_one = norm_fwd(conv_one, norm_gains[0], norm_shifts[0])
    mixed_one = mlp_out(normed_one.reshape(-1, channels), w_in[0], b_in[0], w_out[0], block_len)
    middle = (inputs + mixed_one.reshape(inputs.shape)).astype(jnp.bfloat16)
    padded_mid = jnp.pad(middle.astype(jnp.float32), ((3, 3), (3, 3), (0, 0)))
    conv_two = conv_from(padded_mid, kernels[1], image_rows, image_cols)
    hat_two, inv_two, normed_two = norm_fwd(conv_two, norm_gains[1], norm_shifts[1])
    back_two = layer_back(grad_out, normed_two, hat_two, inv_two, padded_mid, 1, kernels, norm_gains, w_in, b_in, w_out, block_len)
    grad_mid = (grad_out.astype(jnp.float32) + back_two[0]).astype(jnp.bfloat16)
    back_one = layer_back(grad_mid, normed_one, hat_one, inv_one, padded_in, 0, kernels, norm_gains, w_in, b_in, w_out, block_len)
    grad_in = (grad_mid.astype(jnp.float32) + back_one[0]).astype(jnp.bfloat16)
    grad_kernels = jnp.stack([back_one[1], back_two[1]]) * grad_scale
    grad_gains = jnp.stack([back_one[2], back_two[2]]) * grad_scale
    grad_shifts = jnp.stack([back_one[3], back_two[3]]) * grad_scale
    grad_b_in = jnp.stack([back_one[4][2], back_two[4][2]]) * grad_scale
    grad_w_in = jnp.stack([back_one[4][0], back_two[4][0]]) * grad_scale
    grad_w_out = jnp.stack([back_one[4][1], back_two[4][1]]) * grad_scale
    return (grad_in, grad_kernels, grad_gains, grad_shifts, grad_b_in, grad_w_in, grad_w_out)
```

```python
import math

import jax
import jax.numpy as jnp
from jax import lax
from jax.sharding import PartitionSpec as P

EPSILON = 1e-06
ROOT_HALF = 0.7071067811865476
INV_ROOT_TAU = 0.3989422804014327


def with_halo(block, sides, width):
    for axis, dim in sides:
        count = lax.axis_size(axis)
        forward = [(i, i + 1) for i in range(count - 1)]
        backward = [(target, source) for source, target in forward]
        low = lax.ppermute(
            lax.slice_in_dim(block, block.shape[dim] - width, None, axis=dim), axis, forward
        )
        high = lax.ppermute(lax.slice_in_dim(block, 0, width, axis=dim), axis, backward)
        block = jnp.concatenate([low, block, high], axis=dim)
    return block


def gelu_parts(pre_act):
    normal_cdf = 0.5 * (1.0 + lax.erf(pre_act * ROOT_HALF))
    density = jnp.exp(-0.5 * pre_act * pre_act) * INV_ROOT_TAU
    return (pre_act * normal_cdf, normal_cdf + pre_act * density)


def conv_from(padded, kernel, out_rows, out_cols):
    running = jnp.zeros((out_rows, out_cols, padded.shape[2]), jnp.float32)
    for row_off in range(7):
        for col_off in range(7):
            running = (
                running
                + kernel[row_off, col_off]
                * padded[row_off : row_off + out_rows, col_off : col_off + out_cols]
            )
    return running


def conv_back(padded_grad, kernel, out_rows, out_cols):
    running = jnp.zeros((out_rows, out_cols, padded_grad.shape[2]), jnp.float32)
    for row_off in range(7):
        for col_off in range(7):
            running = (
                running
                + kernel[row_off, col_off]
                * padded_grad[
                    6 - row_off : 6 - row_off + out_rows, 6 - col_off : 6 - col_off + out_cols
                ]
            )
    return running


def kernel_grad(grad_z, padded_in):
    out_rows, out_cols = (grad_z.shape[0], grad_z.shape[1])
    kernel_taps = []
    for row_off in range(7):
        for col_off in range(7):
            kernel_taps.append(
                jnp.sum(
                    grad_z * padded_in[row_off : row_off + out_rows, col_off : col_off + out_cols],
                    axis=(0, 1),
                )
            )
    return jnp.stack(kernel_taps).reshape(7, 7, grad_z.shape[2])


def norm_fwd(source, gain, shift):
    center = source - jnp.mean(source, axis=-1, keepdims=True)
    inv_std = lax.rsqrt(jnp.mean(center * center, axis=-1, keepdims=True) + EPSILON)
    norm_hat = center * inv_std
    return (norm_hat, inv_std, (norm_hat * gain + shift).astype(jnp.bfloat16))


def norm_back(grad_n, norm_hat, inv_std, gain):
    scaled = grad_n * gain
    return inv_std * (
        scaled
        - jnp.mean(scaled, axis=-1, keepdims=True)
        - norm_hat * jnp.mean(scaled * norm_hat, axis=-1, keepdims=True)
    )


def mlp_hidden(normed_flat, weight_in, bias_in):
    pre_act = jnp.dot(normed_flat, weight_in, preferred_element_type=jnp.float32) + bias_in
    activation, gelu_slope = gelu_parts(pre_act)
    return (activation.astype(jnp.bfloat16), gelu_slope)


def mlp_forward(normed_flat, weight_in, bias_in, weight_out):
    act_b, gelu_slope = mlp_hidden(normed_flat, weight_in, bias_in)
    mixed = lax.dot_general(
        act_b, weight_out, (((1,), (1,)), ((), ())), preferred_element_type=jnp.float32
    )
    return (act_b, gelu_slope, mixed)


def input_rim(source):
    return with_halo(source, (("rows", 0), ("cols", 1)), 3)


def layer_back(
    grad_b,
    normed_flat,
    act_b,
    gelu_slope,
    norm_hat,
    inv_std,
    kernel,
    gain,
    weight_in,
    weight_out,
    padded_in,
):
    tile_rows, tile_cols, channels = grad_b.shape
    grad_flat = grad_b.reshape(-1, channels)
    grad_wo = lax.dot_general(
        act_b, grad_flat, (((0,), (0,)), ((), ())), preferred_element_type=jnp.float32
    )
    grad_pre = jnp.dot(grad_flat, weight_out, preferred_element_type=jnp.float32) * gelu_slope
    grad_preb = grad_pre.astype(jnp.bfloat16)
    grad_wi = lax.dot_general(
        grad_preb, normed_flat, (((0,), (0,)), ((), ())), preferred_element_type=jnp.float32
    )
    grad_bias = jnp.sum(grad_pre, axis=0)
    grad_n = lax.dot_general(
        grad_preb, weight_in, (((1,), (1,)), ((), ())), preferred_element_type=jnp.float32
    ).reshape(grad_b.shape)
    grad_gain = jnp.sum(grad_n * norm_hat, axis=(0, 1))
    grad_shift = jnp.sum(grad_n, axis=(0, 1))
    grad_z = norm_back(grad_n, norm_hat, inv_std, gain).astype(jnp.bfloat16)
    padded_grad = with_halo(grad_z, (("rows", 0), ("cols", 1)), 3)
    kernel_taps = kernel_grad(grad_z.astype(jnp.float32), padded_in)
    spread = conv_back(padded_grad.astype(jnp.float32), kernel, tile_rows, tile_cols)
    return (spread, kernel_taps, grad_gain, grad_shift, grad_bias, grad_wi, grad_wo)


def shards(activations, grad_out, kernels, norm_gains, norm_shifts, w_in, b_in, w_out):
    tile_rows, tile_cols, channels = activations.shape
    grad_scale = 1.0 / math.sqrt(
        tile_rows * tile_cols * lax.axis_size("rows") * lax.axis_size("cols")
    )
    padded_in = input_rim(activations).astype(jnp.float32)
    conv_one = conv_from(padded_in, kernels[0], tile_rows, tile_cols)
    hat_one, inv_one, normed_grid = norm_fwd(conv_one, norm_gains[0], norm_shifts[0])
    normed_one = normed_grid.reshape(-1, channels)
    act_one, slope_one, mixed_one = mlp_forward(normed_one, w_in[0], b_in[0], w_out[0])
    middle = (activations.astype(jnp.float32) + mixed_one.reshape(activations.shape)).astype(
        jnp.bfloat16
    )
    padded_mid = input_rim(middle)
    padded_mid_wide = padded_mid.astype(jnp.float32)
    conv_two = conv_from(padded_mid_wide, kernels[1], tile_rows, tile_cols)
    hat_two, inv_two, normed_grid_two = norm_fwd(conv_two, norm_gains[1], norm_shifts[1])
    normed_two = normed_grid_two.reshape(-1, channels)
    act_two, slope_two = mlp_hidden(normed_two, w_in[1], b_in[1])
    back_two = layer_back(
        grad_out,
        normed_two,
        act_two,
        slope_two,
        hat_two,
        inv_two,
        kernels[1],
        norm_gains[1],
        w_in[1],
        w_out[1],
        padded_mid_wide,
    )
    grad_mid = (grad_out.astype(jnp.float32) + back_two[0]).astype(jnp.bfloat16)
    back_one = layer_back(
        grad_mid,
        normed_one,
        act_one,
        slope_one,
        hat_one,
        inv_one,
        kernels[0],
        norm_gains[0],
        w_in[0],
        w_out[0],
        padded_in,
    )
    grad_in = (grad_mid.astype(jnp.float32) + back_one[0]).astype(jnp.bfloat16)
    small = jnp.concatenate(
        [
            part.reshape(-1)
            for back in (back_one, back_two)
            for part in (back[1], back[2], back[3], back[4])
        ]
    ).reshape(-1, channels)
    small = lax.psum(small, ("rows", "cols")) * grad_scale
    hidden = w_in.shape[2]
    small = small.reshape(2, -1)
    taps = 49 * channels
    grad_kernels = small[:, :taps].reshape(2, 7, 7, channels)
    grad_gains = small[:, taps : taps + channels]
    grad_shifts = small[:, taps + channels : taps + 2 * channels]
    grad_b_in = small[:, taps + 2 * channels :]
    slices = []
    for back in (back_one, back_two):
        count = lax.axis_size("rows") * lax.axis_size("cols")
        both = jnp.concatenate(
            [
                back[5].astype(jnp.bfloat16).reshape(count, -1, channels),
                back[6].astype(jnp.bfloat16).reshape(count, -1, channels),
            ],
            axis=1,
        )
        mine = lax.psum_scatter(
            both, ("rows", "cols"), scatter_dimension=0, tiled=True
        ).reshape(2, hidden // count, channels)
        slices.append(jnp.swapaxes(mine.astype(jnp.float32) * grad_scale, 1, 2))
    grad_w_in = jnp.stack([slices[0][0], slices[1][0]])
    grad_w_out = jnp.stack([slices[0][1], slices[1][1]])
    return (grad_in, grad_kernels, grad_gains, grad_shifts, grad_b_in, grad_w_in, grad_w_out)


def solution(mesh):
    return jax.shard_map(
        shards,
        mesh=mesh,
        in_specs=(P("rows", "cols", None), P("rows", "cols", None), P(), P(), P(), P(), P(), P()),
        out_specs=(
            P("rows", "cols", None),
            P(),
            P(),
            P(),
            P(),
            P(None, None, ("rows", "cols")),
            P(None, None, ("rows", "cols")),
        ),
        check_vma=False,
    )
```

```python
import functools
import math

import jax
import jax.numpy as jnp
from jax import lax
from jax.experimental import pallas as pl
from jax.experimental.pallas import tpu as pltpu
from jax.sharding import PartitionSpec as P

EPSILON = 1e-06
INV_ROOT_TAU = 0.3989422804014327
HALF_LOG2E = 0.7213475204444817
ERFC_SLOPE = 0.4 * 0.7071067811865476
ERFC_TERMS = (
    0.22479419400284972,
    0.2383621945582281,
    0.12991301634379934,
    0.4353236101490443,
    -0.41611664430523265,
    0.7235898182708315,
    -0.41436965913692125,
    0.07850346878444278,
)
LANES = 128
HALO = 3
WIDE = 9
F32 = jnp.float32
BF16 = jnp.bfloat16


def normal_parts(x):
    bell = jnp.exp2(x * x * (-HALF_LOG2E))
    t = 1.0 / (1.0 + ERFC_SLOPE * jnp.abs(x))
    series = 0.5 * ERFC_TERMS[7]
    for term in ERFC_TERMS[6::-1]:
        series = series * t + 0.5 * term
    tail = series * t * bell
    return jnp.where(x >= 0, 1.0 - tail, tail), bell


def gelu_only(x):
    cdf, _ = normal_parts(x)
    return x * cdf


def gelu_parts(x):
    cdf, bell = normal_parts(x)
    return x * cdf, cdf + x * bell * INV_ROOT_TAU


def strip_rows(rows, cols):
    most = max(1, 288 // cols)
    return max(d for d in range(1, rows + 1) if rows % d == 0 and d <= most)


def conv_pass(source, row0, col0, taps, target, rows, cols):
    strip = strip_rows(rows, cols)
    groups = source.shape[0]

    def one_strip(step, carry):
        g = step // (rows // strip)
        top = (step % (rows // strip)) * strip
        sums = [jnp.zeros((cols, LANES), F32) for _ in range(strip)]
        for b in range(7):
            weights = [taps[g, pl.ds(7 * a + b, 1), :] for a in range(7)]
            for r in range(strip + 6):
                line = source[g, row0 + top + r, pl.ds(col0 + b, cols), :]
                for a in range(7):
                    if 0 <= r - a < strip:
                        sums[r - a] = sums[r - a] + weights[a] * line
        for i in range(strip):
            target[g, top + i] = sums[i]
        return carry

    lax.fori_loop(0, groups * (rows // strip), one_strip, 0)


def tap_pass(source, row0, col0, grad, grow0, gcol0, target, rows, cols):
    for g in range(source.shape[0]):
        lanes = slice(g * LANES, (g + 1) * LANES)
        for b in range(7):
            def one_row(i, sums):
                line = grad[g, grow0 + i, pl.ds(gcol0, cols), :]
                out = []
                for a in range(7):
                    part = line * source[g, row0 + i + a, pl.ds(col0 + b, cols), :]
                    out.append(sums[a] + part.reshape(cols // 8, 8, LANES).sum(0))
                return tuple(out)

            sums = lax.fori_loop(
                0, rows, one_row, tuple(jnp.zeros((8, LANES), F32) for _ in range(7)), unroll=4
            )
            for a in range(7):
                target[pl.ds(7 * a + b, 1), lanes] = jnp.sum(sums[a], axis=0, keepdims=True)


def joined(ref, rows, cols=slice(None)):
    parts = [ref[g, rows, cols, :] for g in range(ref.shape[0])]
    return jnp.concatenate([p.reshape(-1, LANES) for p in parts], axis=1)


def split_to(ref, rows, value, shape):
    for g in range(ref.shape[0]):
        ref[g, rows] = value[:, g * LANES : (g + 1) * LANES].reshape(*shape, LANES)


def norm_parts(z):
    center = z - jnp.mean(z, axis=-1, keepdims=True)
    inv = lax.rsqrt(jnp.mean(center * center, axis=-1, keepdims=True) + EPSILON)
    return center * inv, inv


def norm_back(dn, hat, inv, gain):
    scaled = dn * gain
    return inv * (
        scaled
        - jnp.mean(scaled, axis=-1, keepdims=True)
        - hat * jnp.mean(scaled * hat, axis=-1, keepdims=True)
    )


def dot_nn(a, b):
    return jnp.dot(a, b, preferred_element_type=F32)


def dot_nt(a, b):
    return lax.dot_general(a, b, (((1,), (1,)), ((), ())), preferred_element_type=F32)


def dot_tn(a, b):
    return lax.dot_general(a, b, (((0,), (0,)), ((), ())), preferred_element_type=F32)


def pixel_blocks(pixels):
    best = max(d for d in range(16, 257, 16) if pixels % d == 0)
    return [slice(start, start + best) for start in range(0, pixels, best)]


def hidden_chunks(hidden):
    size = 256 if hidden % 256 == 0 else hidden
    return [slice(start, start + size) for start in range(0, hidden, size)]


def mlp_grads(normed, normed_in, grad, grad_in, inside, w_in, b_in, w_out, act, gpre, dwi, dwo, db):
    pixels = grad.shape[0]
    hidden = w_in.shape[2]
    for cut in hidden_chunks(hidden):
        bias = b_in[:, cut]
        bias_sum = None
        for block in pixel_blocks(pixels):
            pre = dot_nn(normed[block, :], w_in[0, :, cut]) + bias
            value, slope = gelu_parts(pre)
            act[block, cut] = value.astype(BF16)
            gradient = dot_nn(grad[block, :], w_out[0, :, cut]) * slope
            gpre[block, cut] = gradient.astype(BF16)
            if inside is not None:
                gradient = gradient * inside[block, :1]
            part = jnp.sum(gradient, axis=0, keepdims=True)
            bias_sum = part if bias_sum is None else bias_sum + part
        db[:, cut] = bias_sum
        dwo[cut, :] = dot_tn(act[:, cut], grad_in[...]).astype(BF16)
        dwi[cut, :] = dot_tn(gpre[:, cut], normed_in[...]).astype(BF16)


def fetch_layers(triples, arrived):
    copies = [
        pltpu.make_async_copy(source.at[pl.ds(layer, 1)], target, arrived.at[i])
        for i, (source, layer, target) in enumerate(triples)
    ]
    for copy in copies:
        copy.start()
    return copies


def first_kernel(
    place, xpad, gpad, gcenter, taps, gains, shifts, w_in, w_out, b_in, dz_out, z_out, dwi, dwo, db, dgain, dshift, dk,
    xs, zs, mids, zs1, act0, hat1, inv1, normed1, normed1_in, inside, act1, gpre1,
    w_in0, w_out0, w_in1, w_out1, arrived,
):
    waits = fetch_layers(((w_in, 0, w_in0), (w_out, 0, w_out0), (w_in, 1, w_in1), (w_out, 1, w_out1)), arrived)
    groups = xs.shape[0]
    mid_rows, mid_cols = zs.shape[1:3]
    dz_rows, dz_cols = zs1.shape[1:3]
    rows, cols = z_out.shape[1:3]
    side = (mid_rows - rows) // 2
    for g in range(groups):
        xs[g] = xpad[:, :, g * LANES : (g + 1) * LANES].astype(F32)
    conv_pass(xs, 0, 5, taps.at[0], zs, mid_rows, mid_cols)
    z_out[...] = zs[:, side : side + rows, 8 : 8 + cols, :]

    strip = max(d for d in range(1, mid_rows + 1) if mid_rows % d == 0 and d * mid_cols <= 256)
    count = strip * mid_cols
    hidden = w_in0.shape[2]
    waits[0].wait()
    waits[1].wait()

    def one_strip(step, carry):
        top = step * strip
        hat, _ = norm_parts(joined(zs, pl.ds(top, strip)))
        normed = (hat * gains[0:1] + shifts[0:1]).astype(BF16)
        for cut in hidden_chunks(hidden):
            pre = dot_nn(normed, w_in0[0, :, cut]) + b_in[0, :, cut]
            act0[:, cut] = gelu_only(pre).astype(BF16)
        mixed = dot_nt(act0[...], w_out0[0])
        row = lax.broadcasted_iota(jnp.int32, (strip, mid_cols, 1), 0) + (top - side) + place[0]
        col = lax.broadcasted_iota(jnp.int32, (strip, mid_cols, 1), 1) - 8 + place[1]
        real = (row >= 0) & (row < place[2]) & (col >= 0) & (col < place[3])
        real = jnp.where(real, 1.0, 0.0).reshape(count, 1)
        base = joined(xs, pl.ds(top + HALO, strip), slice(8, 8 + mid_cols))
        mid = (base + mixed).astype(BF16).astype(F32) * real
        split_to(mids, pl.ds(top, strip), mid, (strip, mid_cols))
        return carry

    lax.fori_loop(0, mid_rows // strip, one_strip, 0)

    conv_pass(mids, 0, 2, taps.at[1], zs1, dz_rows, dz_cols)
    strip1 = max(
        d for d in range(1, dz_rows + 1) if dz_rows % d == 0 and d * dz_cols <= 64 or d == 1
    )

    def one_norm(step, carry):
        top = step * strip1
        pixels = pl.ds(pl.multiple_of(top * dz_cols, 8), strip1 * dz_cols)
        hat, inv = norm_parts(joined(zs1, pl.ds(top, strip1)))
        row = lax.broadcasted_iota(jnp.int32, (strip1, dz_cols, 1), 0) + top
        col = lax.broadcasted_iota(jnp.int32, (strip1, dz_cols, 1), 1)
        own = (row >= HALO) & (row < HALO + rows) & (col >= HALO) & (col < HALO + cols)
        own = jnp.where(own, 1.0, 0.0).reshape(strip1 * dz_cols, 1)
        normed = hat * gains[1:2] + shifts[1:2]
        hat1[pixels, :] = hat
        normed1[pixels, :] = normed
        inv1[pixels, :] = jnp.broadcast_to(inv, (strip1 * dz_cols, LANES))
        inside[pixels, :] = jnp.broadcast_to(own, (strip1 * dz_cols, LANES))
        return carry

    lax.fori_loop(0, dz_rows // strip1, one_norm, 0)
    normed1_in[...] = (normed1[...] * inside[:, :1]).astype(BF16)
    normed_b = normed1[...].astype(BF16)
    waits[2].wait()
    waits[3].wait()
    mlp_grads(
        normed_b, normed1_in, gpad, gcenter, inside, w_in1, b_in.at[1], w_out1, act1, gpre1,
        dwi, dwo, db,
    )
    gain_sum = jnp.zeros((1, groups * LANES), F32)
    shift_sum = jnp.zeros((1, groups * LANES), F32)
    pixels = dz_rows * dz_cols
    step = max(d for d in range(16, 257, 16) if pixels % d == 0)
    for start in range(0, pixels, step):
        block = slice(start, start + step)
        dn = dot_nt(gpre1[block, :], w_in1[0])
        hat = hat1[block, :]
        kept = dn * inside[block, :1]
        gain_sum += jnp.sum(kept * hat, axis=0, keepdims=True)
        shift_sum += jnp.sum(kept, axis=0, keepdims=True)
        dz = norm_back(dn, hat, inv1[block, :1], gains[1:2])
        hat1[block, :] = dz.astype(BF16).astype(F32)
    dgain[...] = gain_sum
    dshift[...] = shift_sum
    for g in range(groups):
        dz_out[g] = hat1[:, g * LANES : (g + 1) * LANES].reshape(dz_rows, dz_cols, LANES)
    tap_pass(mids, side - HALO, 5, dz_out, HALO, HALO, dk, rows, cols)


def second_kernel(
    dz1, grad, z0, xpad, taps_back, gains, shifts, w_in, w_out, b_in,
    mid_out, dz_out, dwi, dwo, db, dgain, dshift, dk,
    xs, spread, dzs, normed, gmid, act, gpre, w_in0, w_out0, arrived,
):
    waits = fetch_layers(((w_in, 0, w_in0), (w_out, 0, w_out0)), arrived)
    groups, rows, cols = z0.shape[:3]
    pixels = rows * cols
    conv_pass(dz1, 0, 0, taps_back.at[1], spread, rows, cols)
    gm = (grad[...].astype(F32) + joined(spread, slice(None))).astype(BF16)
    gmid[...] = gm
    mid_out[...] = gm
    hat, inv = norm_parts(joined(z0, slice(None)))
    normed[...] = (hat * gains[0:1] + shifts[0:1]).astype(BF16)
    waits[0].wait()
    waits[1].wait()
    mlp_grads(
        normed, normed, gmid, gmid, None, w_in0, b_in.at[0], w_out0, act, gpre, dwi, dwo, db
    )
    dn = dot_nt(gpre[...], w_in0[0])
    dgain[...] = jnp.sum(dn * hat, axis=0, keepdims=True)
    dshift[...] = jnp.sum(dn, axis=0, keepdims=True)
    dz = norm_back(dn, hat, inv, gains[0:1]).astype(BF16)
    dz_out[...] = dz
    split_to(dzs, slice(None), dz.astype(F32), (rows, cols))
    skip = xpad.shape[0] // 2 - rows // 2 - HALO
    for g in range(groups):
        xs[g] = xpad[skip : skip + rows + 2 * HALO, :, g * LANES : (g + 1) * LANES].astype(F32)
    tap_pass(xs, 0, 13, dzs, 0, 0, dk, rows, cols)


def third_kernel(dzpad, gmid, taps_back, out, dzs, spread):
    for g in range(dzs.shape[0]):
        dzs[g] = dzpad[:, :, g * LANES : (g + 1) * LANES].astype(F32)
    rows, cols = spread.shape[1:3]
    conv_pass(dzs, 0, 5, taps_back.at[0], spread, rows, cols)
    out[...] = (gmid[...].astype(F32) + joined(spread, slice(None))).astype(BF16)


def shape(*dims, dtype=F32):
    return jax.ShapeDtypeStruct(dims, dtype)


def run(kernel, outs, scratch, args, specs=None, fetched=0, name=None):
    vmem = pl.BlockSpec(memory_space=pltpu.VMEM)
    semaphores = [pltpu.SemaphoreType.DMA((fetched,))] if fetched else []
    return pl.pallas_call(
        kernel,
        out_shape=outs,
        in_specs=[
            vmem if s is None else pl.BlockSpec(memory_space=s) for s in (specs or [None] * len(args))
        ],
        out_specs=tuple(vmem for _ in outs),
        scratch_shapes=[pltpu.VMEM(s.shape, s.dtype) for s in scratch] + semaphores,
        compiler_params=pltpu.CompilerParams(vmem_limit_bytes=50 * 1024 * 1024),
        name=name,
    )(*args)


def swap_edges(low_edge, high_edge, axis):
    count = lax.axis_size(axis)
    odd = lax.axis_index(axis) % 2 == 1
    first = lax.ppermute(
        jnp.where(odd, low_edge, high_edge), axis, [(i, i ^ 1) for i in range(count) if i ^ 1 < count]
    )
    pairs = [(i, i + 1) for i in range(1, count - 1, 2)]
    second = lax.ppermute(
        jnp.where(odd, high_edge, low_edge), axis, pairs + [(j, i) for i, j in pairs]
    )
    return jnp.where(odd, first, second), jnp.where(odd, second, first)


def padded_tile(tile, width):
    low, high = swap_edges(tile[:, :width], tile[:, -width:], "cols")
    wide = jnp.concatenate([low, tile, high], axis=1)
    low, high = swap_edges(wide[:width], wide[-width:], "rows")
    return jnp.concatenate([low, wide, high], axis=0)


def padded_pair(acts, grads):
    low, high = swap_edges(
        jnp.concatenate([acts[:, :WIDE], grads[:, :HALO]], axis=1),
        jnp.concatenate([acts[:, -WIDE:], grads[:, -HALO:]], axis=1),
        "cols",
    )
    acts = jnp.concatenate([low[:, :WIDE], acts, high[:, :WIDE]], axis=1)
    grads = jnp.concatenate([low[:, WIDE:], grads, high[:, WIDE:]], axis=1)
    room = ((0, 0), (0, acts.shape[1] - grads.shape[1]), (0, 0))
    low, high = swap_edges(
        jnp.concatenate([acts[:WIDE], jnp.pad(grads[:HALO], room)], axis=0),
        jnp.concatenate([acts[-WIDE:], jnp.pad(grads[-HALO:], room)], axis=0),
        "rows",
    )
    used = grads.shape[1]
    acts = jnp.concatenate([low[:WIDE], acts, high[:WIDE]], axis=0)
    grads = jnp.concatenate([low[WIDE:, :used], grads, high[WIDE:, :used]], axis=0)
    return acts, grads


def flip_bit(value, bit):
    both = ("rows", "cols")
    total = lax.axis_size("rows") * lax.axis_size("cols")
    return lax.ppermute(value, both, [(i, i ^ (1 << bit)) for i in range(total)])


def halves(chunks, dim, mine):
    other = lax.dynamic_index_in_dim(chunks, 1 - mine, dim, keepdims=False)
    own = lax.dynamic_index_in_dim(chunks, mine, dim, keepdims=False)
    return other, own


def summed(own, got):
    return (own.astype(F32) + got.astype(F32)).astype(BF16)


def shards(activations, grad_out, kernels, norm_gains, norm_shifts, w_in, b_in, w_out):
    rows, cols, channels = activations.shape
    layers, _, hidden = w_in.shape
    groups = channels // LANES
    n_rows, n_cols = lax.axis_size("rows"), lax.axis_size("cols")
    total = n_rows * n_cols
    bits = total.bit_length() - 1
    me = lax.axis_index("rows") * n_cols + lax.axis_index("cols")
    grad_scale = 1.0 / math.sqrt(rows * cols * total)

    taps = kernels.reshape(layers, 49, groups, LANES).transpose(0, 2, 1, 3)
    taps_back = taps[:, :, ::-1]
    biases = b_in[:, None, :]

    acts, grads = padded_pair(activations, grad_out)
    gap = 16 - WIDE
    xpad = jnp.pad(acts, ((0, 0), (gap, gap), (0, 0)))
    dz_rows, dz_cols = rows + 2 * HALO, cols + 8
    spare = dz_cols - cols - 2 * HALO
    gpad = jnp.pad(grads, ((0, 0), (0, spare), (0, 0))).reshape(-1, channels)
    gcenter = jnp.pad(
        grad_out, ((HALO, HALO), (HALO, HALO + spare), (0, 0))
    ).reshape(-1, channels)
    place = jnp.stack(
        [
            lax.axis_index("rows") * rows,
            lax.axis_index("cols") * cols,
            jnp.int32(rows * n_rows),
            jnp.int32(cols * n_cols),
        ]
    ).astype(jnp.int32)

    mid_rows, mid_cols = rows + 4 * HALO, cols + 16
    count = dz_rows * dz_cols
    strip = max(d for d in range(1, mid_rows + 1) if mid_rows % d == 0 and d * mid_cols <= 256)
    weights = [shape(1, channels, hidden, dtype=BF16)] * 2
    small_outs = (
        shape(hidden, channels, dtype=BF16), shape(hidden, channels, dtype=BF16),
        shape(1, hidden), shape(1, channels), shape(1, channels), shape(49, channels),
    )
    dz1, z0, *back1 = run(
        first_kernel,
        (shape(groups, dz_rows, dz_cols, LANES), shape(groups, rows, cols, LANES)) + small_outs,
        [
            shape(groups, *xpad.shape[:2], LANES),
            shape(groups, mid_rows, mid_cols, LANES),
            shape(groups, mid_rows, mid_cols, LANES),
            shape(groups, dz_rows, dz_cols, LANES),
            shape(strip * mid_cols, hidden, dtype=BF16),
            shape(count, channels),
            shape(count, LANES),
            shape(count, channels),
            shape(count, channels, dtype=BF16),
            shape(count, LANES),
            shape(count, hidden, dtype=BF16),
            shape(count, hidden, dtype=BF16),
        ]
        + weights * 2,
        (place, xpad, gpad, gcenter, taps, norm_gains, norm_shifts, w_in, w_out, biases),
        [pltpu.SMEM] + [None] * 6 + [pl.ANY] * 2 + [None],
        fetched=4,
        name="first",
    )
    pixels = rows * cols
    grad_mid, dz0, *back0 = run(
        second_kernel,
        (shape(pixels, channels, dtype=BF16), shape(pixels, channels, dtype=BF16)) + small_outs,
        [
            shape(groups, rows + 2 * HALO, xpad.shape[1], LANES),
            shape(groups, rows, cols, LANES),
            shape(groups, rows, cols, LANES),
            shape(pixels, channels, dtype=BF16),
            shape(pixels, channels, dtype=BF16),
            shape(pixels, hidden, dtype=BF16),
            shape(pixels, hidden, dtype=BF16),
        ]
        + weights,
        (dz1, grad_out.reshape(pixels, channels), z0, xpad, taps_back, norm_gains, norm_shifts,
         w_in, w_out, biases),
        [None] * 7 + [pl.ANY] * 2 + [None],
        fetched=2,
        name="second",
    )

    mine = [(me >> k) & 1 for k in range(bits)]
    per = hidden // total
    chunks = jnp.stack(
        [grad.reshape(total, per, channels) for back in (back0, back1) for grad in back[:2]], axis=1
    )
    small = jnp.concatenate(
        [part.reshape(-1) for back in (back0, back1) for part in back[2:]]
    ).astype(BF16)
    small_len = small.shape[0]
    small = jnp.pad(small, (0, -small_len % (16 * channels))).reshape(-1, channels)
    for k in range(bits):
        size = chunks.shape[0] // 2
        send, keep = halves(chunks.reshape(size, 2, -1, channels), 1, mine[k])
        send = send.reshape(-1, channels)
        got = flip_bit(jnp.concatenate([send, small], axis=0), k)
        edge = send.shape[0]
        chunks = summed(keep, got[:edge].reshape(keep.shape))
        small = summed(small, got[edge:])
    shares = chunks.reshape(layers, 2, per, channels).astype(F32) * grad_scale
    shares = jnp.swapaxes(shares, 2, 3)
    small = (small.astype(F32) * grad_scale).reshape(-1)[:small_len].reshape(layers, -1)

    dzpad = padded_tile(dz0.reshape(rows, cols, channels), HALO)
    dzpad = jnp.pad(dzpad, ((0, 0), (5, 16 - 5 - 2 * HALO), (0, 0)))
    (grad_in,) = run(
        third_kernel,
        (shape(pixels, channels, dtype=BF16),),
        [shape(groups, *dzpad.shape[:2], LANES), shape(groups, rows, cols, LANES)],
        (dzpad, grad_mid, taps_back),
        name="third",
    )
    cuts = [0, hidden, hidden + channels, hidden + 2 * channels, hidden + 51 * channels]
    parts = [small[:, a:b] for a, b in zip(cuts[:-1], cuts[1:])]
    return (
        grad_in.reshape(rows, cols, channels),
        parts[3].reshape(layers, 7, 7, channels),
        parts[1],
        parts[2],
        parts[0],
        shares[:, 0],
        shares[:, 1],
    )


def solution(mesh):
    tile = P("rows", "cols", None)
    sliced = P(None, None, ("rows", "cols"))
    return jax.shard_map(
        shards,
        mesh=mesh,
        in_specs=(tile, tile, P(), P(), P(), P(), P(), P()),
        out_specs=(tile, P(), P(), P(), P(), sliced, sliced),
        check_vma=False,
    )
```

```python
import functools
import math

import jax
import jax.numpy as jnp
from jax import lax
from jax.experimental import pallas as pl
from jax.experimental.pallas import tpu as pltpu
from jax.sharding import PartitionSpec as P

EPSILON = 1e-06
INV_ROOT_TAU = 0.3989422804014327
HALF_LOG2E = 0.7213475204444817
ERFC_SLOPE = 0.4 * 0.7071067811865476
ERFC_TERMS = (
    0.22479419400284972,
    0.2383621945582281,
    0.12991301634379934,
    0.4353236101490443,
    -0.41611664430523265,
    0.7235898182708315,
    -0.41436965913692125,
    0.07850346878444278,
)
LANES = 128
HALO = 3
WIDE = 2 * HALO
F32 = jnp.float32
BF16 = jnp.bfloat16


def normal_parts(x):
    bell = jnp.exp2(x * x * (-HALF_LOG2E))
    t = 1.0 / (1.0 + ERFC_SLOPE * jnp.abs(x))
    series = 0.5 * ERFC_TERMS[7]
    for term in ERFC_TERMS[6::-1]:
        series = series * t + 0.5 * term
    tail = series * t * bell
    return jnp.where(x >= 0, 1.0 - tail, tail), bell


def gelu_only(x):
    cdf, _ = normal_parts(x)
    return x * cdf


def gelu_parts(x):
    cdf, bell = normal_parts(x)
    return x * cdf, cdf + x * bell * INV_ROOT_TAU


def strip_rows(rows, cols):
    most = max(1, 288 // cols)
    return max(d for d in range(1, rows + 1) if rows % d == 0 and d <= most)


def conv_pass(source, row0, col0, taps, target, rows, cols):
    strip = strip_rows(rows, cols)
    groups = source.shape[0]

    def one_strip(step, carry):
        g = step // (rows // strip)
        top = (step % (rows // strip)) * strip
        sums = [jnp.zeros((cols, LANES), F32) for _ in range(strip)]
        for b in range(7):
            weights = [taps[g, pl.ds(7 * a + b, 1), :] for a in range(7)]
            for r in range(strip + 6):
                line = source[g, row0 + top + r, pl.ds(col0 + b, cols), :]
                for a in range(7):
                    if 0 <= r - a < strip:
                        sums[r - a] = sums[r - a] + weights[a] * line
        for i in range(strip):
            target[g, top + i] = sums[i]
        return carry

    lax.fori_loop(0, groups * (rows // strip), one_strip, 0)


def tap_pass(source, row0, col0, grad, grow0, gcol0, target, first, rows, cols):
    for g in range(source.shape[0]):
        lanes = slice(g * LANES, (g + 1) * LANES)
        for b in range(7):
            def one_row(i, sums):
                line = grad[g, grow0 + i, pl.ds(gcol0, cols), :]
                out = []
                for a in range(7):
                    part = line * source[g, row0 + i + a, pl.ds(col0 + b, cols), :]
                    out.append(sums[a] + part.reshape(cols // 8, 8, LANES).sum(0))
                return tuple(out)

            sums = lax.fori_loop(
                0, rows, one_row, tuple(jnp.zeros((8, LANES), F32) for _ in range(7)), unroll=4
            )
            for a in range(7):
                target[pl.ds(first + 7 * a + b, 1), lanes] = jnp.sum(sums[a], axis=0, keepdims=True)


def joined(ref, rows, cols=slice(None)):
    parts = [ref[g, rows, cols, :] for g in range(ref.shape[0])]
    return jnp.concatenate([p.reshape(-1, LANES) for p in parts], axis=1)


def split_to(ref, rows, value, shape):
    for g in range(ref.shape[0]):
        ref[g, rows] = value[:, g * LANES : (g + 1) * LANES].reshape(*shape, LANES)


def norm_parts(z):
    center = z - jnp.mean(z, axis=-1, keepdims=True)
    inv = lax.rsqrt(jnp.mean(center * center, axis=-1, keepdims=True) + EPSILON)
    return center * inv, inv


def norm_back(dn, hat, inv, gain):
    scaled = dn * gain
    return inv * (
        scaled
        - jnp.mean(scaled, axis=-1, keepdims=True)
        - hat * jnp.mean(scaled * hat, axis=-1, keepdims=True)
    )


def dot_nn(a, b):
    return jnp.dot(a, b, preferred_element_type=F32)


def dot_nt(a, b):
    return lax.dot_general(a, b, (((1,), (1,)), ((), ())), preferred_element_type=F32)


def dot_tn(a, b):
    return lax.dot_general(a, b, (((0,), (0,)), ((), ())), preferred_element_type=F32)


def pixel_blocks(pixels):
    best = max(d for d in range(16, 257, 16) if pixels % d == 0)
    return [slice(start, start + best) for start in range(0, pixels, best)]


def hidden_chunks(hidden):
    size = 256 if hidden % 256 == 0 else hidden
    return [slice(start, start + size) for start in range(0, hidden, size)]


def mlp_grads(normed, grad, w_in, b_in, w_out, act, gpre, dw, db):
    pixels = grad.shape[0]
    for cut in hidden_chunks(w_in.shape[2]):
        bias = b_in[:, cut]
        bias_sum = None
        for block in pixel_blocks(pixels):
            pre = dot_nn(normed[block, :], w_in[0, :, cut]) + bias
            value, slope = gelu_parts(pre)
            act[block, cut] = value.astype(BF16)
            gradient = dot_nn(grad[block, :], w_out[0, :, cut]) * slope
            gpre[block, cut] = gradient.astype(BF16)
            part = jnp.sum(gradient, axis=0, keepdims=True)
            bias_sum = part if bias_sum is None else bias_sum + part
        db[:, cut] = bias_sum
        dw[1, cut, :] = dot_tn(act[:, cut], grad[...]).astype(BF16)
        dw[0, cut, :] = dot_tn(gpre[:, cut], normed[...]).astype(BF16)


def fetch_layers(triples, arrived):
    copies = [
        pltpu.make_async_copy(source.at[pl.ds(layer, 1)], target, arrived.at[i])
        for i, (source, layer, target) in enumerate(triples)
    ]
    for copy in copies:
        copy.start()
    return copies


def block_back(z, grad, layer, gains, shifts, weights, b_in, outs, scratch):
    dz_out, dw, db, dgain, dshift = outs
    normed, act, gpre = scratch
    gain = gains[layer : layer + 1]
    hat, inv = norm_parts(joined(z, slice(None)))
    normed[...] = (hat * gain + shifts[layer : layer + 1]).astype(BF16)
    w_in, w_out, waits = weights
    for wait in waits:
        wait.wait()
    mlp_grads(normed, grad, w_in, b_in.at[layer], w_out, act, gpre, dw, db)
    dn = dot_nt(gpre[...], w_in[0])
    dgain[...] = jnp.sum(dn * hat, axis=0, keepdims=True)
    dshift[...] = jnp.sum(dn, axis=0, keepdims=True)
    dz_out[...] = norm_back(dn, hat, inv, gain).astype(BF16)


def forward_kernel(
    place, xpad, taps, gains, shifts, w_in, w_out, b_in, mids, z_out,
    xs, zs, act, w_in0, w_out0, arrived,
):
    waits = fetch_layers(((w_in, 0, w_in0), (w_out, 0, w_out0)), arrived)
    groups, mid_rows, mid_cols = zs.shape[:3]
    rows, cols = z_out.shape[1:3]
    for g in range(groups):
        xs[g] = xpad[:, :, g * LANES : (g + 1) * LANES].astype(F32)
    conv_pass(xs, 0, 0, taps.at[0], zs, mid_rows, mid_cols)
    z_out[...] = zs[:, HALO : HALO + rows, HALO : HALO + cols, :]
    strip = act.shape[0] // mid_cols
    for wait in waits:
        wait.wait()

    def one_strip(step, carry):
        top = step * strip
        hat, _ = norm_parts(joined(zs, pl.ds(top, strip)))
        normed = (hat * gains[0:1] + shifts[0:1]).astype(BF16)
        for cut in hidden_chunks(w_in0.shape[2]):
            pre = dot_nn(normed, w_in0[0, :, cut]) + b_in[0, :, cut]
            act[:, cut] = gelu_only(pre).astype(BF16)
        mixed = dot_nt(act[...], w_out0[0])
        row = lax.broadcasted_iota(jnp.int32, (strip, mid_cols, 1), 0) + (top - HALO) + place[0]
        col = lax.broadcasted_iota(jnp.int32, (strip, mid_cols, 1), 1) - HALO + place[1]
        real = (row >= 0) & (row < place[2]) & (col >= 0) & (col < place[3])
        real = jnp.where(real, 1.0, 0.0).reshape(strip * mid_cols, 1)
        base = joined(xs, pl.ds(top + HALO, strip), slice(HALO, HALO + mid_cols))
        mid = (base + mixed).astype(BF16).astype(F32) * real
        split_to(mids, pl.ds(top, strip), mid, (strip, mid_cols))
        return carry

    lax.fori_loop(0, mid_rows // strip, one_strip, 0)


def top_kernel(
    mids, grad, taps, gains, shifts, w_in, w_out, b_in, dz_out, dw, db, dgain, dshift,
    z, normed, act, gpre, w_in1, w_out1, arrived,
):
    waits = fetch_layers(((w_in, 1, w_in1), (w_out, 1, w_out1)), arrived)
    conv_pass(mids, 0, 0, taps.at[1], z, *z.shape[1:3])
    block_back(
        z, grad, 1, gains, shifts, (w_in1, w_out1, waits), b_in,
        (dz_out, dw, db, dgain, dshift), (normed, act, gpre),
    )


def low_kernel(
    dzpad, grad, z0, taps_back, gains, shifts, w_in, w_out, b_in,
    gmid, dz_out, dw, db, dgain, dshift,
    dzs, spread, normed, act, gpre, w_in0, w_out0, arrived,
):
    waits = fetch_layers(((w_in, 0, w_in0), (w_out, 0, w_out0)), arrived)
    spread_pass(dzpad, dzs, taps_back.at[1], spread)
    gmid[...] = (grad[...].astype(F32) + joined(spread, slice(None))).astype(BF16)
    block_back(
        z0, gmid, 0, gains, shifts, (w_in0, w_out0, waits), b_in,
        (dz_out, dw, db, dgain, dshift), (normed, act, gpre),
    )


def spread_pass(dzpad, dzs, taps_back, spread):
    for g in range(dzs.shape[0]):
        dzs[g] = dzpad[:, :, g * LANES : (g + 1) * LANES].astype(F32)
    conv_pass(dzs, 0, 0, taps_back, spread, *spread.shape[1:3])


def last_kernel(dzpad, gmid, taps_back, out, dzs, spread):
    spread_pass(dzpad, dzs, taps_back.at[0], spread)
    out[...] = (gmid[...].astype(F32) + joined(spread, slice(None))).astype(BF16)


def taps_kernel(source, row0, col0, dz, db, dgain, dshift, out, xs, dzs, sums):
    rows, cols = dzs.shape[1:3]
    channels = out.shape[1]
    split_to(dzs, slice(None), dz[...].astype(F32), (rows, cols))
    if xs is None:
        values = source
    else:
        for g in range(dzs.shape[0]):
            xs[g] = source[:, :, g * LANES : (g + 1) * LANES].astype(F32)
        values = xs
    sums[...] = jnp.zeros(sums.shape, F32)
    count = db.shape[1] // channels
    for k in range(count):
        sums[k : k + 1, :] = db[:, k * channels : (k + 1) * channels]
    sums[count : count + 1, :] = dgain[...]
    sums[count + 1 : count + 2, :] = dshift[...]
    tap_pass(values, row0, col0, dzs, 0, 0, sums, count + 2, rows, cols)
    out[...] = sums[...].astype(BF16)


def top_taps_kernel(source, dz, db, dgain, dshift, out, dzs, sums):
    taps_kernel(source, 0, 0, dz, db, dgain, dshift, out, None, dzs, sums)


def low_taps_kernel(source, dz, db, dgain, dshift, out, xs, dzs, sums):
    taps_kernel(source, HALO, HALO, dz, db, dgain, dshift, out, xs, dzs, sums)


def shape(*dims, dtype=F32):
    return jax.ShapeDtypeStruct(dims, dtype)


def run(kernel, outs, scratch, args, specs=None, fetched=0, name=None):
    vmem = pl.BlockSpec(memory_space=pltpu.VMEM)
    semaphores = [pltpu.SemaphoreType.DMA((fetched,))] if fetched else []
    return pl.pallas_call(
        kernel,
        out_shape=outs,
        in_specs=[
            vmem if s is None else pl.BlockSpec(memory_space=s) for s in (specs or [None] * len(args))
        ],
        out_specs=tuple(vmem for _ in outs),
        scratch_shapes=[pltpu.VMEM(s.shape, s.dtype) for s in scratch] + semaphores,
        compiler_params=pltpu.CompilerParams(vmem_limit_bytes=50 * 1024 * 1024),
        name=name,
    )(*args)


def swap_edges(low_edge, high_edge, axis):
    count = lax.axis_size(axis)
    odd = lax.axis_index(axis) % 2 == 1
    first = lax.ppermute(
        jnp.where(odd, low_edge, high_edge), axis, [(i, i ^ 1) for i in range(count) if i ^ 1 < count]
    )
    pairs = [(i, i + 1) for i in range(1, count - 1, 2)]
    second = lax.ppermute(
        jnp.where(odd, high_edge, low_edge), axis, pairs + [(j, i) for i, j in pairs]
    )
    return jnp.where(odd, first, second), jnp.where(odd, second, first)


def edges(tile, axis):
    count = tile.shape[axis]
    return (
        lax.slice_in_dim(tile, 0, HALO, axis=axis),
        lax.slice_in_dim(tile, count - HALO, count, axis=axis),
    )


def padded_tile(tile, width):
    low, high = swap_edges(tile[:, :width], tile[:, -width:], "cols")
    wide = jnp.concatenate([low, tile, high], axis=1)
    low, high = swap_edges(wide[:width], wide[-width:], "rows")
    return jnp.concatenate([low, wide, high], axis=0)


def flip_bit(value, bit):
    both = ("rows", "cols")
    total = lax.axis_size("rows") * lax.axis_size("cols")
    return lax.ppermute(value, both, [(i, i ^ (1 << bit)) for i in range(total)])


def halves(chunks, dim, mine):
    other = lax.dynamic_index_in_dim(chunks, 1 - mine, dim, keepdims=False)
    own = lax.dynamic_index_in_dim(chunks, mine, dim, keepdims=False)
    return other, own


def summed(own, got):
    return (own.astype(F32) + got.astype(F32)).astype(BF16)


def step(chunks, order, bit, mine):
    spot = order.index(bit)
    per = chunks.shape[-2:]
    pair = chunks.reshape((-1, 2 ** spot, 2, 2 ** (len(order) - spot - 1)) + per)
    send, keep = halves(pair, 2, mine[bit])
    return keep, flip_bit(send, bit), [b for b in order if b != bit]


def shards(activations, grad_out, kernels, norm_gains, norm_shifts, w_in, b_in, w_out):
    rows, cols, channels = activations.shape
    layers, _, hidden = w_in.shape
    groups = channels // LANES
    n_rows, n_cols = lax.axis_size("rows"), lax.axis_size("cols")
    total = n_rows * n_cols
    bits = total.bit_length() - 1
    col_bits = n_cols.bit_length() - 1
    me = lax.axis_index("rows") * n_cols + lax.axis_index("cols")
    mine = [(me >> k) & 1 for k in range(bits)]
    grad_scale = 1.0 / math.sqrt(rows * cols * total)
    pixels = rows * cols

    taps = kernels.reshape(layers, 49, groups, LANES).transpose(0, 2, 1, 3)
    taps_back = taps[:, :, ::-1]
    biases = b_in[:, None, :]
    place = jnp.stack(
        [
            lax.axis_index("rows") * rows,
            lax.axis_index("cols") * cols,
            jnp.int32(rows * n_rows),
            jnp.int32(cols * n_cols),
        ]
    ).astype(jnp.int32)
    grad_flat = grad_out.reshape(pixels, channels)

    def widened(tile, width, to):
        wide = padded_tile(tile, width)
        return jnp.pad(wide, ((0, 0), (0, to - wide.shape[1]), (0, 0)))

    mid_rows, mid_cols = rows + 2 * HALO, cols + 8
    strip = max(d for d in range(1, mid_rows + 1) if mid_rows % d == 0 and d * mid_cols <= 264)
    weights = [shape(1, channels, hidden, dtype=BF16)] * 2
    tile_scratch = [
        shape(pixels, channels, dtype=BF16),
        shape(pixels, hidden, dtype=BF16),
        shape(pixels, hidden, dtype=BF16),
    ] + weights
    tile_z = shape(groups, rows, cols, LANES)
    tile_b = shape(pixels, channels, dtype=BF16)
    back_outs = (
        tile_b, shape(2, hidden, channels, dtype=BF16),
        shape(1, hidden), shape(1, channels), shape(1, channels),
    )
    small_rows = 64

    xpad = widened(activations, WIDE, cols + 16)
    mids, z0 = run(
        forward_kernel,
        (shape(groups, mid_rows, mid_cols, LANES), tile_z),
        [
            shape(groups, *xpad.shape[:2], LANES),
            shape(groups, mid_rows, mid_cols, LANES),
            shape(strip * mid_cols, hidden, dtype=BF16),
        ]
        + weights,
        (place, xpad, taps, norm_gains, norm_shifts, w_in, w_out, biases),
        [pltpu.SMEM] + [None] * 4 + [pl.ANY] * 2 + [None],
        fetched=2,
        name="forward",
    )
    dz1, dw1, *small1 = run(
        top_kernel,
        back_outs,
        [tile_z] + tile_scratch,
        (mids, grad_flat, taps, norm_gains, norm_shifts, w_in, w_out, biases),
        [None] * 5 + [pl.ANY] * 2 + [None],
        fetched=2,
        name="top",
    )
    fence = lax.optimization_barrier
    per = hidden // total
    every = list(range(bits - 1, -1, -1))
    sides = (col_bits - 1, col_bits)

    def start(dw):
        chunks, order = dw.reshape(2, total, per, channels), every
        for bit in range(col_bits - 2):
            keep, got, order = step(chunks, order, bit, mine)
            chunks = summed(keep, got)
        if col_bits > 1:
            return step(chunks, order, col_bits - 2, mine)
        return chunks, None, order

    def settled(flight):
        keep, got, order = flight
        return (keep if got is None else summed(keep, got)), order

    def fork(flight):
        chunks, order = settled(flight)
        return [step(chunks[i], order, sides[i], mine) for i in range(2)]

    def cross(flights):
        done = [settled(f) for f in flights]
        return [step(done[i][0], done[i][1], sides[1 - i], mine) for i in range(2)]

    def merge(flights):
        done = [settled(f) for f in flights]
        return jnp.stack([d[0].reshape(-1, per, channels) for d in done]), done[0][1]

    def onward(chunks, order):
        return step(chunks, order, order[-1], mine)

    def fenced(values):
        leaves, tree = jax.tree.flatten(values)
        arrays = [i for i, leaf in enumerate(leaves) if not isinstance(leaf, int)]
        for i, value in zip(arrays, fence(tuple(leaves[i] for i in arrays))):
            leaves[i] = value
        return jax.tree.unflatten(tree, leaves)

    dz1, dw1 = fence((dz1, dw1))
    sides1 = swap_edges(*edges(dz1.reshape(rows, cols, channels), 1), "cols")
    run1 = start(dw1)
    (small1,) = run(
        top_taps_kernel,
        (shape(small_rows, channels, dtype=BF16),),
        [tile_z, shape(small_rows, channels)],
        (mids, dz1, *small1),
        name="top_taps",
    )
    sides1, dz1, small1 = fenced((sides1, dz1, small1))
    wide1 = jnp.concatenate([sides1[0], dz1.reshape(rows, cols, channels), sides1[1]], axis=1)
    ends1 = swap_edges(*edges(wide1, 0), "rows")
    ends1, wide1, run1 = fenced((ends1, wide1, run1))
    pair1 = fork(run1)
    dzpad1 = jnp.pad(
        jnp.concatenate([ends1[0], wide1, ends1[1]], axis=0),
        ((0, 0), (0, 16 - 2 * HALO), (0, 0)),
    )
    spread_scratch = [shape(groups, *dzpad1.shape[:2], LANES), tile_z]
    grad_mid, dz0, dw0, *small0 = run(
        low_kernel,
        (tile_b,) + back_outs,
        spread_scratch + tile_scratch,
        (dzpad1, grad_flat, z0, taps_back, norm_gains, norm_shifts, w_in, w_out, biases),
        [None] * 6 + [pl.ANY] * 2 + [None],
        fetched=2,
        name="low",
    )
    dz0, dw0, pair1 = fenced((dz0, dw0, pair1))
    run0 = start(dw0)
    pair1 = cross(pair1)
    sides0 = swap_edges(*edges(dz0.reshape(rows, cols, channels), 1), "cols")
    (small0,) = run(
        low_taps_kernel,
        (shape(small_rows, channels, dtype=BF16),),
        [shape(groups, *xpad.shape[:2], LANES), tile_z, shape(small_rows, channels)],
        (xpad, dz0, *small0),
        name="low_taps",
    )
    small = jnp.concatenate([small0, small1], axis=0)
    run0, pair1, sides0, small, dz0 = fenced((run0, pair1, sides0, small, dz0))
    pair0 = fork(run0)
    wide0 = jnp.concatenate([sides0[0], dz0.reshape(rows, cols, channels), sides0[1]], axis=1)
    ends0 = swap_edges(*edges(wide0, 0), "rows")
    run1 = onward(*merge(pair1))
    small_got = flip_bit(small, 0)
    ends0, wide0, run1, small, small_got = fenced((ends0, wide0, run1, small, small_got))
    run1 = onward(*settled(run1)) if len(run1[2]) else run1
    small = summed(small, small_got)
    small_got = flip_bit(small, 1)
    dzpad0 = jnp.pad(
        jnp.concatenate([ends0[0], wide0, ends0[1]], axis=0),
        ((0, 0), (0, 16 - 2 * HALO), (0, 0)),
    )
    (grad_in,) = run(
        last_kernel, (tile_b,), spread_scratch, (dzpad0, grad_mid, taps_back), name="last"
    )
    pair0, run1, small, small_got, grad_in = fenced((pair0, run1, small, small_got, grad_in))
    pair0 = cross(pair0)
    small = summed(small, small_got)
    small_got = flip_bit(small, 2)

    def finish(flight):
        chunks, order = settled(flight)
        while order:
            chunks, order = settled(onward(chunks, order))
        return jnp.swapaxes(chunks.reshape(2, per, channels).astype(F32) * grad_scale, 1, 2)

    share1 = finish(run1)
    pair0, small, small_got = fenced((pair0, small, small_got))
    run0 = onward(*merge(pair0))
    small = summed(small, small_got)
    bit = 3
    while run0[2]:
        small_got = flip_bit(small, bit)
        run0, small, small_got = fenced((run0, small, small_got))
        run0 = onward(*settled(run0))
        small = summed(small, small_got)
        bit += 1
    for left in range(bit, bits):
        small = summed(small, flip_bit(small, left))
    shares = [finish(run0), share1]
    small = small.reshape(layers, small_rows, channels).astype(F32) * grad_scale
    count = hidden // channels
    return (
        grad_in.reshape(rows, cols, channels),
        small[:, count + 2 : count + 51].reshape(layers, 7, 7, channels),
        small[:, count],
        small[:, count + 1],
        small[:, :count].reshape(layers, hidden),
        jnp.stack([share[0] for share in shares]),
        jnp.stack([share[1] for share in shares]),
    )


def solution(mesh):
    tile = P("rows", "cols", None)
    sliced = P(None, None, ("rows", "cols"))
    return jax.shard_map(
        shards,
        mesh=mesh,
        in_specs=(tile, tile, P(), P(), P(), P(), P(), P()),
        out_specs=(tile, P(), P(), P(), P(), sliced, sliced),
        check_vma=False,
    )
```

```python
import functools
import math

import jax
import jax.numpy as jnp
from jax import lax
from jax.experimental import pallas as pl
from jax.experimental.pallas import tpu as pltpu
from jax.sharding import PartitionSpec as P

EPSILON = 1e-06
INV_ROOT_TAU = 0.3989422804014327
HALF_LOG2E = 0.7213475204444817
ERFC_SLOPE = 0.4 * 0.7071067811865476
ERFC_TERMS = (
    0.22479419400284972,
    0.2383621945582281,
    0.12991301634379934,
    0.4353236101490443,
    -0.41611664430523265,
    0.7235898182708315,
    -0.41436965913692125,
    0.07850346878444278,
)
LANES = 128
HALO = 3
WIDE = 2 * HALO
F32 = jnp.float32
BF16 = jnp.bfloat16


def normal_parts(x):
    bell = jnp.exp2(x * x * (-HALF_LOG2E))
    t = 1.0 / (1.0 + ERFC_SLOPE * jnp.abs(x))
    series = 0.5 * ERFC_TERMS[7]
    for term in ERFC_TERMS[6::-1]:
        series = series * t + 0.5 * term
    tail = series * t * bell
    return jnp.where(x >= 0, 1.0 - tail, tail), bell


def gelu_only(x):
    cdf, _ = normal_parts(x)
    return x * cdf


def gelu_parts(x):
    cdf, bell = normal_parts(x)
    return x * cdf, cdf + x * bell * INV_ROOT_TAU


def strip_rows(rows, cols):
    most = max(1, 288 // cols)
    return max(d for d in range(1, rows + 1) if rows % d == 0 and d <= most)


def conv_pass(source, row0, col0, taps, target, rows, cols):
    strip = strip_rows(rows, cols)
    groups = source.shape[0]

    def one_strip(step, carry):
        g = step // (rows // strip)
        top = (step % (rows // strip)) * strip
        sums = [jnp.zeros((cols, LANES), F32) for _ in range(strip)]
        for b in range(7):
            weights = [taps[g, pl.ds(7 * a + b, 1), :] for a in range(7)]
            for r in range(strip + 6):
                line = source[g, row0 + top + r, pl.ds(col0 + b, cols), :]
                for a in range(7):
                    if 0 <= r - a < strip:
                        sums[r - a] = sums[r - a] + weights[a] * line
        for i in range(strip):
            target[g, top + i] = sums[i]
        return carry

    lax.fori_loop(0, groups * (rows // strip), one_strip, 0)


def tap_pass(source, row0, col0, grad, grow0, gcol0, target, first, rows, cols):
    for g in range(source.shape[0]):
        lanes = slice(g * LANES, (g + 1) * LANES)
        for b in range(7):
            def one_row(i, sums):
                line = grad[g, grow0 + i, pl.ds(gcol0, cols), :]
                out = []
                for a in range(7):
                    part = line * source[g, row0 + i + a, pl.ds(col0 + b, cols), :]
                    out.append(sums[a] + part.reshape(cols // 8, 8, LANES).sum(0))
                return tuple(out)

            sums = lax.fori_loop(
                0, rows, one_row, tuple(jnp.zeros((8, LANES), F32) for _ in range(7)), unroll=4
            )
            for a in range(7):
                target[pl.ds(first + 7 * a + b, 1), lanes] = jnp.sum(sums[a], axis=0, keepdims=True)


def joined(ref, rows, cols=slice(None)):
    parts = [ref[g, rows, cols, :] for g in range(ref.shape[0])]
    return jnp.concatenate([p.reshape(-1, LANES) for p in parts], axis=1)


def split_to(ref, rows, value, shape):
    for g in range(ref.shape[0]):
        ref[g, rows] = value[:, g * LANES : (g + 1) * LANES].reshape(*shape, LANES)


def norm_parts(z):
    center = z - jnp.mean(z, axis=-1, keepdims=True)
    inv = lax.rsqrt(jnp.mean(center * center, axis=-1, keepdims=True) + EPSILON)
    return center * inv, inv


def norm_back(dn, hat, inv, gain):
    scaled = dn * gain
    return inv * (
        scaled
        - jnp.mean(scaled, axis=-1, keepdims=True)
        - hat * jnp.mean(scaled * hat, axis=-1, keepdims=True)
    )


def dot_nn(a, b):
    return jnp.dot(a, b, preferred_element_type=F32)


def dot_nt(a, b):
    return lax.dot_general(a, b, (((1,), (1,)), ((), ())), preferred_element_type=F32)


def dot_tn(a, b):
    return lax.dot_general(a, b, (((0,), (0,)), ((), ())), preferred_element_type=F32)


def pixel_blocks(pixels):
    best = max(d for d in range(16, 257, 16) if pixels % d == 0)
    return [slice(start, start + best) for start in range(0, pixels, best)]


def hidden_chunks(hidden):
    size = 256 if hidden % 256 == 0 else hidden
    return [slice(start, start + size) for start in range(0, hidden, size)]


def mlp_grads(normed, grad, w_in, b_in, w_out, act, gpre, dw, db):
    pixels = grad.shape[0]
    for cut in hidden_chunks(w_in.shape[2]):
        bias = b_in[:, cut]
        bias_sum = None
        for block in pixel_blocks(pixels):
            pre = dot_nn(normed[block, :], w_in[0, :, cut]) + bias
            value, slope = gelu_parts(pre)
            act[block, cut] = value.astype(BF16)
            gradient = dot_nn(grad[block, :], w_out[0, :, cut]) * slope
            gpre[block, cut] = gradient.astype(BF16)
            part = jnp.sum(gradient, axis=0, keepdims=True)
            bias_sum = part if bias_sum is None else bias_sum + part
        db[:, cut] = bias_sum
        if dw is not None:
            weight_grads(normed, grad, act, gpre, dw, cut)


def weight_grads(normed, grad, act, gpre, dw, cut):
    dw[1, cut, :] = dot_tn(act[:, cut], grad[...]).astype(BF16)
    dw[0, cut, :] = dot_tn(gpre[:, cut], normed[...]).astype(BF16)


def fetch_layers(triples, arrived):
    copies = [
        pltpu.make_async_copy(source.at[pl.ds(layer, 1)], target, arrived.at[i])
        for i, (source, layer, target) in enumerate(triples)
    ]
    for copy in copies:
        copy.start()
    return copies


def block_back(z, grad, layer, gains, shifts, weights, b_in, outs, scratch):
    dz_out, dw, db, dgain, dshift = outs
    normed, act, gpre = scratch
    gain = gains[layer : layer + 1]
    hat, inv = norm_parts(joined(z, slice(None)))
    normed[...] = (hat * gain + shifts[layer : layer + 1]).astype(BF16)
    w_in, w_out, waits = weights
    for wait in waits:
        wait.wait()
    mlp_grads(normed, grad, w_in, b_in.at[layer], w_out, act, gpre, dw, db)
    dn = dot_nt(gpre[...], w_in[0])
    dgain[...] = jnp.sum(dn * hat, axis=0, keepdims=True)
    dshift[...] = jnp.sum(dn, axis=0, keepdims=True)
    dz_out[...] = norm_back(dn, hat, inv, gain).astype(BF16)


def forward_kernel(
    place, xpad, taps, gains, shifts, w_in, w_out, b_in, mids, z_out,
    xs, zs, act, w_in0, w_out0, arrived,
):
    waits = fetch_layers(((w_in, 0, w_in0), (w_out, 0, w_out0)), arrived)
    groups, mid_rows, mid_cols = zs.shape[:3]
    rows, cols = z_out.shape[1:3]
    for g in range(groups):
        xs[g] = xpad[:, :, g * LANES : (g + 1) * LANES].astype(F32)
    conv_pass(xs, 0, 0, taps.at[0], zs, mid_rows, mid_cols)
    z_out[...] = zs[:, HALO : HALO + rows, HALO : HALO + cols, :]
    strip = act.shape[0] // mid_cols
    for wait in waits:
        wait.wait()

    def one_strip(step, carry):
        top = step * strip
        hat, _ = norm_parts(joined(zs, pl.ds(top, strip)))
        normed = (hat * gains[0:1] + shifts[0:1]).astype(BF16)
        for cut in hidden_chunks(w_in0.shape[2]):
            pre = dot_nn(normed, w_in0[0, :, cut]) + b_in[0, :, cut]
            act[:, cut] = gelu_only(pre).astype(BF16)
        mixed = dot_nt(act[...], w_out0[0])
        row = lax.broadcasted_iota(jnp.int32, (strip, mid_cols, 1), 0) + (top - HALO) + place[0]
        col = lax.broadcasted_iota(jnp.int32, (strip, mid_cols, 1), 1) - HALO + place[1]
        real = (row >= 0) & (row < place[2]) & (col >= 0) & (col < place[3])
        real = jnp.where(real, 1.0, 0.0).reshape(strip * mid_cols, 1)
        base = joined(xs, pl.ds(top + HALO, strip), slice(HALO, HALO + mid_cols))
        mid = (base + mixed).astype(BF16).astype(F32) * real
        split_to(mids, pl.ds(top, strip), mid, (strip, mid_cols))
        return carry

    lax.fori_loop(0, mid_rows // strip, one_strip, 0)


def top_kernel(
    mids, grad, taps, gains, shifts, w_in, w_out, b_in,
    dz_out, normed, act, gpre, db, dgain, dshift, z, w_in1, w_out1, arrived,
):
    waits = fetch_layers(((w_in, 1, w_in1), (w_out, 1, w_out1)), arrived)
    conv_pass(mids, 0, 0, taps.at[1], z, *z.shape[1:3])
    block_back(
        z, grad, 1, gains, shifts, (w_in1, w_out1, waits), b_in,
        (dz_out, None, db, dgain, dshift), (normed, act, gpre),
    )


def low_kernel(
    dzpad, grad, z0, taps_back, gains, shifts, w_in, w_out, b_in,
    gmid, dz_out, dw, db, dgain, dshift,
    dzs, spread, normed, act, gpre, w_in0, w_out0, arrived,
):
    waits = fetch_layers(((w_in, 0, w_in0), (w_out, 0, w_out0)), arrived)
    spread_pass(dzpad, dzs, taps_back.at[1], spread)
    gmid[...] = (grad[...].astype(F32) + joined(spread, slice(None))).astype(BF16)
    block_back(
        z0, gmid, 0, gains, shifts, (w_in0, w_out0, waits), b_in,
        (dz_out, dw, db, dgain, dshift), (normed, act, gpre),
    )


def spread_pass(dzpad, dzs, taps_back, spread):
    for g in range(dzs.shape[0]):
        dzs[g] = dzpad[:, :, g * LANES : (g + 1) * LANES].astype(F32)
    conv_pass(dzs, 0, 0, taps_back, spread, *spread.shape[1:3])


def last_kernel(dzpad, gmid, taps_back, out, dzs, spread):
    spread_pass(dzpad, dzs, taps_back.at[0], spread)
    out[...] = (gmid[...].astype(F32) + joined(spread, slice(None))).astype(BF16)


def taps_kernel(source, row0, col0, dz, db, dgain, dshift, out, xs, dzs, sums):
    rows, cols = dzs.shape[1:3]
    channels = out.shape[1]
    split_to(dzs, slice(None), dz[...].astype(F32), (rows, cols))
    if xs is None:
        values = source
    else:
        for g in range(dzs.shape[0]):
            xs[g] = source[:, :, g * LANES : (g + 1) * LANES].astype(F32)
        values = xs
    sums[...] = jnp.zeros(sums.shape, F32)
    count = db.shape[1] // channels
    for k in range(count):
        sums[k : k + 1, :] = db[:, k * channels : (k + 1) * channels]
    sums[count : count + 1, :] = dgain[...]
    sums[count + 1 : count + 2, :] = dshift[...]
    tap_pass(values, row0, col0, dzs, 0, 0, sums, count + 2, rows, cols)
    out[...] = sums[...].astype(BF16)


def top_taps_kernel(source, dz, normed, act, gpre, grad, db, dgain, dshift, dw, out, dzs, sums):
    for cut in hidden_chunks(act.shape[1]):
        weight_grads(normed, grad, act, gpre, dw, cut)
    taps_kernel(source, 0, 0, dz, db, dgain, dshift, out, None, dzs, sums)


def low_taps_kernel(source, dz, db, dgain, dshift, out, xs, dzs, sums):
    taps_kernel(source, HALO, HALO, dz, db, dgain, dshift, out, xs, dzs, sums)


def shape(*dims, dtype=F32):
    return jax.ShapeDtypeStruct(dims, dtype)


def run(kernel, outs, scratch, args, specs=None, fetched=0, name=None):
    vmem = pl.BlockSpec(memory_space=pltpu.VMEM)
    semaphores = [pltpu.SemaphoreType.DMA((fetched,))] if fetched else []
    return pl.pallas_call(
        kernel,
        out_shape=outs,
        in_specs=[
            vmem if s is None else pl.BlockSpec(memory_space=s) for s in (specs or [None] * len(args))
        ],
        out_specs=tuple(vmem for _ in outs),
        scratch_shapes=[pltpu.VMEM(s.shape, s.dtype) for s in scratch] + semaphores,
        compiler_params=pltpu.CompilerParams(vmem_limit_bytes=50 * 1024 * 1024),
        name=name,
    )(*args)


def edges(tile, axis, width, odd):
    count = tile.shape[axis]
    low = lax.slice_in_dim(tile, 0, width, axis=axis)
    high = lax.slice_in_dim(tile, count - width, count, axis=axis)
    return jnp.where(odd, low, high), jnp.where(odd, high, low)


def to_twin(edge, axis):
    count = lax.axis_size(axis)
    return lax.ppermute(edge, axis, [(i, i ^ 1) for i in range(count) if i ^ 1 < count])


def to_other(edge, axis):
    pairs = [(i, i + 1) for i in range(1, lax.axis_size(axis) - 1, 2)]
    return lax.ppermute(edge, axis, pairs + [(j, i) for i, j in pairs])


def rimmed(tile, from_twin, from_other, axis, odd):
    low = jnp.where(odd, from_twin, from_other)
    high = jnp.where(odd, from_other, from_twin)
    return jnp.concatenate([low, tile, high], axis=axis)


def flip_bit(value, bit):
    both = ("rows", "cols")
    total = lax.axis_size("rows") * lax.axis_size("cols")
    return lax.ppermute(value, both, [(i, i ^ (1 << bit)) for i in range(total)])


def halves(chunks, dim, mine):
    other = lax.dynamic_index_in_dim(chunks, 1 - mine, dim, keepdims=False)
    own = lax.dynamic_index_in_dim(chunks, mine, dim, keepdims=False)
    return other, own


def summed(own, got):
    return (own.astype(F32) + got.astype(F32)).astype(BF16)


def step(chunks, order, bit, mine, *riders):
    spot = order.index(bit)
    per = chunks.shape[-2:]
    pair = chunks.reshape((-1, 2 ** spot, 2, 2 ** (len(order) - spot - 1)) + per)
    send, keep = halves(pair, 2, mine[bit])
    left = [b for b in order if b != bit]
    if not riders:
        return keep, flip_bit(send, bit), left, ()
    parts = [part.reshape(-1, per[-1]) for part in (send,) + riders]
    got = flip_bit(jnp.concatenate(parts, axis=0), bit)
    came, first = [], 0
    for part, like in zip(parts, (send,) + riders):
        came.append(got[first : first + part.shape[0]].reshape(like.shape))
        first += part.shape[0]
    return keep, came[0], left, tuple(came[1:])


def shards(activations, grad_out, kernels, norm_gains, norm_shifts, w_in, b_in, w_out):
    rows, cols, channels = activations.shape
    layers, _, hidden = w_in.shape
    groups = channels // LANES
    n_rows, n_cols = lax.axis_size("rows"), lax.axis_size("cols")
    total = n_rows * n_cols
    bits = total.bit_length() - 1
    col_bits = n_cols.bit_length() - 1
    me = lax.axis_index("rows") * n_cols + lax.axis_index("cols")
    mine = [(me >> k) & 1 for k in range(bits)]
    grad_scale = 1.0 / math.sqrt(rows * cols * total)
    pixels = rows * cols

    taps = kernels.reshape(layers, 49, groups, LANES).transpose(0, 2, 1, 3)
    taps_back = taps[:, :, ::-1]
    biases = b_in[:, None, :]
    place = jnp.stack(
        [
            lax.axis_index("rows") * rows,
            lax.axis_index("cols") * cols,
            jnp.int32(rows * n_rows),
            jnp.int32(cols * n_cols),
        ]
    ).astype(jnp.int32)
    grad_flat = grad_out.reshape(pixels, channels)

    odd_col = lax.axis_index("cols") % 2 == 1
    odd_row = lax.axis_index("rows") % 2 == 1

    def rim_cols(tile, width):
        twin, other = edges(tile, 1, width, odd_col)
        return rimmed(tile, to_twin(twin, "cols"), to_other(other, "cols"), 1, odd_col)

    def rim_rows(tile, width):
        twin, other = edges(tile, 0, width, odd_row)
        return rimmed(tile, to_twin(twin, "rows"), to_other(other, "rows"), 0, odd_row)

    def filled(wide):
        return jnp.pad(wide, ((0, 0), (0, cols + 16 - wide.shape[1]), (0, 0)))

    mid_rows, mid_cols = rows + 2 * HALO, cols + 8
    strip = max(d for d in range(1, mid_rows + 1) if mid_rows % d == 0 and d * mid_cols <= 264)
    weights = [shape(1, channels, hidden, dtype=BF16)] * 2
    tile_z = shape(groups, rows, cols, LANES)
    tile_b = shape(pixels, channels, dtype=BF16)
    tile_h = shape(pixels, hidden, dtype=BF16)
    grads_b = shape(2, hidden, channels, dtype=BF16)
    small_outs = (shape(1, hidden), shape(1, channels), shape(1, channels))
    small_rows = 64

    xpad = filled(rim_rows(rim_cols(activations, WIDE), WIDE))
    mids, z0 = run(
        forward_kernel,
        (shape(groups, mid_rows, mid_cols, LANES), tile_z),
        [
            shape(groups, *xpad.shape[:2], LANES),
            shape(groups, mid_rows, mid_cols, LANES),
            shape(strip * mid_cols, hidden, dtype=BF16),
        ]
        + weights,
        (place, xpad, taps, norm_gains, norm_shifts, w_in, w_out, biases),
        [pltpu.SMEM] + [None] * 4 + [pl.ANY] * 2 + [None],
        fetched=2,
        name="forward",
    )
    dz1, normed1, act1, gpre1, *small1 = run(
        top_kernel,
        (tile_b, tile_b, tile_h, tile_h) + small_outs,
        [tile_z] + weights,
        (mids, grad_flat, taps, norm_gains, norm_shifts, w_in, w_out, biases),
        [None] * 5 + [pl.ANY] * 2 + [None],
        fetched=2,
        name="top",
    )

    per = hidden // total
    sides = (col_bits - 1, col_bits)

    def fenced(*values):
        leaves, tree = jax.tree.flatten(values)
        arrays = [i for i, leaf in enumerate(leaves) if not isinstance(leaf, int)]
        for i, value in zip(arrays, lax.optimization_barrier(tuple(leaves[i] for i in arrays))):
            leaves[i] = value
        return jax.tree.unflatten(tree, leaves)

    def settled(flight):
        return summed(flight[0], flight[1]), flight[2]

    def start(dw, small, *riders):
        chunks, order = dw.reshape(2, total, per, channels), list(range(bits - 1, -1, -1))
        came = ()
        for bit in range(col_bits - 1):
            if bit:
                chunks, order = settled(flight)
                small = [summed(s, g) for s, g in zip(small, small_got)]
            flight = step(chunks, order, bit, mine, *small, *(() if bit else riders))
            small_got = flight[3][: len(small)]
            came = came or flight[3][len(small) :]
        return flight[:3], small, small_got, came

    def fork(flight, first=(), second=()):
        chunks, order = settled(flight)
        return [step(chunks[i], order, sides[i], mine, *r) for i, r in enumerate((first, second))]

    def cross(flights, first=()):
        done = [settled(f) for f in flights]
        return [step(*done[i], sides[1 - i], mine, *r) for i, r in enumerate((first, ()))]

    def merge(flights):
        done = [settled(f) for f in flights]
        return jnp.stack([d[0].reshape(-1, per, channels) for d in done]), done[0][1]

    def onward(chunks, order, *riders):
        return step(chunks, order, order[-1], mine, *riders)

    def finish(flight):
        chunks, order = settled(flight)
        while order:
            chunks, order = settled(onward(chunks, order))
        return jnp.swapaxes(chunks.reshape(2, per, channels).astype(F32) * grad_scale, 1, 2)

    tile1 = dz1.reshape(rows, cols, channels)
    twin, other = edges(tile1, 1, HALO, odd_col)
    twin, other = to_twin(twin, "cols"), to_other(other, "cols")
    dw1, small1 = run(
        top_taps_kernel,
        (grads_b, shape(small_rows, channels, dtype=BF16)),
        [tile_z, shape(small_rows, channels)],
        (mids, dz1, normed1, act1, gpre1, grad_flat, *small1),
        name="top_taps",
    )
    tile1, twin, other, dw1, small1 = fenced(tile1, twin, other, dw1, small1)
    wide1 = rimmed(tile1, twin, other, 1, odd_col)
    run1, _, _, _ = start(dw1, [])
    twin, other = edges(wide1, 0, HALO, odd_row)
    twin, other = to_twin(twin, "rows"), to_other(other, "rows")
    wide1, twin, other, run1 = fenced(wide1, twin, other, run1)
    pair1 = fork(run1)
    dzpad1 = filled(rimmed(wide1, twin, other, 0, odd_row))
    spread_scratch = [shape(groups, *dzpad1.shape[:2], LANES), tile_z]
    grad_mid, dz0, dw0, *small0 = run(
        low_kernel,
        (tile_b, tile_b, grads_b) + small_outs,
        spread_scratch + [tile_b, tile_h, tile_h] + weights,
        (dzpad1, grad_flat, z0, taps_back, norm_gains, norm_shifts, w_in, w_out, biases),
        [None] * 6 + [pl.ANY] * 2 + [None],
        fetched=2,
        name="low",
    )
    (small0,) = run(
        low_taps_kernel,
        (shape(small_rows, channels, dtype=BF16),),
        [shape(groups, *xpad.shape[:2], LANES), tile_z, shape(small_rows, channels)],
        (xpad, dz0, *small0),
        name="low_taps",
    )
    dz0, dw0, pair1, small0 = fenced(dz0, dw0, pair1, small0)
    tile0 = dz0.reshape(rows, cols, channels)
    small = jnp.concatenate([small0, small1], axis=0)
    twin, other = edges(tile0, 1, HALO, odd_col)
    run0, (small,), small_got, (twin,) = start(dw0, [small], twin)
    other = to_other(other, "cols")
    pair1 = cross(pair1)
    run0, small, small_got, tile0, twin, other = fenced(run0, small, small_got, tile0, twin, other)
    small = summed(small, small_got[0])
    wide0 = rimmed(tile0, twin, other, 1, odd_col)
    twin, other = edges(wide0, 0, HALO, odd_row)
    pair0 = fork(run0, (small,), (twin,))
    other = to_other(other, "rows")
    pair0, pair1, small, wide0, other = fenced(pair0, pair1, small, wide0, other)
    small = summed(small, pair0[0][3][0])
    twin = pair0[1][3][0]
    pair0 = cross(pair0, (small,))
    run1 = onward(*merge(pair1))
    (grad_in,) = run(
        last_kernel,
        (tile_b,),
        spread_scratch,
        (filled(rimmed(wide0, twin, other, 0, odd_row)), grad_mid, taps_back),
        name="last",
    )
    pair0, run1, small, grad_in = fenced(pair0, run1, small, grad_in)
    small = summed(small, pair0[0][3][0])
    run0 = onward(*merge(pair0), small)
    share1 = finish(run1)
    while run0[2]:
        run0, small = fenced(run0, small)
        small = summed(small, run0[3][0])
        run0 = onward(*settled(run0), small)
    small = summed(small, run0[3][0])
    shares = [finish(run0), share1]
    small = small.reshape(layers, small_rows, channels).astype(F32) * grad_scale
    count = hidden // channels
    return (
        grad_in.reshape(rows, cols, channels),
        small[:, count + 2 : count + 51].reshape(layers, 7, 7, channels),
        small[:, count],
        small[:, count + 1],
        small[:, :count].reshape(layers, hidden),
        jnp.stack([share[0] for share in shares]),
        jnp.stack([share[1] for share in shares]),
    )


def solution(mesh):
    tile = P("rows", "cols", None)
    sliced = P(None, None, ("rows", "cols"))
    return jax.shard_map(
        shards,
        mesh=mesh,
        in_specs=(tile, tile, P(), P(), P(), P(), P(), P()),
        out_specs=(tile, P(), P(), P(), P(), sliced, sliced),
        check_vma=False,
    )
```

```python
import functools
import math

import jax
import jax.numpy as jnp
from jax import lax
from jax.experimental import pallas as pl
from jax.experimental.pallas import tpu as pltpu
from jax.sharding import PartitionSpec as P

EPSILON = 1e-06
INV_ROOT_TAU = 0.3989422804014327
HALF_LOG2E = 0.7213475204444817
ERFC_SLOPE = 0.4 * 0.7071067811865476
ERFC_TERMS = (
    0.22479419400284972,
    0.2383621945582281,
    0.12991301634379934,
    0.4353236101490443,
    -0.41611664430523265,
    0.7235898182708315,
    -0.41436965913692125,
    0.07850346878444278,
)
LANES = 128
HALO = 3
WIDE = 2 * HALO
F32 = jnp.float32
BF16 = jnp.bfloat16


def normal_parts(x):
    bell = jnp.exp2(x * x * (-HALF_LOG2E))
    t = 1.0 / (1.0 + ERFC_SLOPE * jnp.abs(x))
    series = 0.5 * ERFC_TERMS[7]
    for term in ERFC_TERMS[6::-1]:
        series = series * t + 0.5 * term
    tail = series * t * bell
    return jnp.where(x >= 0, 1.0 - tail, tail), bell


def gelu_only(x):
    cdf, _ = normal_parts(x)
    return x * cdf


def gelu_parts(x):
    cdf, bell = normal_parts(x)
    return x * cdf, cdf + x * bell * INV_ROOT_TAU


def strip_rows(rows, cols):
    most = max(1, 288 // cols)
    return max(d for d in range(1, rows + 1) if rows % d == 0 and d <= most)


def conv_pass(source, row0, col0, taps, target, rows, cols):
    strip = strip_rows(rows, cols)
    groups = source.shape[0]

    def one_strip(step, carry):
        g = step // (rows // strip)
        top = (step % (rows // strip)) * strip
        sums = [jnp.zeros((cols, LANES), F32) for _ in range(strip)]
        for b in range(7):
            weights = [taps[g, pl.ds(7 * a + b, 1), :] for a in range(7)]
            for r in range(strip + 6):
                line = source[g, row0 + top + r, pl.ds(col0 + b, cols), :]
                for a in range(7):
                    if 0 <= r - a < strip:
                        sums[r - a] = sums[r - a] + weights[a] * line
        for i in range(strip):
            target[g, top + i] = sums[i]
        return carry

    lax.fori_loop(0, groups * (rows // strip), one_strip, 0)


def tap_pass(source, row0, col0, grad, grow0, gcol0, target, first, rows, cols):
    for g in range(source.shape[0]):
        lanes = slice(g * LANES, (g + 1) * LANES)
        for b in range(7):
            def one_row(i, sums):
                line = grad[g, grow0 + i, pl.ds(gcol0, cols), :]
                out = []
                for a in range(7):
                    part = line * source[g, row0 + i + a, pl.ds(col0 + b, cols), :]
                    out.append(sums[a] + part.reshape(cols // 8, 8, LANES).sum(0))
                return tuple(out)

            sums = lax.fori_loop(
                0, rows, one_row, tuple(jnp.zeros((8, LANES), F32) for _ in range(7)), unroll=4
            )
            for a in range(7):
                target[pl.ds(first + 7 * a + b, 1), lanes] = jnp.sum(sums[a], axis=0, keepdims=True)


def joined(ref, rows, cols=slice(None)):
    parts = [ref[g, rows, cols, :] for g in range(ref.shape[0])]
    return jnp.concatenate([p.reshape(-1, LANES) for p in parts], axis=1)


def split_to(ref, rows, value, shape):
    for g in range(ref.shape[0]):
        ref[g, rows] = value[:, g * LANES : (g + 1) * LANES].reshape(*shape, LANES)


def norm_parts(z):
    center = z - jnp.mean(z, axis=-1, keepdims=True)
    inv = lax.rsqrt(jnp.mean(center * center, axis=-1, keepdims=True) + EPSILON)
    return center * inv, inv


def norm_back(dn, hat, inv, gain):
    scaled = dn * gain
    return inv * (
        scaled
        - jnp.mean(scaled, axis=-1, keepdims=True)
        - hat * jnp.mean(scaled * hat, axis=-1, keepdims=True)
    )


def dot_nn(a, b):
    return jnp.dot(a, b, preferred_element_type=F32)


def dot_nt(a, b):
    return lax.dot_general(a, b, (((1,), (1,)), ((), ())), preferred_element_type=F32)


def dot_tn(a, b):
    return lax.dot_general(a, b, (((0,), (0,)), ((), ())), preferred_element_type=F32)


def pixel_blocks(pixels):
    best = max(d for d in range(16, 257, 16) if pixels % d == 0)
    return [slice(start, start + best) for start in range(0, pixels, best)]


def hidden_chunks(hidden):
    size = 256 if hidden % 256 == 0 else hidden
    return [slice(start, start + size) for start in range(0, hidden, size)]


def mlp_grads(normed, grad, w_in, b_in, w_out, act, gpre, dw, db):
    pixels = grad.shape[0]
    for cut in hidden_chunks(w_in.shape[2]):
        bias = b_in[:, cut]
        bias_sum = None
        for block in pixel_blocks(pixels):
            pre = dot_nn(normed[block, :], w_in[0, :, cut]) + bias
            value, slope = gelu_parts(pre)
            act[block, cut] = value.astype(BF16)
            gradient = dot_nn(grad[block, :], w_out[0, :, cut]) * slope
            gpre[block, cut] = gradient.astype(BF16)
            part = jnp.sum(gradient, axis=0, keepdims=True)
            bias_sum = part if bias_sum is None else bias_sum + part
        db[:, cut] = bias_sum
        if dw is not None:
            weight_grads(normed, grad, act, gpre, dw, cut)


def weight_grads(normed, grad, act, gpre, dw, cut):
    dw[1, cut, :] = dot_tn(act[:, cut], grad[...]).astype(BF16)
    dw[0, cut, :] = dot_tn(gpre[:, cut], normed[...]).astype(BF16)


def fetch_layers(triples, arrived):
    copies = [
        pltpu.make_async_copy(source.at[pl.ds(layer, 1)], target, arrived.at[i])
        for i, (source, layer, target) in enumerate(triples)
    ]
    for copy in copies:
        copy.start()
    return copies


def block_back(z, grad, layer, gains, shifts, weights, b_in, outs, scratch):
    dz_out, dw, db, dgain, dshift = outs
    normed, act, gpre = scratch
    gain = gains[layer : layer + 1]
    hat, inv = norm_parts(joined(z, slice(None)))
    normed[...] = (hat * gain + shifts[layer : layer + 1]).astype(BF16)
    w_in, w_out, waits = weights
    for wait in waits:
        wait.wait()
    mlp_grads(normed, grad, w_in, b_in.at[layer], w_out, act, gpre, dw, db)
    dn = dot_nt(gpre[...], w_in[0])
    dgain[...] = jnp.sum(dn * hat, axis=0, keepdims=True)
    dshift[...] = jnp.sum(dn, axis=0, keepdims=True)
    dz_out[...] = norm_back(dn, hat, inv, gain).astype(BF16)


def forward_kernel(
    place, xpad, taps, gains, shifts, w_in, w_out, b_in, mids, z_out,
    xs, zs, act, w_in0, w_out0, arrived,
):
    waits = fetch_layers(((w_in, 0, w_in0), (w_out, 0, w_out0)), arrived)
    groups, mid_rows, mid_cols = zs.shape[:3]
    rows, cols = z_out.shape[1:3]
    for g in range(groups):
        xs[g] = xpad[:, :, g * LANES : (g + 1) * LANES].astype(F32)
    conv_pass(xs, 0, 0, taps.at[0], zs, mid_rows, mid_cols)
    z_out[...] = zs[:, HALO : HALO + rows, HALO : HALO + cols, :]
    strip = act.shape[0] // mid_cols
    for wait in waits:
        wait.wait()

    def one_strip(step, carry):
        top = step * strip
        hat, _ = norm_parts(joined(zs, pl.ds(top, strip)))
        normed = (hat * gains[0:1] + shifts[0:1]).astype(BF16)
        for cut in hidden_chunks(w_in0.shape[2]):
            pre = dot_nn(normed, w_in0[0, :, cut]) + b_in[0, :, cut]
            act[:, cut] = gelu_only(pre).astype(BF16)
        mixed = dot_nt(act[...], w_out0[0])
        row = lax.broadcasted_iota(jnp.int32, (strip, mid_cols, 1), 0) + (top - HALO) + place[0]
        col = lax.broadcasted_iota(jnp.int32, (strip, mid_cols, 1), 1) - HALO + place[1]
        real = (row >= 0) & (row < place[2]) & (col >= 0) & (col < place[3])
        real = jnp.where(real, 1.0, 0.0).reshape(strip * mid_cols, 1)
        base = joined(xs, pl.ds(top + HALO, strip), slice(HALO, HALO + mid_cols))
        mid = (base + mixed).astype(BF16).astype(F32) * real
        split_to(mids, pl.ds(top, strip), mid, (strip, mid_cols))
        return carry

    lax.fori_loop(0, mid_rows // strip, one_strip, 0)


def top_kernel(
    mids, grad, taps, gains, shifts, w_in, w_out, b_in,
    dz_out, normed, act, gpre, db, dgain, dshift, z, w_in1, w_out1, arrived,
):
    waits = fetch_layers(((w_in, 1, w_in1), (w_out, 1, w_out1)), arrived)
    conv_pass(mids, 0, 0, taps.at[1], z, *z.shape[1:3])
    block_back(
        z, grad, 1, gains, shifts, (w_in1, w_out1, waits), b_in,
        (dz_out, None, db, dgain, dshift), (normed, act, gpre),
    )


def low_kernel(
    dzpad, grad, z0, taps_back, gains, shifts, w_in, w_out, b_in,
    gmid, dz_out, dw, db, dgain, dshift,
    dzs, spread, normed, act, gpre, w_in0, w_out0, arrived,
):
    waits = fetch_layers(((w_in, 0, w_in0), (w_out, 0, w_out0)), arrived)
    spread_pass(dzpad, dzs, taps_back.at[1], spread)
    gmid[...] = (grad[...].astype(F32) + joined(spread, slice(None))).astype(BF16)
    block_back(
        z0, gmid, 0, gains, shifts, (w_in0, w_out0, waits), b_in,
        (dz_out, dw, db, dgain, dshift), (normed, act, gpre),
    )


def spread_pass(dzpad, dzs, taps_back, spread):
    for g in range(dzs.shape[0]):
        dzs[g] = dzpad[:, :, g * LANES : (g + 1) * LANES].astype(F32)
    conv_pass(dzs, 0, 0, taps_back, spread, *spread.shape[1:3])


def last_kernel(dzpad, gmid, taps_back, out, dzs, spread):
    spread_pass(dzpad, dzs, taps_back.at[0], spread)
    out[...] = (gmid[...].astype(F32) + joined(spread, slice(None))).astype(BF16)


def taps_kernel(source, row0, col0, dz, db, dgain, dshift, out, xs, dzs, sums):
    rows, cols = dzs.shape[1:3]
    channels = out.shape[1]
    split_to(dzs, slice(None), dz[...].astype(F32), (rows, cols))
    if xs is None:
        values = source
    else:
        for g in range(dzs.shape[0]):
            xs[g] = source[:, :, g * LANES : (g + 1) * LANES].astype(F32)
        values = xs
    sums[...] = jnp.zeros(sums.shape, F32)
    count = db.shape[1] // channels
    for k in range(count):
        sums[k : k + 1, :] = db[:, k * channels : (k + 1) * channels]
    sums[count : count + 1, :] = dgain[...]
    sums[count + 1 : count + 2, :] = dshift[...]
    tap_pass(values, row0, col0, dzs, 0, 0, sums, count + 2, rows, cols)
    out[...] = sums[...].astype(BF16)


def top_taps_kernel(source, dz, normed, act, gpre, grad, db, dgain, dshift, dw, out, dzs, sums):
    for cut in hidden_chunks(act.shape[1]):
        weight_grads(normed, grad, act, gpre, dw, cut)
    taps_kernel(source, 0, 0, dz, db, dgain, dshift, out, None, dzs, sums)


def low_taps_kernel(source, dz, db, dgain, dshift, out, xs, dzs, sums):
    taps_kernel(source, HALO, HALO, dz, db, dgain, dshift, out, xs, dzs, sums)


def shape(*dims, dtype=F32):
    return jax.ShapeDtypeStruct(dims, dtype)


def run(kernel, outs, scratch, args, specs=None, fetched=0, name=None):
    vmem = pl.BlockSpec(memory_space=pltpu.VMEM)
    semaphores = [pltpu.SemaphoreType.DMA((fetched,))] if fetched else []
    return pl.pallas_call(
        kernel,
        out_shape=outs,
        in_specs=[
            vmem if s is None else pl.BlockSpec(memory_space=s) for s in (specs or [None] * len(args))
        ],
        out_specs=tuple(vmem for _ in outs),
        scratch_shapes=[pltpu.VMEM(s.shape, s.dtype) for s in scratch] + semaphores,
        compiler_params=pltpu.CompilerParams(vmem_limit_bytes=24 * 1024 * 1024),
        name=name,
    )(*args)


def edges(tile, axis, width, odd):
    count = tile.shape[axis]
    low = lax.slice_in_dim(tile, 0, width, axis=axis)
    high = lax.slice_in_dim(tile, count - width, count, axis=axis)
    return jnp.where(odd, low, high), jnp.where(odd, high, low)


def to_twin(edge, axis):
    count = lax.axis_size(axis)
    return lax.ppermute(edge, axis, [(i, i ^ 1) for i in range(count) if i ^ 1 < count])


def to_other(edge, axis):
    pairs = [(i, i + 1) for i in range(1, lax.axis_size(axis) - 1, 2)]
    return lax.ppermute(edge, axis, pairs + [(j, i) for i, j in pairs])


def rimmed(tile, from_twin, from_other, axis, odd):
    low = jnp.where(odd, from_twin, from_other)
    high = jnp.where(odd, from_other, from_twin)
    return jnp.concatenate([low, tile, high], axis=axis)


def flip_bit(value, bit):
    both = ("rows", "cols")
    total = lax.axis_size("rows") * lax.axis_size("cols")
    return lax.ppermute(value, both, [(i, i ^ (1 << bit)) for i in range(total)])


def halves(chunks, dim, mine):
    other = lax.dynamic_index_in_dim(chunks, 1 - mine, dim, keepdims=False)
    own = lax.dynamic_index_in_dim(chunks, mine, dim, keepdims=False)
    return other, own


def summed(own, got):
    return (own.astype(F32) + got.astype(F32)).astype(BF16)


def step(chunks, order, bit, mine):
    spot = order.index(bit)
    per = chunks.shape[-2:]
    pair = chunks.reshape((-1, 2 ** spot, 2, 2 ** (len(order) - spot - 1)) + per)
    send, keep = halves(pair, 2, mine[bit])
    return keep, flip_bit(send, bit), [b for b in order if b != bit]


def shards(activations, grad_out, kernels, norm_gains, norm_shifts, w_in, b_in, w_out):
    rows, cols, channels = activations.shape
    layers, _, hidden = w_in.shape
    groups = channels // LANES
    n_rows, n_cols = lax.axis_size("rows"), lax.axis_size("cols")
    total = n_rows * n_cols
    bits = total.bit_length() - 1
    col_bits = n_cols.bit_length() - 1
    me = lax.axis_index("rows") * n_cols + lax.axis_index("cols")
    mine = [(me >> k) & 1 for k in range(bits)]
    grad_scale = 1.0 / math.sqrt(rows * cols * total)
    pixels = rows * cols

    taps = kernels.reshape(layers, 49, groups, LANES).transpose(0, 2, 1, 3)
    taps_back = taps[:, :, ::-1]
    biases = b_in[:, None, :]
    place = jnp.stack(
        [
            lax.axis_index("rows") * rows,
            lax.axis_index("cols") * cols,
            jnp.int32(rows * n_rows),
            jnp.int32(cols * n_cols),
        ]
    ).astype(jnp.int32)
    grad_flat = grad_out.reshape(pixels, channels)

    odd_col = lax.axis_index("cols") % 2 == 1
    odd_row = lax.axis_index("rows") % 2 == 1

    def rim_cols(tile, width):
        twin, other = edges(tile, 1, width, odd_col)
        return rimmed(tile, to_twin(twin, "cols"), to_other(other, "cols"), 1, odd_col)

    def rim_rows(tile, width):
        twin, other = edges(tile, 0, width, odd_row)
        return rimmed(tile, to_twin(twin, "rows"), to_other(other, "rows"), 0, odd_row)

    def filled(wide):
        return jnp.pad(wide, ((0, 0), (0, cols + 16 - wide.shape[1]), (0, 0)))

    mid_rows, mid_cols = rows + 2 * HALO, cols + 8
    strip = max(d for d in range(1, mid_rows + 1) if mid_rows % d == 0 and d * mid_cols <= 264)
    weights = [shape(1, channels, hidden, dtype=BF16)] * 2
    tile_z = shape(groups, rows, cols, LANES)
    tile_b = shape(pixels, channels, dtype=BF16)
    tile_h = shape(pixels, hidden, dtype=BF16)
    grads_b = shape(2, hidden, channels, dtype=BF16)
    small_outs = (shape(1, hidden), shape(1, channels), shape(1, channels))
    small_rows = 64

    xpad = filled(rim_rows(rim_cols(activations, WIDE), WIDE))
    mids, z0 = run(
        forward_kernel,
        (shape(groups, mid_rows, mid_cols, LANES), tile_z),
        [
            shape(groups, *xpad.shape[:2], LANES),
            shape(groups, mid_rows, mid_cols, LANES),
            shape(strip * mid_cols, hidden, dtype=BF16),
        ]
        + weights,
        (place, xpad, taps, norm_gains, norm_shifts, w_in, w_out, biases),
        [pltpu.SMEM] + [None] * 4 + [pl.ANY] * 2 + [None],
        fetched=2,
        name="forward",
    )
    dz1, normed1, act1, gpre1, *small1 = run(
        top_kernel,
        (tile_b, tile_b, tile_h, tile_h) + small_outs,
        [tile_z] + weights,
        (mids, grad_flat, taps, norm_gains, norm_shifts, w_in, w_out, biases),
        [None] * 5 + [pl.ANY] * 2 + [None],
        fetched=2,
        name="top",
    )

    per = hidden // total
    sides = (col_bits - 1, col_bits)

    def fenced(*values):
        leaves, tree = jax.tree.flatten(values)
        arrays = [i for i, leaf in enumerate(leaves) if not isinstance(leaf, int)]
        for i, value in zip(arrays, lax.optimization_barrier(tuple(leaves[i] for i in arrays))):
            leaves[i] = value
        return jax.tree.unflatten(tree, leaves)

    def settled(flight):
        return summed(flight[0], flight[1]), flight[2]

    def start(dw):
        chunks, order = dw.reshape(2, total, per, channels), list(range(bits - 1, -1, -1))
        for bit in range(col_bits - 2):
            chunks, order = settled(step(chunks, order, bit, mine))
        return step(chunks, order, col_bits - 2, mine)

    def fork(flight):
        chunks, order = settled(flight)
        return [step(chunks[i], order, sides[i], mine) for i in range(2)]

    def cross(flights):
        done = [settled(f) for f in flights]
        return [step(*done[i], sides[1 - i], mine) for i in range(2)]

    def merge(flights):
        done = [settled(f) for f in flights]
        return jnp.stack([d[0].reshape(-1, per, channels) for d in done]), done[0][1]

    def onward(chunks, order):
        return step(chunks, order, order[-1], mine) if order else (chunks, jnp.zeros_like(chunks), order)

    def finish(flight):
        chunks, order = settled(flight)
        while order:
            chunks, order = settled(onward(chunks, order))
        return jnp.swapaxes(chunks.reshape(2, per, channels).astype(F32) * grad_scale, 1, 2)

    tile1 = dz1.reshape(rows, cols, channels)
    twin, other = edges(tile1, 1, HALO, odd_col)
    twin, other = to_twin(twin, "cols"), to_other(other, "cols")
    dw1, small1 = run(
        top_taps_kernel,
        (grads_b, shape(small_rows, channels, dtype=BF16)),
        [tile_z, shape(small_rows, channels)],
        (mids, dz1, normed1, act1, gpre1, grad_flat, *small1),
        name="top_taps",
    )
    tile1, twin, other, dw1, small1 = fenced(tile1, twin, other, dw1, small1)
    wide1 = rimmed(tile1, twin, other, 1, odd_col)
    run1 = start(dw1)
    twin, other = edges(wide1, 0, HALO, odd_row)
    twin, other = to_twin(twin, "rows"), to_other(other, "rows")
    wide1, twin, other, run1 = fenced(wide1, twin, other, run1)
    pair1 = fork(run1)
    dzpad1 = filled(rimmed(wide1, twin, other, 0, odd_row))
    spread_scratch = [shape(groups, *dzpad1.shape[:2], LANES), tile_z]
    grad_mid, dz0, dw0, *small0 = run(
        low_kernel,
        (tile_b, tile_b, grads_b) + small_outs,
        spread_scratch + [tile_b, tile_h, tile_h] + weights,
        (dzpad1, grad_flat, z0, taps_back, norm_gains, norm_shifts, w_in, w_out, biases),
        [None] * 6 + [pl.ANY] * 2 + [None],
        fetched=2,
        name="low",
    )
    dz0, dw0, pair1, *small0 = fenced(dz0, dw0, pair1, *small0)
    run0 = start(dw0)
    pair1 = cross(pair1)
    tile0 = dz0.reshape(rows, cols, channels)
    twin, other = edges(tile0, 1, HALO, odd_col)
    twin = to_twin(twin, "cols")
    (small0,) = run(
        low_taps_kernel,
        (shape(small_rows, channels, dtype=BF16),),
        [shape(groups, *xpad.shape[:2], LANES), tile_z, shape(small_rows, channels)],
        (xpad, dz0, *small0),
        name="low_taps",
    )
    small = jnp.concatenate([small0, small1], axis=0)
    small_got = flip_bit(small, 0)
    run0, pair1, small, small_got, tile0, twin, other = fenced(
        run0, pair1, small, small_got, tile0, twin, other
    )
    pair0 = fork(run0)
    run1 = onward(*merge(pair1))
    other = to_other(other, "cols")
    small = summed(small, small_got)
    small_got = flip_bit(small, 1)
    pair0, run1, tile0, twin, other, small, small_got = fenced(
        pair0, run1, tile0, twin, other, small, small_got
    )
    pair0 = cross(pair0)
    run1 = onward(*settled(run1))
    wide0 = rimmed(tile0, twin, other, 1, odd_col)
    twin, other = edges(wide0, 0, HALO, odd_row)
    twin = to_twin(twin, "rows")
    small = summed(small, small_got)
    small_got = flip_bit(small, 2)
    pair0, run1, wide0, twin, other, small, small_got = fenced(
        pair0, run1, wide0, twin, other, small, small_got
    )
    run0 = onward(*merge(pair0))
    other = to_other(other, "rows")
    share1 = finish(run1)
    wait = (wide0, twin, other)
    for bit in range(3, bits):
        small = summed(small, small_got)
        small_got = flip_bit(small, bit)
        if run0[2]:
            run0, small, small_got, wait = fenced(run0, small, small_got, wait)
            run0 = onward(*settled(run0))
        if bit == 3:
            (wait,) = run(
                last_kernel,
                (tile_b,),
                spread_scratch,
                (filled(rimmed(*wait, 0, odd_row)), grad_mid, taps_back),
                name="last",
            )
    grad_in = wait
    small = summed(small, small_got)
    shares = [finish(run0), share1]
    small = small.reshape(layers, small_rows, channels).astype(F32) * grad_scale
    count = hidden // channels
    return (
        grad_in.reshape(rows, cols, channels),
        small[:, count + 2 : count + 51].reshape(layers, 7, 7, channels),
        small[:, count],
        small[:, count + 1],
        small[:, :count].reshape(layers, hidden),
        jnp.stack([share[0] for share in shares]),
        jnp.stack([share[1] for share in shares]),
    )


def solution(mesh):
    tile = P("rows", "cols", None)
    sliced = P(None, None, ("rows", "cols"))
    return jax.shard_map(
        shards,
        mesh=mesh,
        in_specs=(tile, tile, P(), P(), P(), P(), P(), P()),
        out_specs=(tile, P(), P(), P(), P(), sliced, sliced),
        check_vma=False,
    )
```

```python
import functools
import math

import jax
import jax.numpy as jnp
from jax import lax
from jax.experimental import pallas as pl
from jax.experimental.pallas import tpu as pltpu
from jax.sharding import PartitionSpec as P

EPSILON = 1e-06
INV_ROOT_TAU = 0.3989422804014327
HALF_LOG2E = 0.7213475204444817
ERFC_SLOPE = 0.4 * 0.7071067811865476
ERFC_TERMS = (
    0.22479419400284972,
    0.2383621945582281,
    0.12991301634379934,
    0.4353236101490443,
    -0.41611664430523265,
    0.7235898182708315,
    -0.41436965913692125,
    0.07850346878444278,
)
LANES = 128
HALO = 3
WIDE = 2 * HALO
F32 = jnp.float32
BF16 = jnp.bfloat16


def normal_parts(x):
    bell = jnp.exp2(x * x * (-HALF_LOG2E))
    t = 1.0 / (1.0 + ERFC_SLOPE * jnp.abs(x))
    series = 0.5 * ERFC_TERMS[7]
    for term in ERFC_TERMS[6::-1]:
        series = series * t + 0.5 * term
    tail = series * t * bell
    return jnp.where(x >= 0, 1.0 - tail, tail), bell


def gelu_only(x):
    cdf, _ = normal_parts(x)
    return x * cdf


def gelu_parts(x):
    cdf, bell = normal_parts(x)
    return x * cdf, cdf + x * bell * INV_ROOT_TAU


def strip_rows(rows, cols):
    most = max(1, 288 // cols)
    return max(d for d in range(1, rows + 1) if rows % d == 0 and d <= most)


def conv_pass(source, row0, col0, taps, target, rows, cols, back=False):
    strip = strip_rows(rows, cols)
    groups = source.shape[0]

    def one_strip(step, carry):
        g = step // (rows // strip)
        top = (step % (rows // strip)) * strip
        sums = [jnp.zeros((cols, LANES), F32) for _ in range(strip)]
        for b in range(7):
            spots = [48 - 7 * a - b if back else 7 * a + b for a in range(7)]
            weights = [taps[g, pl.ds(spot, 1), :] for spot in spots]
            for r in range(strip + 6):
                line = source[g, row0 + top + r, pl.ds(col0 + b, cols), :]
                for a in range(7):
                    if 0 <= r - a < strip:
                        sums[r - a] = sums[r - a] + weights[a] * line
        for i in range(strip):
            target[g, top + i] = sums[i]
        return carry

    lax.fori_loop(0, groups * (rows // strip), one_strip, 0)


def tap_pass(source, row0, col0, grad, grow0, gcol0, target, first, rows, cols):
    for g in range(source.shape[0]):
        lanes = slice(g * LANES, (g + 1) * LANES)
        for b in range(7):
            def one_row(i, sums):
                line = grad[g, grow0 + i, pl.ds(gcol0, cols), :]
                out = []
                for a in range(7):
                    part = line * source[g, row0 + i + a, pl.ds(col0 + b, cols), :]
                    out.append(sums[a] + part.reshape(cols // 8, 8, LANES).sum(0))
                return tuple(out)

            sums = lax.fori_loop(
                0, rows, one_row, tuple(jnp.zeros((8, LANES), F32) for _ in range(7)), unroll=4
            )
            for a in range(7):
                target[pl.ds(first + 7 * a + b, 1), lanes] = jnp.sum(sums[a], axis=0, keepdims=True)


def joined(ref, rows, cols=slice(None)):
    parts = [ref[g, rows, cols, :] for g in range(ref.shape[0])]
    return jnp.concatenate([p.reshape(-1, LANES) for p in parts], axis=1)


def split_to(ref, rows, value, shape):
    for g in range(ref.shape[0]):
        ref[g, rows] = value[:, g * LANES : (g + 1) * LANES].reshape(*shape, LANES)


def norm_parts(z):
    center = z - jnp.mean(z, axis=-1, keepdims=True)
    inv = lax.rsqrt(jnp.mean(center * center, axis=-1, keepdims=True) + EPSILON)
    return center * inv, inv


def norm_back(dn, hat, inv, gain):
    scaled = dn * gain
    return inv * (
        scaled
        - jnp.mean(scaled, axis=-1, keepdims=True)
        - hat * jnp.mean(scaled * hat, axis=-1, keepdims=True)
    )


def dot_nn(a, b):
    return jnp.dot(a, b, preferred_element_type=F32)


def dot_nt(a, b):
    return lax.dot_general(a, b, (((1,), (1,)), ((), ())), preferred_element_type=F32)


def dot_tn(a, b):
    return lax.dot_general(a, b, (((0,), (0,)), ((), ())), preferred_element_type=F32)


def pixel_blocks(pixels):
    best = max(d for d in range(16, 257, 16) if pixels % d == 0)
    return [slice(start, start + best) for start in range(0, pixels, best)]


def hidden_chunks(hidden):
    size = 256 if hidden % 256 == 0 else hidden
    return [slice(start, start + size) for start in range(0, hidden, size)]


def mlp_grads(normed, grad, w_in, b_in, w_out, act, gpre, dw, db):
    pixels = grad.shape[0]
    for cut in hidden_chunks(w_in.shape[2]):
        bias = b_in[:, cut]
        bias_sum = None
        for block in pixel_blocks(pixels):
            pre = dot_nn(normed[block, :], w_in[0, :, cut]) + bias
            value, slope = gelu_parts(pre)
            act[block, cut] = value.astype(BF16)
            gradient = dot_nn(grad[block, :], w_out[0, :, cut]) * slope
            gpre[block, cut] = gradient.astype(BF16)
            part = jnp.sum(gradient, axis=0, keepdims=True)
            bias_sum = part if bias_sum is None else bias_sum + part
        db[:, cut] = bias_sum
        if dw is not None:
            weight_grads(normed, grad, act, gpre, dw, cut)


def weight_grads(normed, grad, act, gpre, dw, cut):
    dw[1, cut, :] = dot_tn(act[:, cut], grad[...]).astype(BF16)
    dw[0, cut, :] = dot_tn(gpre[:, cut], normed[...]).astype(BF16)


def fetch_layers(triples, arrived):
    copies = [
        pltpu.make_async_copy(source.at[pl.ds(layer, 1)], target, arrived.at[i])
        for i, (source, layer, target) in enumerate(triples)
    ]
    for copy in copies:
        copy.start()
    return copies


def block_back(z, grad, layer, gains, shifts, weights, b_in, outs, scratch):
    dz_out, dw, db, dgain, dshift = outs
    normed, act, gpre = scratch
    gain = gains[layer : layer + 1]
    hat, inv = norm_parts(joined(z, slice(None)))
    normed[...] = (hat * gain + shifts[layer : layer + 1]).astype(BF16)
    w_in, w_out, waits = weights
    for wait in waits:
        wait.wait()
    mlp_grads(normed, grad, w_in, b_in.at[layer], w_out, act, gpre, dw, db)
    dn = dot_nt(gpre[...], w_in[0])
    dgain[...] = jnp.sum(dn * hat, axis=0, keepdims=True)
    dshift[...] = jnp.sum(dn, axis=0, keepdims=True)
    dz_out[...] = norm_back(dn, hat, inv, gain).astype(BF16)


def forward_kernel(
    place, xpad, taps, gains, shifts, w_in, w_out, b_in, mids, z_out,
    xs, zs, act, w_in0, w_out0, arrived,
):
    waits = fetch_layers(((w_in, 0, w_in0), (w_out, 0, w_out0)), arrived)
    groups, mid_rows, mid_cols = zs.shape[:3]
    rows, cols = z_out.shape[1:3]
    for g in range(groups):
        xs[g] = xpad[:, :, g * LANES : (g + 1) * LANES].astype(F32)
    conv_pass(xs, 0, 0, taps.at[0], zs, mid_rows, mid_cols)
    z_out[...] = zs[:, HALO : HALO + rows, HALO : HALO + cols, :]
    strip = act.shape[0] // mid_cols
    for wait in waits:
        wait.wait()

    def one_strip(step, carry):
        top = step * strip
        hat, _ = norm_parts(joined(zs, pl.ds(top, strip)))
        normed = (hat * gains[0:1] + shifts[0:1]).astype(BF16)
        for cut in hidden_chunks(w_in0.shape[2]):
            pre = dot_nn(normed, w_in0[0, :, cut]) + b_in[0, :, cut]
            act[:, cut] = gelu_only(pre).astype(BF16)
        mixed = dot_nt(act[...], w_out0[0])
        row = lax.broadcasted_iota(jnp.int32, (strip, mid_cols, 1), 0) + (top - HALO) + place[0]
        col = lax.broadcasted_iota(jnp.int32, (strip, mid_cols, 1), 1) - HALO + place[1]
        real = (row >= 0) & (row < place[2]) & (col >= 0) & (col < place[3])
        real = jnp.where(real, 1.0, 0.0).reshape(strip * mid_cols, 1)
        base = joined(xs, pl.ds(top + HALO, strip), slice(HALO, HALO + mid_cols))
        mid = (base + mixed).astype(BF16).astype(F32) * real
        split_to(mids, pl.ds(top, strip), mid, (strip, mid_cols))
        return carry

    lax.fori_loop(0, mid_rows // strip, one_strip, 0)


def top_kernel(
    mids, grad, taps, gains, shifts, w_in, w_out, b_in,
    dz_out, normed, act, gpre, db, dgain, dshift, z, w_in1, w_out1, arrived,
):
    waits = fetch_layers(((w_in, 1, w_in1), (w_out, 1, w_out1)), arrived)
    conv_pass(mids, 0, 0, taps.at[1], z, *z.shape[1:3])
    block_back(
        z, grad, 1, gains, shifts, (w_in1, w_out1, waits), b_in,
        (dz_out, None, db, dgain, dshift), (normed, act, gpre),
    )


def low_kernel(
    dzpad, grad, z0, taps, gains, shifts, w_in, w_out, b_in,
    gmid, dz_out, dw, db, dgain, dshift,
    dzs, spread, normed, act, gpre, w_in0, w_out0, arrived,
):
    waits = fetch_layers(((w_in, 0, w_in0), (w_out, 0, w_out0)), arrived)
    spread_pass(dzpad, dzs, taps.at[1], spread)
    gmid[...] = (grad[...].astype(F32) + joined(spread, slice(None))).astype(BF16)
    block_back(
        z0, gmid, 0, gains, shifts, (w_in0, w_out0, waits), b_in,
        (dz_out, dw, db, dgain, dshift), (normed, act, gpre),
    )


def spread_pass(dzpad, dzs, taps, spread):
    for g in range(dzs.shape[0]):
        dzs[g] = dzpad[:, :, g * LANES : (g + 1) * LANES].astype(F32)
    conv_pass(dzs, 0, 0, taps, spread, *spread.shape[1:3], back=True)


def last_kernel(dzpad, gmid, taps, out, dzs, spread):
    spread_pass(dzpad, dzs, taps.at[0], spread)
    out[...] = (gmid[...].astype(F32) + joined(spread, slice(None))).astype(BF16)


def taps_kernel(source, row0, col0, dz, db, dgain, dshift, out, xs, dzs, sums):
    rows, cols = dzs.shape[1:3]
    channels = out.shape[1]
    split_to(dzs, slice(None), dz[...].astype(F32), (rows, cols))
    if xs is None:
        values = source
    else:
        for g in range(dzs.shape[0]):
            xs[g] = source[:, :, g * LANES : (g + 1) * LANES].astype(F32)
        values = xs
    sums[...] = jnp.zeros(sums.shape, F32)
    count = db.shape[1] // channels
    for k in range(count):
        sums[k : k + 1, :] = db[:, k * channels : (k + 1) * channels]
    sums[count : count + 1, :] = dgain[...]
    sums[count + 1 : count + 2, :] = dshift[...]
    tap_pass(values, row0, col0, dzs, 0, 0, sums, count + 2, rows, cols)
    out[...] = sums[...].astype(BF16)


def top_taps_kernel(source, dz, normed, act, gpre, grad, db, dgain, dshift, dw, out, dzs, sums):
    for cut in hidden_chunks(act.shape[1]):
        weight_grads(normed, grad, act, gpre, dw, cut)
    taps_kernel(source, 0, 0, dz, db, dgain, dshift, out, None, dzs, sums)


def low_taps_kernel(source, dz, db, dgain, dshift, out, xs, dzs, sums):
    taps_kernel(source, HALO, HALO, dz, db, dgain, dshift, out, xs, dzs, sums)


def shape(*dims, dtype=F32):
    return jax.ShapeDtypeStruct(dims, dtype)


def run(kernel, outs, scratch, args, specs=None, fetched=0, name=None):
    vmem = pl.BlockSpec(memory_space=pltpu.VMEM)
    semaphores = [pltpu.SemaphoreType.DMA((fetched,))] if fetched else []
    return pl.pallas_call(
        kernel,
        out_shape=outs,
        in_specs=[
            vmem if s is None else pl.BlockSpec(memory_space=s) for s in (specs or [None] * len(args))
        ],
        out_specs=tuple(vmem for _ in outs),
        scratch_shapes=[pltpu.VMEM(s.shape, s.dtype) for s in scratch] + semaphores,
        compiler_params=pltpu.CompilerParams(vmem_limit_bytes=50 * 1024 * 1024),
        name=name,
    )(*args)


def edges(tile, axis, width, odd):
    count = tile.shape[axis]
    low = lax.slice_in_dim(tile, 0, width, axis=axis)
    high = lax.slice_in_dim(tile, count - width, count, axis=axis)
    return jnp.where(odd, low, high), jnp.where(odd, high, low)


def to_twin(edge, axis):
    count = lax.axis_size(axis)
    return lax.ppermute(edge, axis, [(i, i ^ 1) for i in range(count) if i ^ 1 < count])


def to_other(edge, axis):
    pairs = [(i, i + 1) for i in range(1, lax.axis_size(axis) - 1, 2)]
    return lax.ppermute(edge, axis, pairs + [(j, i) for i, j in pairs])


def rimmed(tile, from_twin, from_other, axis, odd):
    low = jnp.where(odd, from_twin, from_other)
    high = jnp.where(odd, from_other, from_twin)
    return jnp.concatenate([low, tile, high], axis=axis)


def flip_bit(value, bit):
    both = ("rows", "cols")
    total = lax.axis_size("rows") * lax.axis_size("cols")
    return lax.ppermute(value, both, [(i, i ^ (1 << bit)) for i in range(total)])


def halves(chunks, dim, mine):
    sizes = [1 if d == dim else n for d, n in enumerate(chunks.shape)]

    def one(bit):
        starts = [bit if d == dim else jnp.uint32(0) for d in range(chunks.ndim)]
        return lax.squeeze(lax.dynamic_slice(chunks, starts, sizes), (dim,))

    return one(mine[1]), one(mine[0])


def summed(own, got):
    return (own.astype(F32) + got.astype(F32)).astype(BF16)


def step(chunks, order, bit, mine):
    spot = order.index(bit)
    per = chunks.shape[-2:]
    pair = chunks.reshape((-1, 2 ** spot, 2, 2 ** (len(order) - spot - 1)) + per)
    send, keep = halves(pair, 2, mine[bit])
    return keep, flip_bit(send, bit), [b for b in order if b != bit]


def shards(activations, grad_out, kernels, norm_gains, norm_shifts, w_in, b_in, w_out):
    rows, cols, channels = activations.shape
    layers, _, hidden = w_in.shape
    groups = channels // LANES
    n_rows, n_cols = lax.axis_size("rows"), lax.axis_size("cols")
    total = n_rows * n_cols
    bits = total.bit_length() - 1
    col_bits = n_cols.bit_length() - 1
    me = (lax.axis_index("rows") * n_cols + lax.axis_index("cols")).astype(jnp.uint32)
    mine = [(((me >> k) & 1), 1 - ((me >> k) & 1)) for k in range(bits)]
    grad_scale = 1.0 / math.sqrt(rows * cols * total)
    pixels = rows * cols

    taps = kernels.reshape(layers, 49, groups, LANES).transpose(0, 2, 1, 3)
    biases = b_in[:, None, :]
    place = jnp.stack(
        [
            lax.axis_index("rows") * rows,
            lax.axis_index("cols") * cols,
            jnp.int32(rows * n_rows),
            jnp.int32(cols * n_cols),
        ]
    ).astype(jnp.int32)
    grad_flat = grad_out.reshape(pixels, channels)

    odd_col = (lax.axis_index("cols") & 1) == 1
    odd_row = (lax.axis_index("rows") & 1) == 1

    def rim_cols(tile, width):
        twin, other = edges(tile, 1, width, odd_col)
        return rimmed(tile, to_twin(twin, "cols"), to_other(other, "cols"), 1, odd_col)

    def rim_rows(tile, width):
        twin, other = edges(tile, 0, width, odd_row)
        return rimmed(tile, to_twin(twin, "rows"), to_other(other, "rows"), 0, odd_row)

    def filled(wide):
        return jnp.pad(wide, ((0, 0), (0, cols + 16 - wide.shape[1]), (0, 0)))

    mid_rows, mid_cols = rows + 2 * HALO, cols + 8
    strip = max(d for d in range(1, mid_rows + 1) if mid_rows % d == 0 and d * mid_cols <= 264)
    weights = [shape(1, channels, hidden, dtype=BF16)] * 2
    tile_z = shape(groups, rows, cols, LANES)
    tile_b = shape(pixels, channels, dtype=BF16)
    tile_h = shape(pixels, hidden, dtype=BF16)
    grads_b = shape(2, hidden, channels, dtype=BF16)
    small_outs = (shape(1, hidden), shape(1, channels), shape(1, channels))
    small_rows = 64

    xpad = filled(rim_rows(rim_cols(activations, WIDE), WIDE))
    xpad, place, mine, odd_col, odd_row = lax.optimization_barrier((xpad, place, mine, odd_col, odd_row))
    mids, z0 = run(
        forward_kernel,
        (shape(groups, mid_rows, mid_cols, LANES), tile_z),
        [
            shape(groups, *xpad.shape[:2], LANES),
            shape(groups, mid_rows, mid_cols, LANES),
            shape(strip * mid_cols, hidden, dtype=BF16),
        ]
        + weights,
        (place, xpad, taps, norm_gains, norm_shifts, w_in, w_out, biases),
        [pltpu.SMEM] + [None] * 4 + [pl.ANY] * 2 + [None],
        fetched=2,
        name="forward",
    )
    dz1, normed1, act1, gpre1, *small1 = run(
        top_kernel,
        (tile_b, tile_b, tile_h, tile_h) + small_outs,
        [tile_z] + weights,
        (mids, grad_flat, taps, norm_gains, norm_shifts, w_in, w_out, biases),
        [None] * 5 + [pl.ANY] * 2 + [None],
        fetched=2,
        name="top",
    )

    per = hidden // total
    sides = (col_bits - 1, col_bits)

    def fenced(*values):
        leaves, tree = jax.tree.flatten(values)
        arrays = [i for i, leaf in enumerate(leaves) if not isinstance(leaf, int)]
        for i, value in zip(arrays, lax.optimization_barrier(tuple(leaves[i] for i in arrays))):
            leaves[i] = value
        return jax.tree.unflatten(tree, leaves)

    def settled(flight):
        return summed(flight[0], flight[1]), flight[2]

    def start(dw):
        chunks, order = dw.reshape(2, total, per, channels), list(range(bits - 1, -1, -1))
        for bit in range(col_bits - 2):
            chunks, order = settled(step(chunks, order, bit, mine))
        return step(chunks, order, col_bits - 2, mine)

    def fork(flight):
        chunks, order = settled(flight)
        return [step(chunks[i], order, sides[i], mine) for i in range(2)]

    def cross(flights):
        done = [settled(f) for f in flights]
        return [step(*done[i], sides[1 - i], mine) for i in range(2)]

    def merge(flights):
        done = [settled(f) for f in flights]
        return jnp.stack([d[0].reshape(-1, per, channels) for d in done]), done[0][1]

    def onward(chunks, order):
        return step(chunks, order, order[-1], mine) if order else (chunks, jnp.zeros_like(chunks), order)

    def finish(flight):
        chunks, order = settled(flight)
        while order:
            chunks, order = settled(onward(chunks, order))
        return jnp.swapaxes(chunks.reshape(2, per, channels).astype(F32) * grad_scale, 1, 2)

    tile1 = dz1.reshape(rows, cols, channels)
    twin, other = edges(tile1, 1, HALO, odd_col)
    twin, other = to_twin(twin, "cols"), to_other(other, "cols")
    dw1, small1 = run(
        top_taps_kernel,
        (grads_b, shape(small_rows, channels, dtype=BF16)),
        [tile_z, shape(small_rows, channels)],
        (mids, dz1, normed1, act1, gpre1, grad_flat, *small1),
        name="top_taps",
    )
    tile1, twin, other, dw1, small1 = fenced(tile1, twin, other, dw1, small1)
    wide1 = rimmed(tile1, twin, other, 1, odd_col)
    run1 = start(dw1)
    twin, other = edges(wide1, 0, HALO, odd_row)
    twin, other = to_twin(twin, "rows"), to_other(other, "rows")
    wide1, twin, other, run1 = fenced(wide1, twin, other, run1)
    pair1 = fork(run1)
    dzpad1 = filled(rimmed(wide1, twin, other, 0, odd_row))
    spread_scratch = [shape(groups, *dzpad1.shape[:2], LANES), tile_z]
    grad_mid, dz0, dw0, *small0 = run(
        low_kernel,
        (tile_b, tile_b, grads_b) + small_outs,
        spread_scratch + [tile_b, tile_h, tile_h] + weights,
        (dzpad1, grad_flat, z0, taps, norm_gains, norm_shifts, w_in, w_out, biases),
        [None] * 6 + [pl.ANY] * 2 + [None],
        fetched=2,
        name="low",
    )
    dz0, dw0, pair1, *small0 = fenced(dz0, dw0, pair1, *small0)
    run0 = start(dw0)
    pair1 = cross(pair1)
    tile0 = dz0.reshape(rows, cols, channels)
    twin, other = edges(tile0, 1, HALO, odd_col)
    twin = to_twin(twin, "cols")
    (small0,) = run(
        low_taps_kernel,
        (shape(small_rows, channels, dtype=BF16),),
        [shape(groups, *xpad.shape[:2], LANES), tile_z, shape(small_rows, channels)],
        (xpad, dz0, *small0),
        name="low_taps",
    )
    small = jnp.concatenate([small0, small1], axis=0)
    small_got = flip_bit(small, 0)
    run0, pair1, small, small_got, tile0, twin, other = fenced(
        run0, pair1, small, small_got, tile0, twin, other
    )
    pair0 = fork(run0)
    run1 = onward(*merge(pair1))
    other = to_other(other, "cols")
    small = summed(small, small_got)
    small_got = flip_bit(small, 1)
    pair0, run1, tile0, twin, other, small, small_got = fenced(
        pair0, run1, tile0, twin, other, small, small_got
    )
    pair0 = cross(pair0)
    run1 = onward(*settled(run1))
    wide0 = rimmed(tile0, twin, other, 1, odd_col)
    twin, other = edges(wide0, 0, HALO, odd_row)
    twin = to_twin(twin, "rows")
    small = summed(small, small_got)
    small_got = flip_bit(small, 2)
    pair0, run1, wide0, twin, other, small, small_got = fenced(
        pair0, run1, wide0, twin, other, small, small_got
    )
    run0 = onward(*merge(pair0))
    other = to_other(other, "rows")
    share1 = finish(run1)
    wait = (wide0, twin, other)
    for bit in range(3, bits):
        small = summed(small, small_got)
        small_got = flip_bit(small, bit)
        if run0[2]:
            run0, small, small_got, wait = fenced(run0, small, small_got, wait)
            run0 = onward(*settled(run0))
        if bit == 3:
            (wait,) = run(
                last_kernel,
                (tile_b,),
                spread_scratch,
                (filled(rimmed(*wait, 0, odd_row)), grad_mid, taps),
                name="last",
            )
    grad_in = wait
    small = summed(small, small_got)
    shares = [finish(run0), share1]
    small = small.reshape(layers, small_rows, channels).astype(F32) * grad_scale
    count = hidden // channels
    return (
        grad_in.reshape(rows, cols, channels),
        small[:, count + 2 : count + 51].reshape(layers, 7, 7, channels),
        small[:, count],
        small[:, count + 1],
        small[:, :count].reshape(layers, hidden),
        jnp.stack([share[0] for share in shares]),
        jnp.stack([share[1] for share in shares]),
    )


def solution(mesh):
    tile = P("rows", "cols", None)
    sliced = P(None, None, ("rows", "cols"))
    return jax.shard_map(
        shards,
        mesh=mesh,
        in_specs=(tile, tile, P(), P(), P(), P(), P(), P()),
        out_specs=(tile, P(), P(), P(), P(), sliced, sliced),
        check_vma=False,
    )
```

```python
import functools
import math

import jax
import jax.numpy as jnp
from jax import lax
from jax.experimental import pallas as pl
from jax.experimental.pallas import tpu as pltpu
from jax.sharding import PartitionSpec as P

EPSILON = 1e-06
INV_ROOT_TAU = 0.3989422804014327
HALF_LOG2E = 0.7213475204444817
ERFC_SLOPE = 0.4 * 0.7071067811865476
ERFC_TERMS = (
    0.22479419400284972,
    0.2383621945582281,
    0.12991301634379934,
    0.4353236101490443,
    -0.41611664430523265,
    0.7235898182708315,
    -0.41436965913692125,
    0.07850346878444278,
)
LANES = 128
HALO = 3
WIDE = 2 * HALO
F32 = jnp.float32
BF16 = jnp.bfloat16


def normal_parts(x):
    bell = jnp.exp2(x * x * (-HALF_LOG2E))
    t = 1.0 / (1.0 + ERFC_SLOPE * jnp.abs(x))
    series = 0.5 * ERFC_TERMS[7]
    for term in ERFC_TERMS[6::-1]:
        series = series * t + 0.5 * term
    tail = series * t * bell
    return jnp.where(x >= 0, 1.0 - tail, tail), bell


def gelu_only(x):
    cdf, _ = normal_parts(x)
    return x * cdf


def gelu_parts(x):
    cdf, bell = normal_parts(x)
    return x * cdf, cdf + x * bell * INV_ROOT_TAU


def strip_rows(rows, cols):
    most = max(1, 288 // cols)
    return max(d for d in range(1, rows + 1) if rows % d == 0 and d <= most)


def conv_pass(source, row0, col0, taps, target, rows, cols, back=False):
    strip = strip_rows(rows, cols)
    groups = source.shape[0]

    def one_strip(step, carry):
        g = step // (rows // strip)
        top = (step % (rows // strip)) * strip
        sums = [jnp.zeros((cols, LANES), F32) for _ in range(strip)]
        for b in range(7):
            spots = [48 - 7 * a - b if back else 7 * a + b for a in range(7)]
            weights = [taps[g, pl.ds(spot, 1), :] for spot in spots]
            for r in range(strip + 6):
                line = source[g, row0 + top + r, pl.ds(col0 + b, cols), :]
                for a in range(7):
                    if 0 <= r - a < strip:
                        sums[r - a] = sums[r - a] + weights[a] * line
        for i in range(strip):
            target[g, top + i] = sums[i]
        return carry

    lax.fori_loop(0, groups * (rows // strip), one_strip, 0)


def tap_pass(source, row0, col0, grad, grow0, gcol0, target, first, rows, cols):
    for g in range(source.shape[0]):
        lanes = slice(g * LANES, (g + 1) * LANES)
        for b in range(7):
            def one_row(i, sums):
                line = grad[g, grow0 + i, pl.ds(gcol0, cols), :]
                out = []
                for a in range(7):
                    part = line * source[g, row0 + i + a, pl.ds(col0 + b, cols), :]
                    out.append(sums[a] + part.reshape(cols // 8, 8, LANES).sum(0))
                return tuple(out)

            sums = lax.fori_loop(
                0, rows, one_row, tuple(jnp.zeros((8, LANES), F32) for _ in range(7)), unroll=4
            )
            for a in range(7):
                target[pl.ds(first + 7 * a + b, 1), lanes] = jnp.sum(sums[a], axis=0, keepdims=True)


def joined(ref, rows, cols=slice(None)):
    parts = [ref[g, rows, cols, :] for g in range(ref.shape[0])]
    return jnp.concatenate([p.reshape(-1, LANES) for p in parts], axis=1)


def split_to(ref, rows, value, shape):
    for g in range(ref.shape[0]):
        ref[g, rows] = value[:, g * LANES : (g + 1) * LANES].reshape(*shape, LANES)


def norm_parts(z):
    center = z - jnp.mean(z, axis=-1, keepdims=True)
    inv = lax.rsqrt(jnp.mean(center * center, axis=-1, keepdims=True) + EPSILON)
    return center * inv, inv


def norm_back(dn, hat, inv, gain):
    scaled = dn * gain
    return inv * (
        scaled
        - jnp.mean(scaled, axis=-1, keepdims=True)
        - hat * jnp.mean(scaled * hat, axis=-1, keepdims=True)
    )


def dot_nn(a, b):
    return jnp.dot(a, b, preferred_element_type=F32)


def dot_nt(a, b):
    return lax.dot_general(a, b, (((1,), (1,)), ((), ())), preferred_element_type=F32)


def dot_tn(a, b):
    return lax.dot_general(a, b, (((0,), (0,)), ((), ())), preferred_element_type=F32)


def pixel_blocks(pixels):
    best = max(d for d in range(16, 257, 16) if pixels % d == 0)
    return [slice(start, start + best) for start in range(0, pixels, best)]


def hidden_chunks(hidden):
    size = 256 if hidden % 256 == 0 else hidden
    return [slice(start, start + size) for start in range(0, hidden, size)]


def mlp_grads(normed, grad, w_in, b_in, w_out, act, gpre, db):
    pixels = grad.shape[0]
    for cut in hidden_chunks(w_in.shape[2]):
        bias = b_in[:, cut]
        bias_sum = None
        for block in pixel_blocks(pixels):
            pre = dot_nn(normed[block, :], w_in[0, :, cut]) + bias
            value, slope = gelu_parts(pre)
            act[block, cut] = value.astype(BF16)
            gradient = dot_nn(grad[block, :], w_out[0, :, cut]) * slope
            gpre[block, cut] = gradient.astype(BF16)
            part = jnp.sum(gradient, axis=0, keepdims=True)
            bias_sum = part if bias_sum is None else bias_sum + part
        db[:, cut] = bias_sum


def weight_grads(place, normed, grad, act, gpre, dw, per):
    hidden, channels = act.shape[1], grad.shape[1]
    size = min(n for n in range(128, hidden + 1, 128) if hidden % n == 0 and n % (2 * per) == 0 and n >= 256)
    for first in range(0, hidden, size):
        cut = slice(first, first + size)
        for i, (left, right) in enumerate(((gpre, normed), (act, grad))):
            value = dot_tn(left[:, cut], right[...]).astype(BF16)
            if len(dw) == 1:
                dw[0][i, cut, :] = value
                continue
            value = value.reshape(size // (2 * per), 2, per, channels)
            upper = place[4] == 1
            half = slice(first // 2, (first + size) // 2)
            dw[0][i, half, :] = jnp.where(upper, value[:, 0], value[:, 1]).reshape(-1, channels)
            dw[1][i, half, :] = jnp.where(upper, value[:, 1], value[:, 0]).reshape(-1, channels)


def fetch_layers(triples, arrived):
    copies = [
        pltpu.make_async_copy(source.at[pl.ds(layer, 1)], target, arrived.at[i])
        for i, (source, layer, target) in enumerate(triples)
    ]
    for copy in copies:
        copy.start()
    return copies


def block_back(z, grad, layer, gains, shifts, weights, b_in, outs, scratch):
    dz_out, db, dgain, dshift = outs
    normed, act, gpre = scratch
    gain = gains[layer : layer + 1]
    hat, inv = norm_parts(joined(z, slice(None)))
    normed[...] = (hat * gain + shifts[layer : layer + 1]).astype(BF16)
    w_in, w_out, waits = weights
    for wait in waits:
        wait.wait()
    mlp_grads(normed, grad, w_in, b_in.at[layer], w_out, act, gpre, db)
    dn = dot_nt(gpre[...], w_in[0])
    dgain[...] = jnp.sum(dn * hat, axis=0, keepdims=True)
    dshift[...] = jnp.sum(dn, axis=0, keepdims=True)
    dz_out[...] = norm_back(dn, hat, inv, gain).astype(BF16)


def forward_kernel(
    place, xpad, taps, gains, shifts, w_in, w_out, b_in, mids, z_out,
    xs, zs, act, w_in0, w_out0, arrived,
):
    waits = fetch_layers(((w_in, 0, w_in0), (w_out, 0, w_out0)), arrived)
    groups, mid_rows, mid_cols = zs.shape[:3]
    rows, cols = z_out.shape[1:3]
    for g in range(groups):
        xs[g] = xpad[:, :, g * LANES : (g + 1) * LANES].astype(F32)
    conv_pass(xs, 0, 0, taps.at[0], zs, mid_rows, mid_cols)
    z_out[...] = zs[:, HALO : HALO + rows, HALO : HALO + cols, :]
    strip = act.shape[0] // mid_cols
    for wait in waits:
        wait.wait()

    def one_strip(step, carry):
        top = step * strip
        hat, _ = norm_parts(joined(zs, pl.ds(top, strip)))
        normed = (hat * gains[0:1] + shifts[0:1]).astype(BF16)
        for cut in hidden_chunks(w_in0.shape[2]):
            pre = dot_nn(normed, w_in0[0, :, cut]) + b_in[0, :, cut]
            act[:, cut] = gelu_only(pre).astype(BF16)
        mixed = dot_nt(act[...], w_out0[0])
        row = lax.broadcasted_iota(jnp.int32, (strip, mid_cols, 1), 0) + (top - HALO) + place[0]
        col = lax.broadcasted_iota(jnp.int32, (strip, mid_cols, 1), 1) - HALO + place[1]
        real = (row >= 0) & (row < place[2]) & (col >= 0) & (col < place[3])
        real = jnp.where(real, 1.0, 0.0).reshape(strip * mid_cols, 1)
        base = joined(xs, pl.ds(top + HALO, strip), slice(HALO, HALO + mid_cols))
        mid = (base + mixed).astype(BF16).astype(F32) * real
        split_to(mids, pl.ds(top, strip), mid, (strip, mid_cols))
        return carry

    lax.fori_loop(0, mid_rows // strip, one_strip, 0)


def top_kernel(
    mids, grad, taps, gains, shifts, w_in, w_out, b_in,
    dz_out, normed, act, gpre, db, dgain, dshift, z, w_in1, w_out1, arrived,
):
    waits = fetch_layers(((w_in, 1, w_in1), (w_out, 1, w_out1)), arrived)
    conv_pass(mids, 0, 0, taps.at[1], z, *z.shape[1:3])
    block_back(
        z, grad, 1, gains, shifts, (w_in1, w_out1, waits), b_in,
        (dz_out, db, dgain, dshift), (normed, act, gpre),
    )


def low_kernel(
    per, place, dzpad, grad, z0, taps, gains, shifts, w_in, w_out, b_in,
    gmid, dz_out, db, dgain, dshift, *rest,
):
    *dw, dzs, spread, normed, act, gpre, w_in0, w_out0, arrived = rest
    waits = fetch_layers(((w_in, 0, w_in0), (w_out, 0, w_out0)), arrived)
    spread_pass(dzpad, dzs, taps.at[1], spread)
    gmid[...] = (grad[...].astype(F32) + joined(spread, slice(None))).astype(BF16)
    block_back(
        z0, gmid, 0, gains, shifts, (w_in0, w_out0, waits), b_in,
        (dz_out, db, dgain, dshift), (normed, act, gpre),
    )
    weight_grads(place, normed, gmid, act, gpre, dw, per)


def spread_pass(dzpad, dzs, taps, spread):
    for g in range(dzs.shape[0]):
        dzs[g] = dzpad[:, :, g * LANES : (g + 1) * LANES].astype(F32)
    conv_pass(dzs, 0, 0, taps, spread, *spread.shape[1:3], back=True)


def last_kernel(dzpad, gmid, taps, out, dzs, spread):
    spread_pass(dzpad, dzs, taps.at[0], spread)
    out[...] = (gmid[...].astype(F32) + joined(spread, slice(None))).astype(BF16)


def taps_kernel(source, row0, col0, dz, db, dgain, dshift, out, xs, dzs, sums):
    rows, cols = dzs.shape[1:3]
    channels = out.shape[1]
    split_to(dzs, slice(None), dz[...].astype(F32), (rows, cols))
    if xs is None:
        values = source
    else:
        for g in range(dzs.shape[0]):
            xs[g] = source[:, :, g * LANES : (g + 1) * LANES].astype(F32)
        values = xs
    sums[...] = jnp.zeros(sums.shape, F32)
    count = db.shape[1] // channels
    for k in range(count):
        sums[k : k + 1, :] = db[:, k * channels : (k + 1) * channels]
    sums[count : count + 1, :] = dgain[...]
    sums[count + 1 : count + 2, :] = dshift[...]
    tap_pass(values, row0, col0, dzs, 0, 0, sums, count + 2, rows, cols)
    out[...] = sums[...].astype(BF16)


def top_taps_kernel(per, place, source, dz, normed, act, gpre, grad, db, dgain, dshift, out, *rest):
    *dw, dzs, sums = rest
    weight_grads(place, normed, grad, act, gpre, dw, per)
    taps_kernel(source, 0, 0, dz, db, dgain, dshift, out, None, dzs, sums)


def low_taps_kernel(source, dz, db, dgain, dshift, out, xs, dzs, sums):
    taps_kernel(source, HALO, HALO, dz, db, dgain, dshift, out, xs, dzs, sums)


def shape(*dims, dtype=F32):
    return jax.ShapeDtypeStruct(dims, dtype)


def run(kernel, outs, scratch, args, specs=None, fetched=0, name=None):
    vmem = pl.BlockSpec(memory_space=pltpu.VMEM)
    semaphores = [pltpu.SemaphoreType.DMA((fetched,))] if fetched else []
    return pl.pallas_call(
        kernel,
        out_shape=outs,
        in_specs=[
            vmem if s is None else pl.BlockSpec(memory_space=s) for s in (specs or [None] * len(args))
        ],
        out_specs=tuple(vmem for _ in outs),
        scratch_shapes=[pltpu.VMEM(s.shape, s.dtype) for s in scratch] + semaphores,
        compiler_params=pltpu.CompilerParams(vmem_limit_bytes=50 * 1024 * 1024),
        name=name,
    )(*args)


def edges(tile, axis, width, odd):
    count = tile.shape[axis]
    low = lax.slice_in_dim(tile, 0, width, axis=axis)
    high = lax.slice_in_dim(tile, count - width, count, axis=axis)
    return jnp.where(odd, low, high), jnp.where(odd, high, low)


def to_twin(edge, axis):
    count = lax.axis_size(axis)
    return lax.ppermute(edge, axis, [(i, i ^ 1) for i in range(count) if i ^ 1 < count])


def to_other(edge, axis):
    n_rows, n_cols = lax.axis_size("rows"), lax.axis_size("cols")
    count = lax.axis_size(axis)
    pairs = []
    for r in range(n_rows):
        for c in range(n_cols):
            at = r if axis == "rows" else c
            partner = at + 1 if at % 2 else at - 1
            if 0 <= partner < count:
                there = (partner, c) if axis == "rows" else (r, partner)
            else:
                there = (r, c ^ 1) if axis == "rows" else (r ^ 1, c)
            pairs.append((r * n_cols + c, there[0] * n_cols + there[1]))
    return lax.ppermute(edge, ("rows", "cols"), pairs)


def rimmed(tile, from_twin, from_other, axis, odd, outer):
    from_other = jnp.where(outer, jnp.zeros_like(from_other), from_other)
    low = jnp.where(odd, from_twin, from_other)
    high = jnp.where(odd, from_other, from_twin)
    return jnp.concatenate([low, tile, high], axis=axis)


def flip_bit(value, bit):
    both = ("rows", "cols")
    total = lax.axis_size("rows") * lax.axis_size("cols")
    return lax.ppermute(value, both, [(i, i ^ (1 << bit)) for i in range(total)])


def halves(chunks, dim, mine):
    sizes = [1 if d == dim else n for d, n in enumerate(chunks.shape)]

    def one(bit):
        starts = [bit if d == dim else jnp.uint32(0) for d in range(chunks.ndim)]
        return lax.squeeze(lax.dynamic_slice(chunks, starts, sizes), (dim,))

    return one(mine[1]), one(mine[0])


def summed(own, got):
    return (own.astype(F32) + got.astype(F32)).astype(BF16)


def step(chunks, order, bit, mine):
    spot = order.index(bit)
    per = chunks.shape[-2:]
    pair = chunks.reshape((-1, 2 ** spot, 2, 2 ** (len(order) - spot - 1)) + per)
    send, keep = halves(pair, 2, mine[bit])
    return keep, flip_bit(send, bit), [b for b in order if b != bit]


def shards(activations, grad_out, kernels, norm_gains, norm_shifts, w_in, b_in, w_out):
    rows, cols, channels = activations.shape
    layers, _, hidden = w_in.shape
    groups = channels // LANES
    n_rows, n_cols = lax.axis_size("rows"), lax.axis_size("cols")
    total = n_rows * n_cols
    bits = total.bit_length() - 1
    col_bits = n_cols.bit_length() - 1
    me = (lax.axis_index("rows") * n_cols + lax.axis_index("cols")).astype(jnp.uint32)
    mine = [(((me >> k) & 1), 1 - ((me >> k) & 1)) for k in range(bits)]
    grad_scale = 1.0 / math.sqrt(rows * cols * total)
    pixels = rows * cols

    taps = kernels.reshape(layers, 49, groups, LANES).transpose(0, 2, 1, 3)
    biases = b_in[:, None, :]
    place = jnp.stack(
        [
            lax.axis_index("rows") * rows,
            lax.axis_index("cols") * cols,
            jnp.int32(rows * n_rows),
            jnp.int32(cols * n_cols),
            lax.axis_index("cols") & 1,
        ]
    ).astype(jnp.int32)
    grad_flat = grad_out.reshape(pixels, channels)

    at_row, at_col = lax.axis_index("rows"), lax.axis_index("cols")
    odd_col, odd_row = (at_col & 1) == 1, (at_row & 1) == 1
    outer_col = (at_col == 0) | (at_col == n_cols - 1)
    outer_row = (at_row == 0) | (at_row == n_rows - 1)

    def rim_cols(tile, width):
        twin, other = edges(tile, 1, width, odd_col)
        return rimmed(tile, to_twin(twin, "cols"), to_other(other, "cols"), 1, odd_col, outer_col)

    def rim_rows(tile, width):
        twin, other = edges(tile, 0, width, odd_row)
        return rimmed(tile, to_twin(twin, "rows"), to_other(other, "rows"), 0, odd_row, outer_row)

    def filled(wide):
        return jnp.pad(wide, ((0, 0), (0, cols + 16 - wide.shape[1]), (0, 0)))

    mid_rows, mid_cols = rows + 2 * HALO, cols + 8
    strip = max(d for d in range(1, mid_rows + 1) if mid_rows % d == 0 and d * mid_cols <= 264)
    weights = [shape(1, channels, hidden, dtype=BF16)] * 2
    tile_z = shape(groups, rows, cols, LANES)
    tile_b = shape(pixels, channels, dtype=BF16)
    tile_h = shape(pixels, hidden, dtype=BF16)
    per = hidden // total
    split = 2 if per % 16 == 0 and col_bits == 2 else 1
    grads_b = (shape(2, hidden // split, channels, dtype=BF16),) * split
    small_outs = (shape(1, hidden), shape(1, channels), shape(1, channels))
    small_rows = 64

    xpad = filled(rim_rows(rim_cols(activations, WIDE), WIDE))
    xpad, place, mine, odd_col, odd_row, outer_col, outer_row = lax.optimization_barrier(
        (xpad, place, mine, odd_col, odd_row, outer_col, outer_row)
    )
    mids, z0 = run(
        forward_kernel,
        (shape(groups, mid_rows, mid_cols, LANES), tile_z),
        [
            shape(groups, *xpad.shape[:2], LANES),
            shape(groups, mid_rows, mid_cols, LANES),
            shape(strip * mid_cols, hidden, dtype=BF16),
        ]
        + weights,
        (place, xpad, taps, norm_gains, norm_shifts, w_in, w_out, biases),
        [pltpu.SMEM] + [None] * 4 + [pl.ANY] * 2 + [None],
        fetched=2,
        name="forward",
    )
    dz1, normed1, act1, gpre1, *small1 = run(
        top_kernel,
        (tile_b, tile_b, tile_h, tile_h) + small_outs,
        [tile_z] + weights,
        (mids, grad_flat, taps, norm_gains, norm_shifts, w_in, w_out, biases),
        [None] * 5 + [pl.ANY] * 2 + [None],
        fetched=2,
        name="top",
    )

    sides = (col_bits - 1, col_bits)

    def fenced(*values):
        leaves, tree = jax.tree.flatten(values)
        arrays = [i for i, leaf in enumerate(leaves) if not isinstance(leaf, int)]
        for i, value in zip(arrays, lax.optimization_barrier(tuple(leaves[i] for i in arrays))):
            leaves[i] = value
        return jax.tree.unflatten(tree, leaves)

    def settled(flight):
        return summed(flight[0], flight[1]), flight[2]

    def start(dw):
        order = list(range(bits - 1, -1, -1))
        if split == 2:
            send, keep = (d.reshape(2, total // 2, per, channels) for d in dw)
            return keep, flip_bit(send, 0), order[:-1]
        chunks = dw[0].reshape(2, total, per, channels)
        for bit in range(col_bits - 2):
            chunks, order = settled(step(chunks, order, bit, mine))
        return step(chunks, order, col_bits - 2, mine)

    def fork(flight):
        chunks, order = settled(flight)
        return [step(chunks[i], order, sides[i], mine) for i in range(2)]

    def cross(flights):
        done = [settled(f) for f in flights]
        return [step(*done[i], sides[1 - i], mine) for i in range(2)]

    def merge(flights):
        done = [settled(f) for f in flights]
        return jnp.stack([d[0].reshape(-1, per, channels) for d in done]), done[0][1]

    def onward(chunks, order):
        return step(chunks, order, order[-1], mine) if order else (chunks, jnp.zeros_like(chunks), order)

    def finish(flight):
        chunks, order = settled(flight)
        while order:
            chunks, order = settled(onward(chunks, order))
        return jnp.swapaxes(chunks.reshape(2, per, channels).astype(F32) * grad_scale, 1, 2)

    tile1 = dz1.reshape(rows, cols, channels)
    twin, other = edges(tile1, 1, HALO, odd_col)
    twin, other = to_twin(twin, "cols"), to_other(other, "cols")
    small1, *dw1 = run(
        functools.partial(top_taps_kernel, per),
        (shape(small_rows, channels, dtype=BF16),) + grads_b,
        [tile_z, shape(small_rows, channels)],
        (place, mids, dz1, normed1, act1, gpre1, grad_flat, *small1),
        [pltpu.SMEM] + [None] * 9,
        name="top_taps",
    )
    tile1, twin, other, dw1, small1 = fenced(tile1, twin, other, dw1, small1)
    wide1 = rimmed(tile1, twin, other, 1, odd_col, outer_col)
    run1 = start(dw1)
    twin, other = edges(wide1, 0, HALO, odd_row)
    twin, other = to_twin(twin, "rows"), to_other(other, "rows")
    wide1, twin, other, run1 = fenced(wide1, twin, other, run1)
    pair1 = fork(run1)
    dzpad1 = filled(rimmed(wide1, twin, other, 0, odd_row, outer_row))
    spread_scratch = [shape(groups, *dzpad1.shape[:2], LANES), tile_z]
    grad_mid, dz0, *rest = run(
        functools.partial(low_kernel, per),
        (tile_b, tile_b) + small_outs + grads_b,
        spread_scratch + [tile_b, tile_h, tile_h] + weights,
        (place, dzpad1, grad_flat, z0, taps, norm_gains, norm_shifts, w_in, w_out, biases),
        [pltpu.SMEM] + [None] * 6 + [pl.ANY] * 2 + [None],
        fetched=2,
        name="low",
    )
    small0, dw0 = rest[:3], rest[3:]
    dz0, dw0, pair1, *small0 = fenced(dz0, dw0, pair1, *small0)
    run0 = start(dw0)
    pair1 = cross(pair1)
    (small0,) = run(
        low_taps_kernel,
        (shape(small_rows, channels, dtype=BF16),),
        [shape(groups, *xpad.shape[:2], LANES), tile_z, shape(small_rows, channels)],
        (xpad, dz0, *small0),
        name="low_taps",
    )
    small = jnp.concatenate([small0, small1], axis=0)
    small_got = flip_bit(small, 0)
    run0, small, small_got, dz0 = fenced(run0, small, small_got, dz0)
    pair0 = fork(run0)
    tile0 = dz0.reshape(rows, cols, channels)
    twin, other = edges(tile0, 1, HALO, odd_col)
    twin, other = to_twin(twin, "cols"), to_other(other, "cols")
    small = summed(small, small_got)
    small_got = flip_bit(small, 1)
    pair0, pair1, tile0, twin, other, small, small_got = fenced(
        pair0, pair1, tile0, twin, other, small, small_got
    )
    pair0 = cross(pair0)
    run1 = onward(*merge(pair1))
    wide0 = rimmed(tile0, twin, other, 1, odd_col, outer_col)
    twin, other = edges(wide0, 0, HALO, odd_row)
    twin = to_twin(twin, "rows")
    small = summed(small, small_got)
    small_got = flip_bit(small, 2)
    pair0, run1, wide0, twin, other, small, small_got = fenced(
        pair0, run1, wide0, twin, other, small, small_got
    )
    run0 = onward(*merge(pair0))
    run1 = onward(*settled(run1))
    other = to_other(other, "rows")
    wait = (wide0, twin, other)
    for bit in range(3, bits):
        small = summed(small, small_got)
        small_got = flip_bit(small, bit)
        if run0[2]:
            run0, run1, small, small_got, wait = fenced(run0, run1, small, small_got, wait)
            run0 = onward(*settled(run0))
        if bit == 3:
            (wait,) = run(
                last_kernel,
                (tile_b,),
                spread_scratch,
                (filled(rimmed(*wait, 0, odd_row, outer_row)), grad_mid, taps),
                name="last",
            )
    grad_in, share1 = wait, finish(run1)
    small = summed(small, small_got)
    shares = [finish(run0), share1]
    small = small.reshape(layers, small_rows, channels).astype(F32) * grad_scale
    count = hidden // channels
    return (
        grad_in.reshape(rows, cols, channels),
        small[:, count + 2 : count + 51].reshape(layers, 7, 7, channels),
        small[:, count],
        small[:, count + 1],
        small[:, :count].reshape(layers, hidden),
        jnp.stack([share[0] for share in shares]),
        jnp.stack([share[1] for share in shares]),
    )


def solution(mesh):
    tile = P("rows", "cols", None)
    sliced = P(None, None, ("rows", "cols"))
    return jax.shard_map(
        shards,
        mesh=mesh,
        in_specs=(tile, tile, P(), P(), P(), P(), P(), P()),
        out_specs=(tile, P(), P(), P(), P(), sliced, sliced),
        check_vma=False,
    )
```

```python
import functools
import math

import jax
import jax.numpy as jnp
from jax import lax
from jax.experimental import pallas as pl
from jax.experimental.pallas import tpu as pltpu
from jax.sharding import PartitionSpec as P

EPSILON = 1e-06
INV_ROOT_TAU = 0.3989422804014327
HALF_LOG2E = 0.7213475204444817
ERFC_SLOPE = 0.4 * 0.7071067811865476
ERFC_TERMS = (
    0.22479419400284972,
    0.2383621945582281,
    0.12991301634379934,
    0.4353236101490443,
    -0.41611664430523265,
    0.7235898182708315,
    -0.41436965913692125,
    0.07850346878444278,
)
LANES = 128
HALO = 3
WIDE = 2 * HALO
F32 = jnp.float32
BF16 = jnp.bfloat16


def normal_parts(x):
    bell = jnp.exp2(x * x * (-HALF_LOG2E))
    t = 1.0 / (1.0 + ERFC_SLOPE * jnp.abs(x))
    series = 0.5 * ERFC_TERMS[7]
    for term in ERFC_TERMS[6::-1]:
        series = series * t + 0.5 * term
    tail = series * t * bell
    return jnp.where(x >= 0, 1.0 - tail, tail), bell


def gelu_only(x):
    cdf, _ = normal_parts(x)
    return x * cdf


def gelu_parts(x):
    cdf, bell = normal_parts(x)
    return x * cdf, cdf + x * bell * INV_ROOT_TAU


def strip_rows(rows, cols):
    most = max(1, 288 // cols)
    return max(d for d in range(1, rows + 1) if rows % d == 0 and d <= most)


def conv_pass(source, row0, col0, taps, target, rows, cols, back=False):
    strip = strip_rows(rows, cols)
    groups = source.shape[0]

    def one_strip(step, carry):
        g = step // (rows // strip)
        top = (step % (rows // strip)) * strip
        sums = [jnp.zeros((cols, LANES), F32) for _ in range(strip)]
        for b in range(7):
            spots = [48 - 7 * a - b if back else 7 * a + b for a in range(7)]
            weights = [taps[g, pl.ds(spot, 1), :] for spot in spots]
            for r in range(strip + 6):
                line = source[g, row0 + top + r, pl.ds(col0 + b, cols), :]
                for a in range(7):
                    if 0 <= r - a < strip:
                        sums[r - a] = sums[r - a] + weights[a] * line
        for i in range(strip):
            target[g, top + i] = sums[i]
        return carry

    lax.fori_loop(0, groups * (rows // strip), one_strip, 0)


def tap_pass(source, row0, col0, grad, grow0, gcol0, target, first, rows, cols):
    for g in range(source.shape[0]):
        lanes = slice(g * LANES, (g + 1) * LANES)
        for b in range(7):
            def one_row(i, sums):
                line = grad[g, grow0 + i, pl.ds(gcol0, cols), :]
                out = []
                for a in range(7):
                    part = line * source[g, row0 + i + a, pl.ds(col0 + b, cols), :]
                    out.append(sums[a] + part.reshape(cols // 8, 8, LANES).sum(0))
                return tuple(out)

            sums = lax.fori_loop(
                0, rows, one_row, tuple(jnp.zeros((8, LANES), F32) for _ in range(7)), unroll=4
            )
            for a in range(7):
                target[pl.ds(first + 7 * a + b, 1), lanes] = jnp.sum(sums[a], axis=0, keepdims=True)


def joined(ref, rows, cols=slice(None)):
    parts = [ref[g, rows, cols, :] for g in range(ref.shape[0])]
    return jnp.concatenate([p.reshape(-1, LANES) for p in parts], axis=1)


def split_to(ref, rows, value, shape):
    for g in range(ref.shape[0]):
        ref[g, rows] = value[:, g * LANES : (g + 1) * LANES].reshape(*shape, LANES)


def norm_parts(z):
    center = z - jnp.mean(z, axis=-1, keepdims=True)
    inv = lax.rsqrt(jnp.mean(center * center, axis=-1, keepdims=True) + EPSILON)
    return center * inv, inv


def norm_back(dn, hat, inv, gain):
    scaled = dn * gain
    return inv * (
        scaled
        - jnp.mean(scaled, axis=-1, keepdims=True)
        - hat * jnp.mean(scaled * hat, axis=-1, keepdims=True)
    )


def dot_nn(a, b):
    return jnp.dot(a, b, preferred_element_type=F32)


def dot_nt(a, b):
    return lax.dot_general(a, b, (((1,), (1,)), ((), ())), preferred_element_type=F32)


def dot_tn(a, b):
    return lax.dot_general(a, b, (((0,), (0,)), ((), ())), preferred_element_type=F32)


def pixel_blocks(pixels):
    best = max(d for d in range(16, 257, 16) if pixels % d == 0)
    return [slice(start, start + best) for start in range(0, pixels, best)]


def hidden_chunks(hidden):
    size = 256 if hidden % 256 == 0 else hidden
    return [slice(start, start + size) for start in range(0, hidden, size)]


def mlp_grads(normed, grad, w_in, b_in, w_out, act, gpre, db):
    pixels = grad.shape[0]
    for cut in hidden_chunks(w_in.shape[2]):
        bias = b_in[:, cut]
        bias_sum = None
        for block in pixel_blocks(pixels):
            pre = dot_nn(normed[block, :], w_in[0, :, cut]) + bias
            value, slope = gelu_parts(pre)
            act[block, cut] = value.astype(BF16)
            gradient = dot_nn(grad[block, :], w_out[0, :, cut]) * slope
            gpre[block, cut] = gradient.astype(BF16)
            part = jnp.sum(gradient, axis=0, keepdims=True)
            bias_sum = part if bias_sum is None else bias_sum + part
        db[:, cut] = bias_sum


def weight_grads(place, normed, grad, act, gpre, dw, per):
    hidden, channels = act.shape[1], grad.shape[1]
    size = min(n for n in range(128, hidden + 1, 128) if hidden % n == 0 and n % (2 * per) == 0 and n >= 256)
    for first in range(0, hidden, size):
        cut = slice(first, first + size)
        for i, (left, right) in enumerate(((gpre, normed), (act, grad))):
            value = dot_tn(left[:, cut], right[...]).astype(BF16)
            if len(dw) == 1:
                dw[0][i, cut, :] = value
                continue
            value = value.reshape(size // (2 * per), 2, per, channels)
            upper = place[4] == 1
            half = slice(first // 2, (first + size) // 2)
            dw[0][i, half, :] = jnp.where(upper, value[:, 0], value[:, 1]).reshape(-1, channels)
            dw[1][i, half, :] = jnp.where(upper, value[:, 1], value[:, 0]).reshape(-1, channels)


def fetch_layers(triples, arrived):
    copies = [
        pltpu.make_async_copy(source.at[pl.ds(layer, 1)], target, arrived.at[i])
        for i, (source, layer, target) in enumerate(triples)
    ]
    for copy in copies:
        copy.start()
    return copies


def block_back(z, grad, layer, gains, shifts, weights, b_in, outs, scratch):
    dz_out, db, dgain, dshift = outs
    normed, act, gpre = scratch
    gain = gains[layer : layer + 1]
    hat, inv = norm_parts(joined(z, slice(None)))
    normed[...] = (hat * gain + shifts[layer : layer + 1]).astype(BF16)
    w_in, w_out, waits = weights
    for wait in waits:
        wait.wait()
    mlp_grads(normed, grad, w_in, b_in.at[layer], w_out, act, gpre, db)
    dn = dot_nt(gpre[...], w_in[0])
    dgain[...] = jnp.sum(dn * hat, axis=0, keepdims=True)
    dshift[...] = jnp.sum(dn, axis=0, keepdims=True)
    dz_out[...] = norm_back(dn, hat, inv, gain).astype(BF16)


def forward_kernel(
    place, xpad, taps, gains, shifts, w_in, w_out, b_in, mids, z_out,
    xs, zs, act, w_in0, w_out0, arrived,
):
    waits = fetch_layers(((w_in, 0, w_in0), (w_out, 0, w_out0)), arrived)
    groups, mid_rows, mid_cols = zs.shape[:3]
    rows, cols = z_out.shape[1:3]
    for g in range(groups):
        xs[g] = xpad[:, :, g * LANES : (g + 1) * LANES].astype(F32)
    conv_pass(xs, 0, 0, taps.at[0], zs, mid_rows, mid_cols)
    z_out[...] = zs[:, HALO : HALO + rows, HALO : HALO + cols, :]
    strip = act.shape[0] // mid_cols
    for wait in waits:
        wait.wait()

    def one_strip(step, carry):
        top = step * strip
        hat, _ = norm_parts(joined(zs, pl.ds(top, strip)))
        normed = (hat * gains[0:1] + shifts[0:1]).astype(BF16)
        for cut in hidden_chunks(w_in0.shape[2]):
            pre = dot_nn(normed, w_in0[0, :, cut]) + b_in[0, :, cut]
            act[:, cut] = gelu_only(pre).astype(BF16)
        mixed = dot_nt(act[...], w_out0[0])
        row = lax.broadcasted_iota(jnp.int32, (strip, mid_cols, 1), 0) + (top - HALO) + place[0]
        col = lax.broadcasted_iota(jnp.int32, (strip, mid_cols, 1), 1) - HALO + place[1]
        real = (row >= 0) & (row < place[2]) & (col >= 0) & (col < place[3])
        real = jnp.where(real, 1.0, 0.0).reshape(strip * mid_cols, 1)
        base = joined(xs, pl.ds(top + HALO, strip), slice(HALO, HALO + mid_cols))
        mid = (base + mixed).astype(BF16).astype(F32) * real
        split_to(mids, pl.ds(top, strip), mid, (strip, mid_cols))
        return carry

    lax.fori_loop(0, mid_rows // strip, one_strip, 0)


def top_kernel(
    mids, grad, taps, gains, shifts, w_in, w_out, b_in,
    dz_out, normed, act, gpre, db, dgain, dshift, z, w_in1, w_out1, arrived,
):
    waits = fetch_layers(((w_in, 1, w_in1), (w_out, 1, w_out1)), arrived)
    conv_pass(mids, 0, 0, taps.at[1], z, *z.shape[1:3])
    block_back(
        z, grad, 1, gains, shifts, (w_in1, w_out1, waits), b_in,
        (dz_out, db, dgain, dshift), (normed, act, gpre),
    )


def low_kernel(
    per, place, dzpad, grad, z0, taps, gains, shifts, w_in, w_out, b_in,
    gmid, dz_out, db, dgain, dshift, *rest,
):
    *dw, dzs, spread, normed, act, gpre, w_in0, w_out0, arrived = rest
    waits = fetch_layers(((w_in, 0, w_in0), (w_out, 0, w_out0)), arrived)
    spread_pass(dzpad, dzs, taps.at[1], spread)
    gmid[...] = (grad[...].astype(F32) + joined(spread, slice(None))).astype(BF16)
    block_back(
        z0, gmid, 0, gains, shifts, (w_in0, w_out0, waits), b_in,
        (dz_out, db, dgain, dshift), (normed, act, gpre),
    )
    weight_grads(place, normed, gmid, act, gpre, dw, per)


def weights_top_kernel(per, place, normed, act, gpre, grad, *dw):
    weight_grads(place, normed, grad, act, gpre, dw, per)


def spread_pass(dzpad, dzs, taps, spread):
    for g in range(dzs.shape[0]):
        dzs[g] = dzpad[:, :, g * LANES : (g + 1) * LANES].astype(F32)
    conv_pass(dzs, 0, 0, taps, spread, *spread.shape[1:3], back=True)


def last_kernel(dzpad, gmid, taps, out, dzs, spread):
    spread_pass(dzpad, dzs, taps.at[0], spread)
    out[...] = (gmid[...].astype(F32) + joined(spread, slice(None))).astype(BF16)


def small_rows_of(values, row0, col0, dz, dzs, db, dgain, dshift, sums):
    rows, cols = dzs.shape[1:3]
    channels = sums.shape[1]
    split_to(dzs, slice(None), dz[...].astype(F32), (rows, cols))
    count = db.shape[1] // channels
    for k in range(count):
        sums[k : k + 1, :] = db[:, k * channels : (k + 1) * channels]
    sums[count : count + 1, :] = dgain[...]
    sums[count + 1 : count + 2, :] = dshift[...]
    tap_pass(values, row0, col0, dzs, 0, 0, sums, count + 2, rows, cols)


def taps_kernel(
    place, mids, xpad, dz0, dz1, db0, dgain0, dshift0, db1, dgain1, dshift1, send, keep,
    xs, dzs, sums0, sums1,
):
    for g in range(dzs.shape[0]):
        xs[g] = xpad[:, :, g * LANES : (g + 1) * LANES].astype(F32)
    sums0[...] = jnp.zeros(sums0.shape, F32)
    sums1[...] = jnp.zeros(sums1.shape, F32)
    small_rows_of(mids, 0, 0, dz1, dzs, db1, dgain1, dshift1, sums1)
    small_rows_of(xs, HALO, HALO, dz0, dzs, db0, dgain0, dshift0, sums0)
    upper = place[4] == 1
    send[...] = jnp.where(upper, sums0[...], sums1[...]).astype(BF16)
    keep[...] = jnp.where(upper, sums1[...], sums0[...]).astype(BF16)


def small_kernel(scale, place, mine, got, taps_out, gains, shifts, biases):
    upper = place[4] == 1
    own, came = mine[...].astype(F32) * scale, got[...].astype(F32) * scale
    channels = own.shape[1]
    count = biases.shape[1] // channels
    for layer, part in enumerate((jnp.where(upper, came, own), jnp.where(upper, own, came))):
        at = slice(layer, layer + 1)
        for k in range(count):
            biases[at, k * channels : (k + 1) * channels] = part[k : k + 1, :]
        gains[at, :] = part[count : count + 1, :]
        shifts[at, :] = part[count + 1 : count + 2, :]
        for tap in range(49):
            taps_out[tap, at, :] = part[count + 2 + tap : count + 3 + tap, :]


def weights_kernel(scale, keep0, got0, keep1, got1, out_in, out_out):
    for layer, (keep, got) in enumerate(((keep0, got0), (keep1, got1))):
        for i, out in enumerate((out_in, out_out)):
            out[layer] = (keep[i].astype(F32) + got[i].astype(F32)) * scale


def shape(*dims, dtype=F32):
    return jax.ShapeDtypeStruct(dims, dtype)


def run(kernel, outs, scratch, args, specs=None, fetched=0, name=None):
    vmem = pl.BlockSpec(memory_space=pltpu.VMEM)
    semaphores = [pltpu.SemaphoreType.DMA((fetched,))] if fetched else []
    return pl.pallas_call(
        kernel,
        out_shape=outs,
        in_specs=[
            vmem if s is None else pl.BlockSpec(memory_space=s) for s in (specs or [None] * len(args))
        ],
        out_specs=tuple(vmem for _ in outs),
        scratch_shapes=[pltpu.VMEM(s.shape, s.dtype) for s in scratch] + semaphores,
        compiler_params=pltpu.CompilerParams(vmem_limit_bytes=50 * 1024 * 1024),
        name=name,
    )(*args)


def edges(tile, axis, width, odd):
    count = tile.shape[axis]
    low = lax.slice_in_dim(tile, 0, width, axis=axis)
    high = lax.slice_in_dim(tile, count - width, count, axis=axis)
    return jnp.where(odd, low, high), jnp.where(odd, high, low)


def to_twin(edge, axis):
    count = lax.axis_size(axis)
    return lax.ppermute(edge, axis, [(i, i ^ 1) for i in range(count) if i ^ 1 < count])


def to_other(edge, axis):
    n_rows, n_cols = lax.axis_size("rows"), lax.axis_size("cols")
    count = lax.axis_size(axis)
    pairs = []
    for r in range(n_rows):
        for c in range(n_cols):
            at = r if axis == "rows" else c
            partner = at + 1 if at % 2 else at - 1
            if 0 <= partner < count:
                there = (partner, c) if axis == "rows" else (r, partner)
            else:
                there = (r, c ^ 1) if axis == "rows" else (r ^ 1, c)
            pairs.append((r * n_cols + c, there[0] * n_cols + there[1]))
    return lax.ppermute(edge, ("rows", "cols"), pairs)


def rimmed(tile, from_twin, from_other, axis, odd, outer):
    from_other = jnp.where(outer, jnp.zeros_like(from_other), from_other)
    low = jnp.where(odd, from_twin, from_other)
    high = jnp.where(odd, from_other, from_twin)
    return jnp.concatenate([low, tile, high], axis=axis)


def flip_bit(value, bit):
    both = ("rows", "cols")
    total = lax.axis_size("rows") * lax.axis_size("cols")
    return lax.ppermute(value, both, [(i, i ^ (1 << bit)) for i in range(total)])


def halves(chunks, dim, mine):
    sizes = [1 if d == dim else n for d, n in enumerate(chunks.shape)]

    def one(bit):
        starts = [bit if d == dim else jnp.uint32(0) for d in range(chunks.ndim)]
        return lax.squeeze(lax.dynamic_slice(chunks, starts, sizes), (dim,))

    return one(mine[1]), one(mine[0])


def summed(own, got):
    return (own.astype(F32) + got.astype(F32)).astype(BF16)


def cut(chunks, order, bit, mine):
    spot = order.index(bit)
    per = chunks.shape[-2:]
    pair = chunks.reshape((-1, 2 ** spot, 2, 2 ** (len(order) - spot - 1)) + per)
    send, keep = halves(pair, 2, mine[bit])
    return send, keep, [b for b in order if b != bit]


def step(chunks, order, bit, mine):
    send, keep, left = cut(chunks, order, bit, mine)
    return keep, flip_bit(send, bit), left


def shards(activations, grad_out, kernels, norm_gains, norm_shifts, w_in, b_in, w_out):
    rows, cols, channels = activations.shape
    layers, _, hidden = w_in.shape
    groups = channels // LANES
    n_rows, n_cols = lax.axis_size("rows"), lax.axis_size("cols")
    total = n_rows * n_cols
    bits = total.bit_length() - 1
    col_bits = n_cols.bit_length() - 1
    me = (lax.axis_index("rows") * n_cols + lax.axis_index("cols")).astype(jnp.uint32)
    mine = [(((me >> k) & 1), 1 - ((me >> k) & 1)) for k in range(bits)]
    grad_scale = 1.0 / math.sqrt(rows * cols * total)
    pixels = rows * cols

    taps = kernels.reshape(layers, 49, groups, LANES).transpose(0, 2, 1, 3)
    biases = b_in[:, None, :]
    place = jnp.stack(
        [
            lax.axis_index("rows") * rows,
            lax.axis_index("cols") * cols,
            jnp.int32(rows * n_rows),
            jnp.int32(cols * n_cols),
            lax.axis_index("cols") & 1,
        ]
    ).astype(jnp.int32)
    grad_flat = grad_out.reshape(pixels, channels)

    at_row, at_col = lax.axis_index("rows"), lax.axis_index("cols")
    odd_col, odd_row = (at_col & 1) == 1, (at_row & 1) == 1
    outer_col = (at_col == 0) | (at_col == n_cols - 1)
    outer_row = (at_row == 0) | (at_row == n_rows - 1)

    def rim_cols(tile, width):
        twin, other = edges(tile, 1, width, odd_col)
        return rimmed(tile, to_twin(twin, "cols"), to_other(other, "cols"), 1, odd_col, outer_col)

    def rim_rows(tile, width):
        twin, other = edges(tile, 0, width, odd_row)
        return rimmed(tile, to_twin(twin, "rows"), to_other(other, "rows"), 0, odd_row, outer_row)

    def filled(wide):
        return jnp.pad(wide, ((0, 0), (0, cols + 16 - wide.shape[1]), (0, 0)))

    mid_rows, mid_cols = rows + 2 * HALO, cols + 8
    strip = max(d for d in range(1, mid_rows + 1) if mid_rows % d == 0 and d * mid_cols <= 264)
    weights = [shape(1, channels, hidden, dtype=BF16)] * 2
    tile_z = shape(groups, rows, cols, LANES)
    tile_b = shape(pixels, channels, dtype=BF16)
    tile_h = shape(pixels, hidden, dtype=BF16)
    per = hidden // total
    split = 2 if per % 16 == 0 and col_bits == 2 else 1
    grads_b = (shape(2, hidden // split, channels, dtype=BF16),) * split
    small_outs = (shape(1, hidden), shape(1, channels), shape(1, channels))
    small_rows = 64

    xpad = filled(rim_cols(rim_rows(activations, WIDE), WIDE))
    xpad, place, mine, odd_col, odd_row, outer_col, outer_row = lax.optimization_barrier(
        (xpad, place, mine, odd_col, odd_row, outer_col, outer_row)
    )
    mids, z0 = run(
        forward_kernel,
        (shape(groups, mid_rows, mid_cols, LANES), tile_z),
        [
            shape(groups, *xpad.shape[:2], LANES),
            shape(groups, mid_rows, mid_cols, LANES),
            shape(strip * mid_cols, hidden, dtype=BF16),
        ]
        + weights,
        (place, xpad, taps, norm_gains, norm_shifts, w_in, w_out, biases),
        [pltpu.SMEM] + [None] * 4 + [pl.ANY] * 2 + [None],
        fetched=2,
        name="forward",
    )
    dz1, normed1, act1, gpre1, *small1 = run(
        top_kernel,
        (tile_b, tile_b, tile_h, tile_h) + small_outs,
        [tile_z] + weights,
        (mids, grad_flat, taps, norm_gains, norm_shifts, w_in, w_out, biases),
        [None] * 5 + [pl.ANY] * 2 + [None],
        fetched=2,
        name="top",
    )

    sides = (col_bits - 1, col_bits)

    def fenced(*values):
        leaves, tree = jax.tree.flatten(values)
        arrays = [i for i, leaf in enumerate(leaves) if not isinstance(leaf, int)]
        for i, value in zip(arrays, lax.optimization_barrier(tuple(leaves[i] for i in arrays))):
            leaves[i] = value
        return jax.tree.unflatten(tree, leaves)

    def settled(flight):
        return summed(flight[0], flight[1]), flight[2]

    def start(dw):
        order = list(range(bits - 1, -1, -1))
        if split == 2:
            send, keep = (d.reshape(2, total // 2, per, channels) for d in dw)
            return keep, flip_bit(send, 0), order[:-1]
        chunks = dw[0].reshape(2, total, per, channels)
        for bit in range(col_bits - 2):
            chunks, order = settled(step(chunks, order, bit, mine))
        return step(chunks, order, col_bits - 2, mine)

    def fork(flight):
        chunks, order = settled(flight)
        return [step(chunks[i], order, sides[i], mine) for i in range(2)]

    def onward(parts, bit):
        kept, sent, lefts = [], [], []
        for chunks, order in parts:
            send, keep, left = cut(chunks, order, bit, mine)
            kept.append(keep)
            sent.append(send.reshape(-1, per, channels))
            lefts.append(left)
        got = flip_bit(jnp.concatenate(sent, axis=0), bit)
        flights, first = [], 0
        for keep, send, left in zip(kept, sent, lefts):
            came = got[first : first + send.shape[0]].reshape(keep.shape)
            flights.append((keep, came, left))
            first += send.shape[0]
        return flights

    def merged(flights):
        done = [settled(f) for f in flights]
        return jnp.stack([d[0].reshape(-1, per, channels) for d in done]), done[0][1]

    tile1 = dz1.reshape(rows, cols, channels)
    twin, other = edges(tile1, 0, HALO, odd_row)
    twin, other = to_twin(twin, "rows"), to_other(other, "rows")
    dw1 = run(
        functools.partial(weights_top_kernel, per),
        grads_b,
        [],
        (place, normed1, act1, gpre1, grad_flat),
        [pltpu.SMEM] + [None] * 4,
        name="weights_top",
    )
    tile1, twin, other, dw1 = fenced(tile1, twin, other, dw1)
    wide1 = rimmed(tile1, twin, other, 0, odd_row, outer_row)
    run1 = start(dw1)
    twin, other = edges(wide1, 1, HALO, odd_col)
    twin, other = to_twin(twin, "cols"), to_other(other, "cols")
    wide1, twin, other, run1 = fenced(wide1, twin, other, run1)
    pair1 = fork(run1)
    dzpad1 = filled(rimmed(wide1, twin, other, 1, odd_col, outer_col))
    spread_scratch = [shape(groups, *dzpad1.shape[:2], LANES), tile_z]
    grad_mid, dz0, *rest = run(
        functools.partial(low_kernel, per),
        (tile_b, tile_b) + small_outs + grads_b,
        spread_scratch + [tile_b, tile_h, tile_h] + weights,
        (place, dzpad1, grad_flat, z0, taps, norm_gains, norm_shifts, w_in, w_out, biases),
        [pltpu.SMEM] + [None] * 6 + [pl.ANY] * 2 + [None],
        fetched=2,
        name="low",
    )
    small0, dw0 = rest[:3], rest[3:]
    dz0, dw0, pair1, small0 = fenced(dz0, dw0, pair1, small0)
    run0 = start(dw0)
    low_bit = col_bits + 1
    pair1 = onward([settled(f) for f in pair1], low_bit)
    small_b = shape(small_rows, channels, dtype=BF16)
    small_f = shape(small_rows, channels)
    send, small = run(
        taps_kernel,
        (small_b, small_b),
        [shape(groups, *xpad.shape[:2], LANES), tile_z, small_f, small_f],
        (place, mids, xpad, dz0, dz1, *small0, *small1),
        [pltpu.SMEM] + [None] * 10,
        name="taps",
    )
    small_got = flip_bit(send, 0)
    run0, small, small_got, dz0 = fenced(run0, small, small_got, dz0)
    pair0 = fork(run0)
    tile0 = dz0.reshape(rows, cols, channels)
    twin, other = edges(tile0, 0, HALO, odd_row)
    twin, other = to_twin(twin, "rows"), to_other(other, "rows")
    small = summed(small, small_got)
    small_got = flip_bit(small, 1)
    pair0, pair1, tile0, twin, other, small, small_got = fenced(
        pair0, pair1, tile0, twin, other, small, small_got
    )
    both = [onward([settled(pair0[i]), settled(pair1[i])], sides[1 - i]) for i in range(2)]
    wide0 = rimmed(tile0, twin, other, 0, odd_row, outer_row)
    twin, other = edges(wide0, 1, HALO, odd_col)
    twin, other = to_twin(twin, "cols"), to_other(other, "cols")
    small = summed(small, small_got)
    small_got = flip_bit(small, 2)
    both, wide0, twin, other, small, small_got = fenced(both, wide0, twin, other, small, small_got)
    (run0,) = onward([merged([both[0][0], both[1][0]])], low_bit)
    part1, order1 = merged([both[0][1], both[1][1]])
    flight1 = (part1, jnp.zeros_like(part1), order1)
    if order1:
        (flight1,) = onward([(part1, order1)], order1[-1])
    small = summed(small, small_got)
    small_got = flip_bit(small, 3)
    (grad_in,) = run(
        last_kernel,
        (tile_b,),
        spread_scratch,
        (filled(rimmed(wide0, twin, other, 1, odd_col, outer_col)), grad_mid, taps),
        name="last",
    )
    for bit in range(4, bits):
        run0, flight1, small, small_got, grad_in = fenced(run0, flight1, small, small_got, grad_in)
        if run0[2]:
            (run0,) = onward([settled(run0)], run0[2][-1])
        if flight1[2]:
            (flight1,) = onward([settled(flight1)], flight1[2][-1])
        small = summed(small, small_got)
        small_got = flip_bit(small, bit)
    run0, flight1, small, small_got = fenced(run0, flight1, small, small_got)
    small = summed(small, small_got)
    small_got = flip_bit(small, 0)
    share = shape(layers, per, channels)
    grad_w_in, grad_w_out = run(
        functools.partial(weights_kernel, grad_scale),
        (share, share),
        [],
        [part.reshape(2, per, channels) for part in run0[:2] + flight1[:2]],
        name="weights",
    )
    grad_taps, grad_gains, grad_shifts, grad_b_in = run(
        functools.partial(small_kernel, grad_scale),
        (
            shape(49, layers, channels),
            shape(layers, channels),
            shape(layers, channels),
            shape(layers, hidden),
        ),
        [],
        (place, small, small_got),
        [pltpu.SMEM, None, None],
        name="small",
    )
    return (
        grad_in.reshape(rows, cols, channels),
        grad_taps.reshape(7, 7, layers, channels).transpose(2, 0, 1, 3),
        grad_gains,
        grad_shifts,
        grad_b_in,
        jnp.swapaxes(grad_w_in, 1, 2),
        jnp.swapaxes(grad_w_out, 1, 2),
    )


def solution(mesh):
    tile = P("rows", "cols", None)
    sliced = P(None, None, ("rows", "cols"))
    return jax.shard_map(
        shards,
        mesh=mesh,
        in_specs=(tile, tile, P(), P(), P(), P(), P(), P()),
        out_specs=(tile, P(), P(), P(), P(), sliced, sliced),
        check_vma=False,
    )
```

```python
import functools
import math

import jax
import jax.numpy as jnp
from jax import lax
from jax.experimental import pallas as pl
from jax.experimental.pallas import tpu as pltpu
from jax.sharding import PartitionSpec as P

EPSILON = 1e-06
INV_ROOT_TAU = 0.3989422804014327
HALF_LOG2E = 0.7213475204444817
ERFC_SLOPE = 0.4 * 0.7071067811865476
ERFC_TERMS = (
    0.22479419400284972,
    0.2383621945582281,
    0.12991301634379934,
    0.4353236101490443,
    -0.41611664430523265,
    0.7235898182708315,
    -0.41436965913692125,
    0.07850346878444278,
)
LANES = 128
HALO = 3
WIDE = 2 * HALO
F32 = jnp.float32
BF16 = jnp.bfloat16


def normal_parts(x):
    bell = jnp.exp2(x * x * (-HALF_LOG2E))
    t = 1.0 / (1.0 + ERFC_SLOPE * jnp.abs(x))
    series = 0.5 * ERFC_TERMS[7]
    for term in ERFC_TERMS[6::-1]:
        series = series * t + 0.5 * term
    tail = series * t * bell
    return jnp.where(x >= 0, 1.0 - tail, tail), bell


def gelu_only(x):
    cdf, _ = normal_parts(x)
    return x * cdf


def gelu_parts(x):
    cdf, bell = normal_parts(x)
    return x * cdf, cdf + x * bell * INV_ROOT_TAU


def strip_rows(rows, cols):
    most = max(1, 288 // cols)
    return max(d for d in range(1, rows + 1) if rows % d == 0 and d <= most)


def conv_pass(source, row0, col0, taps, target, rows, cols, back=False):
    strip = strip_rows(rows, cols)
    groups = source.shape[0]

    def one_strip(step, carry):
        g = step // (rows // strip)
        top = (step % (rows // strip)) * strip
        sums = [jnp.zeros((cols, LANES), F32) for _ in range(strip)]
        for b in range(7):
            spots = [48 - 7 * a - b if back else 7 * a + b for a in range(7)]
            weights = [taps[g, pl.ds(spot, 1), :] for spot in spots]
            for r in range(strip + 6):
                line = source[g, row0 + top + r, pl.ds(col0 + b, cols), :]
                for a in range(7):
                    if 0 <= r - a < strip:
                        sums[r - a] = sums[r - a] + weights[a] * line
        for i in range(strip):
            target[g, top + i] = sums[i]
        return carry

    lax.fori_loop(0, groups * (rows // strip), one_strip, 0)


def tap_pass(source, row0, col0, grad, target, rows, cols):
    def one_group(g, carry):
        lines = [grad[g, i] for i in range(rows)]
        for b in range(7):
            sums = [None] * 7
            for r in range(rows + 6):
                line = source[g, row0 + r, pl.ds(col0 + b, cols), :]
                for a in range(7):
                    if 0 <= r - a < rows:
                        part = lines[r - a] * line
                        sums[a] = part if sums[a] is None else sums[a] + part
            for a in range(7):
                total = jnp.sum(sums[a], axis=0, keepdims=True)
                target[g, pl.ds(7 * a + b, 1), :] = total
        return carry

    lax.fori_loop(0, source.shape[0], one_group, 0)


def joined(ref, rows, cols=slice(None)):
    parts = [ref[g, rows, cols, :] for g in range(ref.shape[0])]
    return jnp.concatenate([p.reshape(-1, LANES) for p in parts], axis=1)


def split_to(ref, rows, value, shape):
    for g in range(ref.shape[0]):
        ref[g, rows] = value[:, g * LANES : (g + 1) * LANES].reshape(*shape, LANES)


def norm_parts(z):
    center = z - jnp.mean(z, axis=-1, keepdims=True)
    inv = lax.rsqrt(jnp.mean(center * center, axis=-1, keepdims=True) + EPSILON)
    return center * inv, inv


def norm_back(dn, hat, inv, gain):
    scaled = dn * gain
    return inv * (
        scaled
        - jnp.mean(scaled, axis=-1, keepdims=True)
        - hat * jnp.mean(scaled * hat, axis=-1, keepdims=True)
    )


def dot_nn(a, b):
    return jnp.dot(a, b, preferred_element_type=F32)


def dot_nt(a, b):
    return lax.dot_general(a, b, (((1,), (1,)), ((), ())), preferred_element_type=F32)


def dot_tn(a, b):
    return lax.dot_general(a, b, (((0,), (0,)), ((), ())), preferred_element_type=F32)


def pixel_blocks(pixels):
    best = max(d for d in range(16, 257, 16) if pixels % d == 0)
    return [slice(start, start + best) for start in range(0, pixels, best)]


def hidden_chunks(hidden):
    size = 256 if hidden % 256 == 0 else hidden
    return [slice(start, start + size) for start in range(0, hidden, size)]


def hidden_forward(normed, w_in, bias, act, slope):
    for cut in hidden_chunks(w_in.shape[2]):
        for block in pixel_blocks(normed.shape[0]):
            value, factor = gelu_parts(dot_nn(normed[block, :], w_in[0, :, cut]) + bias[:, cut])
            act[block, cut] = value.astype(BF16)
            slope[block, cut] = factor


def hidden_back(grad, w_out, slope, gpre, db):
    for cut in hidden_chunks(w_out.shape[2]):
        bias_sum = None
        for block in pixel_blocks(grad.shape[0]):
            gradient = dot_nn(grad[block, :], w_out[0, :, cut]) * slope[block, cut]
            gpre[block, cut] = gradient.astype(BF16)
            part = jnp.sum(gradient, axis=0, keepdims=True)
            bias_sum = part if bias_sum is None else bias_sum + part
        db[:, cut] = bias_sum


def dz_of(gpre, w_in, hat, inv, gain, dz_out, dgain, dshift):
    dn = dot_nt(gpre[...], w_in[0])
    dgain[...] = jnp.sum(dn * hat, axis=0, keepdims=True)
    dshift[...] = jnp.sum(dn, axis=0, keepdims=True)
    dz_out[...] = norm_back(dn, hat, inv, gain).astype(BF16)


def mlp_grads(normed, grad, w_in, b_in, w_out, act, gpre, db):
    pixels = grad.shape[0]
    for cut in hidden_chunks(w_in.shape[2]):
        bias = b_in[:, cut]
        bias_sum = None
        for block in pixel_blocks(pixels):
            pre = dot_nn(normed[block, :], w_in[0, :, cut]) + bias
            value, slope = gelu_parts(pre)
            act[block, cut] = value.astype(BF16)
            gradient = dot_nn(grad[block, :], w_out[0, :, cut]) * slope
            gpre[block, cut] = gradient.astype(BF16)
            part = jnp.sum(gradient, axis=0, keepdims=True)
            bias_sum = part if bias_sum is None else bias_sum + part
        db[:, cut] = bias_sum


def weight_grads(place, normed, grad, act, gpre, dw, per):
    hidden, channels = act.shape[1], grad.shape[1]
    size = min(n for n in range(128, hidden + 1, 128) if hidden % n == 0 and n % (2 * per) == 0 and n >= 256)
    for first in range(0, hidden, size):
        cut = slice(first, first + size)
        for i, (left, right) in enumerate(((gpre, normed), (act, grad))):
            value = dot_tn(left[:, cut], right[...]).astype(BF16)
            if len(dw) == 1:
                dw[0][i, cut, :] = value
                continue
            value = value.reshape(size // (2 * per), 2, per, channels)
            upper = place[4] == 1
            half = slice(first // 2, (first + size) // 2)
            dw[0][i, half, :] = jnp.where(upper, value[:, 0], value[:, 1]).reshape(-1, channels)
            dw[1][i, half, :] = jnp.where(upper, value[:, 1], value[:, 0]).reshape(-1, channels)


def fetch_layers(triples, arrived):
    copies = [
        pltpu.make_async_copy(source.at[pl.ds(layer, 1)], target, arrived.at[i])
        for i, (source, layer, target) in enumerate(triples)
    ]
    for copy in copies:
        copy.start()
    return copies


def forward_kernel(
    place, xpad, taps, gains, shifts, w_in, w_out, b_in, mids, z_out,
    xs, zs, act, w_in0, w_out0, arrived,
):
    waits = fetch_layers(((w_in, 0, w_in0), (w_out, 0, w_out0)), arrived)
    groups, mid_rows, mid_cols = zs.shape[:3]
    rows, cols = z_out.shape[1:3]
    for g in range(groups):
        xs[g] = xpad[:, :, g * LANES : (g + 1) * LANES].astype(F32)
    conv_pass(xs, 0, 0, taps.at[0], zs, mid_rows, mid_cols)
    z_out[...] = zs[:, HALO : HALO + rows, HALO : HALO + cols, :]
    strip = act.shape[0] // mid_cols
    for wait in waits:
        wait.wait()

    def one_strip(step, carry):
        top = step * strip
        hat, _ = norm_parts(joined(zs, pl.ds(top, strip)))
        normed = (hat * gains[0:1] + shifts[0:1]).astype(BF16)
        for cut in hidden_chunks(w_in0.shape[2]):
            pre = dot_nn(normed, w_in0[0, :, cut]) + b_in[0, :, cut]
            act[:, cut] = gelu_only(pre).astype(BF16)
        mixed = dot_nt(act[...], w_out0[0])
        row = lax.broadcasted_iota(jnp.int32, (strip, mid_cols, 1), 0) + (top - HALO) + place[0]
        col = lax.broadcasted_iota(jnp.int32, (strip, mid_cols, 1), 1) - HALO + place[1]
        real = (row >= 0) & (row < place[2]) & (col >= 0) & (col < place[3])
        real = jnp.where(real, 1.0, 0.0).reshape(strip * mid_cols, 1)
        base = joined(xs, pl.ds(top + HALO, strip), slice(HALO, HALO + mid_cols))
        mid = (base + mixed).astype(BF16).astype(F32) * real
        split_to(mids, pl.ds(top, strip), mid, (strip, mid_cols))
        return carry

    lax.fori_loop(0, mid_rows // strip, one_strip, 0)


def top_kernel(
    mids, grad, taps, gains, shifts, w_in, w_out, b_in,
    dz_out, normed, act, gpre, db, dgain, dshift, z, w_in1, w_out1, arrived,
):
    waits = fetch_layers(((w_in, 1, w_in1), (w_out, 1, w_out1)), arrived)
    conv_pass(mids, 0, 0, taps.at[1], z, *z.shape[1:3])
    hat, inv = norm_parts(joined(z, slice(None)))
    normed[...] = (hat * gains[1:2] + shifts[1:2]).astype(BF16)
    for wait in waits:
        wait.wait()
    mlp_grads(normed, grad, w_in1, b_in.at[1], w_out1, act, gpre, db)
    dz_of(gpre, w_in1, hat, inv, gains[1:2], dz_out, dgain, dshift)


def again_kernel(z0, gains, shifts, w_in, b_in, hat_out, inv_out, normed, act, slope, w_in0, arrived):
    (wait,) = fetch_layers(((w_in, 0, w_in0),), arrived)
    hat, inv = norm_parts(joined(z0, slice(None)))
    hat_out[...] = hat
    inv_out[...] = jnp.broadcast_to(inv, inv_out.shape)
    normed[...] = (hat * gains[0:1] + shifts[0:1]).astype(BF16)
    wait.wait()
    hidden_forward(normed, w_in0, b_in.at[0], act, slope)


def low_kernel(
    per, place, dzpad, grad, hat, inv, normed, act, slope, taps, gains, w_in, w_out,
    gmid, dz_out, db, dgain, dshift, *rest,
):
    *dw, dzs, spread, gpre, w_in0, w_out0, arrived = rest
    waits = fetch_layers(((w_out, 0, w_out0), (w_in, 0, w_in0)), arrived)
    spread_pass(dzpad, dzs, taps.at[1], spread)
    gmid[...] = (grad[...].astype(F32) + joined(spread, slice(None))).astype(BF16)
    for wait in waits:
        wait.wait()
    hidden_back(gmid, w_out0, slope, gpre, db)
    dz_of(gpre, w_in0, hat[...], inv[:, :1], gains[0:1], dz_out, dgain, dshift)
    weight_grads(place, normed, gmid, act, gpre, dw, per)


def weights_top_kernel(per, place, normed, act, gpre, grad, *dw):
    weight_grads(place, normed, grad, act, gpre, dw, per)


def spread_pass(dzpad, dzs, taps, spread):
    for g in range(dzs.shape[0]):
        dzs[g] = dzpad[:, :, g * LANES : (g + 1) * LANES].astype(F32)
    conv_pass(dzs, 0, 0, taps, spread, *spread.shape[1:3], back=True)


def last_kernel(dzpad, gmid, taps, out, dzs, spread):
    spread_pass(dzpad, dzs, taps.at[0], spread)
    out[...] = (gmid[...].astype(F32) + joined(spread, slice(None))).astype(BF16)


def small_rows_of(values, row0, col0, dz, dzs, taps, db, dgain, dshift, sums):
    rows, cols = dzs.shape[1:3]
    channels = sums.shape[1]
    split_to(dzs, slice(None), dz[...].astype(F32), (rows, cols))
    count = db.shape[1] // channels
    for k in range(count):
        sums[k : k + 1, :] = db[:, k * channels : (k + 1) * channels]
    sums[count : count + 1, :] = dgain[...]
    sums[count + 1 : count + 2, :] = dshift[...]
    tap_pass(values, row0, col0, dzs, taps, rows, cols)
    for g in range(taps.shape[0]):
        sums[count + 2 : count + 51, g * LANES : (g + 1) * LANES] = taps[g]


def taps_kernel(
    place, mids, xpad, dz0, dz1, db0, dgain0, dshift0, db1, dgain1, dshift1, send, keep,
    xs, dzs, taps, sums0, sums1,
):
    for g in range(dzs.shape[0]):
        xs[g] = xpad[:, :, g * LANES : (g + 1) * LANES].astype(F32)
    sums0[...] = jnp.zeros(sums0.shape, F32)
    sums1[...] = jnp.zeros(sums1.shape, F32)
    small_rows_of(mids, 0, 0, dz1, dzs, taps, db1, dgain1, dshift1, sums1)
    small_rows_of(xs, HALO, HALO, dz0, dzs, taps, db0, dgain0, dshift0, sums0)
    upper = place[4] == 1
    send[...] = jnp.where(upper, sums0[...], sums1[...]).astype(BF16)
    keep[...] = jnp.where(upper, sums1[...], sums0[...]).astype(BF16)


def small_kernel(scale, place, mine, got, taps_out, gains, shifts, biases):
    upper = place[4] == 1
    own, came = mine[...].astype(F32) * scale, got[...].astype(F32) * scale
    channels = own.shape[1]
    count = biases.shape[1] // channels
    for layer, part in enumerate((jnp.where(upper, came, own), jnp.where(upper, own, came))):
        at = slice(layer, layer + 1)
        for k in range(count):
            biases[at, k * channels : (k + 1) * channels] = part[k : k + 1, :]
        gains[at, :] = part[count : count + 1, :]
        shifts[at, :] = part[count + 1 : count + 2, :]
        for tap in range(49):
            taps_out[tap, at, :] = part[count + 2 + tap : count + 3 + tap, :]


def weights_kernel(scale, keep0, got0, keep1, got1, out_in, out_out):
    for layer, (keep, got) in enumerate(((keep0, got0), (keep1, got1))):
        for i, out in enumerate((out_in, out_out)):
            out[layer] = (keep[i].astype(F32) + got[i].astype(F32)) * scale


def shape(*dims, dtype=F32):
    return jax.ShapeDtypeStruct(dims, dtype)


def run(kernel, outs, scratch, args, specs=None, fetched=0, name=None):
    vmem = pl.BlockSpec(memory_space=pltpu.VMEM)
    semaphores = [pltpu.SemaphoreType.DMA((fetched,))] if fetched else []
    return pl.pallas_call(
        kernel,
        out_shape=outs,
        in_specs=[
            vmem if s is None else pl.BlockSpec(memory_space=s) for s in (specs or [None] * len(args))
        ],
        out_specs=tuple(vmem for _ in outs),
        scratch_shapes=[pltpu.VMEM(s.shape, s.dtype) for s in scratch] + semaphores,
        compiler_params=pltpu.CompilerParams(vmem_limit_bytes=46 * 1024 * 1024),
        name=name,
    )(*args)


def edges(tile, axis, width, odd):
    count = tile.shape[axis]
    low = lax.slice_in_dim(tile, 0, width, axis=axis)
    high = lax.slice_in_dim(tile, count - width, count, axis=axis)
    return jnp.where(odd, low, high), jnp.where(odd, high, low)


def to_twin(edge, axis):
    count = lax.axis_size(axis)
    return lax.ppermute(edge, axis, [(i, i ^ 1) for i in range(count) if i ^ 1 < count])


def to_other(edge, axis):
    n_rows, n_cols = lax.axis_size("rows"), lax.axis_size("cols")
    count = lax.axis_size(axis)
    pairs = []
    for r in range(n_rows):
        for c in range(n_cols):
            at = r if axis == "rows" else c
            partner = at + 1 if at % 2 else at - 1
            if 0 <= partner < count:
                there = (partner, c) if axis == "rows" else (r, partner)
            else:
                there = (r, c ^ 1) if axis == "rows" else (r ^ 1, c)
            pairs.append((r * n_cols + c, there[0] * n_cols + there[1]))
    return lax.ppermute(edge, ("rows", "cols"), pairs)


def rimmed(tile, from_twin, from_other, axis, odd, outer):
    from_other = jnp.where(outer, jnp.zeros_like(from_other), from_other)
    low = jnp.where(odd, from_twin, from_other)
    high = jnp.where(odd, from_other, from_twin)
    return jnp.concatenate([low, tile, high], axis=axis)


def flip_bit(value, *bits):
    flip = sum(1 << bit for bit in bits)
    both = ("rows", "cols")
    total = lax.axis_size("rows") * lax.axis_size("cols")
    return lax.ppermute(value, both, [(i, i ^ flip) for i in range(total)])


def halves(chunks, dim, mine):
    sizes = [1 if d == dim else n for d, n in enumerate(chunks.shape)]

    def one(bit):
        starts = [bit if d == dim else jnp.uint32(0) for d in range(chunks.ndim)]
        return lax.squeeze(lax.dynamic_slice(chunks, starts, sizes), (dim,))

    return one(mine[1]), one(mine[0])


def summed(own, *got):
    parts = [part.astype(F32) for part in (own,) + got]
    while len(parts) > 1:
        parts = [a + b for a, b in zip(parts[::2], parts[1::2])]
    return parts[0].astype(BF16)


def cut(chunks, order, bit, mine):
    spot = order.index(bit)
    per = chunks.shape[-2:]
    pair = chunks.reshape((-1, 2 ** spot, 2, 2 ** (len(order) - spot - 1)) + per)
    send, keep = halves(pair, 2, mine[bit])
    return send, keep, [b for b in order if b != bit]


def step(chunks, order, bit, mine):
    send, keep, left = cut(chunks, order, bit, mine)
    return keep, flip_bit(send, bit), left


def shards(activations, grad_out, kernels, norm_gains, norm_shifts, w_in, b_in, w_out):
    rows, cols, channels = activations.shape
    layers, _, hidden = w_in.shape
    groups = channels // LANES
    n_rows, n_cols = lax.axis_size("rows"), lax.axis_size("cols")
    total = n_rows * n_cols
    bits = total.bit_length() - 1
    col_bits = n_cols.bit_length() - 1
    me = (lax.axis_index("rows") * n_cols + lax.axis_index("cols")).astype(jnp.uint32)
    mine = [(((me >> k) & 1), 1 - ((me >> k) & 1)) for k in range(bits)]
    grad_scale = 1.0 / math.sqrt(rows * cols * total)
    pixels = rows * cols

    taps = kernels.reshape(layers, 49, groups, LANES).transpose(0, 2, 1, 3)
    biases = b_in[:, None, :]
    place = jnp.stack(
        [
            lax.axis_index("rows") * rows,
            lax.axis_index("cols") * cols,
            jnp.int32(rows * n_rows),
            jnp.int32(cols * n_cols),
            lax.axis_index("cols") & 1,
        ]
    ).astype(jnp.int32)
    grad_flat = grad_out.reshape(pixels, channels)

    at_row, at_col = lax.axis_index("rows"), lax.axis_index("cols")
    odd_col, odd_row = (at_col & 1) == 1, (at_row & 1) == 1
    outer_col = (at_col == 0) | (at_col == n_cols - 1)
    outer_row = (at_row == 0) | (at_row == n_rows - 1)

    def rim_cols(tile, width):
        twin, other = edges(tile, 1, width, odd_col)
        return rimmed(tile, to_twin(twin, "cols"), to_other(other, "cols"), 1, odd_col, outer_col)

    def rim_rows(tile, width):
        twin, other = edges(tile, 0, width, odd_row)
        return rimmed(tile, to_twin(twin, "rows"), to_other(other, "rows"), 0, odd_row, outer_row)

    def filled(wide):
        return jnp.pad(wide, ((0, 0), (0, cols + 16 - wide.shape[1]), (0, 0)))

    mid_rows, mid_cols = rows + 2 * HALO, cols + 8
    strip = max(d for d in range(1, mid_rows + 1) if mid_rows % d == 0 and d * mid_cols <= 264)
    weights = [shape(1, channels, hidden, dtype=BF16)] * 2
    tile_z = shape(groups, rows, cols, LANES)
    tile_b = shape(pixels, channels, dtype=BF16)
    tile_h = shape(pixels, hidden, dtype=BF16)
    per = hidden // total
    split = 2 if per % 16 == 0 and col_bits == 2 else 1
    grads_b = (shape(2, hidden // split, channels, dtype=BF16),) * split
    small_outs = (shape(1, hidden), shape(1, channels), shape(1, channels))
    small_rows = 64

    xpad = filled(rim_cols(rim_rows(activations, WIDE), WIDE))
    xpad, place, mine, odd_col, odd_row, outer_col, outer_row = lax.optimization_barrier(
        (xpad, place, mine, odd_col, odd_row, outer_col, outer_row)
    )
    mids, z0 = run(
        forward_kernel,
        (shape(groups, mid_rows, mid_cols, LANES), tile_z),
        [
            shape(groups, *xpad.shape[:2], LANES),
            shape(groups, mid_rows, mid_cols, LANES),
            shape(strip * mid_cols, hidden, dtype=BF16),
        ]
        + weights,
        (place, xpad, taps, norm_gains, norm_shifts, w_in, w_out, biases),
        [pltpu.SMEM] + [None] * 4 + [pl.ANY] * 2 + [None],
        fetched=2,
        name="forward",
    )
    dz1, normed1, act1, gpre1, *small1 = run(
        top_kernel,
        (tile_b, tile_b, tile_h, tile_h) + small_outs,
        [tile_z] + weights,
        (mids, grad_flat, taps, norm_gains, norm_shifts, w_in, w_out, biases),
        [None] * 5 + [pl.ANY] * 2 + [None],
        fetched=2,
        name="top",
    )

    sides = (col_bits - 1, col_bits)

    def fenced(*values):
        leaves, tree = jax.tree.flatten(values)
        arrays = [i for i, leaf in enumerate(leaves) if not isinstance(leaf, int)]
        for i, value in zip(arrays, lax.optimization_barrier(tuple(leaves[i] for i in arrays))):
            leaves[i] = value
        return jax.tree.unflatten(tree, leaves)

    def settled(flight):
        return summed(flight[0], flight[1]), flight[2]

    def start(dw):
        order = list(range(bits - 1, -1, -1))
        if split == 2:
            send, keep = (d.reshape(2, total // 2, per, channels) for d in dw)
            return keep, flip_bit(send, 0), order[:-1]
        chunks = dw[0].reshape(2, total, per, channels)
        for bit in range(col_bits - 2):
            chunks, order = settled(step(chunks, order, bit, mine))
        return step(chunks, order, col_bits - 2, mine)

    def fork(flight):
        chunks, order = settled(flight)
        return [step(chunks[i], order, sides[i], mine) for i in range(2)]

    def onward(parts, bit, *riders):
        kept, sent, lefts = [], [], []
        for chunks, order in parts:
            send, keep, left = cut(chunks, order, bit, mine)
            kept.append(keep)
            sent.append(send.reshape(-1, channels))
            lefts.append(left)
        got = flip_bit(jnp.concatenate(sent + list(riders), axis=0), bit)
        flights, first = [], 0
        for keep, send, left in zip(kept, sent, lefts):
            came = got[first : first + send.shape[0]].reshape(keep.shape)
            flights.append((keep, came, left))
            first += send.shape[0]
        return flights, [got[first:]] if riders else []

    def merged(flights):
        done = [settled(f) for f in flights]
        return jnp.stack([d[0].reshape(-1, per, channels) for d in done]), done[0][1]

    tile1 = dz1.reshape(rows, cols, channels)
    twin, other = edges(tile1, 0, HALO, odd_row)
    twin, other = to_twin(twin, "rows"), to_other(other, "rows")
    dw1 = run(
        functools.partial(weights_top_kernel, per),
        grads_b,
        [],
        (place, normed1, act1, gpre1, grad_flat),
        [pltpu.SMEM] + [None] * 4,
        name="weights_top",
    )
    tile1, twin, other, dw1, z0 = fenced(tile1, twin, other, dw1, z0)
    wide1 = rimmed(tile1, twin, other, 0, odd_row, outer_row)
    run1 = start(dw1)
    twin, other = edges(wide1, 1, HALO, odd_col)
    twin, other = to_twin(twin, "cols"), to_other(other, "cols")
    tile_f = shape(pixels, channels)
    again = run(
        again_kernel,
        (tile_f, shape(pixels, LANES), tile_b, tile_h, shape(pixels, hidden)),
        weights[:1],
        (z0, norm_gains, norm_shifts, w_in, biases),
        [None] * 3 + [pl.ANY, None],
        fetched=1,
        name="again",
    )
    wide1, twin, other, run1, again = fenced(wide1, twin, other, run1, again)
    pair1 = fork(run1)
    dzpad1 = filled(rimmed(wide1, twin, other, 1, odd_col, outer_col))
    spread_scratch = [shape(groups, *dzpad1.shape[:2], LANES), tile_z]
    grad_mid, dz0, *rest = run(
        functools.partial(low_kernel, per),
        (tile_b, tile_b) + small_outs + grads_b,
        spread_scratch + [tile_h] + weights,
        (place, dzpad1, grad_flat, *again, taps, norm_gains, w_in, w_out),
        [pltpu.SMEM] + [None] * 9 + [pl.ANY] * 2,
        fetched=2,
        name="low",
    )
    small0, dw0 = rest[:3], rest[3:]
    dz0, dw0, pair1, small0 = fenced(dz0, dw0, pair1, small0)
    run0 = start(dw0)
    low_bit = col_bits + 1
    pair1, _ = onward([settled(f) for f in pair1], low_bit)
    run0, dz0, small0 = fenced(run0, dz0, small0)
    pair0 = fork(run0)
    tile0 = dz0.reshape(rows, cols, channels)
    twin, other = edges(tile0, 0, HALO, odd_row)
    twin, other = to_twin(twin, "rows"), to_other(other, "rows")
    small_b = shape(small_rows, channels, dtype=BF16)
    small_f = shape(small_rows, channels)
    send, small = run(
        taps_kernel,
        (small_b, small_b),
        [
            shape(groups, *xpad.shape[:2], LANES), tile_z, shape(groups, 49, LANES),
            small_f, small_f,
        ],
        (place, mids, xpad, dz0, dz1, *small0, *small1),
        [pltpu.SMEM] + [None] * 10,
        name="taps",
    )
    small_got = flip_bit(send, 0)
    pair0, pair1, tile0, twin, other, small, small_got = fenced(
        pair0, pair1, tile0, twin, other, small, small_got
    )
    small = summed(small, small_got)
    for bit in range(1, col_bits - 1):
        small = summed(small, flip_bit(small, bit))
    both, small_by = [], []
    for i in range(2):
        flights, (came,) = onward([settled(pair0[i]), settled(pair1[i])], sides[1 - i], small)
        both.append(flights)
        small_by.append(came)
    small_by.append(flip_bit(small, *sides))
    wide0 = rimmed(tile0, twin, other, 0, odd_row, outer_row)
    twin, other = edges(wide0, 1, HALO, odd_col)
    twin, other = to_twin(twin, "cols"), to_other(other, "cols")
    both, wide0, twin, other, small, small_by = fenced(both, wide0, twin, other, small, small_by)
    small = summed(small, small_by[0], small_by[1], small_by[2])
    (run0,), (small_got,) = onward([merged([both[0][0], both[1][0]])], low_bit, small)
    part1, order1 = merged([both[0][1], both[1][1]])
    flight1 = (part1, jnp.zeros_like(part1), order1)
    if order1:
        (flight1,), _ = onward([(part1, order1)], order1[-1])
    (grad_in,) = run(
        last_kernel,
        (tile_b,),
        spread_scratch,
        (filled(rimmed(wide0, twin, other, 1, odd_col, outer_col)), grad_mid, taps),
        name="last",
    )
    while run0[2]:
        run0, flight1, small, small_got, grad_in = fenced(run0, flight1, small, small_got, grad_in)
        small = summed(small, small_got)
        (run0,), (small_got,) = onward([settled(run0)], run0[2][-1], small)
        if flight1[2]:
            (flight1,), _ = onward([settled(flight1)], flight1[2][-1])
    run0, flight1, small, small_got = fenced(run0, flight1, small, small_got)
    small = summed(small, small_got)
    small_got = flip_bit(small, 0)
    share = shape(layers, per, channels)
    grad_w_in, grad_w_out = run(
        functools.partial(weights_kernel, grad_scale),
        (share, share),
        [],
        [part.reshape(2, per, channels) for part in run0[:2] + flight1[:2]],
        name="weights",
    )
    grad_taps, grad_gains, grad_shifts, grad_b_in = run(
        functools.partial(small_kernel, grad_scale),
        (
            shape(49, layers, channels),
            shape(layers, channels),
            shape(layers, channels),
            shape(layers, hidden),
        ),
        [],
        (place, small, small_got),
        [pltpu.SMEM, None, None],
        name="small",
    )
    return (
        grad_in.reshape(rows, cols, channels),
        grad_taps.reshape(7, 7, layers, channels).transpose(2, 0, 1, 3),
        grad_gains,
        grad_shifts,
        grad_b_in,
        jnp.swapaxes(grad_w_in, 1, 2),
        jnp.swapaxes(grad_w_out, 1, 2),
    )


def solution(mesh):
    tile = P("rows", "cols", None)
    sliced = P(None, None, ("rows", "cols"))
    return jax.shard_map(
        shards,
        mesh=mesh,
        in_specs=(tile, tile, P(), P(), P(), P(), P(), P()),
        out_specs=(tile, P(), P(), P(), P(), sliced, sliced),
        check_vma=False,
    )
```

```python
import functools
import math

import jax
import jax.numpy as jnp
from jax import lax
from jax.experimental import pallas as pl
from jax.experimental.pallas import tpu as pltpu
from jax.sharding import PartitionSpec as P

EPSILON = 1e-06
INV_ROOT_TAU = 0.3989422804014327
HALF_LOG2E = 0.7213475204444817
ERFC_SLOPE = 0.4 * 0.7071067811865476
ERFC_TERMS = (
    0.22479419400284972,
    0.2383621945582281,
    0.12991301634379934,
    0.4353236101490443,
    -0.41611664430523265,
    0.7235898182708315,
    -0.41436965913692125,
    0.07850346878444278,
)
LANES = 128
HALO = 3
WIDE = 2 * HALO
F32 = jnp.float32
BF16 = jnp.bfloat16


def normal_parts(x):
    bell = jnp.exp2(x * x * (-HALF_LOG2E))
    t = 1.0 / (1.0 + ERFC_SLOPE * jnp.abs(x))
    series = 0.5 * ERFC_TERMS[7]
    for term in ERFC_TERMS[6::-1]:
        series = series * t + 0.5 * term
    tail = series * t * bell
    return jnp.where(x >= 0, 1.0 - tail, tail), bell


def gelu_only(x):
    cdf, _ = normal_parts(x)
    return x * cdf


def gelu_parts(x):
    cdf, bell = normal_parts(x)
    return x * cdf, cdf + x * bell * INV_ROOT_TAU


def strip_rows(rows, cols):
    most = max(1, 288 // cols)
    return max(d for d in range(1, rows + 1) if rows % d == 0 and d <= most)


def conv_pass(source, row0, col0, taps, layer, target, rows, cols, back=False):
    strip = strip_rows(rows, cols)
    groups = source.shape[0]

    def one_strip(step, carry):
        g = step // (rows // strip)
        top = (step % (rows // strip)) * strip
        lanes = pl.ds(pl.multiple_of(g * LANES, LANES), LANES)
        sums = [jnp.zeros((cols, LANES), F32) for _ in range(strip)]
        for b in range(7):
            spots = [48 - 7 * a - b if back else 7 * a + b for a in range(7)]
            weights = [taps[spot, pl.ds(layer, 1), lanes] for spot in spots]
            for r in range(strip + 6):
                line = source[g, row0 + top + r, pl.ds(col0 + b, cols), :]
                for a in range(7):
                    if 0 <= r - a < strip:
                        sums[r - a] = sums[r - a] + weights[a] * line
        for i in range(strip):
            target[g, top + i] = sums[i]
        return carry

    lax.fori_loop(0, groups * (rows // strip), one_strip, 0)


def tap_pass(source, row0, col0, grad, target, rows, cols):
    def one_group(g, carry):
        lines = [grad[g, i] for i in range(rows)]
        for b in range(7):
            sums = [None] * 7
            for r in range(rows + 6):
                line = source[g, row0 + r, pl.ds(col0 + b, cols), :]
                for a in range(7):
                    if 0 <= r - a < rows:
                        part = lines[r - a] * line
                        sums[a] = part if sums[a] is None else sums[a] + part
            for a in range(7):
                total = jnp.sum(sums[a], axis=0, keepdims=True)
                target[g, pl.ds(7 * a + b, 1), :] = total
        return carry

    lax.fori_loop(0, source.shape[0], one_group, 0)


def joined(ref, rows, cols=slice(None)):
    parts = [ref[g, rows, cols, :] for g in range(ref.shape[0])]
    return jnp.concatenate([p.reshape(-1, LANES) for p in parts], axis=1)


def split_to(ref, rows, value, shape):
    for g in range(ref.shape[0]):
        ref[g, rows] = value[:, g * LANES : (g + 1) * LANES].reshape(*shape, LANES)


def norm_parts(z):
    center = z - jnp.mean(z, axis=-1, keepdims=True)
    inv = lax.rsqrt(jnp.mean(center * center, axis=-1, keepdims=True) + EPSILON)
    return center * inv, inv


def norm_back(dn, hat, inv, gain):
    scaled = dn * gain
    return inv * (
        scaled
        - jnp.mean(scaled, axis=-1, keepdims=True)
        - hat * jnp.mean(scaled * hat, axis=-1, keepdims=True)
    )


def dot_nn(a, b):
    return jnp.dot(a, b, preferred_element_type=F32)


def dot_nt(a, b):
    return lax.dot_general(a, b, (((1,), (1,)), ((), ())), preferred_element_type=F32)


def dot_tn(a, b):
    return lax.dot_general(a, b, (((0,), (0,)), ((), ())), preferred_element_type=F32)


def pixel_blocks(pixels):
    best = max(d for d in range(16, 257, 16) if pixels % d == 0)
    return [slice(start, start + best) for start in range(0, pixels, best)]


def hidden_chunks(hidden):
    size = 256 if hidden % 256 == 0 else hidden
    return [slice(start, start + size) for start in range(0, hidden, size)]


def hidden_forward(normed, w_in, bias, act, slope):
    for cut in hidden_chunks(w_in.shape[2]):
        for block in pixel_blocks(normed.shape[0]):
            value, factor = gelu_parts(dot_nn(normed[block, :], w_in[0, :, cut]) + bias[0:1, cut])
            act[block, cut] = value.astype(BF16)
            slope[block, cut] = factor


def hidden_back(grad, w_out, slope, gpre, db):
    for cut in hidden_chunks(w_out.shape[2]):
        bias_sum = None
        for block in pixel_blocks(grad.shape[0]):
            gradient = dot_nn(grad[block, :], w_out[0, :, cut]) * slope[block, cut]
            gpre[block, cut] = gradient.astype(BF16)
            part = jnp.sum(gradient, axis=0, keepdims=True)
            bias_sum = part if bias_sum is None else bias_sum + part
        db[:, cut] = bias_sum


def dz_of(gpre, w_in, hat, inv, gain, dz_out, dgain, dshift):
    dn = dot_nt(gpre[...], w_in)
    dgain[...] = jnp.sum(dn * hat, axis=0, keepdims=True)
    dshift[...] = jnp.sum(dn, axis=0, keepdims=True)
    dz_out[...] = norm_back(dn, hat, inv, gain).astype(BF16)


def mlp_grads(normed, grad, w_in, b_in, w_out, layer, act, gpre, db):
    pixels = grad.shape[0]
    for cut in hidden_chunks(w_in.shape[2]):
        bias = b_in[layer : layer + 1, cut]
        bias_sum = None
        for block in pixel_blocks(pixels):
            pre = dot_nn(normed[block, :], w_in[layer, :, cut]) + bias
            value, slope = gelu_parts(pre)
            act[block, cut] = value.astype(BF16)
            gradient = dot_nn(grad[block, :], w_out[layer, :, cut]) * slope
            gpre[block, cut] = gradient.astype(BF16)
            part = jnp.sum(gradient, axis=0, keepdims=True)
            bias_sum = part if bias_sum is None else bias_sum + part
        db[:, cut] = bias_sum


def weight_grads(place, normed, grad, act, gpre, dw, per):
    hidden, channels = act.shape[1], grad.shape[1]
    size = min(n for n in range(128, hidden + 1, 128) if hidden % n == 0 and n % (2 * per) == 0 and n >= 256)
    for first in range(0, hidden, size):
        cut = slice(first, first + size)
        for i, (left, right) in enumerate(((gpre, normed), (act, grad))):
            value = dot_tn(left[:, cut], right[...]).astype(BF16)
            if len(dw) == 1:
                dw[0][i, cut, :] = value
                continue
            value = value.reshape(size // (2 * per), 2, per, channels)
            upper = place[4] == 1
            half = slice(first // 2, (first + size) // 2)
            dw[0][i, half, :] = jnp.where(upper, value[:, 0], value[:, 1]).reshape(-1, channels)
            dw[1][i, half, :] = jnp.where(upper, value[:, 1], value[:, 0]).reshape(-1, channels)


def forward_kernel(
    place, xpad, taps, gains, shifts, w_in, w_out, b_in, mids, z_out,
    xs, zs, act,
):
    groups, mid_rows, mid_cols = zs.shape[:3]
    rows, cols = z_out.shape[1:3]
    for g in range(groups):
        xs[g] = xpad[:, :, g * LANES : (g + 1) * LANES].astype(F32)
    conv_pass(xs, 0, 0, taps, 0, zs, mid_rows, mid_cols)
    z_out[...] = zs[:, HALO : HALO + rows, HALO : HALO + cols, :]
    strip = act.shape[0] // mid_cols

    def one_strip(step, carry):
        top = step * strip
        hat, _ = norm_parts(joined(zs, pl.ds(top, strip)))
        normed = (hat * gains[0:1] + shifts[0:1]).astype(BF16)
        for cut in hidden_chunks(w_in.shape[2]):
            pre = dot_nn(normed, w_in[0, :, cut]) + b_in[0:1, cut]
            act[:, cut] = gelu_only(pre).astype(BF16)
        mixed = dot_nt(act[...], w_out[0])
        row = lax.broadcasted_iota(jnp.int32, (strip, mid_cols, 1), 0) + (top - HALO) + place[0]
        col = lax.broadcasted_iota(jnp.int32, (strip, mid_cols, 1), 1) - HALO + place[1]
        real = (row >= 0) & (row < place[2]) & (col >= 0) & (col < place[3])
        real = jnp.where(real, 1.0, 0.0).reshape(strip * mid_cols, 1)
        base = joined(xs, pl.ds(top + HALO, strip), slice(HALO, HALO + mid_cols))
        mid = (base + mixed).astype(BF16).astype(F32) * real
        split_to(mids, pl.ds(top, strip), mid, (strip, mid_cols))
        return carry

    lax.fori_loop(0, mid_rows // strip, one_strip, 0)


def top_kernel(
    mids, grad, taps, gains, shifts, w_in, w_out, b_in,
    dz_out, normed, act, gpre, db, dgain, dshift, z,
):
    conv_pass(mids, 0, 0, taps, 1, z, *z.shape[1:3])
    hat, inv = norm_parts(joined(z, slice(None)))
    normed[...] = (hat * gains[1:2] + shifts[1:2]).astype(BF16)
    mlp_grads(normed, grad, w_in, b_in, w_out, 1, act, gpre, db)
    dz_of(gpre, w_in[1], hat, inv, gains[1:2], dz_out, dgain, dshift)


def again_kernel(z0, gains, shifts, w_in, b_in, hat_out, inv_out, normed, act, slope):
    hat, inv = norm_parts(joined(z0, slice(None)))
    hat_out[...] = hat
    inv_out[...] = jnp.broadcast_to(inv, inv_out.shape)
    normed[...] = (hat * gains[0:1] + shifts[0:1]).astype(BF16)
    hidden_forward(normed, w_in, b_in, act, slope)


def low_kernel(
    per, place, dzpad, grad, hat, inv, normed, act, slope, taps, gains, w_in, w_out,
    gmid, dz_out, db, dgain, dshift, *rest,
):
    *dw, dzs, spread, gpre = rest
    spread_pass(dzpad, dzs, taps, 1, spread)
    gmid[...] = (grad[...].astype(F32) + joined(spread, slice(None))).astype(BF16)
    hidden_back(gmid, w_out, slope, gpre, db)
    dz_of(gpre, w_in[0], hat[...], inv[:, :1], gains[0:1], dz_out, dgain, dshift)
    weight_grads(place, normed, gmid, act, gpre, dw, per)


def weights_top_kernel(per, place, normed, act, gpre, grad, *dw):
    weight_grads(place, normed, grad, act, gpre, dw, per)


def spread_pass(dzpad, dzs, taps, layer, spread):
    for g in range(dzs.shape[0]):
        dzs[g] = dzpad[:, :, g * LANES : (g + 1) * LANES].astype(F32)
    conv_pass(dzs, 0, 0, taps, layer, spread, *spread.shape[1:3], back=True)


def last_kernel(dzpad, gmid, taps, out, dzs, spread):
    spread_pass(dzpad, dzs, taps, 0, spread)
    out[...] = (gmid[...].astype(F32) + joined(spread, slice(None))).astype(BF16)


def small_rows_of(values, row0, col0, dz, dzs, taps, db, dgain, dshift, sums):
    rows, cols = dzs.shape[1:3]
    channels = sums.shape[1]
    split_to(dzs, slice(None), dz[...].astype(F32), (rows, cols))
    count = db.shape[1] // channels
    for k in range(count):
        sums[k : k + 1, :] = db[:, k * channels : (k + 1) * channels]
    sums[count : count + 1, :] = dgain[...]
    sums[count + 1 : count + 2, :] = dshift[...]
    tap_pass(values, row0, col0, dzs, taps, rows, cols)
    for g in range(taps.shape[0]):
        sums[count + 2 : count + 51, g * LANES : (g + 1) * LANES] = taps[g]


def taps_kernel(
    place, mids, xpad, dz0, dz1, db0, dgain0, dshift0, db1, dgain1, dshift1, send, keep,
    xs, dzs, taps, sums0, sums1,
):
    for g in range(dzs.shape[0]):
        xs[g] = xpad[:, :, g * LANES : (g + 1) * LANES].astype(F32)
    sums0[...] = jnp.zeros(sums0.shape, F32)
    sums1[...] = jnp.zeros(sums1.shape, F32)
    small_rows_of(mids, 0, 0, dz1, dzs, taps, db1, dgain1, dshift1, sums1)
    small_rows_of(xs, HALO, HALO, dz0, dzs, taps, db0, dgain0, dshift0, sums0)
    upper = place[4] == 1
    send[...] = jnp.where(upper, sums0[...], sums1[...]).astype(BF16)
    keep[...] = jnp.where(upper, sums1[...], sums0[...]).astype(BF16)


def small_kernel(scale, place, mine, got, taps_out, gains, shifts, biases):
    upper = place[4] == 1
    own, came = mine[...].astype(F32) * scale, got[...].astype(F32) * scale
    channels = own.shape[1]
    count = biases.shape[1] // channels
    for layer, part in enumerate((jnp.where(upper, came, own), jnp.where(upper, own, came))):
        at = slice(layer, layer + 1)
        for k in range(count):
            biases[at, k * channels : (k + 1) * channels] = part[k : k + 1, :]
        gains[at, :] = part[count : count + 1, :]
        shifts[at, :] = part[count + 1 : count + 2, :]
        for tap in range(49):
            taps_out[tap, at, :] = part[count + 2 + tap : count + 3 + tap, :]


def weights_kernel(scale, keep0, got0, keep1, got1, out_in, out_out):
    for layer, (keep, got) in enumerate(((keep0, got0), (keep1, got1))):
        for i, out in enumerate((out_in, out_out)):
            out[layer] = (keep[i].astype(F32) + got[i].astype(F32)) * scale


def shape(*dims, dtype=F32):
    return jax.ShapeDtypeStruct(dims, dtype)


def run(kernel, outs, scratch, args, specs=None, name=None):
    vmem = pl.BlockSpec(memory_space=pltpu.VMEM)
    return pl.pallas_call(
        kernel,
        out_shape=outs,
        in_specs=[
            vmem if s is None else pl.BlockSpec(memory_space=s) for s in (specs or [None] * len(args))
        ],
        out_specs=tuple(vmem for _ in outs),
        scratch_shapes=[pltpu.VMEM(s.shape, s.dtype) for s in scratch],
        compiler_params=pltpu.CompilerParams(vmem_limit_bytes=46 * 1024 * 1024),
        name=name,
    )(*args)


def edges(tile, axis, width, odd):
    count = tile.shape[axis]
    low = lax.slice_in_dim(tile, 0, width, axis=axis)
    high = lax.slice_in_dim(tile, count - width, count, axis=axis)
    return jnp.where(odd, low, high), jnp.where(odd, high, low)


def to_twin(edge, axis):
    count = lax.axis_size(axis)
    return lax.ppermute(edge, axis, [(i, i ^ 1) for i in range(count) if i ^ 1 < count])


def to_other(edge, axis):
    n_rows, n_cols = lax.axis_size("rows"), lax.axis_size("cols")
    count = lax.axis_size(axis)
    pairs = []
    for r in range(n_rows):
        for c in range(n_cols):
            at = r if axis == "rows" else c
            partner = at + 1 if at % 2 else at - 1
            if 0 <= partner < count:
                there = (partner, c) if axis == "rows" else (r, partner)
            else:
                there = (r, c ^ 1) if axis == "rows" else (r ^ 1, c)
            pairs.append((r * n_cols + c, there[0] * n_cols + there[1]))
    return lax.ppermute(edge, ("rows", "cols"), pairs)


def rimmed(tile, from_twin, from_other, axis, odd, outer):
    from_other = jnp.where(outer, jnp.zeros_like(from_other), from_other)
    low = jnp.where(odd, from_twin, from_other)
    high = jnp.where(odd, from_other, from_twin)
    return jnp.concatenate([low, tile, high], axis=axis)


def flip_bit(value, *bits):
    flip = sum(1 << bit for bit in bits)
    both = ("rows", "cols")
    total = lax.axis_size("rows") * lax.axis_size("cols")
    return lax.ppermute(value, both, [(i, i ^ flip) for i in range(total)])


def halves(chunks, dim, mine):
    sizes = [1 if d == dim else n for d, n in enumerate(chunks.shape)]

    def one(bit):
        starts = [bit if d == dim else jnp.uint32(0) for d in range(chunks.ndim)]
        return lax.squeeze(lax.dynamic_slice(chunks, starts, sizes), (dim,))

    return one(mine[1]), one(mine[0])


def summed(own, *got):
    parts = [part.astype(F32) for part in (own,) + got]
    while len(parts) > 1:
        parts = [a + b for a, b in zip(parts[::2], parts[1::2])]
    return parts[0].astype(BF16)


def cut(chunks, order, bit, mine):
    spot = order.index(bit)
    per = chunks.shape[-2:]
    pair = chunks.reshape((-1, 2 ** spot, 2, 2 ** (len(order) - spot - 1)) + per)
    send, keep = halves(pair, 2, mine[bit])
    return send, keep, [b for b in order if b != bit]


def step(chunks, order, bit, mine):
    send, keep, left = cut(chunks, order, bit, mine)
    return keep, flip_bit(send, bit), left


def shards(activations, grad_out, kernels, norm_gains, norm_shifts, w_in, b_in, w_out):
    rows, cols, channels = activations.shape
    layers, _, hidden = w_in.shape
    groups = channels // LANES
    n_rows, n_cols = lax.axis_size("rows"), lax.axis_size("cols")
    total = n_rows * n_cols
    bits = total.bit_length() - 1
    col_bits = n_cols.bit_length() - 1
    me = (lax.axis_index("rows") * n_cols + lax.axis_index("cols")).astype(jnp.uint32)
    mine = [(((me >> k) & 1), 1 - ((me >> k) & 1)) for k in range(bits)]
    grad_scale = 1.0 / math.sqrt(rows * cols * total)
    pixels = rows * cols

    taps = kernels.transpose(1, 2, 0, 3).reshape(49, layers, channels)
    place = jnp.stack(
        [
            lax.axis_index("rows") * rows,
            lax.axis_index("cols") * cols,
            jnp.int32(rows * n_rows),
            jnp.int32(cols * n_cols),
            lax.axis_index("cols") & 1,
        ]
    ).astype(jnp.int32)
    grad_flat = grad_out.reshape(pixels, channels)

    at_row, at_col = lax.axis_index("rows"), lax.axis_index("cols")
    odd_col, odd_row = (at_col & 1) == 1, (at_row & 1) == 1
    outer_col = (at_col == 0) | (at_col == n_cols - 1)
    outer_row = (at_row == 0) | (at_row == n_rows - 1)
    activations, place, mine, odd_col, odd_row, outer_col, outer_row = lax.optimization_barrier(
        (activations, place, mine, odd_col, odd_row, outer_col, outer_row)
    )

    def rim_cols(tile, width):
        twin, other = edges(tile, 1, width, odd_col)
        return rimmed(tile, to_twin(twin, "cols"), to_other(other, "cols"), 1, odd_col, outer_col)

    def rim_rows(tile, width):
        twin, other = edges(tile, 0, width, odd_row)
        return rimmed(tile, to_twin(twin, "rows"), to_other(other, "rows"), 0, odd_row, outer_row)

    def filled(wide):
        return jnp.pad(wide, ((0, 0), (0, cols + 16 - wide.shape[1]), (0, 0)))

    mid_rows, mid_cols = rows + 2 * HALO, cols + 8
    strip = max(d for d in range(1, mid_rows + 1) if mid_rows % d == 0 and d * mid_cols <= 264)
    tile_z = shape(groups, rows, cols, LANES)
    tile_b = shape(pixels, channels, dtype=BF16)
    tile_h = shape(pixels, hidden, dtype=BF16)
    per = hidden // total
    split = 2 if per % 16 == 0 and col_bits == 2 else 1
    grads_b = (shape(2, hidden // split, channels, dtype=BF16),) * split
    small_outs = (shape(1, hidden), shape(1, channels), shape(1, channels))
    small_rows = 64

    xpad = filled(rim_cols(rim_rows(activations, WIDE), WIDE))
    mids, z0 = run(
        forward_kernel,
        (shape(groups, mid_rows, mid_cols, LANES), tile_z),
        [
            shape(groups, *xpad.shape[:2], LANES),
            shape(groups, mid_rows, mid_cols, LANES),
            shape(strip * mid_cols, hidden, dtype=BF16),
        ],
        (place, xpad, taps, norm_gains, norm_shifts, w_in, w_out, b_in),
        [pltpu.SMEM] + [None] * 7,
        name="forward",
    )
    dz1, normed1, act1, gpre1, *small1 = run(
        top_kernel,
        (tile_b, tile_b, tile_h, tile_h) + small_outs,
        [tile_z],
        (mids, grad_flat, taps, norm_gains, norm_shifts, w_in, w_out, b_in),
        name="top",
    )

    sides = (col_bits - 1, col_bits)

    def fenced(*values):
        leaves, tree = jax.tree.flatten(values)
        arrays = [i for i, leaf in enumerate(leaves) if not isinstance(leaf, int)]
        for i, value in zip(arrays, lax.optimization_barrier(tuple(leaves[i] for i in arrays))):
            leaves[i] = value
        return jax.tree.unflatten(tree, leaves)

    def settled(flight):
        return summed(flight[0], flight[1]), flight[2]

    def start(dw):
        order = list(range(bits - 1, -1, -1))
        if split == 2:
            send, keep = (d.reshape(2, total // 2, per, channels) for d in dw)
            return keep, flip_bit(send, 0), order[:-1]
        chunks = dw[0].reshape(2, total, per, channels)
        for bit in range(col_bits - 2):
            chunks, order = settled(step(chunks, order, bit, mine))
        return step(chunks, order, col_bits - 2, mine)

    def fork(flight):
        chunks, order = settled(flight)
        return [step(chunks[i], order, sides[i], mine) for i in range(2)]

    def onward(parts, bit, *riders):
        kept, sent, lefts = [], [], []
        for chunks, order in parts:
            send, keep, left = cut(chunks, order, bit, mine)
            kept.append(keep)
            sent.append(send.reshape(-1, channels))
            lefts.append(left)
        got = flip_bit(jnp.concatenate(sent + list(riders), axis=0), bit)
        flights, first = [], 0
        for keep, send, left in zip(kept, sent, lefts):
            came = got[first : first + send.shape[0]].reshape(keep.shape)
            flights.append((keep, came, left))
            first += send.shape[0]
        return flights, [got[first:]] if riders else []

    def merged(flights):
        done = [settled(f) for f in flights]
        return jnp.stack([d[0].reshape(-1, per, channels) for d in done]), done[0][1]

    tile1 = dz1.reshape(rows, cols, channels)
    twin, other = edges(tile1, 0, HALO, odd_row)
    twin, other = to_twin(twin, "rows"), to_other(other, "rows")
    dw1 = run(
        functools.partial(weights_top_kernel, per),
        grads_b,
        [],
        (place, normed1, act1, gpre1, grad_flat),
        [pltpu.SMEM] + [None] * 4,
        name="weights_top",
    )
    tile1, twin, other, dw1, z0 = fenced(tile1, twin, other, dw1, z0)
    wide1 = rimmed(tile1, twin, other, 0, odd_row, outer_row)
    run1 = start(dw1)
    twin, other = edges(wide1, 1, HALO, odd_col)
    twin, other = to_twin(twin, "cols"), to_other(other, "cols")
    tile_f = shape(pixels, channels)
    again = run(
        again_kernel,
        (tile_f, shape(pixels, LANES), tile_b, tile_h, shape(pixels, hidden)),
        [],
        (z0, norm_gains, norm_shifts, w_in, b_in),
        name="again",
    )
    wide1, twin, other, run1, again = fenced(wide1, twin, other, run1, again)
    pair1 = fork(run1)
    dzpad1 = filled(rimmed(wide1, twin, other, 1, odd_col, outer_col))
    spread_scratch = [shape(groups, *dzpad1.shape[:2], LANES), tile_z]
    grad_mid, dz0, *rest = run(
        functools.partial(low_kernel, per),
        (tile_b, tile_b) + small_outs + grads_b,
        spread_scratch + [tile_h],
        (place, dzpad1, grad_flat, *again, taps, norm_gains, w_in, w_out),
        [pltpu.SMEM] + [None] * 11,
        name="low",
    )
    small0, dw0 = rest[:3], rest[3:]
    dz0, dw0, small0 = fenced(dz0, dw0, small0)
    run0 = start(dw0)
    low_bit = col_bits + 1
    pair1, _ = onward([settled(f) for f in pair1], low_bit)
    run0, dz0, small0 = fenced(run0, dz0, small0)
    pair0 = fork(run0)
    tile0 = dz0.reshape(rows, cols, channels)
    twin, other = edges(tile0, 0, HALO, odd_row)
    twin, other = to_twin(twin, "rows"), to_other(other, "rows")
    small_b = shape(small_rows, channels, dtype=BF16)
    small_f = shape(small_rows, channels)
    send, small = run(
        taps_kernel,
        (small_b, small_b),
        [
            shape(groups, *xpad.shape[:2], LANES), tile_z, shape(groups, 49, LANES),
            small_f, small_f,
        ],
        (place, mids, xpad, dz0, dz1, *small0, *small1),
        [pltpu.SMEM] + [None] * 10,
        name="taps",
    )
    small_got = flip_bit(send, 0)
    pair0, pair1, tile0, twin, other, small, small_got = fenced(
        pair0, pair1, tile0, twin, other, small, small_got
    )
    small = summed(small, small_got)
    for bit in range(1, col_bits - 1):
        small = summed(small, flip_bit(small, bit))
    both, small_by = [], []
    for i in range(2):
        flights, (came,) = onward([settled(pair0[i]), settled(pair1[i])], sides[1 - i], small)
        both.append(flights)
        small_by.append(came)
    small_by.append(flip_bit(small, *sides))
    wide0 = rimmed(tile0, twin, other, 0, odd_row, outer_row)
    twin, other = edges(wide0, 1, HALO, odd_col)
    twin, other = to_twin(twin, "cols"), to_other(other, "cols")
    both, wide0, twin, other, small, small_by = fenced(both, wide0, twin, other, small, small_by)
    small = summed(small, small_by[0], small_by[1], small_by[2])
    (run0,), (small_got,) = onward([merged([both[0][0], both[1][0]])], low_bit, small)
    part1, order1 = merged([both[0][1], both[1][1]])
    flight1 = (part1, jnp.zeros_like(part1), order1)
    if order1:
        (flight1,), _ = onward([(part1, order1)], order1[-1])
    (grad_in,) = run(
        last_kernel,
        (tile_b,),
        spread_scratch,
        (filled(rimmed(wide0, twin, other, 1, odd_col, outer_col)), grad_mid, taps),
        name="last",
    )
    while run0[2]:
        run0, flight1, small, small_got, grad_in = fenced(run0, flight1, small, small_got, grad_in)
        small = summed(small, small_got)
        (run0,), (small_got,) = onward([settled(run0)], run0[2][-1], small)
        if flight1[2]:
            (flight1,), _ = onward([settled(flight1)], flight1[2][-1])
    run0, flight1, small, small_got = fenced(run0, flight1, small, small_got)
    small = summed(small, small_got)
    small_got = flip_bit(small, 0)
    share = shape(layers, per, channels)
    grad_w_in, grad_w_out = run(
        functools.partial(weights_kernel, grad_scale),
        (share, share),
        [],
        [part.reshape(2, per, channels) for part in run0[:2] + flight1[:2]],
        name="weights",
    )
    grad_taps, grad_gains, grad_shifts, grad_b_in = run(
        functools.partial(small_kernel, grad_scale),
        (
            shape(49, layers, channels),
            shape(layers, channels),
            shape(layers, channels),
            shape(layers, hidden),
        ),
        [],
        (place, small, small_got),
        [pltpu.SMEM, None, None],
        name="small",
    )
    return (
        grad_in.reshape(rows, cols, channels),
        grad_taps.reshape(7, 7, layers, channels).transpose(2, 0, 1, 3),
        grad_gains,
        grad_shifts,
        grad_b_in,
        jnp.swapaxes(grad_w_in, 1, 2),
        jnp.swapaxes(grad_w_out, 1, 2),
    )


def solution(mesh):
    tile = P("rows", "cols", None)
    sliced = P(None, None, ("rows", "cols"))
    return jax.shard_map(
        shards,
        mesh=mesh,
        in_specs=(tile, tile, P(), P(), P(), P(), P(), P()),
        out_specs=(tile, P(), P(), P(), P(), sliced, sliced),
        check_vma=False,
    )
```

```python
import functools
import math

import jax
import jax.numpy as jnp
from jax import lax
from jax.experimental import pallas as pl
from jax.experimental.pallas import tpu as pltpu
from jax.sharding import PartitionSpec as P

EPSILON = 1e-06
INV_ROOT_TAU = 0.3989422804014327
HALF_LOG2E = 0.7213475204444817
ERFC_SLOPE = 0.4 * 0.7071067811865476
ERFC_TERMS = (
    0.22479419400284972,
    0.2383621945582281,
    0.12991301634379934,
    0.4353236101490443,
    -0.41611664430523265,
    0.7235898182708315,
    -0.41436965913692125,
    0.07850346878444278,
)
LANES = 128
HALO = 3
WIDE = 2 * HALO
F32 = jnp.float32
BF16 = jnp.bfloat16


def normal_parts(x):
    bell = jnp.exp2(x * x * (-HALF_LOG2E))
    t = 1.0 / (1.0 + ERFC_SLOPE * jnp.abs(x))
    series = 0.5 * ERFC_TERMS[7]
    for term in ERFC_TERMS[6::-1]:
        series = series * t + 0.5 * term
    tail = series * t * bell
    return jnp.where(x >= 0, 1.0 - tail, tail), bell


def gelu_only(x):
    cdf, _ = normal_parts(x)
    return x * cdf


def gelu_parts(x):
    cdf, bell = normal_parts(x)
    return x * cdf, cdf + x * bell * INV_ROOT_TAU


def strip_rows(rows, cols):
    most = max(1, 288 // cols)
    return max(d for d in range(1, rows + 1) if rows % d == 0 and d <= most)


def conv_pass(source, row0, col0, taps, layer, target, rows, cols, back=False):
    strip = strip_rows(rows, cols)
    groups = source.shape[0]

    def one_strip(step, carry):
        g = step // (rows // strip)
        top = (step % (rows // strip)) * strip
        lanes = pl.ds(pl.multiple_of(g * LANES, LANES), LANES)
        sums = [jnp.zeros((cols, LANES), F32) for _ in range(strip)]
        for b in range(7):
            spots = [48 - 7 * a - b if back else 7 * a + b for a in range(7)]
            weights = [taps[spot, pl.ds(layer, 1), lanes] for spot in spots]
            for r in range(strip + 6):
                line = source[g, row0 + top + r, pl.ds(col0 + b, cols), :]
                for a in range(7):
                    if 0 <= r - a < strip:
                        sums[r - a] = sums[r - a] + weights[a] * line
        for i in range(strip):
            target[g, top + i] = sums[i]
        return carry

    lax.fori_loop(0, groups * (rows // strip), one_strip, 0)


def tap_pass(source, row0, col0, grad, target, rows, cols):
    def one_group(g, carry):
        lines = [grad[g, i] for i in range(rows)]
        for b in range(7):
            sums = [None] * 7
            for r in range(rows + 6):
                line = source[g, row0 + r, pl.ds(col0 + b, cols), :]
                for a in range(7):
                    if 0 <= r - a < rows:
                        part = lines[r - a] * line
                        sums[a] = part if sums[a] is None else sums[a] + part
            for a in range(7):
                total = jnp.sum(sums[a], axis=0, keepdims=True)
                target[g, pl.ds(7 * a + b, 1), :] = total
        return carry

    lax.fori_loop(0, source.shape[0], one_group, 0)


def joined(ref, rows, cols=slice(None)):
    parts = [ref[g, rows, cols, :] for g in range(ref.shape[0])]
    return jnp.concatenate([p.reshape(-1, LANES) for p in parts], axis=1)


def split_to(ref, rows, value, shape):
    for g in range(ref.shape[0]):
        ref[g, rows] = value[:, g * LANES : (g + 1) * LANES].reshape(*shape, LANES)


def norm_parts(z):
    center = z - jnp.mean(z, axis=-1, keepdims=True)
    inv = lax.rsqrt(jnp.mean(center * center, axis=-1, keepdims=True) + EPSILON)
    return center * inv, inv


def norm_back(dn, hat, inv, gain):
    scaled = dn * gain
    return inv * (
        scaled
        - jnp.mean(scaled, axis=-1, keepdims=True)
        - hat * jnp.mean(scaled * hat, axis=-1, keepdims=True)
    )


def dot_nn(a, b):
    return jnp.dot(a, b, preferred_element_type=F32)


def dot_nt(a, b):
    return lax.dot_general(a, b, (((1,), (1,)), ((), ())), preferred_element_type=F32)


def dot_tn(a, b):
    return lax.dot_general(a, b, (((0,), (0,)), ((), ())), preferred_element_type=F32)


def pixel_blocks(pixels):
    best = max(d for d in range(16, 257, 16) if pixels % d == 0)
    return [slice(start, start + best) for start in range(0, pixels, best)]


def hidden_chunks(hidden):
    size = 256 if hidden % 256 == 0 else hidden
    return [slice(start, start + size) for start in range(0, hidden, size)]


def hidden_forward(normed, w_in, bias, act, slope):
    for cut in hidden_chunks(w_in.shape[2]):
        for block in pixel_blocks(normed.shape[0]):
            value, factor = gelu_parts(dot_nn(normed[block, :], w_in[0, :, cut]) + bias[:, cut])
            act[block, cut] = value.astype(BF16)
            slope[block, cut] = factor


def hidden_back(grad, w_out, slope, gpre, db):
    for cut in hidden_chunks(w_out.shape[2]):
        bias_sum = None
        for block in pixel_blocks(grad.shape[0]):
            gradient = dot_nn(grad[block, :], w_out[0, :, cut]) * slope[block, cut]
            gpre[block, cut] = gradient.astype(BF16)
            part = jnp.sum(gradient, axis=0, keepdims=True)
            bias_sum = part if bias_sum is None else bias_sum + part
        db[:, cut] = bias_sum


def dz_of(gpre, w_in, hat, inv, gain, dz_out, dgain, dshift):
    dn = dot_nt(gpre[...], w_in[0])
    dgain[...] = jnp.sum(dn * hat, axis=0, keepdims=True)
    dshift[...] = jnp.sum(dn, axis=0, keepdims=True)
    dz_out[...] = norm_back(dn, hat, inv, gain).astype(BF16)


def mlp_grads(normed, grad, w_in, b_in, w_out, act, gpre, db):
    pixels = grad.shape[0]
    for cut in hidden_chunks(w_in.shape[2]):
        bias = b_in[:, cut]
        bias_sum = None
        for block in pixel_blocks(pixels):
            pre = dot_nn(normed[block, :], w_in[0, :, cut]) + bias
            value, slope = gelu_parts(pre)
            act[block, cut] = value.astype(BF16)
            gradient = dot_nn(grad[block, :], w_out[0, :, cut]) * slope
            gpre[block, cut] = gradient.astype(BF16)
            part = jnp.sum(gradient, axis=0, keepdims=True)
            bias_sum = part if bias_sum is None else bias_sum + part
        db[:, cut] = bias_sum


def weight_grads(place, normed, grad, act, gpre, dw, per):
    hidden, channels = act.shape[1], grad.shape[1]
    size = min(n for n in range(128, hidden + 1, 128) if hidden % n == 0 and n % (2 * per) == 0 and n >= 256)
    for first in range(0, hidden, size):
        cut = slice(first, first + size)
        for i, (left, right) in enumerate(((gpre, normed), (act, grad))):
            value = dot_tn(left[:, cut], right[...]).astype(BF16)
            if len(dw) == 1:
                dw[0][i, cut, :] = value
                continue
            value = value.reshape(size // (2 * per), 2, per, channels)
            upper = place[4] == 1
            half = slice(first // 2, (first + size) // 2)
            dw[0][i, half, :] = jnp.where(upper, value[:, 0], value[:, 1]).reshape(-1, channels)
            dw[1][i, half, :] = jnp.where(upper, value[:, 1], value[:, 0]).reshape(-1, channels)


def fetch_layers(triples, arrived):
    copies = [
        pltpu.make_async_copy(source.at[pl.ds(layer, 1)], target, arrived.at[i])
        for i, (source, layer, target) in enumerate(triples)
    ]
    for copy in copies:
        copy.start()
    return copies


def forward_kernel(
    place, xpad, taps, gains, shifts, w_in, w_out, b_in, mids, z_out,
    xs, zs, act, w_in0, w_out0, arrived,
):
    waits = fetch_layers(((w_in, 0, w_in0), (w_out, 0, w_out0)), arrived)
    groups, mid_rows, mid_cols = zs.shape[:3]
    rows, cols = z_out.shape[1:3]
    for g in range(groups):
        xs[g] = xpad[:, :, g * LANES : (g + 1) * LANES].astype(F32)
    conv_pass(xs, 0, 0, taps, 0, zs, mid_rows, mid_cols)
    z_out[...] = zs[:, HALO : HALO + rows, HALO : HALO + cols, :]
    strip = act.shape[0] // mid_cols
    for wait in waits:
        wait.wait()

    def one_strip(step, carry):
        top = step * strip
        hat, _ = norm_parts(joined(zs, pl.ds(top, strip)))
        normed = (hat * gains[0:1] + shifts[0:1]).astype(BF16)
        for cut in hidden_chunks(w_in0.shape[2]):
            pre = dot_nn(normed, w_in0[0, :, cut]) + b_in[0:1, cut]
            act[:, cut] = gelu_only(pre).astype(BF16)
        mixed = dot_nt(act[...], w_out0[0])
        row = lax.broadcasted_iota(jnp.int32, (strip, mid_cols, 1), 0) + (top - HALO) + place[0]
        col = lax.broadcasted_iota(jnp.int32, (strip, mid_cols, 1), 1) - HALO + place[1]
        real = (row >= 0) & (row < place[2]) & (col >= 0) & (col < place[3])
        real = jnp.where(real, 1.0, 0.0).reshape(strip * mid_cols, 1)
        base = joined(xs, pl.ds(top + HALO, strip), slice(HALO, HALO + mid_cols))
        mid = (base + mixed).astype(BF16).astype(F32) * real
        split_to(mids, pl.ds(top, strip), mid, (strip, mid_cols))
        return carry

    lax.fori_loop(0, mid_rows // strip, one_strip, 0)


def top_kernel(
    mids, grad, taps, gains, shifts, w_in, w_out, b_in,
    dz_out, normed, act, gpre, db, dgain, dshift, z, w_in1, w_out1, arrived,
):
    waits = fetch_layers(((w_in, 1, w_in1), (w_out, 1, w_out1)), arrived)
    conv_pass(mids, 0, 0, taps, 1, z, *z.shape[1:3])
    hat, inv = norm_parts(joined(z, slice(None)))
    normed[...] = (hat * gains[1:2] + shifts[1:2]).astype(BF16)
    for wait in waits:
        wait.wait()
    mlp_grads(normed, grad, w_in1, b_in.at[pl.ds(1, 1)], w_out1, act, gpre, db)
    dz_of(gpre, w_in1, hat, inv, gains[1:2], dz_out, dgain, dshift)


def again_kernel(z0, gains, shifts, w_in, b_in, hat_out, inv_out, normed, act, slope, w_in0, arrived):
    (wait,) = fetch_layers(((w_in, 0, w_in0),), arrived)
    hat, inv = norm_parts(joined(z0, slice(None)))
    hat_out[...] = hat
    inv_out[...] = jnp.broadcast_to(inv, inv_out.shape)
    normed[...] = (hat * gains[0:1] + shifts[0:1]).astype(BF16)
    wait.wait()
    hidden_forward(normed, w_in0, b_in.at[pl.ds(0, 1)], act, slope)


def low_kernel(
    per, place, dzpad, grad, hat, inv, normed, act, slope, taps, gains, w_in, w_out,
    gmid, dz_out, db, dgain, dshift, *rest,
):
    *dw, dzs, spread, gpre, w_in0, w_out0, arrived = rest
    waits = fetch_layers(((w_out, 0, w_out0), (w_in, 0, w_in0)), arrived)
    spread_pass(dzpad, dzs, taps, 1, spread)
    gmid[...] = (grad[...].astype(F32) + joined(spread, slice(None))).astype(BF16)
    for wait in waits:
        wait.wait()
    hidden_back(gmid, w_out0, slope, gpre, db)
    dz_of(gpre, w_in0, hat[...], inv[:, :1], gains[0:1], dz_out, dgain, dshift)
    weight_grads(place, normed, gmid, act, gpre, dw, per)


def weights_top_kernel(per, place, normed, act, gpre, grad, *dw):
    weight_grads(place, normed, grad, act, gpre, dw, per)


def spread_pass(dzpad, dzs, taps, layer, spread):
    for g in range(dzs.shape[0]):
        dzs[g] = dzpad[:, :, g * LANES : (g + 1) * LANES].astype(F32)
    conv_pass(dzs, 0, 0, taps, layer, spread, *spread.shape[1:3], back=True)


def last_kernel(dzpad, gmid, taps, out, dzs, spread):
    spread_pass(dzpad, dzs, taps, 0, spread)
    out[...] = (gmid[...].astype(F32) + joined(spread, slice(None))).astype(BF16)


def small_rows_of(values, row0, col0, dz, dzs, taps, db, dgain, dshift, sums):
    rows, cols = dzs.shape[1:3]
    channels = sums.shape[1]
    split_to(dzs, slice(None), dz[...].astype(F32), (rows, cols))
    count = db.shape[1] // channels
    for k in range(count):
        sums[k : k + 1, :] = db[:, k * channels : (k + 1) * channels]
    sums[count : count + 1, :] = dgain[...]
    sums[count + 1 : count + 2, :] = dshift[...]
    tap_pass(values, row0, col0, dzs, taps, rows, cols)
    for g in range(taps.shape[0]):
        sums[count + 2 : count + 51, g * LANES : (g + 1) * LANES] = taps[g]


def taps_kernel(
    place, mids, xpad, dz0, dz1, db0, dgain0, dshift0, db1, dgain1, dshift1, send, keep,
    xs, dzs, taps, sums0, sums1,
):
    for g in range(dzs.shape[0]):
        xs[g] = xpad[:, :, g * LANES : (g + 1) * LANES].astype(F32)
    sums0[...] = jnp.zeros(sums0.shape, F32)
    sums1[...] = jnp.zeros(sums1.shape, F32)
    small_rows_of(mids, 0, 0, dz1, dzs, taps, db1, dgain1, dshift1, sums1)
    small_rows_of(xs, HALO, HALO, dz0, dzs, taps, db0, dgain0, dshift0, sums0)
    upper = place[4] == 1
    send[...] = jnp.where(upper, sums0[...], sums1[...]).astype(BF16)
    keep[...] = jnp.where(upper, sums1[...], sums0[...]).astype(BF16)


def small_kernel(scale, place, mine, got, taps_out, gains, shifts, biases):
    upper = place[4] == 1
    own, came = mine[...].astype(F32) * scale, got[...].astype(F32) * scale
    channels = own.shape[1]
    count = biases.shape[1] // channels
    for layer, part in enumerate((jnp.where(upper, came, own), jnp.where(upper, own, came))):
        at = slice(layer, layer + 1)
        for k in range(count):
            biases[at, k * channels : (k + 1) * channels] = part[k : k + 1, :]
        gains[at, :] = part[count : count + 1, :]
        shifts[at, :] = part[count + 1 : count + 2, :]
        for tap in range(49):
            taps_out[tap, at, :] = part[count + 2 + tap : count + 3 + tap, :]


def weights_kernel(scale, keep0, got0, keep1, got1, out_in, out_out):
    for layer, (keep, got) in enumerate(((keep0, got0), (keep1, got1))):
        for i, out in enumerate((out_in, out_out)):
            out[layer] = (keep[i].astype(F32) + got[i].astype(F32)) * scale


def shape(*dims, dtype=F32):
    return jax.ShapeDtypeStruct(dims, dtype)


def run(kernel, outs, scratch, args, specs=None, fetched=0, name=None, room=46):
    vmem = pl.BlockSpec(memory_space=pltpu.VMEM)
    semaphores = [pltpu.SemaphoreType.DMA((fetched,))] if fetched else []
    return pl.pallas_call(
        kernel,
        out_shape=outs,
        in_specs=[
            vmem if s is None else pl.BlockSpec(memory_space=s) for s in (specs or [None] * len(args))
        ],
        out_specs=tuple(vmem for _ in outs),
        scratch_shapes=[pltpu.VMEM(s.shape, s.dtype) for s in scratch] + semaphores,
        compiler_params=pltpu.CompilerParams(vmem_limit_bytes=room * 1024 * 1024),
        name=name,
    )(*args)


def edges(tile, axis, width, odd):
    count = tile.shape[axis]
    low = lax.slice_in_dim(tile, 0, width, axis=axis)
    high = lax.slice_in_dim(tile, count - width, count, axis=axis)
    return jnp.where(odd, low, high), jnp.where(odd, high, low)


def to_twin(edge, axis):
    count = lax.axis_size(axis)
    return lax.ppermute(edge, axis, [(i, i ^ 1) for i in range(count) if i ^ 1 < count])


def to_other(edge, axis):
    n_rows, n_cols = lax.axis_size("rows"), lax.axis_size("cols")
    count = lax.axis_size(axis)
    pairs = []
    for r in range(n_rows):
        for c in range(n_cols):
            at = r if axis == "rows" else c
            partner = at + 1 if at % 2 else at - 1
            if 0 <= partner < count:
                there = (partner, c) if axis == "rows" else (r, partner)
            else:
                there = (r, c ^ 1) if axis == "rows" else (r ^ 1, c)
            pairs.append((r * n_cols + c, there[0] * n_cols + there[1]))
    return lax.ppermute(edge, ("rows", "cols"), pairs)


def rimmed(tile, from_twin, from_other, axis, odd, outer):
    from_other = jnp.where(outer, jnp.zeros_like(from_other), from_other)
    low = jnp.where(odd, from_twin, from_other)
    high = jnp.where(odd, from_other, from_twin)
    return jnp.concatenate([low, tile, high], axis=axis)


def flip_bit(value, *bits):
    flip = sum(1 << bit for bit in bits)
    both = ("rows", "cols")
    total = lax.axis_size("rows") * lax.axis_size("cols")
    return lax.ppermute(value, both, [(i, i ^ flip) for i in range(total)])


def halves(chunks, dim, mine):
    sizes = [1 if d == dim else n for d, n in enumerate(chunks.shape)]

    def one(bit):
        starts = [bit if d == dim else jnp.uint32(0) for d in range(chunks.ndim)]
        return lax.squeeze(lax.dynamic_slice(chunks, starts, sizes), (dim,))

    return one(mine[1]), one(mine[0])


def summed(own, *got):
    parts = [part.astype(F32) for part in (own,) + got]
    while len(parts) > 1:
        parts = [a + b for a, b in zip(parts[::2], parts[1::2])]
    return parts[0].astype(BF16)


def cut(chunks, order, bit, mine):
    spot = order.index(bit)
    per = chunks.shape[-2:]
    pair = chunks.reshape((-1, 2 ** spot, 2, 2 ** (len(order) - spot - 1)) + per)
    send, keep = halves(pair, 2, mine[bit])
    return send, keep, [b for b in order if b != bit]


def step(chunks, order, bit, mine):
    send, keep, left = cut(chunks, order, bit, mine)
    return keep, flip_bit(send, bit), left


def shards(activations, grad_out, kernels, norm_gains, norm_shifts, w_in, b_in, w_out):
    rows, cols, channels = activations.shape
    layers, _, hidden = w_in.shape
    groups = channels // LANES
    n_rows, n_cols = lax.axis_size("rows"), lax.axis_size("cols")
    total = n_rows * n_cols
    bits = total.bit_length() - 1
    col_bits = n_cols.bit_length() - 1
    me = (lax.axis_index("rows") * n_cols + lax.axis_index("cols")).astype(jnp.uint32)
    mine = [(((me >> k) & 1), 1 - ((me >> k) & 1)) for k in range(bits)]
    grad_scale = 1.0 / math.sqrt(rows * cols * total)
    pixels = rows * cols

    taps = kernels.transpose(1, 2, 0, 3).reshape(49, layers, channels)
    place = jnp.stack(
        [
            lax.axis_index("rows") * rows,
            lax.axis_index("cols") * cols,
            jnp.int32(rows * n_rows),
            jnp.int32(cols * n_cols),
            lax.axis_index("cols") & 1,
        ]
    ).astype(jnp.int32)
    grad_flat = grad_out.reshape(pixels, channels)

    at_row, at_col = lax.axis_index("rows"), lax.axis_index("cols")
    odd_col, odd_row = (at_col & 1) == 1, (at_row & 1) == 1
    outer_col = (at_col == 0) | (at_col == n_cols - 1)
    outer_row = (at_row == 0) | (at_row == n_rows - 1)
    activations, place, mine, odd_col, odd_row, outer_col, outer_row = lax.optimization_barrier(
        (activations, place, mine, odd_col, odd_row, outer_col, outer_row)
    )

    def rim_cols(tile, width):
        twin, other = edges(tile, 1, width, odd_col)
        return rimmed(tile, to_twin(twin, "cols"), to_other(other, "cols"), 1, odd_col, outer_col)

    def rim_rows(tile, width):
        twin, other = edges(tile, 0, width, odd_row)
        return rimmed(tile, to_twin(twin, "rows"), to_other(other, "rows"), 0, odd_row, outer_row)

    def filled(wide):
        return jnp.pad(wide, ((0, 0), (0, cols + 16 - wide.shape[1]), (0, 0)))

    mid_rows, mid_cols = rows + 2 * HALO, cols + 8
    strip = max(d for d in range(1, mid_rows + 1) if mid_rows % d == 0 and d * mid_cols <= 264)
    weights = [shape(1, channels, hidden, dtype=BF16)] * 2
    tile_z = shape(groups, rows, cols, LANES)
    tile_b = shape(pixels, channels, dtype=BF16)
    tile_h = shape(pixels, hidden, dtype=BF16)
    per = hidden // total
    split = 2 if per % 16 == 0 and col_bits == 2 else 1
    grads_b = (shape(2, hidden // split, channels, dtype=BF16),) * split
    small_outs = (shape(1, hidden), shape(1, channels), shape(1, channels))
    small_rows = 64

    xpad = filled(rim_cols(rim_rows(activations, WIDE), WIDE))
    mids, z0 = run(
        forward_kernel,
        (shape(groups, mid_rows, mid_cols, LANES), tile_z),
        [
            shape(groups, *xpad.shape[:2], LANES),
            shape(groups, mid_rows, mid_cols, LANES),
            shape(strip * mid_cols, hidden, dtype=BF16),
        ]
        + weights,
        (place, xpad, taps, norm_gains, norm_shifts, w_in, w_out, b_in),
        [pltpu.SMEM] + [None] * 4 + [pl.ANY] * 2 + [None],
        fetched=2,
        name="forward",
        room=50,
    )
    dz1, normed1, act1, gpre1, *small1 = run(
        top_kernel,
        (tile_b, tile_b, tile_h, tile_h) + small_outs,
        [tile_z] + weights,
        (mids, grad_flat, taps, norm_gains, norm_shifts, w_in, w_out, b_in),
        [None] * 5 + [pl.ANY] * 2 + [None],
        fetched=2,
        name="top",
        room=50,
    )

    sides = (col_bits - 1, col_bits)

    def fenced(*values):
        leaves, tree = jax.tree.flatten(values)
        arrays = [i for i, leaf in enumerate(leaves) if not isinstance(leaf, int)]
        for i, value in zip(arrays, lax.optimization_barrier(tuple(leaves[i] for i in arrays))):
            leaves[i] = value
        return jax.tree.unflatten(tree, leaves)

    def settled(flight):
        return summed(flight[0], flight[1]), flight[2]

    def start(dw):
        order = list(range(bits - 1, -1, -1))
        if split == 2:
            send, keep = (d.reshape(2, total // 2, per, channels) for d in dw)
            return keep, flip_bit(send, 0), order[:-1]
        chunks = dw[0].reshape(2, total, per, channels)
        for bit in range(col_bits - 2):
            chunks, order = settled(step(chunks, order, bit, mine))
        return step(chunks, order, col_bits - 2, mine)

    def fork(flight):
        chunks, order = settled(flight)
        return [step(chunks[i], order, sides[i], mine) for i in range(2)]

    def onward(parts, bit, *riders):
        kept, sent, lefts = [], [], []
        for chunks, order in parts:
            send, keep, left = cut(chunks, order, bit, mine)
            kept.append(keep)
            sent.append(send.reshape(-1, channels))
            lefts.append(left)
        got = flip_bit(jnp.concatenate(sent + list(riders), axis=0), bit)
        flights, first = [], 0
        for keep, send, left in zip(kept, sent, lefts):
            came = got[first : first + send.shape[0]].reshape(keep.shape)
            flights.append((keep, came, left))
            first += send.shape[0]
        return flights, [got[first:]] if riders else []

    def merged(flights):
        done = [settled(f) for f in flights]
        return jnp.stack([d[0].reshape(-1, per, channels) for d in done]), done[0][1]

    tile1 = dz1.reshape(rows, cols, channels)
    twin, other = edges(tile1, 0, HALO, odd_row)
    twin, other = to_twin(twin, "rows"), to_other(other, "rows")
    dw1 = run(
        functools.partial(weights_top_kernel, per),
        grads_b,
        [],
        (place, normed1, act1, gpre1, grad_flat),
        [pltpu.SMEM] + [None] * 4,
        name="weights_top",
    )
    tile1, twin, other, dw1, z0 = fenced(tile1, twin, other, dw1, z0)
    wide1 = rimmed(tile1, twin, other, 0, odd_row, outer_row)
    run1 = start(dw1)
    twin, other = edges(wide1, 1, HALO, odd_col)
    twin, other = to_twin(twin, "cols"), to_other(other, "cols")
    tile_f = shape(pixels, channels)
    again = run(
        again_kernel,
        (tile_f, shape(pixels, LANES), tile_b, tile_h, shape(pixels, hidden)),
        weights[:1],
        (z0, norm_gains, norm_shifts, w_in, b_in),
        [None] * 3 + [pl.ANY, None],
        fetched=1,
        name="again",
    )
    wide1, twin, other, run1, again = fenced(wide1, twin, other, run1, again)
    pair1 = fork(run1)
    dzpad1 = filled(rimmed(wide1, twin, other, 1, odd_col, outer_col))
    spread_scratch = [shape(groups, *dzpad1.shape[:2], LANES), tile_z]
    grad_mid, dz0, *rest = run(
        functools.partial(low_kernel, per),
        (tile_b, tile_b) + small_outs + grads_b,
        spread_scratch + [tile_h] + weights,
        (place, dzpad1, grad_flat, *again, taps, norm_gains, w_in, w_out),
        [pltpu.SMEM] + [None] * 9 + [pl.ANY] * 2,
        fetched=2,
        name="low",
    )
    small0, dw0 = rest[:3], rest[3:]
    dz0, dw0, pair1, small0 = fenced(dz0, dw0, pair1, small0)
    run0 = start(dw0)
    low_bit = col_bits + 1
    pair1, _ = onward([settled(f) for f in pair1], low_bit)
    run0, dz0, small0 = fenced(run0, dz0, small0)
    pair0 = fork(run0)
    tile0 = dz0.reshape(rows, cols, channels)
    twin, other = edges(tile0, 0, HALO, odd_row)
    twin, other = to_twin(twin, "rows"), to_other(other, "rows")
    small_b = shape(small_rows, channels, dtype=BF16)
    small_f = shape(small_rows, channels)
    send, small = run(
        taps_kernel,
        (small_b, small_b),
        [
            shape(groups, *xpad.shape[:2], LANES), tile_z, shape(groups, 49, LANES),
            small_f, small_f,
        ],
        (place, mids, xpad, dz0, dz1, *small0, *small1),
        [pltpu.SMEM] + [None] * 10,
        name="taps",
    )
    small_got = flip_bit(send, 0)
    pair0, pair1, tile0, twin, other, small, small_got = fenced(
        pair0, pair1, tile0, twin, other, small, small_got
    )
    small = summed(small, small_got)
    for bit in range(1, col_bits - 1):
        small = summed(small, flip_bit(small, bit))
    both, small_by = [], []
    for i in range(2):
        flights, (came,) = onward([settled(pair0[i]), settled(pair1[i])], sides[1 - i], small)
        both.append(flights)
        small_by.append(came)
    small_by.append(flip_bit(small, *sides))
    wide0 = rimmed(tile0, twin, other, 0, odd_row, outer_row)
    twin, other = edges(wide0, 1, HALO, odd_col)
    twin, other = to_twin(twin, "cols"), to_other(other, "cols")
    both, wide0, twin, other, small, small_by = fenced(both, wide0, twin, other, small, small_by)
    small = summed(small, small_by[0], small_by[1], small_by[2])
    (run0,), (small_got,) = onward([merged([both[0][0], both[1][0]])], low_bit, small)
    part1, order1 = merged([both[0][1], both[1][1]])
    flight1 = (part1, jnp.zeros_like(part1), order1)
    if order1:
        (flight1,), _ = onward([(part1, order1)], order1[-1])
    (grad_in,) = run(
        last_kernel,
        (tile_b,),
        spread_scratch,
        (filled(rimmed(wide0, twin, other, 1, odd_col, outer_col)), grad_mid, taps),
        name="last",
    )
    while run0[2]:
        run0, flight1, small, small_got, grad_in = fenced(run0, flight1, small, small_got, grad_in)
        small = summed(small, small_got)
        (run0,), (small_got,) = onward([settled(run0)], run0[2][-1], small)
        if flight1[2]:
            (flight1,), _ = onward([settled(flight1)], flight1[2][-1])
    run0, flight1, small, small_got = fenced(run0, flight1, small, small_got)
    small = summed(small, small_got)
    small_got = flip_bit(small, 0)
    share = shape(layers, per, channels)
    grad_w_in, grad_w_out = run(
        functools.partial(weights_kernel, grad_scale),
        (share, share),
        [],
        [part.reshape(2, per, channels) for part in run0[:2] + flight1[:2]],
        name="weights",
    )
    grad_taps, grad_gains, grad_shifts, grad_b_in = run(
        functools.partial(small_kernel, grad_scale),
        (
            shape(49, layers, channels),
            shape(layers, channels),
            shape(layers, channels),
            shape(layers, hidden),
        ),
        [],
        (place, small, small_got),
        [pltpu.SMEM, None, None],
        name="small",
    )
    return (
        grad_in.reshape(rows, cols, channels),
        grad_taps.reshape(7, 7, layers, channels).transpose(2, 0, 1, 3),
        grad_gains,
        grad_shifts,
        grad_b_in,
        jnp.swapaxes(grad_w_in, 1, 2),
        jnp.swapaxes(grad_w_out, 1, 2),
    )


def solution(mesh):
    tile = P("rows", "cols", None)
    sliced = P(None, None, ("rows", "cols"))
    return jax.shard_map(
        shards,
        mesh=mesh,
        in_specs=(tile, tile, P(), P(), P(), P(), P(), P()),
        out_specs=(tile, P(), P(), P(), P(), sliced, sliced),
        check_vma=False,
    )
```

```python
import functools
import math

import jax
import jax.numpy as jnp
from jax import lax
from jax.experimental import pallas as pl
from jax.experimental.pallas import tpu as pltpu
from jax.sharding import PartitionSpec as P

EPSILON = 1e-06
INV_ROOT_TAU = 0.3989422804014327
HALF_LOG2E = 0.7213475204444817
ERFC_SLOPE = 0.4 * 0.7071067811865476
ERFC_TERMS = (
    0.23195388609975262,
    0.16163296978938874,
    0.4687286953098433,
    -0.3714470456115026,
    0.7094654203066808,
    -0.2003339536843631,
)
LANES = 128
HALO = 3
WIDE = 2 * HALO
F32 = jnp.float32
BF16 = jnp.bfloat16


def normal_parts(x):
    size = jnp.abs(x)
    bell = jnp.exp2(x * x * (-HALF_LOG2E))
    t = pl.reciprocal(1.0 + ERFC_SLOPE * size, approx=True)
    series = 0.5 * ERFC_TERMS[-1]
    for term in ERFC_TERMS[-2::-1]:
        series = series * t + 0.5 * term
    return size, series * t * bell, bell


def gelu_only(x):
    size, tail, _ = normal_parts(x)
    return jnp.maximum(x, 0.0) - size * tail


def gelu_parts(x):
    size, tail, bell = normal_parts(x)
    cdf = jnp.where(x >= 0, 1.0 - tail, tail)
    return jnp.maximum(x, 0.0) - size * tail, cdf + x * bell * INV_ROOT_TAU


def strip_rows(rows, cols):
    most = max(1, 288 // cols)
    return max(d for d in range(1, rows + 1) if rows % d == 0 and d <= most)


def conv_pass(source, row0, col0, taps, layer, target, rows, cols, back=False):
    strip = strip_rows(rows, cols)
    groups = source.shape[0]

    def one_strip(step, carry):
        g = step // (rows // strip)
        top = (step % (rows // strip)) * strip
        lanes = pl.ds(pl.multiple_of(g * LANES, LANES), LANES)
        sums = [jnp.zeros((cols, LANES), F32) for _ in range(strip)]
        for b in range(7):
            spots = [48 - 7 * a - b if back else 7 * a + b for a in range(7)]
            weights = [taps[spot, pl.ds(layer, 1), lanes] for spot in spots]
            for r in range(strip + 6):
                line = source[g, row0 + top + r, pl.ds(col0 + b, cols), :]
                for a in range(7):
                    if 0 <= r - a < strip:
                        sums[r - a] = sums[r - a] + weights[a] * line
        for i in range(strip):
            target[g, top + i] = sums[i]
        return carry

    lax.fori_loop(0, groups * (rows // strip), one_strip, 0)


def tap_pass(source, row0, col0, grad, target, rows, cols):
    def one_group(g, carry):
        lines = [grad[g, i] for i in range(rows)]
        for b in range(7):
            sums = [None] * 7
            for r in range(rows + 6):
                line = source[g, row0 + r, pl.ds(col0 + b, cols), :]
                for a in range(7):
                    if 0 <= r - a < rows:
                        part = lines[r - a] * line
                        sums[a] = part if sums[a] is None else sums[a] + part
            for a in range(7):
                total = jnp.sum(sums[a], axis=0, keepdims=True)
                target[g, pl.ds(7 * a + b, 1), :] = total
        return carry

    lax.fori_loop(0, source.shape[0], one_group, 0)


def joined(ref, rows, cols=slice(None)):
    parts = [ref[g, rows, cols, :] for g in range(ref.shape[0])]
    return jnp.concatenate([p.reshape(-1, LANES) for p in parts], axis=1)


def split_to(ref, rows, value, shape):
    for g in range(ref.shape[0]):
        ref[g, rows] = value[:, g * LANES : (g + 1) * LANES].reshape(*shape, LANES)


def norm_parts(z):
    center = z - jnp.mean(z, axis=-1, keepdims=True)
    inv = lax.rsqrt(jnp.mean(center * center, axis=-1, keepdims=True) + EPSILON)
    return center * inv, inv


def norm_back(dn, hat, inv, gain):
    scaled = dn * gain
    return inv * (
        scaled
        - jnp.mean(scaled, axis=-1, keepdims=True)
        - hat * jnp.mean(scaled * hat, axis=-1, keepdims=True)
    )


def dot_nn(a, b):
    return jnp.dot(a, b, preferred_element_type=F32)


def dot_nt(a, b):
    return lax.dot_general(a, b, (((1,), (1,)), ((), ())), preferred_element_type=F32)


def dot_tn(a, b):
    return lax.dot_general(a, b, (((0,), (0,)), ((), ())), preferred_element_type=F32)


def pixel_blocks(pixels):
    best = max(d for d in range(16, 257, 16) if pixels % d == 0)
    return [slice(start, start + best) for start in range(0, pixels, best)]


def hidden_chunks(hidden):
    size = 256 if hidden % 256 == 0 else hidden
    return [slice(start, start + size) for start in range(0, hidden, size)]


def hidden_forward(normed, w_in, bias, act, slope):
    for cut in hidden_chunks(w_in.shape[2]):
        for block in pixel_blocks(normed.shape[0]):
            value, factor = gelu_parts(dot_nn(normed[block, :], w_in[0, :, cut]) + bias[:, cut])
            act[block, cut] = value.astype(BF16)
            slope[block, cut] = factor


def hidden_back(grad, w_out, slope, gpre, db):
    for cut in hidden_chunks(w_out.shape[2]):
        bias_sum = None
        for block in pixel_blocks(grad.shape[0]):
            gradient = dot_nn(grad[block, :], w_out[0, :, cut]) * slope[block, cut]
            gpre[block, cut] = gradient.astype(BF16)
            part = jnp.sum(gradient, axis=0, keepdims=True)
            bias_sum = part if bias_sum is None else bias_sum + part
        db[:, cut] = bias_sum


def dz_of(gpre, w_in, hat, inv, gain, dz_out, dgain, dshift):
    dn = dot_nt(gpre[...], w_in[0])
    dgain[...] = jnp.sum(dn * hat, axis=0, keepdims=True)
    dshift[...] = jnp.sum(dn, axis=0, keepdims=True)
    dz_out[...] = norm_back(dn, hat, inv, gain).astype(BF16)


def mlp_grads(normed, grad, w_in, b_in, w_out, act, gpre, db):
    pixels = grad.shape[0]
    for cut in hidden_chunks(w_in.shape[2]):
        bias = b_in[:, cut]
        bias_sum = None
        for block in pixel_blocks(pixels):
            pre = dot_nn(normed[block, :], w_in[0, :, cut]) + bias
            value, slope = gelu_parts(pre)
            act[block, cut] = value.astype(BF16)
            gradient = dot_nn(grad[block, :], w_out[0, :, cut]) * slope
            gpre[block, cut] = gradient.astype(BF16)
            part = jnp.sum(gradient, axis=0, keepdims=True)
            bias_sum = part if bias_sum is None else bias_sum + part
        db[:, cut] = bias_sum


def weight_grads(place, normed, grad, act, gpre, dw, per):
    hidden, channels = act.shape[1], grad.shape[1]
    size = min(n for n in range(128, hidden + 1, 128) if hidden % n == 0 and n % (2 * per) == 0 and n >= 256)
    for first in range(0, hidden, size):
        cut = slice(first, first + size)
        for i, (left, right) in enumerate(((gpre, normed), (act, grad))):
            value = dot_tn(left[:, cut], right[...]).astype(BF16)
            if len(dw) == 1:
                dw[0][i, cut, :] = value
                continue
            value = value.reshape(size // (2 * per), 2, per, channels)
            upper = place[4] == 1
            half = slice(first // 2, (first + size) // 2)
            dw[0][i, half, :] = jnp.where(upper, value[:, 0], value[:, 1]).reshape(-1, channels)
            dw[1][i, half, :] = jnp.where(upper, value[:, 1], value[:, 0]).reshape(-1, channels)


def fetch_layers(triples, arrived):
    copies = [
        pltpu.make_async_copy(source.at[pl.ds(layer, 1)], target, arrived.at[i])
        for i, (source, layer, target) in enumerate(triples)
    ]
    for copy in copies:
        copy.start()
    return copies


def forward_kernel(
    place, xpad, taps, gains, shifts, w_in, w_out, b_in, mids, z_out,
    xs, zs, act, w_in0, w_out0, arrived,
):
    waits = fetch_layers(((w_in, 0, w_in0), (w_out, 0, w_out0)), arrived)
    groups, mid_rows, mid_cols = zs.shape[:3]
    rows, cols = z_out.shape[1:3]
    for g in range(groups):
        xs[g] = xpad[:, :, g * LANES : (g + 1) * LANES].astype(F32)
    conv_pass(xs, 0, 0, taps, 0, zs, mid_rows, mid_cols)
    z_out[...] = zs[:, HALO : HALO + rows, HALO : HALO + cols, :]
    strip = act.shape[0] // mid_cols
    for wait in waits:
        wait.wait()

    def one_strip(step, carry):
        top = step * strip
        hat, _ = norm_parts(joined(zs, pl.ds(top, strip)))
        normed = (hat * gains[0:1] + shifts[0:1]).astype(BF16)
        for cut in hidden_chunks(w_in0.shape[2]):
            pre = dot_nn(normed, w_in0[0, :, cut]) + b_in[0:1, cut]
            act[:, cut] = gelu_only(pre).astype(BF16)
        mixed = dot_nt(act[...], w_out0[0])
        row = lax.broadcasted_iota(jnp.int32, (strip, mid_cols, 1), 0) + (top - HALO) + place[0]
        col = lax.broadcasted_iota(jnp.int32, (strip, mid_cols, 1), 1) - HALO + place[1]
        real = (row >= 0) & (row < place[2]) & (col >= 0) & (col < place[3])
        real = jnp.where(real, 1.0, 0.0).reshape(strip * mid_cols, 1)
        base = joined(xs, pl.ds(top + HALO, strip), slice(HALO, HALO + mid_cols))
        mid = (base + mixed).astype(BF16).astype(F32) * real
        split_to(mids, pl.ds(top, strip), mid, (strip, mid_cols))
        return carry

    lax.fori_loop(0, mid_rows // strip, one_strip, 0)


def top_kernel(
    mids, grad, taps, gains, shifts, w_in, w_out, b_in,
    dz_out, normed, act, gpre, db, dgain, dshift, z, w_in1, w_out1, arrived,
):
    waits = fetch_layers(((w_in, 1, w_in1), (w_out, 1, w_out1)), arrived)
    conv_pass(mids, 0, 0, taps, 1, z, *z.shape[1:3])
    hat, inv = norm_parts(joined(z, slice(None)))
    normed[...] = (hat * gains[1:2] + shifts[1:2]).astype(BF16)
    for wait in waits:
        wait.wait()
    mlp_grads(normed, grad, w_in1, b_in.at[pl.ds(1, 1)], w_out1, act, gpre, db)
    dz_of(gpre, w_in1, hat, inv, gains[1:2], dz_out, dgain, dshift)


def again_kernel(z0, gains, shifts, w_in, b_in, hat_out, inv_out, normed, act, slope, w_in0, arrived):
    (wait,) = fetch_layers(((w_in, 0, w_in0),), arrived)
    hat, inv = norm_parts(joined(z0, slice(None)))
    hat_out[...] = hat
    inv_out[...] = jnp.broadcast_to(inv, inv_out.shape)
    normed[...] = (hat * gains[0:1] + shifts[0:1]).astype(BF16)
    wait.wait()
    hidden_forward(normed, w_in0, b_in.at[pl.ds(0, 1)], act, slope)


def low_kernel(
    per, place, dzpad, grad, hat, inv, normed, act, slope, taps, gains, w_in, w_out,
    gmid, dz_out, db, dgain, dshift, *rest,
):
    *dw, dzs, spread, gpre, w_in0, w_out0, arrived = rest
    waits = fetch_layers(((w_out, 0, w_out0), (w_in, 0, w_in0)), arrived)
    spread_pass(dzpad, dzs, taps, 1, spread)
    gmid[...] = (grad[...].astype(F32) + joined(spread, slice(None))).astype(BF16)
    for wait in waits:
        wait.wait()
    hidden_back(gmid, w_out0, slope, gpre, db)
    dz_of(gpre, w_in0, hat[...], inv[:, :1], gains[0:1], dz_out, dgain, dshift)
    weight_grads(place, normed, gmid, act, gpre, dw, per)


def weights_top_kernel(per, place, normed, act, gpre, grad, *dw):
    weight_grads(place, normed, grad, act, gpre, dw, per)


def spread_pass(dzpad, dzs, taps, layer, spread):
    for g in range(dzs.shape[0]):
        dzs[g] = dzpad[:, :, g * LANES : (g + 1) * LANES].astype(F32)
    conv_pass(dzs, 0, 0, taps, layer, spread, *spread.shape[1:3], back=True)


def last_kernel(dzpad, gmid, taps, out, dzs, spread):
    spread_pass(dzpad, dzs, taps, 0, spread)
    out[...] = (gmid[...].astype(F32) + joined(spread, slice(None))).astype(BF16)


def small_rows_of(values, row0, col0, dz, dzs, taps, db, dgain, dshift, sums):
    rows, cols = dzs.shape[1:3]
    channels = sums.shape[1]
    split_to(dzs, slice(None), dz[...].astype(F32), (rows, cols))
    count = db.shape[1] // channels
    for k in range(count):
        sums[k : k + 1, :] = db[:, k * channels : (k + 1) * channels]
    sums[count : count + 1, :] = dgain[...]
    sums[count + 1 : count + 2, :] = dshift[...]
    tap_pass(values, row0, col0, dzs, taps, rows, cols)
    for g in range(taps.shape[0]):
        sums[count + 2 : count + 51, g * LANES : (g + 1) * LANES] = taps[g]


def taps_kernel(
    place, mids, xpad, dz0, dz1, db0, dgain0, dshift0, db1, dgain1, dshift1, send, keep,
    xs, dzs, taps, sums0, sums1,
):
    for g in range(dzs.shape[0]):
        xs[g] = xpad[:, :, g * LANES : (g + 1) * LANES].astype(F32)
    sums0[...] = jnp.zeros(sums0.shape, F32)
    sums1[...] = jnp.zeros(sums1.shape, F32)
    small_rows_of(mids, 0, 0, dz1, dzs, taps, db1, dgain1, dshift1, sums1)
    small_rows_of(xs, HALO, HALO, dz0, dzs, taps, db0, dgain0, dshift0, sums0)
    upper = place[4] == 1
    send[...] = jnp.where(upper, sums0[...], sums1[...]).astype(BF16)
    keep[...] = jnp.where(upper, sums1[...], sums0[...]).astype(BF16)


def small_kernel(scale, place, mine, got, taps_out, gains, shifts, biases):
    upper = place[4] == 1
    own, came = mine[...].astype(F32) * scale, got[...].astype(F32) * scale
    channels = own.shape[1]
    count = biases.shape[1] // channels
    for layer, part in enumerate((jnp.where(upper, came, own), jnp.where(upper, own, came))):
        at = slice(layer, layer + 1)
        for k in range(count):
            biases[at, k * channels : (k + 1) * channels] = part[k : k + 1, :]
        gains[at, :] = part[count : count + 1, :]
        shifts[at, :] = part[count + 1 : count + 2, :]
        for tap in range(49):
            taps_out[tap, at, :] = part[count + 2 + tap : count + 3 + tap, :]


def weights_kernel(scale, keep0, got0, keep1, got1, out_in, out_out):
    for layer, (keep, got) in enumerate(((keep0, got0), (keep1, got1))):
        for i, out in enumerate((out_in, out_out)):
            out[layer] = (keep[i].astype(F32) + got[i].astype(F32)) * scale


def shape(*dims, dtype=F32):
    return jax.ShapeDtypeStruct(dims, dtype)


def run(kernel, outs, scratch, args, specs=None, fetched=0, name=None, room=46):
    vmem = pl.BlockSpec(memory_space=pltpu.VMEM)
    semaphores = [pltpu.SemaphoreType.DMA((fetched,))] if fetched else []
    return pl.pallas_call(
        kernel,
        out_shape=outs,
        in_specs=[
            vmem if s is None else pl.BlockSpec(memory_space=s) for s in (specs or [None] * len(args))
        ],
        out_specs=tuple(vmem for _ in outs),
        scratch_shapes=[pltpu.VMEM(s.shape, s.dtype) for s in scratch] + semaphores,
        compiler_params=pltpu.CompilerParams(vmem_limit_bytes=room * 1024 * 1024),
        name=name,
    )(*args)


def edges(tile, axis, width, odd):
    count = tile.shape[axis]
    low = lax.slice_in_dim(tile, 0, width, axis=axis)
    high = lax.slice_in_dim(tile, count - width, count, axis=axis)
    return jnp.where(odd, low, high), jnp.where(odd, high, low)


def to_twin(edge, axis):
    count = lax.axis_size(axis)
    return lax.ppermute(edge, axis, [(i, i ^ 1) for i in range(count) if i ^ 1 < count])


def to_other(edge, axis):
    n_rows, n_cols = lax.axis_size("rows"), lax.axis_size("cols")
    count = lax.axis_size(axis)
    pairs = []
    for r in range(n_rows):
        for c in range(n_cols):
            at = r if axis == "rows" else c
            partner = at + 1 if at % 2 else at - 1
            if 0 <= partner < count:
                there = (partner, c) if axis == "rows" else (r, partner)
            else:
                there = (r, c ^ 1) if axis == "rows" else (r ^ 1, c)
            pairs.append((r * n_cols + c, there[0] * n_cols + there[1]))
    return lax.ppermute(edge, ("rows", "cols"), pairs)


def rimmed(tile, from_twin, from_other, axis, odd, outer):
    from_other = jnp.where(outer, jnp.zeros_like(from_other), from_other)
    low = jnp.where(odd, from_twin, from_other)
    high = jnp.where(odd, from_other, from_twin)
    return jnp.concatenate([low, tile, high], axis=axis)


def flip_bit(value, *bits):
    flip = sum(1 << bit for bit in bits)
    both = ("rows", "cols")
    total = lax.axis_size("rows") * lax.axis_size("cols")
    return lax.ppermute(value, both, [(i, i ^ flip) for i in range(total)])


def halves(chunks, dim, mine):
    sizes = [1 if d == dim else n for d, n in enumerate(chunks.shape)]

    def one(bit):
        starts = [bit if d == dim else jnp.uint32(0) for d in range(chunks.ndim)]
        return lax.squeeze(lax.dynamic_slice(chunks, starts, sizes), (dim,))

    return one(mine[1]), one(mine[0])


def summed(own, *got):
    parts = [part.astype(F32) for part in (own,) + got]
    while len(parts) > 1:
        parts = [a + b for a, b in zip(parts[::2], parts[1::2])]
    return parts[0].astype(BF16)


def cut(chunks, order, bit, mine):
    spot = order.index(bit)
    per = chunks.shape[-2:]
    pair = chunks.reshape((-1, 2 ** spot, 2, 2 ** (len(order) - spot - 1)) + per)
    send, keep = halves(pair, 2, mine[bit])
    return send, keep, [b for b in order if b != bit]


def step(chunks, order, bit, mine):
    send, keep, left = cut(chunks, order, bit, mine)
    return keep, flip_bit(send, bit), left


def shards(activations, grad_out, kernels, norm_gains, norm_shifts, w_in, b_in, w_out):
    rows, cols, channels = activations.shape
    layers, _, hidden = w_in.shape
    groups = channels // LANES
    n_rows, n_cols = lax.axis_size("rows"), lax.axis_size("cols")
    total = n_rows * n_cols
    bits = total.bit_length() - 1
    col_bits = n_cols.bit_length() - 1
    me = (lax.axis_index("rows") * n_cols + lax.axis_index("cols")).astype(jnp.uint32)
    mine = [(((me >> k) & 1), 1 - ((me >> k) & 1)) for k in range(bits)]
    grad_scale = 1.0 / math.sqrt(rows * cols * total)
    pixels = rows * cols

    taps = kernels.transpose(1, 2, 0, 3).reshape(49, layers, channels)
    place = jnp.stack(
        [
            lax.axis_index("rows") * rows,
            lax.axis_index("cols") * cols,
            jnp.int32(rows * n_rows),
            jnp.int32(cols * n_cols),
            lax.axis_index("cols") & 1,
        ]
    ).astype(jnp.int32)
    grad_flat = grad_out.reshape(pixels, channels)

    at_row, at_col = lax.axis_index("rows"), lax.axis_index("cols")
    odd_col, odd_row = (at_col & 1) == 1, (at_row & 1) == 1
    outer_col = (at_col == 0) | (at_col == n_cols - 1)
    outer_row = (at_row == 0) | (at_row == n_rows - 1)
    activations, place, mine, odd_col, odd_row, outer_col, outer_row = lax.optimization_barrier(
        (activations, place, mine, odd_col, odd_row, outer_col, outer_row)
    )

    def rim_cols(tile, width):
        twin, other = edges(tile, 1, width, odd_col)
        return rimmed(tile, to_twin(twin, "cols"), to_other(other, "cols"), 1, odd_col, outer_col)

    def rim_rows(tile, width):
        twin, other = edges(tile, 0, width, odd_row)
        return rimmed(tile, to_twin(twin, "rows"), to_other(other, "rows"), 0, odd_row, outer_row)

    def filled(wide):
        return jnp.pad(wide, ((0, 0), (0, cols + 16 - wide.shape[1]), (0, 0)))

    mid_rows, mid_cols = rows + 2 * HALO, cols + 8
    strip = max(d for d in range(1, mid_rows + 1) if mid_rows % d == 0 and d * mid_cols <= 264)
    weights = [shape(1, channels, hidden, dtype=BF16)] * 2
    tile_z = shape(groups, rows, cols, LANES)
    tile_b = shape(pixels, channels, dtype=BF16)
    tile_h = shape(pixels, hidden, dtype=BF16)
    per = hidden // total
    split = 2 if per % 16 == 0 and col_bits == 2 else 1
    grads_b = (shape(2, hidden // split, channels, dtype=BF16),) * split
    small_outs = (shape(1, hidden), shape(1, channels), shape(1, channels))
    small_rows = 64

    xpad = filled(rim_cols(rim_rows(activations, WIDE), WIDE))
    mids, z0 = run(
        forward_kernel,
        (shape(groups, mid_rows, mid_cols, LANES), tile_z),
        [
            shape(groups, *xpad.shape[:2], LANES),
            shape(groups, mid_rows, mid_cols, LANES),
            shape(strip * mid_cols, hidden, dtype=BF16),
        ]
        + weights,
        (place, xpad, taps, norm_gains, norm_shifts, w_in, w_out, b_in),
        [pltpu.SMEM] + [None] * 4 + [pl.ANY] * 2 + [None],
        fetched=2,
        name="forward",
        room=50,
    )
    dz1, normed1, act1, gpre1, *small1 = run(
        top_kernel,
        (tile_b, tile_b, tile_h, tile_h) + small_outs,
        [tile_z] + weights,
        (mids, grad_flat, taps, norm_gains, norm_shifts, w_in, w_out, b_in),
        [None] * 5 + [pl.ANY] * 2 + [None],
        fetched=2,
        name="top",
        room=50,
    )

    sides = (col_bits - 1, col_bits)

    def fenced(*values):
        leaves, tree = jax.tree.flatten(values)
        arrays = [i for i, leaf in enumerate(leaves) if not isinstance(leaf, int)]
        for i, value in zip(arrays, lax.optimization_barrier(tuple(leaves[i] for i in arrays))):
            leaves[i] = value
        return jax.tree.unflatten(tree, leaves)

    def settled(flight):
        return summed(flight[0], flight[1]), flight[2]

    def start(dw):
        order = list(range(bits - 1, -1, -1))
        if split == 2:
            send, keep = (d.reshape(2, total // 2, per, channels) for d in dw)
            return keep, flip_bit(send, 0), order[:-1]
        chunks = dw[0].reshape(2, total, per, channels)
        for bit in range(col_bits - 2):
            chunks, order = settled(step(chunks, order, bit, mine))
        return step(chunks, order, col_bits - 2, mine)

    def fork(flight):
        chunks, order = settled(flight)
        return [step(chunks[i], order, sides[i], mine) for i in range(2)]

    def onward(parts, bit, *riders):
        kept, sent, lefts = [], [], []
        for chunks, order in parts:
            send, keep, left = cut(chunks, order, bit, mine)
            kept.append(keep)
            sent.append(send.reshape(-1, channels))
            lefts.append(left)
        got = flip_bit(jnp.concatenate(sent + list(riders), axis=0), bit)
        flights, first = [], 0
        for keep, send, left in zip(kept, sent, lefts):
            came = got[first : first + send.shape[0]].reshape(keep.shape)
            flights.append((keep, came, left))
            first += send.shape[0]
        return flights, [got[first:]] if riders else []

    def merged(flights):
        done = [settled(f) for f in flights]
        return jnp.stack([d[0].reshape(-1, per, channels) for d in done]), done[0][1]

    tile1 = dz1.reshape(rows, cols, channels)
    twin, other = edges(tile1, 0, HALO, odd_row)
    twin, other = to_twin(twin, "rows"), to_other(other, "rows")
    dw1 = run(
        functools.partial(weights_top_kernel, per),
        grads_b,
        [],
        (place, normed1, act1, gpre1, grad_flat),
        [pltpu.SMEM] + [None] * 4,
        name="weights_top",
    )
    tile1, twin, other, dw1, z0 = fenced(tile1, twin, other, dw1, z0)
    wide1 = rimmed(tile1, twin, other, 0, odd_row, outer_row)
    run1 = start(dw1)
    twin, other = edges(wide1, 1, HALO, odd_col)
    twin, other = to_twin(twin, "cols"), to_other(other, "cols")
    tile_f = shape(pixels, channels)
    again = run(
        again_kernel,
        (tile_f, shape(pixels, LANES), tile_b, tile_h, shape(pixels, hidden)),
        weights[:1],
        (z0, norm_gains, norm_shifts, w_in, b_in),
        [None] * 3 + [pl.ANY, None],
        fetched=1,
        name="again",
    )
    wide1, twin, other, run1, again = fenced(wide1, twin, other, run1, again)
    pair1 = fork(run1)
    dzpad1 = filled(rimmed(wide1, twin, other, 1, odd_col, outer_col))
    spread_scratch = [shape(groups, *dzpad1.shape[:2], LANES), tile_z]
    grad_mid, dz0, *rest = run(
        functools.partial(low_kernel, per),
        (tile_b, tile_b) + small_outs + grads_b,
        spread_scratch + [tile_h] + weights,
        (place, dzpad1, grad_flat, *again, taps, norm_gains, w_in, w_out),
        [pltpu.SMEM] + [None] * 9 + [pl.ANY] * 2,
        fetched=2,
        name="low",
    )
    small0, dw0 = rest[:3], rest[3:]
    dz0, dw0, pair1, small0 = fenced(dz0, dw0, pair1, small0)
    run0 = start(dw0)
    low_bit = col_bits + 1
    pair1, _ = onward([settled(f) for f in pair1], low_bit)
    run0, dz0, small0 = fenced(run0, dz0, small0)
    pair0 = fork(run0)
    tile0 = dz0.reshape(rows, cols, channels)
    twin, other = edges(tile0, 0, HALO, odd_row)
    twin, other = to_twin(twin, "rows"), to_other(other, "rows")
    small_b = shape(small_rows, channels, dtype=BF16)
    small_f = shape(small_rows, channels)
    send, small = run(
        taps_kernel,
        (small_b, small_b),
        [
            shape(groups, *xpad.shape[:2], LANES), tile_z, shape(groups, 49, LANES),
            small_f, small_f,
        ],
        (place, mids, xpad, dz0, dz1, *small0, *small1),
        [pltpu.SMEM] + [None] * 10,
        name="taps",
    )
    small_got = flip_bit(send, 0)
    pair0, pair1, tile0, twin, other, small, small_got = fenced(
        pair0, pair1, tile0, twin, other, small, small_got
    )
    small = summed(small, small_got)
    for bit in range(1, col_bits - 1):
        small = summed(small, flip_bit(small, bit))
    both, small_by = [], []
    for i in range(2):
        flights, (came,) = onward([settled(pair0[i]), settled(pair1[i])], sides[1 - i], small)
        both.append(flights)
        small_by.append(came)
    small_by.append(flip_bit(small, *sides))
    wide0 = rimmed(tile0, twin, other, 0, odd_row, outer_row)
    twin, other = edges(wide0, 1, HALO, odd_col)
    twin, other = to_twin(twin, "cols"), to_other(other, "cols")
    both, wide0, twin, other, small, small_by = fenced(both, wide0, twin, other, small, small_by)
    small = summed(small, small_by[0], small_by[1], small_by[2])
    (run0,), (small_got,) = onward([merged([both[0][0], both[1][0]])], low_bit, small)
    part1, order1 = merged([both[0][1], both[1][1]])
    flight1 = (part1, jnp.zeros_like(part1), order1)
    if order1:
        (flight1,), _ = onward([(part1, order1)], order1[-1])
    (grad_in,) = run(
        last_kernel,
        (tile_b,),
        spread_scratch,
        (filled(rimmed(wide0, twin, other, 1, odd_col, outer_col)), grad_mid, taps),
        name="last",
    )
    while run0[2]:
        run0, flight1, small, small_got, grad_in = fenced(run0, flight1, small, small_got, grad_in)
        small = summed(small, small_got)
        (run0,), (small_got,) = onward([settled(run0)], run0[2][-1], small)
        if flight1[2]:
            (flight1,), _ = onward([settled(flight1)], flight1[2][-1])
    run0, flight1, small, small_got = fenced(run0, flight1, small, small_got)
    small = summed(small, small_got)
    small_got = flip_bit(small, 0)
    share = shape(layers, per, channels)
    grad_w_in, grad_w_out = run(
        functools.partial(weights_kernel, grad_scale),
        (share, share),
        [],
        [part.reshape(2, per, channels) for part in run0[:2] + flight1[:2]],
        name="weights",
    )
    grad_taps, grad_gains, grad_shifts, grad_b_in = run(
        functools.partial(small_kernel, grad_scale),
        (
            shape(49, layers, channels),
            shape(layers, channels),
            shape(layers, channels),
            shape(layers, hidden),
        ),
        [],
        (place, small, small_got),
        [pltpu.SMEM, None, None],
        name="small",
    )
    return (
        grad_in.reshape(rows, cols, channels),
        grad_taps.reshape(7, 7, layers, channels).transpose(2, 0, 1, 3),
        grad_gains,
        grad_shifts,
        grad_b_in,
        jnp.swapaxes(grad_w_in, 1, 2),
        jnp.swapaxes(grad_w_out, 1, 2),
    )


def solution(mesh):
    tile = P("rows", "cols", None)
    sliced = P(None, None, ("rows", "cols"))
    return jax.shard_map(
        shards,
        mesh=mesh,
        in_specs=(tile, tile, P(), P(), P(), P(), P(), P()),
        out_specs=(tile, P(), P(), P(), P(), sliced, sliced),
        check_vma=False,
    )
```

```python
import functools
import math

import jax
import jax.numpy as jnp
from jax import lax
from jax.experimental import pallas as pl
from jax.experimental.pallas import tpu as pltpu
from jax.sharding import PartitionSpec as P

EPSILON = 1e-06
INV_ROOT_TAU = 0.3989422804014327
HALF_LOG2E = 0.7213475204444817
ERFC_SLOPE = 0.4 * 0.7071067811865476
ERFC_TERMS = (
    0.23195388609975262,
    0.16163296978938874,
    0.4687286953098433,
    -0.3714470456115026,
    0.7094654203066808,
    -0.2003339536843631,
)
LANES = 128
HALO = 3
WIDE = 2 * HALO
F32 = jnp.float32
BF16 = jnp.bfloat16


def normal_parts(x):
    size = jnp.abs(x)
    bell = jnp.exp2(x * x * (-HALF_LOG2E))
    t = pl.reciprocal(1.0 + ERFC_SLOPE * size, approx=True)
    series = 0.5 * ERFC_TERMS[-1]
    for term in ERFC_TERMS[-2::-1]:
        series = series * t + 0.5 * term
    return size, series * t * bell, bell


def gelu_only(x):
    size, tail, _ = normal_parts(x)
    return jnp.maximum(x, 0.0) - size * tail


def gelu_parts(x):
    size, tail, bell = normal_parts(x)
    cdf = jnp.where(x >= 0, 1.0 - tail, tail)
    return jnp.maximum(x, 0.0) - size * tail, cdf + x * bell * INV_ROOT_TAU


def strip_rows(rows, cols):
    most = max(1, 288 // cols)
    return max(d for d in range(1, rows + 1) if rows % d == 0 and d <= most)


def conv_pass(source, row0, col0, taps, layer, target, rows, cols, back=False):
    strip = strip_rows(rows, cols)
    groups = source.shape[0]

    def one_strip(step, carry):
        g = step // (rows // strip)
        top = (step % (rows // strip)) * strip
        lanes = pl.ds(pl.multiple_of(g * LANES, LANES), LANES)
        sums = [jnp.zeros((cols, LANES), F32) for _ in range(strip)]
        for b in range(7):
            spots = [48 - 7 * a - b if back else 7 * a + b for a in range(7)]
            weights = [taps[spot, pl.ds(layer, 1), lanes] for spot in spots]
            for r in range(strip + 6):
                line = source[g, row0 + top + r, pl.ds(col0 + b, cols), :]
                for a in range(7):
                    if 0 <= r - a < strip:
                        sums[r - a] = sums[r - a] + weights[a] * line
        for i in range(strip):
            target[g, top + i] = sums[i]
        return carry

    lax.fori_loop(0, groups * (rows // strip), one_strip, 0)


def tap_pass(source, row0, col0, grad, target, rows, cols):
    def one_group(g, carry):
        lines = [grad[g, i] for i in range(rows)]
        for b in range(7):
            sums = [None] * 7
            for r in range(rows + 6):
                line = source[g, row0 + r, pl.ds(col0 + b, cols), :]
                for a in range(7):
                    if 0 <= r - a < rows:
                        part = lines[r - a] * line
                        sums[a] = part if sums[a] is None else sums[a] + part
            for a in range(7):
                total = jnp.sum(sums[a], axis=0, keepdims=True)
                target[g, pl.ds(7 * a + b, 1), :] = total
        return carry

    lax.fori_loop(0, source.shape[0], one_group, 0)


def joined(ref, rows, cols=slice(None)):
    parts = [ref[g, rows, cols, :] for g in range(ref.shape[0])]
    return jnp.concatenate([p.reshape(-1, LANES) for p in parts], axis=1)


def split_to(ref, rows, value, shape):
    for g in range(ref.shape[0]):
        ref[g, rows] = value[:, g * LANES : (g + 1) * LANES].reshape(*shape, LANES)


def norm_parts(z):
    center = z - jnp.mean(z, axis=-1, keepdims=True)
    inv = lax.rsqrt(jnp.mean(center * center, axis=-1, keepdims=True) + EPSILON)
    return center * inv, inv


def norm_back(dn, hat, inv, gain):
    scaled = dn * gain
    return inv * (
        scaled
        - jnp.mean(scaled, axis=-1, keepdims=True)
        - hat * jnp.mean(scaled * hat, axis=-1, keepdims=True)
    )


def dot_nn(a, b):
    return jnp.dot(a, b, preferred_element_type=F32)


def dot_nt(a, b):
    return lax.dot_general(a, b, (((1,), (1,)), ((), ())), preferred_element_type=F32)


def dot_tn(a, b):
    return lax.dot_general(a, b, (((0,), (0,)), ((), ())), preferred_element_type=F32)


def pixel_blocks(pixels):
    best = max(d for d in range(16, 257, 16) if pixels % d == 0)
    return [slice(start, start + best) for start in range(0, pixels, best)]


def hidden_chunks(hidden):
    size = 256 if hidden % 256 == 0 else hidden
    return [slice(start, start + size) for start in range(0, hidden, size)]


def hidden_forward(normed, w_in, bias, act, slope):
    for cut in hidden_chunks(w_in.shape[2]):
        for block in pixel_blocks(normed.shape[0]):
            value, factor = gelu_parts(dot_nn(normed[block, :], w_in[0, :, cut]) + bias[:, cut])
            act[block, cut] = value.astype(BF16)
            slope[block, cut] = factor


def hidden_back(grad, w_out, slope, gpre, db):
    for cut in hidden_chunks(w_out.shape[2]):
        bias_sum = None
        for block in pixel_blocks(grad.shape[0]):
            gradient = dot_nn(grad[block, :], w_out[0, :, cut]) * slope[block, cut]
            gpre[block, cut] = gradient.astype(BF16)
            part = jnp.sum(gradient, axis=0, keepdims=True)
            bias_sum = part if bias_sum is None else bias_sum + part
        db[:, cut] = bias_sum


def dz_of(gpre, w_in, hat, inv, gain, dz_out, dgain, dshift):
    dn = dot_nt(gpre[...], w_in[0])
    dgain[...] = jnp.sum(dn * hat, axis=0, keepdims=True)
    dshift[...] = jnp.sum(dn, axis=0, keepdims=True)
    dz_out[...] = norm_back(dn, hat, inv, gain).astype(BF16)


def mlp_grads(normed, grad, w_in, b_in, w_out, act, gpre, db):
    pixels = grad.shape[0]
    for cut in hidden_chunks(w_in.shape[2]):
        bias = b_in[:, cut]
        bias_sum = None
        for block in pixel_blocks(pixels):
            pre = dot_nn(normed[block, :], w_in[0, :, cut]) + bias
            value, slope = gelu_parts(pre)
            act[block, cut] = value.astype(BF16)
            gradient = dot_nn(grad[block, :], w_out[0, :, cut]) * slope
            gpre[block, cut] = gradient.astype(BF16)
            part = jnp.sum(gradient, axis=0, keepdims=True)
            bias_sum = part if bias_sum is None else bias_sum + part
        db[:, cut] = bias_sum


def weight_grads(place, normed, grad, act, gpre, dw, per):
    hidden, channels = act.shape[1], grad.shape[1]
    size = min(n for n in range(128, hidden + 1, 128) if hidden % n == 0 and n % (2 * per) == 0 and n >= 256)
    for first in range(0, hidden, size):
        cut = slice(first, first + size)
        for i, (left, right) in enumerate(((gpre, normed), (act, grad))):
            value = dot_tn(left[:, cut], right[...]).astype(BF16)
            if len(dw) == 1:
                dw[0][i, cut, :] = value
                continue
            value = value.reshape(size // (2 * per), 2, per, channels)
            upper = place[4] == 1
            half = slice(first // 2, (first + size) // 2)
            dw[0][i, half, :] = jnp.where(upper, value[:, 0], value[:, 1]).reshape(-1, channels)
            dw[1][i, half, :] = jnp.where(upper, value[:, 1], value[:, 0]).reshape(-1, channels)


def fetch_layers(triples, arrived):
    copies = [
        pltpu.make_async_copy(source.at[pl.ds(layer, 1)], target, arrived.at[i])
        for i, (source, layer, target) in enumerate(triples)
    ]
    for copy in copies:
        copy.start()
    return copies


def forward_kernel(
    place, xpad, taps, gains, shifts, w_in, w_out, b_in, mids, z_out,
    xs, zs, act, w_in0, w_out0, arrived,
):
    waits = fetch_layers(((w_in, 0, w_in0), (w_out, 0, w_out0)), arrived)
    groups, mid_rows, mid_cols = zs.shape[:3]
    rows, cols = z_out.shape[1:3]
    for g in range(groups):
        xs[g] = xpad[:, :, g * LANES : (g + 1) * LANES].astype(F32)
    conv_pass(xs, 0, 0, taps, 0, zs, mid_rows, mid_cols)
    z_out[...] = zs[:, HALO : HALO + rows, HALO : HALO + cols, :]
    strip = act.shape[0] // mid_cols
    for wait in waits:
        wait.wait()

    def one_strip(step, carry):
        top = step * strip
        hat, _ = norm_parts(joined(zs, pl.ds(top, strip)))
        normed = (hat * gains[0:1] + shifts[0:1]).astype(BF16)
        for cut in hidden_chunks(w_in0.shape[2]):
            pre = dot_nn(normed, w_in0[0, :, cut]) + b_in[0:1, cut]
            act[:, cut] = gelu_only(pre).astype(BF16)
        mixed = dot_nt(act[...], w_out0[0])
        row = lax.broadcasted_iota(jnp.int32, (strip, mid_cols, 1), 0) + (top - HALO) + place[0]
        col = lax.broadcasted_iota(jnp.int32, (strip, mid_cols, 1), 1) - HALO + place[1]
        real = (row >= 0) & (row < place[2]) & (col >= 0) & (col < place[3])
        real = jnp.where(real, 1.0, 0.0).reshape(strip * mid_cols, 1)
        base = joined(xs, pl.ds(top + HALO, strip), slice(HALO, HALO + mid_cols))
        mid = (base + mixed).astype(BF16).astype(F32) * real
        split_to(mids, pl.ds(top, strip), mid, (strip, mid_cols))
        return carry

    lax.fori_loop(0, mid_rows // strip, one_strip, 0, unroll=True)


def top_kernel(
    mids, grad, taps, gains, shifts, w_in, w_out, b_in,
    dz_out, normed, act, gpre, db, dgain, dshift, z, w_in1, w_out1, arrived,
):
    waits = fetch_layers(((w_in, 1, w_in1), (w_out, 1, w_out1)), arrived)
    conv_pass(mids, 0, 0, taps, 1, z, *z.shape[1:3])
    hat, inv = norm_parts(joined(z, slice(None)))
    normed[...] = (hat * gains[1:2] + shifts[1:2]).astype(BF16)
    for wait in waits:
        wait.wait()
    mlp_grads(normed, grad, w_in1, b_in.at[pl.ds(1, 1)], w_out1, act, gpre, db)
    dz_of(gpre, w_in1, hat, inv, gains[1:2], dz_out, dgain, dshift)


def again_kernel(z0, gains, shifts, w_in, b_in, hat_out, inv_out, normed, act, slope, w_in0, arrived):
    (wait,) = fetch_layers(((w_in, 0, w_in0),), arrived)
    hat, inv = norm_parts(joined(z0, slice(None)))
    hat_out[...] = hat
    inv_out[...] = jnp.broadcast_to(inv, inv_out.shape)
    normed[...] = (hat * gains[0:1] + shifts[0:1]).astype(BF16)
    wait.wait()
    hidden_forward(normed, w_in0, b_in.at[pl.ds(0, 1)], act, slope)


def low_kernel(
    per, place, dzpad, grad, hat, inv, normed, act, slope, taps, gains, w_in, w_out,
    gmid, dz_out, db, dgain, dshift, *rest,
):
    *dw, dzs, spread, gpre, w_in0, w_out0, arrived = rest
    waits = fetch_layers(((w_out, 0, w_out0), (w_in, 0, w_in0)), arrived)
    spread_pass(dzpad, dzs, taps, 1, spread)
    gmid[...] = (grad[...].astype(F32) + joined(spread, slice(None))).astype(BF16)
    for wait in waits:
        wait.wait()
    hidden_back(gmid, w_out0, slope, gpre, db)
    dz_of(gpre, w_in0, hat[...], inv[:, :1], gains[0:1], dz_out, dgain, dshift)
    weight_grads(place, normed, gmid, act, gpre, dw, per)


def weights_top_kernel(per, place, normed, act, gpre, grad, *dw):
    weight_grads(place, normed, grad, act, gpre, dw, per)


def spread_pass(dzpad, dzs, taps, layer, spread):
    for g in range(dzs.shape[0]):
        dzs[g] = dzpad[:, :, g * LANES : (g + 1) * LANES].astype(F32)
    conv_pass(dzs, 0, 0, taps, layer, spread, *spread.shape[1:3], back=True)


def last_kernel(dzpad, gmid, taps, out, dzs, spread):
    spread_pass(dzpad, dzs, taps, 0, spread)
    out[...] = (gmid[...].astype(F32) + joined(spread, slice(None))).astype(BF16)


def small_rows_of(values, row0, col0, dz, dzs, taps, db, dgain, dshift, sums):
    rows, cols = dzs.shape[1:3]
    channels = sums.shape[1]
    split_to(dzs, slice(None), dz[...].astype(F32), (rows, cols))
    count = db.shape[1] // channels
    for k in range(count):
        sums[k : k + 1, :] = db[:, k * channels : (k + 1) * channels]
    sums[count : count + 1, :] = dgain[...]
    sums[count + 1 : count + 2, :] = dshift[...]
    tap_pass(values, row0, col0, dzs, taps, rows, cols)
    for g in range(taps.shape[0]):
        sums[count + 2 : count + 51, g * LANES : (g + 1) * LANES] = taps[g]


def taps_kernel(
    place, mids, xpad, dz0, dz1, db0, dgain0, dshift0, db1, dgain1, dshift1, send, keep,
    xs, dzs, taps, sums0, sums1,
):
    for g in range(dzs.shape[0]):
        xs[g] = xpad[:, :, g * LANES : (g + 1) * LANES].astype(F32)
    sums0[...] = jnp.zeros(sums0.shape, F32)
    sums1[...] = jnp.zeros(sums1.shape, F32)
    small_rows_of(mids, 0, 0, dz1, dzs, taps, db1, dgain1, dshift1, sums1)
    small_rows_of(xs, HALO, HALO, dz0, dzs, taps, db0, dgain0, dshift0, sums0)
    upper = place[4] == 1
    send[...] = jnp.where(upper, sums0[...], sums1[...]).astype(BF16)
    keep[...] = jnp.where(upper, sums1[...], sums0[...]).astype(BF16)


def small_kernel(scale, place, mine, got, taps_out, gains, shifts, biases):
    upper = place[4] == 1
    own, came = mine[...].astype(F32) * scale, got[...].astype(F32) * scale
    channels = own.shape[1]
    count = biases.shape[1] // channels
    for layer, part in enumerate((jnp.where(upper, came, own), jnp.where(upper, own, came))):
        at = slice(layer, layer + 1)
        for k in range(count):
            biases[at, k * channels : (k + 1) * channels] = part[k : k + 1, :]
        gains[at, :] = part[count : count + 1, :]
        shifts[at, :] = part[count + 1 : count + 2, :]
        for tap in range(49):
            taps_out[tap, at, :] = part[count + 2 + tap : count + 3 + tap, :]


def weights_kernel(scale, keep0, got0, keep1, got1, out_in, out_out):
    for layer, (keep, got) in enumerate(((keep0, got0), (keep1, got1))):
        for i, out in enumerate((out_in, out_out)):
            out[layer] = (keep[i].astype(F32) + got[i].astype(F32)) * scale


def shape(*dims, dtype=F32):
    return jax.ShapeDtypeStruct(dims, dtype)


def run(kernel, outs, scratch, args, specs=None, fetched=0, name=None, room=46):
    vmem = pl.BlockSpec(memory_space=pltpu.VMEM)
    semaphores = [pltpu.SemaphoreType.DMA((fetched,))] if fetched else []
    return pl.pallas_call(
        kernel,
        out_shape=outs,
        in_specs=[
            vmem if s is None else pl.BlockSpec(memory_space=s) for s in (specs or [None] * len(args))
        ],
        out_specs=tuple(vmem for _ in outs),
        scratch_shapes=[pltpu.VMEM(s.shape, s.dtype) for s in scratch] + semaphores,
        compiler_params=pltpu.CompilerParams(vmem_limit_bytes=room * 1024 * 1024),
        name=name,
    )(*args)


def edges(tile, axis, width, odd):
    count = tile.shape[axis]
    low = lax.slice_in_dim(tile, 0, width, axis=axis)
    high = lax.slice_in_dim(tile, count - width, count, axis=axis)
    return jnp.where(odd, low, high), jnp.where(odd, high, low)


def to_twin(edge, axis):
    count = lax.axis_size(axis)
    return lax.ppermute(edge, axis, [(i, i ^ 1) for i in range(count) if i ^ 1 < count])


def to_other(edge, axis):
    n_rows, n_cols = lax.axis_size("rows"), lax.axis_size("cols")
    count = lax.axis_size(axis)
    pairs = []
    for r in range(n_rows):
        for c in range(n_cols):
            at = r if axis == "rows" else c
            partner = at + 1 if at % 2 else at - 1
            if 0 <= partner < count:
                there = (partner, c) if axis == "rows" else (r, partner)
            else:
                there = (r, c ^ 1) if axis == "rows" else (r ^ 1, c)
            pairs.append((r * n_cols + c, there[0] * n_cols + there[1]))
    return lax.ppermute(edge, ("rows", "cols"), pairs)


def rimmed(tile, from_twin, from_other, axis, odd, outer):
    from_other = jnp.where(outer, jnp.zeros_like(from_other), from_other)
    low = jnp.where(odd, from_twin, from_other)
    high = jnp.where(odd, from_other, from_twin)
    return jnp.concatenate([low, tile, high], axis=axis)


def flip_bit(value, *bits):
    flip = sum(1 << bit for bit in bits)
    both = ("rows", "cols")
    total = lax.axis_size("rows") * lax.axis_size("cols")
    return lax.ppermute(value, both, [(i, i ^ flip) for i in range(total)])


def halves(chunks, dim, mine):
    sizes = [1 if d == dim else n for d, n in enumerate(chunks.shape)]

    def one(bit):
        starts = [bit if d == dim else jnp.uint32(0) for d in range(chunks.ndim)]
        return lax.squeeze(lax.dynamic_slice(chunks, starts, sizes), (dim,))

    return one(mine[1]), one(mine[0])


def summed(own, *got):
    parts = [part.astype(F32) for part in (own,) + got]
    while len(parts) > 1:
        parts = [a + b for a, b in zip(parts[::2], parts[1::2])]
    return parts[0].astype(BF16)


def cut(chunks, order, bit, mine):
    spot = order.index(bit)
    per = chunks.shape[-2:]
    pair = chunks.reshape((-1, 2 ** spot, 2, 2 ** (len(order) - spot - 1)) + per)
    send, keep = halves(pair, 2, mine[bit])
    return send, keep, [b for b in order if b != bit]


def step(chunks, order, bit, mine):
    send, keep, left = cut(chunks, order, bit, mine)
    return keep, flip_bit(send, bit), left


def shards(activations, grad_out, kernels, norm_gains, norm_shifts, w_in, b_in, w_out):
    rows, cols, channels = activations.shape
    layers, _, hidden = w_in.shape
    groups = channels // LANES
    n_rows, n_cols = lax.axis_size("rows"), lax.axis_size("cols")
    total = n_rows * n_cols
    bits = total.bit_length() - 1
    col_bits = n_cols.bit_length() - 1
    me = (lax.axis_index("rows") * n_cols + lax.axis_index("cols")).astype(jnp.uint32)
    mine = [(((me >> k) & 1), 1 - ((me >> k) & 1)) for k in range(bits)]
    grad_scale = 1.0 / math.sqrt(rows * cols * total)
    pixels = rows * cols

    taps = kernels.transpose(1, 2, 0, 3).reshape(49, layers, channels)
    place = jnp.stack(
        [
            lax.axis_index("rows") * rows,
            lax.axis_index("cols") * cols,
            jnp.int32(rows * n_rows),
            jnp.int32(cols * n_cols),
            lax.axis_index("cols") & 1,
        ]
    ).astype(jnp.int32)
    grad_flat = grad_out.reshape(pixels, channels)

    at_row, at_col = lax.axis_index("rows"), lax.axis_index("cols")
    odd_col, odd_row = (at_col & 1) == 1, (at_row & 1) == 1
    outer_col = (at_col == 0) | (at_col == n_cols - 1)
    outer_row = (at_row == 0) | (at_row == n_rows - 1)
    activations, place, mine, odd_col, odd_row, outer_col, outer_row = lax.optimization_barrier(
        (activations, place, mine, odd_col, odd_row, outer_col, outer_row)
    )

    def rim_cols(tile, width):
        twin, other = edges(tile, 1, width, odd_col)
        return rimmed(tile, to_twin(twin, "cols"), to_other(other, "cols"), 1, odd_col, outer_col)

    def rim_rows(tile, width):
        twin, other = edges(tile, 0, width, odd_row)
        return rimmed(tile, to_twin(twin, "rows"), to_other(other, "rows"), 0, odd_row, outer_row)

    def filled(wide):
        return jnp.pad(wide, ((0, 0), (0, cols + 16 - wide.shape[1]), (0, 0)))

    mid_rows, mid_cols = rows + 2 * HALO, cols + 8
    strip = max(d for d in range(1, mid_rows + 1) if mid_rows % d == 0 and d * mid_cols <= 264)
    weights = [shape(1, channels, hidden, dtype=BF16)] * 2
    tile_z = shape(groups, rows, cols, LANES)
    tile_b = shape(pixels, channels, dtype=BF16)
    tile_h = shape(pixels, hidden, dtype=BF16)
    per = hidden // total
    split = 2 if per % 16 == 0 and col_bits == 2 else 1
    grads_b = (shape(2, hidden // split, channels, dtype=BF16),) * split
    small_outs = (shape(1, hidden), shape(1, channels), shape(1, channels))
    small_rows = 64

    xpad = filled(rim_cols(rim_rows(activations, WIDE), WIDE))
    mids, z0 = run(
        forward_kernel,
        (shape(groups, mid_rows, mid_cols, LANES), tile_z),
        [
            shape(groups, *xpad.shape[:2], LANES),
            shape(groups, mid_rows, mid_cols, LANES),
            shape(strip * mid_cols, hidden, dtype=BF16),
        ]
        + weights,
        (place, xpad, taps, norm_gains, norm_shifts, w_in, w_out, b_in),
        [pltpu.SMEM] + [None] * 4 + [pl.ANY] * 2 + [None],
        fetched=2,
        name="forward",
        room=50,
    )
    dz1, normed1, act1, gpre1, *small1 = run(
        top_kernel,
        (tile_b, tile_b, tile_h, tile_h) + small_outs,
        [tile_z] + weights,
        (mids, grad_flat, taps, norm_gains, norm_shifts, w_in, w_out, b_in),
        [None] * 5 + [pl.ANY] * 2 + [None],
        fetched=2,
        name="top",
        room=50,
    )

    sides = (col_bits - 1, col_bits)

    def fenced(*values):
        leaves, tree = jax.tree.flatten(values)
        arrays = [i for i, leaf in enumerate(leaves) if not isinstance(leaf, int)]
        for i, value in zip(arrays, lax.optimization_barrier(tuple(leaves[i] for i in arrays))):
            leaves[i] = value
        return jax.tree.unflatten(tree, leaves)

    def settled(flight):
        return summed(flight[0], flight[1]), flight[2]

    def start(dw):
        order = list(range(bits - 1, -1, -1))
        if split == 2:
            send, keep = (d.reshape(2, total // 2, per, channels) for d in dw)
            return keep, flip_bit(send, 0), order[:-1]
        chunks = dw[0].reshape(2, total, per, channels)
        for bit in range(col_bits - 2):
            chunks, order = settled(step(chunks, order, bit, mine))
        return step(chunks, order, col_bits - 2, mine)

    def fork(flight):
        chunks, order = settled(flight)
        return [step(chunks[i], order, sides[i], mine) for i in range(2)]

    def onward(parts, bit, *riders):
        kept, sent, lefts = [], [], []
        for chunks, order in parts:
            send, keep, left = cut(chunks, order, bit, mine)
            kept.append(keep)
            sent.append(send.reshape(-1, channels))
            lefts.append(left)
        got = flip_bit(jnp.concatenate(sent + list(riders), axis=0), bit)
        flights, first = [], 0
        for keep, send, left in zip(kept, sent, lefts):
            came = got[first : first + send.shape[0]].reshape(keep.shape)
            flights.append((keep, came, left))
            first += send.shape[0]
        return flights, [got[first:]] if riders else []

    def merged(flights):
        done = [settled(f) for f in flights]
        return jnp.stack([d[0].reshape(-1, per, channels) for d in done]), done[0][1]

    tile1 = dz1.reshape(rows, cols, channels)
    twin, other = edges(tile1, 0, HALO, odd_row)
    twin, other = to_twin(twin, "rows"), to_other(other, "rows")
    dw1 = run(
        functools.partial(weights_top_kernel, per),
        grads_b,
        [],
        (place, normed1, act1, gpre1, grad_flat),
        [pltpu.SMEM] + [None] * 4,
        name="weights_top",
    )
    run1 = start(dw1)
    tile1, twin, other = fenced(tile1, twin, other)
    wide1 = rimmed(tile1, twin, other, 0, odd_row, outer_row)
    twin, other = edges(wide1, 1, HALO, odd_col)
    twin, other = to_twin(twin, "cols"), to_other(other, "cols")
    run1, z0 = fenced(run1, z0)
    pair1 = fork(run1)
    tile_f = shape(pixels, channels)
    again = run(
        again_kernel,
        (tile_f, shape(pixels, LANES), tile_b, tile_h, shape(pixels, hidden)),
        weights[:1],
        (z0, norm_gains, norm_shifts, w_in, b_in),
        [None] * 3 + [pl.ANY, None],
        fetched=1,
        name="again",
    )
    wide1, twin, other, again = fenced(wide1, twin, other, again)
    dzpad1 = filled(rimmed(wide1, twin, other, 1, odd_col, outer_col))
    spread_scratch = [shape(groups, *dzpad1.shape[:2], LANES), tile_z]
    grad_mid, dz0, *rest = run(
        functools.partial(low_kernel, per),
        (tile_b, tile_b) + small_outs + grads_b,
        spread_scratch + [tile_h] + weights,
        (place, dzpad1, grad_flat, *again, taps, norm_gains, w_in, w_out),
        [pltpu.SMEM] + [None] * 9 + [pl.ANY] * 2,
        fetched=2,
        name="low",
    )
    small0, dw0 = rest[:3], rest[3:]
    dz0, dw0, pair1, small0 = fenced(dz0, dw0, pair1, small0)
    run0 = start(dw0)
    low_bit = col_bits + 1
    pair1, _ = onward([settled(f) for f in pair1], low_bit)
    run0, dz0, small0 = fenced(run0, dz0, small0)
    pair0 = fork(run0)
    tile0 = dz0.reshape(rows, cols, channels)
    twin, other = edges(tile0, 0, HALO, odd_row)
    twin, other = to_twin(twin, "rows"), to_other(other, "rows")
    small_b = shape(small_rows, channels, dtype=BF16)
    small_f = shape(small_rows, channels)
    send, small = run(
        taps_kernel,
        (small_b, small_b),
        [
            shape(groups, *xpad.shape[:2], LANES), tile_z, shape(groups, 49, LANES),
            small_f, small_f,
        ],
        (place, mids, xpad, dz0, dz1, *small0, *small1),
        [pltpu.SMEM] + [None] * 10,
        name="taps",
    )
    small_got = flip_bit(send, 0)
    pair0, pair1, tile0, twin, other, small, small_got = fenced(
        pair0, pair1, tile0, twin, other, small, small_got
    )
    small = summed(small, small_got)
    for bit in range(1, col_bits - 1):
        small = summed(small, flip_bit(small, bit))
    both, small_by = [], []
    for i in range(2):
        flights, (came,) = onward([settled(pair0[i]), settled(pair1[i])], sides[1 - i], small)
        both.append(flights)
        small_by.append(came)
    small_by.append(flip_bit(small, *sides))
    wide0 = rimmed(tile0, twin, other, 0, odd_row, outer_row)
    twin, other = edges(wide0, 1, HALO, odd_col)
    twin, other = to_twin(twin, "cols"), to_other(other, "cols")
    both, wide0, twin, other, small, small_by = fenced(both, wide0, twin, other, small, small_by)
    small = summed(small, small_by[0], small_by[1], small_by[2])
    (run0,), (small_got,) = onward([merged([both[0][0], both[1][0]])], low_bit, small)
    part1, order1 = merged([both[0][1], both[1][1]])
    flight1 = (part1, jnp.zeros_like(part1), order1)
    if order1:
        (flight1,), _ = onward([(part1, order1)], order1[-1])
    (grad_in,) = run(
        last_kernel,
        (tile_b,),
        spread_scratch,
        (filled(rimmed(wide0, twin, other, 1, odd_col, outer_col)), grad_mid, taps),
        name="last",
    )
    while run0[2]:
        run0, flight1, small, small_got, grad_in = fenced(run0, flight1, small, small_got, grad_in)
        small = summed(small, small_got)
        (run0,), (small_got,) = onward([settled(run0)], run0[2][-1], small)
        if flight1[2]:
            (flight1,), _ = onward([settled(flight1)], flight1[2][-1])
    run0, flight1, small, small_got = fenced(run0, flight1, small, small_got)
    small = summed(small, small_got)
    small_got = flip_bit(small, 0)
    share = shape(layers, per, channels)
    grad_w_in, grad_w_out = run(
        functools.partial(weights_kernel, grad_scale),
        (share, share),
        [],
        [part.reshape(2, per, channels) for part in run0[:2] + flight1[:2]],
        name="weights",
    )
    grad_taps, grad_gains, grad_shifts, grad_b_in = run(
        functools.partial(small_kernel, grad_scale),
        (
            shape(49, layers, channels),
            shape(layers, channels),
            shape(layers, channels),
            shape(layers, hidden),
        ),
        [],
        (place, small, small_got),
        [pltpu.SMEM, None, None],
        name="small",
    )
    return (
        grad_in.reshape(rows, cols, channels),
        grad_taps.reshape(7, 7, layers, channels).transpose(2, 0, 1, 3),
        grad_gains,
        grad_shifts,
        grad_b_in,
        jnp.swapaxes(grad_w_in, 1, 2),
        jnp.swapaxes(grad_w_out, 1, 2),
    )


def solution(mesh):
    tile = P("rows", "cols", None)
    sliced = P(None, None, ("rows", "cols"))
    return jax.shard_map(
        shards,
        mesh=mesh,
        in_specs=(tile, tile, P(), P(), P(), P(), P(), P()),
        out_specs=(tile, P(), P(), P(), P(), sliced, sliced),
        check_vma=False,
    )
```

```python
import functools
import math

import jax
import jax.numpy as jnp
from jax import lax
from jax.experimental import pallas as pl
from jax.experimental.pallas import tpu as pltpu
from jax.sharding import PartitionSpec as P

EPSILON = 1e-06
INV_ROOT_TAU = 0.3989422804014327
HALF_LOG2E = 0.7213475204444817
ERFC_SLOPE = 0.4 * 0.7071067811865476
ERFC_TERMS = (
    0.23195388609975262,
    0.16163296978938874,
    0.4687286953098433,
    -0.3714470456115026,
    0.7094654203066808,
    -0.2003339536843631,
)
LANES = 128
HALO = 3
WIDE = 2 * HALO
F32 = jnp.float32
BF16 = jnp.bfloat16


def normal_parts(x):
    size = jnp.abs(x)
    bell = jnp.exp2(x * x * (-HALF_LOG2E))
    t = pl.reciprocal(1.0 + ERFC_SLOPE * size, approx=True)
    series = 0.5 * ERFC_TERMS[-1]
    for term in ERFC_TERMS[-2::-1]:
        series = series * t + 0.5 * term
    return size, series * t * bell, bell


def gelu_only(x):
    size, tail, _ = normal_parts(x)
    return jnp.maximum(x, 0.0) - size * tail


def gelu_parts(x):
    size, tail, bell = normal_parts(x)
    cdf = jnp.where(x >= 0, 1.0 - tail, tail)
    return jnp.maximum(x, 0.0) - size * tail, cdf + x * bell * INV_ROOT_TAU


def strip_rows(rows, cols):
    most = max(1, 288 // cols)
    return max(d for d in range(1, rows + 1) if rows % d == 0 and d <= most)


def conv_pass(source, row0, col0, taps, layer, target, rows, cols, back=False):
    strip = strip_rows(rows, cols)
    groups = source.shape[0]

    def one_strip(step, carry):
        g = step // (rows // strip)
        top = (step % (rows // strip)) * strip
        lanes = pl.ds(pl.multiple_of(g * LANES, LANES), LANES)
        sums = [jnp.zeros((cols, LANES), F32) for _ in range(strip)]
        for b in range(7):
            spots = [48 - 7 * a - b if back else 7 * a + b for a in range(7)]
            weights = [taps[spot, pl.ds(layer, 1), lanes] for spot in spots]
            for r in range(strip + 6):
                line = source[g, row0 + top + r, pl.ds(col0 + b, cols), :]
                for a in range(7):
                    if 0 <= r - a < strip:
                        sums[r - a] = sums[r - a] + weights[a] * line
        for i in range(strip):
            target[g, top + i] = sums[i]
        return carry

    lax.fori_loop(0, groups * (rows // strip), one_strip, 0)


def tap_pass(source, row0, col0, grad, target, rows, cols):
    def one_group(g, carry):
        lines = [grad[g, i] for i in range(rows)]
        for b in range(7):
            sums = [None] * 7
            for r in range(rows + 6):
                line = source[g, row0 + r, pl.ds(col0 + b, cols), :]
                for a in range(7):
                    if 0 <= r - a < rows:
                        part = lines[r - a] * line
                        sums[a] = part if sums[a] is None else sums[a] + part
            for a in range(7):
                total = jnp.sum(sums[a], axis=0, keepdims=True)
                target[g, pl.ds(7 * a + b, 1), :] = total
        return carry

    lax.fori_loop(0, source.shape[0], one_group, 0)


def joined(ref, rows, cols=slice(None)):
    parts = [ref[g, rows, cols, :] for g in range(ref.shape[0])]
    return jnp.concatenate([p.reshape(-1, LANES) for p in parts], axis=1)


def split_to(ref, rows, value, shape):
    for g in range(ref.shape[0]):
        ref[g, rows] = value[:, g * LANES : (g + 1) * LANES].reshape(*shape, LANES)


def norm_parts(z):
    center = z - jnp.mean(z, axis=-1, keepdims=True)
    inv = lax.rsqrt(jnp.mean(center * center, axis=-1, keepdims=True) + EPSILON)
    return center * inv, inv


def norm_back(dn, hat, inv, gain):
    scaled = dn * gain
    return inv * (
        scaled
        - jnp.mean(scaled, axis=-1, keepdims=True)
        - hat * jnp.mean(scaled * hat, axis=-1, keepdims=True)
    )


def dot_nn(a, b):
    return jnp.dot(a, b, preferred_element_type=F32)


def dot_nt(a, b):
    return lax.dot_general(a, b, (((1,), (1,)), ((), ())), preferred_element_type=F32)


def dot_tn(a, b):
    return lax.dot_general(a, b, (((0,), (0,)), ((), ())), preferred_element_type=F32)


def pixel_blocks(pixels):
    best = max(d for d in range(16, 257, 16) if pixels % d == 0)
    return [slice(start, start + best) for start in range(0, pixels, best)]


def hidden_chunks(hidden):
    size = 256 if hidden % 256 == 0 else hidden
    return [slice(start, start + size) for start in range(0, hidden, size)]


def hidden_forward(normed, w_in, bias, act, slope):
    for cut in hidden_chunks(w_in.shape[2]):
        for block in pixel_blocks(normed.shape[0]):
            value, factor = gelu_parts(dot_nn(normed[block, :], w_in[0, :, cut]) + bias[:, cut])
            act[block, cut] = value.astype(BF16)
            slope[block, cut] = factor


def hidden_back(grad, w_out, slope, gpre, db):
    for cut in hidden_chunks(w_out.shape[2]):
        bias_sum = None
        for block in pixel_blocks(grad.shape[0]):
            gradient = dot_nn(grad[block, :], w_out[0, :, cut]) * slope[block, cut]
            gpre[block, cut] = gradient.astype(BF16)
            part = jnp.sum(gradient, axis=0, keepdims=True)
            bias_sum = part if bias_sum is None else bias_sum + part
        db[:, cut] = bias_sum


def dz_of(gpre, w_in, hat, inv, gain, dz_out, dgain, dshift):
    dn = dot_nt(gpre[...], w_in[0])
    dgain[...] = jnp.sum(dn * hat, axis=0, keepdims=True)
    dshift[...] = jnp.sum(dn, axis=0, keepdims=True)
    dz_out[...] = norm_back(dn, hat, inv, gain).astype(BF16)


def mlp_grads(normed, grad, w_in, b_in, w_out, act, gpre, db):
    pixels = grad.shape[0]
    for cut in hidden_chunks(w_in.shape[2]):
        bias = b_in[:, cut]
        bias_sum = None
        for block in pixel_blocks(pixels):
            pre = dot_nn(normed[block, :], w_in[0, :, cut]) + bias
            value, slope = gelu_parts(pre)
            act[block, cut] = value.astype(BF16)
            gradient = dot_nn(grad[block, :], w_out[0, :, cut]) * slope
            gpre[block, cut] = gradient.astype(BF16)
            part = jnp.sum(gradient, axis=0, keepdims=True)
            bias_sum = part if bias_sum is None else bias_sum + part
        db[:, cut] = bias_sum


def weight_grads(place, normed, grad, act, gpre, dw, per):
    hidden, channels = act.shape[1], grad.shape[1]
    size = min(n for n in range(128, hidden + 1, 128) if hidden % n == 0 and n % (2 * per) == 0 and n >= 256)
    for first in range(0, hidden, size):
        cut = slice(first, first + size)
        for i, (left, right) in enumerate(((gpre, normed), (act, grad))):
            value = dot_tn(left[:, cut], right[...]).astype(BF16)
            if len(dw) == 1:
                dw[0][i, cut, :] = value
                continue
            value = value.reshape(size // (2 * per), 2, per, channels)
            upper = place[4] == 1
            half = slice(first // 2, (first + size) // 2)
            dw[0][i, half, :] = jnp.where(upper, value[:, 0], value[:, 1]).reshape(-1, channels)
            dw[1][i, half, :] = jnp.where(upper, value[:, 1], value[:, 0]).reshape(-1, channels)


def fetch_layers(triples, arrived):
    copies = [
        pltpu.make_async_copy(source.at[pl.ds(layer, 1)], target, arrived.at[i])
        for i, (source, layer, target) in enumerate(triples)
    ]
    for copy in copies:
        copy.start()
    return copies


def edges_kernel(place, tile, copy, twin, other):
    width = twin.shape[0]
    odd = place[5] == 1
    copy[...] = tile[...]
    low, high = tile[:width].astype(F32), tile[tile.shape[0] - width :].astype(F32)
    twin[...] = jnp.where(odd, low, high).astype(BF16)
    other[...] = jnp.where(odd, high, low).astype(BF16)


def forward_kernel(
    place, xpad, taps, gains, shifts, w_in, w_out, b_in, mids, z_out,
    xs, zs, act, w_in0, w_out0, arrived,
):
    waits = fetch_layers(((w_in, 0, w_in0), (w_out, 0, w_out0)), arrived)
    groups, mid_rows, mid_cols = zs.shape[:3]
    rows, cols = z_out.shape[1:3]
    for g in range(groups):
        xs[g] = xpad[:, :, g * LANES : (g + 1) * LANES].astype(F32)
    conv_pass(xs, 0, 0, taps, 0, zs, mid_rows, mid_cols)
    z_out[...] = zs[:, HALO : HALO + rows, HALO : HALO + cols, :]
    strip = act.shape[0] // mid_cols
    for wait in waits:
        wait.wait()

    def one_strip(step, carry):
        top = step * strip
        hat, _ = norm_parts(joined(zs, pl.ds(top, strip)))
        normed = (hat * gains[0:1] + shifts[0:1]).astype(BF16)
        for cut in hidden_chunks(w_in0.shape[2]):
            pre = dot_nn(normed, w_in0[0, :, cut]) + b_in[0:1, cut]
            act[:, cut] = gelu_only(pre).astype(BF16)
        mixed = dot_nt(act[...], w_out0[0])
        row = lax.broadcasted_iota(jnp.int32, (strip, mid_cols, 1), 0) + (top - HALO) + place[0]
        col = lax.broadcasted_iota(jnp.int32, (strip, mid_cols, 1), 1) - HALO + place[1]
        real = (row >= 0) & (row < place[2]) & (col >= 0) & (col < place[3])
        real = jnp.where(real, 1.0, 0.0).reshape(strip * mid_cols, 1)
        base = joined(xs, pl.ds(top + HALO, strip), slice(HALO, HALO + mid_cols))
        mid = (base + mixed).astype(BF16).astype(F32) * real
        split_to(mids, pl.ds(top, strip), mid, (strip, mid_cols))
        return carry

    lax.fori_loop(0, mid_rows // strip, one_strip, 0, unroll=True)


def top_kernel(
    mids, grad, taps, gains, shifts, w_in, w_out, b_in,
    dz_out, normed, act, gpre, db, dgain, dshift, z, w_in1, w_out1, arrived,
):
    waits = fetch_layers(((w_in, 1, w_in1), (w_out, 1, w_out1)), arrived)
    conv_pass(mids, 0, 0, taps, 1, z, *z.shape[1:3])
    hat, inv = norm_parts(joined(z, slice(None)))
    normed[...] = (hat * gains[1:2] + shifts[1:2]).astype(BF16)
    for wait in waits:
        wait.wait()
    mlp_grads(normed, grad, w_in1, b_in.at[pl.ds(1, 1)], w_out1, act, gpre, db)
    dz_of(gpre, w_in1, hat, inv, gains[1:2], dz_out, dgain, dshift)


def again_kernel(z0, gains, shifts, w_in, b_in, hat_out, inv_out, normed, act, slope, w_in0, arrived):
    (wait,) = fetch_layers(((w_in, 0, w_in0),), arrived)
    hat, inv = norm_parts(joined(z0, slice(None)))
    hat_out[...] = hat
    inv_out[...] = jnp.broadcast_to(inv, inv_out.shape)
    normed[...] = (hat * gains[0:1] + shifts[0:1]).astype(BF16)
    wait.wait()
    hidden_forward(normed, w_in0, b_in.at[pl.ds(0, 1)], act, slope)


def low_kernel(
    per, place, dzpad, grad, hat, inv, normed, act, slope, taps, gains, w_in, w_out,
    gmid, dz_out, db, dgain, dshift, *rest,
):
    *dw, dzs, spread, gpre, w_in0, w_out0, arrived = rest
    waits = fetch_layers(((w_out, 0, w_out0), (w_in, 0, w_in0)), arrived)
    spread_pass(dzpad, dzs, taps, 1, spread)
    gmid[...] = (grad[...].astype(F32) + joined(spread, slice(None))).astype(BF16)
    for wait in waits:
        wait.wait()
    hidden_back(gmid, w_out0, slope, gpre, db)
    dz_of(gpre, w_in0, hat[...], inv[:, :1], gains[0:1], dz_out, dgain, dshift)
    weight_grads(place, normed, gmid, act, gpre, dw, per)


def weights_top_kernel(per, place, normed, act, gpre, grad, *dw):
    weight_grads(place, normed, grad, act, gpre, dw, per)


def spread_pass(dzpad, dzs, taps, layer, spread):
    for g in range(dzs.shape[0]):
        dzs[g] = dzpad[:, :, g * LANES : (g + 1) * LANES].astype(F32)
    conv_pass(dzs, 0, 0, taps, layer, spread, *spread.shape[1:3], back=True)


def last_kernel(dzpad, gmid, taps, out, dzs, spread):
    spread_pass(dzpad, dzs, taps, 0, spread)
    out[...] = (gmid[...].astype(F32) + joined(spread, slice(None))).astype(BF16)


def small_rows_of(values, row0, col0, dz, dzs, taps, db, dgain, dshift, sums):
    rows, cols = dzs.shape[1:3]
    channels = sums.shape[1]
    split_to(dzs, slice(None), dz[...].astype(F32), (rows, cols))
    count = db.shape[1] // channels
    for k in range(count):
        sums[k : k + 1, :] = db[:, k * channels : (k + 1) * channels]
    sums[count : count + 1, :] = dgain[...]
    sums[count + 1 : count + 2, :] = dshift[...]
    tap_pass(values, row0, col0, dzs, taps, rows, cols)
    for g in range(taps.shape[0]):
        sums[count + 2 : count + 51, g * LANES : (g + 1) * LANES] = taps[g]


def top_taps_kernel(mids, dz, db, dgain, dshift, sums, dzs, taps):
    sums[...] = jnp.zeros(sums.shape, F32)
    small_rows_of(mids, 0, 0, dz, dzs, taps, db, dgain, dshift, sums)


def taps_kernel(place, xpad, dz, db, dgain, dshift, sums1, send, keep, xs, dzs, taps, sums0):
    for g in range(dzs.shape[0]):
        xs[g] = xpad[:, :, g * LANES : (g + 1) * LANES].astype(F32)
    sums0[...] = jnp.zeros(sums0.shape, F32)
    small_rows_of(xs, HALO, HALO, dz, dzs, taps, db, dgain, dshift, sums0)
    upper = place[4] == 1
    send[...] = jnp.where(upper, sums0[...], sums1[...]).astype(BF16)
    keep[...] = jnp.where(upper, sums1[...], sums0[...]).astype(BF16)


def small_kernel(scale, place, mine, got, taps_out, gains, shifts, biases):
    upper = place[4] == 1
    own, came = mine[...].astype(F32) * scale, got[...].astype(F32) * scale
    channels = own.shape[1]
    count = biases.shape[1] // channels
    for layer, part in enumerate((jnp.where(upper, came, own), jnp.where(upper, own, came))):
        at = slice(layer, layer + 1)
        for k in range(count):
            biases[at, k * channels : (k + 1) * channels] = part[k : k + 1, :]
        gains[at, :] = part[count : count + 1, :]
        shifts[at, :] = part[count + 1 : count + 2, :]
        for tap in range(49):
            taps_out[tap, at, :] = part[count + 2 + tap : count + 3 + tap, :]


def weights_kernel(scale, keep0, got0, keep1, got1, out_in, out_out):
    for layer, (keep, got) in enumerate(((keep0, got0), (keep1, got1))):
        for i, out in enumerate((out_in, out_out)):
            out[layer] = (keep[i].astype(F32) + got[i].astype(F32)) * scale


def shape(*dims, dtype=F32):
    return jax.ShapeDtypeStruct(dims, dtype)


def run(kernel, outs, scratch, args, specs=None, fetched=0, name=None, room=46):
    vmem = pl.BlockSpec(memory_space=pltpu.VMEM)
    semaphores = [pltpu.SemaphoreType.DMA((fetched,))] if fetched else []
    return pl.pallas_call(
        kernel,
        out_shape=outs,
        in_specs=[
            vmem if s is None else pl.BlockSpec(memory_space=s) for s in (specs or [None] * len(args))
        ],
        out_specs=tuple(vmem for _ in outs),
        scratch_shapes=[pltpu.VMEM(s.shape, s.dtype) for s in scratch] + semaphores,
        compiler_params=pltpu.CompilerParams(vmem_limit_bytes=room * 1024 * 1024),
        name=name,
    )(*args)


def edges(tile, axis, width, odd):
    count = tile.shape[axis]
    low = lax.slice_in_dim(tile, 0, width, axis=axis)
    high = lax.slice_in_dim(tile, count - width, count, axis=axis)
    return jnp.where(odd, low, high), jnp.where(odd, high, low)


def to_twin(edge, axis):
    count = lax.axis_size(axis)
    return lax.ppermute(edge, axis, [(i, i ^ 1) for i in range(count) if i ^ 1 < count])


def to_other(edge, axis):
    n_rows, n_cols = lax.axis_size("rows"), lax.axis_size("cols")
    count = lax.axis_size(axis)
    pairs = []
    for r in range(n_rows):
        for c in range(n_cols):
            at = r if axis == "rows" else c
            partner = at + 1 if at % 2 else at - 1
            if 0 <= partner < count:
                there = (partner, c) if axis == "rows" else (r, partner)
            else:
                there = (r, c ^ 1) if axis == "rows" else (r ^ 1, c)
            pairs.append((r * n_cols + c, there[0] * n_cols + there[1]))
    return lax.ppermute(edge, ("rows", "cols"), pairs)


def rimmed(tile, from_twin, from_other, axis, odd, outer):
    from_other = jnp.where(outer, jnp.zeros_like(from_other), from_other)
    low = jnp.where(odd, from_twin, from_other)
    high = jnp.where(odd, from_other, from_twin)
    return jnp.concatenate([low, tile, high], axis=axis)


def flip_bit(value, *bits):
    flip = sum(1 << bit for bit in bits)
    both = ("rows", "cols")
    total = lax.axis_size("rows") * lax.axis_size("cols")
    return lax.ppermute(value, both, [(i, i ^ flip) for i in range(total)])


def halves(chunks, dim, mine):
    sizes = [1 if d == dim else n for d, n in enumerate(chunks.shape)]

    def one(bit):
        starts = [bit if d == dim else jnp.uint32(0) for d in range(chunks.ndim)]
        return lax.squeeze(lax.dynamic_slice(chunks, starts, sizes), (dim,))

    return one(mine[1]), one(mine[0])


def summed(own, *got):
    parts = [part.astype(F32) for part in (own,) + got]
    while len(parts) > 1:
        parts = [a + b for a, b in zip(parts[::2], parts[1::2])]
    return parts[0].astype(BF16)


def cut(chunks, order, bit, mine):
    spot = order.index(bit)
    per = chunks.shape[-2:]
    pair = chunks.reshape((-1, 2 ** spot, 2, 2 ** (len(order) - spot - 1)) + per)
    send, keep = halves(pair, 2, mine[bit])
    return send, keep, [b for b in order if b != bit]


def step(chunks, order, bit, mine):
    send, keep, left = cut(chunks, order, bit, mine)
    return keep, flip_bit(send, bit), left


def shards(activations, grad_out, kernels, norm_gains, norm_shifts, w_in, b_in, w_out):
    rows, cols, channels = activations.shape
    layers, _, hidden = w_in.shape
    groups = channels // LANES
    n_rows, n_cols = lax.axis_size("rows"), lax.axis_size("cols")
    total = n_rows * n_cols
    bits = total.bit_length() - 1
    col_bits = n_cols.bit_length() - 1
    me = (lax.axis_index("rows") * n_cols + lax.axis_index("cols")).astype(jnp.uint32)
    mine = [(((me >> k) & 1), 1 - ((me >> k) & 1)) for k in range(bits)]
    grad_scale = 1.0 / math.sqrt(rows * cols * total)
    pixels = rows * cols

    taps = kernels.transpose(1, 2, 0, 3).reshape(49, layers, channels)
    place = jnp.stack(
        [
            lax.axis_index("rows") * rows,
            lax.axis_index("cols") * cols,
            jnp.int32(rows * n_rows),
            jnp.int32(cols * n_cols),
            lax.axis_index("cols") & 1,
            lax.axis_index("rows") & 1,
        ]
    ).astype(jnp.int32)
    grad_flat = grad_out.reshape(pixels, channels)

    at_row, at_col = lax.axis_index("rows"), lax.axis_index("cols")
    odd_col, odd_row = (at_col & 1) == 1, (at_row & 1) == 1
    outer_col = (at_col == 0) | (at_col == n_cols - 1)
    outer_row = (at_row == 0) | (at_row == n_rows - 1)
    activations, place, mine, odd_col, odd_row, outer_col, outer_row = lax.optimization_barrier(
        (activations, place, mine, odd_col, odd_row, outer_col, outer_row)
    )

    def rim_cols(tile, width):
        twin, other = edges(tile, 1, width, odd_col)
        return rimmed(tile, to_twin(twin, "cols"), to_other(other, "cols"), 1, odd_col, outer_col)

    def filled(wide):
        return jnp.pad(wide, ((0, 0), (0, cols + 16 - wide.shape[1]), (0, 0)))

    mid_rows, mid_cols = rows + 2 * HALO, cols + 8
    strip = max(d for d in range(1, mid_rows + 1) if mid_rows % d == 0 and d * mid_cols <= 264)
    weights = [shape(1, channels, hidden, dtype=BF16)] * 2
    tile_z = shape(groups, rows, cols, LANES)
    tile_b = shape(pixels, channels, dtype=BF16)
    tile_h = shape(pixels, hidden, dtype=BF16)
    per = hidden // total
    split = 2 if per % 16 == 0 and col_bits == 2 else 1
    grads_b = (shape(2, hidden // split, channels, dtype=BF16),) * split
    small_outs = (shape(1, hidden), shape(1, channels), shape(1, channels))
    small_rows = -(-(hidden // channels + 51) // 8) * 8

    edge = shape(WIDE, cols, channels, dtype=BF16)
    tile, twin, other = run(
        edges_kernel,
        (shape(rows, cols, channels, dtype=BF16), edge, edge),
        [],
        (place, activations),
        [pltpu.SMEM, None],
        name="edges",
    )
    wide = rimmed(tile, to_twin(twin, "rows"), to_other(other, "rows"), 0, odd_row, outer_row)
    xpad = filled(rim_cols(wide, WIDE))
    mids, z0 = run(
        forward_kernel,
        (shape(groups, mid_rows, mid_cols, LANES), tile_z),
        [
            shape(groups, *xpad.shape[:2], LANES),
            shape(groups, mid_rows, mid_cols, LANES),
            shape(strip * mid_cols, hidden, dtype=BF16),
        ]
        + weights,
        (place, xpad, taps, norm_gains, norm_shifts, w_in, w_out, b_in),
        [pltpu.SMEM] + [None] * 4 + [pl.ANY] * 2 + [None],
        fetched=2,
        name="forward",
        room=50,
    )
    dz1, normed1, act1, gpre1, *small1 = run(
        top_kernel,
        (tile_b, tile_b, tile_h, tile_h) + small_outs,
        [tile_z] + weights,
        (mids, grad_flat, taps, norm_gains, norm_shifts, w_in, w_out, b_in),
        [None] * 5 + [pl.ANY] * 2 + [None],
        fetched=2,
        name="top",
        room=50,
    )

    sides = (col_bits - 1, col_bits)

    def fenced(*values):
        leaves, tree = jax.tree.flatten(values)
        arrays = [i for i, leaf in enumerate(leaves) if not isinstance(leaf, int)]
        for i, value in zip(arrays, lax.optimization_barrier(tuple(leaves[i] for i in arrays))):
            leaves[i] = value
        return jax.tree.unflatten(tree, leaves)

    def settled(flight):
        return summed(flight[0], flight[1]), flight[2]

    def start(dw):
        order = list(range(bits - 1, -1, -1))
        if split == 2:
            send, keep = (d.reshape(2, total // 2, per, channels) for d in dw)
            return keep, flip_bit(send, 0), order[:-1]
        chunks = dw[0].reshape(2, total, per, channels)
        for bit in range(col_bits - 2):
            chunks, order = settled(step(chunks, order, bit, mine))
        return step(chunks, order, col_bits - 2, mine)

    def fork(flight):
        chunks, order = settled(flight)
        return [step(chunks[i], order, sides[i], mine) for i in range(2)]

    def onward(parts, bit, *riders):
        kept, sent, lefts = [], [], []
        for chunks, order in parts:
            send, keep, left = cut(chunks, order, bit, mine)
            kept.append(keep)
            sent.append(send.reshape(-1, channels))
            lefts.append(left)
        got = flip_bit(jnp.concatenate(sent + list(riders), axis=0), bit)
        flights, first = [], 0
        for keep, send, left in zip(kept, sent, lefts):
            came = got[first : first + send.shape[0]].reshape(keep.shape)
            flights.append((keep, came, left))
            first += send.shape[0]
        return flights, [got[first:]] if riders else []

    def merged(flights):
        done = [settled(f) for f in flights]
        return jnp.stack([d[0].reshape(-1, per, channels) for d in done]), done[0][1]

    tile1 = dz1.reshape(rows, cols, channels)
    twin, other = edges(tile1, 0, HALO, odd_row)
    twin, other = to_twin(twin, "rows"), to_other(other, "rows")
    dw1 = run(
        functools.partial(weights_top_kernel, per),
        grads_b,
        [],
        (place, normed1, act1, gpre1, grad_flat),
        [pltpu.SMEM] + [None] * 4,
        name="weights_top",
    )
    run1 = start(dw1)
    small_f = shape(small_rows, channels)
    (small1,) = run(
        top_taps_kernel,
        (small_f,),
        [tile_z, shape(groups, 49, LANES)],
        (mids, dz1, *small1),
        name="top_taps",
    )
    tile1, twin, other, small1 = fenced(tile1, twin, other, small1)
    wide1 = rimmed(tile1, twin, other, 0, odd_row, outer_row)
    twin, other = edges(wide1, 1, HALO, odd_col)
    twin, other = to_twin(twin, "cols"), to_other(other, "cols")
    run1, z0 = fenced(run1, z0)
    pair1 = fork(run1)
    tile_f = shape(pixels, channels)
    again = run(
        again_kernel,
        (tile_f, shape(pixels, LANES), tile_b, tile_h, shape(pixels, hidden)),
        weights[:1],
        (z0, norm_gains, norm_shifts, w_in, b_in),
        [None] * 3 + [pl.ANY, None],
        fetched=1,
        name="again",
    )
    wide1, twin, other, again = fenced(wide1, twin, other, again)
    dzpad1 = filled(rimmed(wide1, twin, other, 1, odd_col, outer_col))
    spread_scratch = [shape(groups, *dzpad1.shape[:2], LANES), tile_z]
    grad_mid, dz0, *rest = run(
        functools.partial(low_kernel, per),
        (tile_b, tile_b) + small_outs + grads_b,
        spread_scratch + [tile_h] + weights,
        (place, dzpad1, grad_flat, *again, taps, norm_gains, w_in, w_out),
        [pltpu.SMEM] + [None] * 9 + [pl.ANY] * 2,
        fetched=2,
        name="low",
    )
    small0, dw0 = rest[:3], rest[3:]
    dz0, dw0, pair1, small0 = fenced(dz0, dw0, pair1, small0)
    run0 = start(dw0)
    low_bit = col_bits + 1
    pair1, _ = onward([settled(f) for f in pair1], low_bit)
    small_b = shape(small_rows, channels, dtype=BF16)
    send, small = run(
        taps_kernel,
        (small_b, small_b),
        [shape(groups, *xpad.shape[:2], LANES), tile_z, shape(groups, 49, LANES), small_f],
        (place, xpad, dz0, *small0, small1),
        [pltpu.SMEM] + [None] * 6,
        name="taps",
    )
    small_got = flip_bit(send, 0)
    run0, dz0, small, small_got = fenced(run0, dz0, small, small_got)
    pair0 = fork(run0)
    tile0 = dz0.reshape(rows, cols, channels)
    twin, other = edges(tile0, 0, HALO, odd_row)
    twin, other = to_twin(twin, "rows"), to_other(other, "rows")
    small = summed(small, small_got)
    for bit in range(1, col_bits - 1):
        small = summed(small, flip_bit(small, bit))
    small_got = flip_bit(small, sides[0])
    pair0, pair1, tile0, twin, other, small, small_got = fenced(
        pair0, pair1, tile0, twin, other, small, small_got
    )
    small = summed(small, small_got)
    moved_in, (small_got,) = onward([settled(pair0[0]), settled(pair1[0])], sides[1], small)
    moved_out, _ = onward([settled(pair0[1]), settled(pair1[1])], sides[0])
    both = [moved_in, moved_out]
    wide0 = rimmed(tile0, twin, other, 0, odd_row, outer_row)
    twin, other = edges(wide0, 1, HALO, odd_col)
    twin, other = to_twin(twin, "cols"), to_other(other, "cols")
    both, wide0, twin, other, small, small_got = fenced(both, wide0, twin, other, small, small_got)
    small = summed(small, small_got)
    (run0,), (small_got,) = onward([merged([both[0][0], both[1][0]])], low_bit, small)
    part1, order1 = merged([both[0][1], both[1][1]])
    flight1 = (part1, jnp.zeros_like(part1), order1)
    if order1:
        (flight1,), _ = onward([(part1, order1)], order1[-1])
    (grad_in,) = run(
        last_kernel,
        (tile_b,),
        spread_scratch,
        (filled(rimmed(wide0, twin, other, 1, odd_col, outer_col)), grad_mid, taps),
        name="last",
    )
    while run0[2]:
        run0, flight1, small, small_got, grad_in = fenced(run0, flight1, small, small_got, grad_in)
        small = summed(small, small_got)
        (run0,), (small_got,) = onward([settled(run0)], run0[2][-1], small)
        if flight1[2]:
            (flight1,), _ = onward([settled(flight1)], flight1[2][-1])
    run0, flight1, small, small_got = fenced(run0, flight1, small, small_got)
    small = summed(small, small_got)
    small_got = flip_bit(small, 0)
    share = shape(layers, per, channels)
    grad_w_in, grad_w_out = run(
        functools.partial(weights_kernel, grad_scale),
        (share, share),
        [],
        [part.reshape(2, per, channels) for part in run0[:2] + flight1[:2]],
        name="weights",
    )
    grad_taps, grad_gains, grad_shifts, grad_b_in = run(
        functools.partial(small_kernel, grad_scale),
        (
            shape(49, layers, channels),
            shape(layers, channels),
            shape(layers, channels),
            shape(layers, hidden),
        ),
        [],
        (place, small, small_got),
        [pltpu.SMEM, None, None],
        name="small",
    )
    return (
        grad_in.reshape(rows, cols, channels),
        grad_taps.reshape(7, 7, layers, channels).transpose(2, 0, 1, 3),
        grad_gains,
        grad_shifts,
        grad_b_in,
        jnp.swapaxes(grad_w_in, 1, 2),
        jnp.swapaxes(grad_w_out, 1, 2),
    )


def solution(mesh):
    tile = P("rows", "cols", None)
    sliced = P(None, None, ("rows", "cols"))
    return jax.shard_map(
        shards,
        mesh=mesh,
        in_specs=(tile, tile, P(), P(), P(), P(), P(), P()),
        out_specs=(tile, P(), P(), P(), P(), sliced, sliced),
        check_vma=False,
    )
```

```python
import functools
import math

import jax
import jax.numpy as jnp
from jax import lax
from jax.experimental import pallas as pl
from jax.experimental.pallas import tpu as pltpu
from jax.sharding import PartitionSpec as P

EPSILON = 1e-06
INV_ROOT_TAU = 0.3989422804014327
HALF_LOG2E = 0.7213475204444817
ERFC_SLOPE = 0.4 * 0.7071067811865476
ERFC_TERMS = (
    0.23195388609975262,
    0.16163296978938874,
    0.4687286953098433,
    -0.3714470456115026,
    0.7094654203066808,
    -0.2003339536843631,
)
LANES = 128
HALO = 3
WIDE = 2 * HALO
F32 = jnp.float32
BF16 = jnp.bfloat16


def normal_parts(x):
    size = jnp.abs(x)
    bell = jnp.exp2(x * x * (-HALF_LOG2E))
    t = pl.reciprocal(1.0 + ERFC_SLOPE * size, approx=True)
    series = 0.5 * ERFC_TERMS[-1]
    for term in ERFC_TERMS[-2::-1]:
        series = series * t + 0.5 * term
    return size, series * t * bell, bell


def gelu_only(x):
    size, tail, _ = normal_parts(x)
    return jnp.maximum(x, 0.0) - size * tail


def gelu_parts(x):
    size, tail, bell = normal_parts(x)
    cdf = jnp.where(x >= 0, 1.0 - tail, tail)
    return jnp.maximum(x, 0.0) - size * tail, cdf + x * bell * INV_ROOT_TAU


def strip_rows(rows, cols):
    most = max(1, 288 // cols)
    return max(d for d in range(1, rows + 1) if rows % d == 0 and d <= most)


def conv_pass(source, row0, col0, taps, layer, target, rows, cols, back=False):
    strip = strip_rows(rows, cols)
    groups = source.shape[0]

    def one_strip(step, carry):
        g = step // (rows // strip)
        top = (step % (rows // strip)) * strip
        lanes = pl.ds(pl.multiple_of(g * LANES, LANES), LANES)
        sums = [jnp.zeros((cols, LANES), F32) for _ in range(strip)]
        for b in range(7):
            spots = [48 - 7 * a - b if back else 7 * a + b for a in range(7)]
            weights = [taps[spot, pl.ds(layer, 1), lanes] for spot in spots]
            for r in range(strip + 6):
                line = source[g, row0 + top + r, pl.ds(col0 + b, cols), :]
                for a in range(7):
                    if 0 <= r - a < strip:
                        sums[r - a] = sums[r - a] + weights[a] * line
        for i in range(strip):
            target[g, top + i] = sums[i]
        return carry

    lax.fori_loop(0, groups * (rows // strip), one_strip, 0)


def tap_pass(source, row0, col0, grad, target, rows, cols):
    def one_group(g, carry):
        lines = [grad[g, i] for i in range(rows)]
        for b in range(7):
            sums = [None] * 7
            for r in range(rows + 6):
                line = source[g, row0 + r, pl.ds(col0 + b, cols), :]
                for a in range(7):
                    if 0 <= r - a < rows:
                        part = lines[r - a] * line
                        sums[a] = part if sums[a] is None else sums[a] + part
            for a in range(7):
                total = jnp.sum(sums[a], axis=0, keepdims=True)
                target[g, pl.ds(7 * a + b, 1), :] = total
        return carry

    lax.fori_loop(0, source.shape[0], one_group, 0)


def joined(ref, rows, cols=slice(None)):
    parts = [ref[g, rows, cols, :] for g in range(ref.shape[0])]
    return jnp.concatenate([p.reshape(-1, LANES) for p in parts], axis=1)


def split_to(ref, rows, value, shape):
    for g in range(ref.shape[0]):
        ref[g, rows] = value[:, g * LANES : (g + 1) * LANES].reshape(*shape, LANES)


def norm_parts(z):
    center = z - jnp.mean(z, axis=-1, keepdims=True)
    inv = lax.rsqrt(jnp.mean(center * center, axis=-1, keepdims=True) + EPSILON)
    return center * inv, inv


def norm_back(dn, hat, inv, gain):
    scaled = dn * gain
    return inv * (
        scaled
        - jnp.mean(scaled, axis=-1, keepdims=True)
        - hat * jnp.mean(scaled * hat, axis=-1, keepdims=True)
    )


def dot_nn(a, b):
    return jnp.dot(a, b, preferred_element_type=F32)


def dot_nt(a, b):
    return lax.dot_general(a, b, (((1,), (1,)), ((), ())), preferred_element_type=F32)


def dot_tn(a, b):
    return lax.dot_general(a, b, (((0,), (0,)), ((), ())), preferred_element_type=F32)


def pixel_blocks(pixels):
    best = max(d for d in range(16, 257, 16) if pixels % d == 0)
    return [slice(start, start + best) for start in range(0, pixels, best)]


def hidden_chunks(hidden):
    size = 256 if hidden % 256 == 0 else hidden
    return [slice(start, start + size) for start in range(0, hidden, size)]


def hidden_forward(normed, w_in, bias, act, slope):
    for cut in hidden_chunks(w_in.shape[2]):
        for block in pixel_blocks(normed.shape[0]):
            value, factor = gelu_parts(dot_nn(normed[block, :], w_in[0, :, cut]) + bias[:, cut])
            act[block, cut] = value.astype(BF16)
            slope[block, cut] = factor


def hidden_back(grad, w_out, slope, gpre, db):
    for cut in hidden_chunks(w_out.shape[2]):
        bias_sum = None
        for block in pixel_blocks(grad.shape[0]):
            gradient = dot_nn(grad[block, :], w_out[0, :, cut]) * slope[block, cut]
            gpre[block, cut] = gradient.astype(BF16)
            part = jnp.sum(gradient, axis=0, keepdims=True)
            bias_sum = part if bias_sum is None else bias_sum + part
        db[:, cut] = bias_sum


def dz_of(gpre, w_in, hat, inv, gain, dz_out, dgain, dshift):
    dn = dot_nt(gpre[...], w_in[0])
    dgain[...] = jnp.sum(dn * hat, axis=0, keepdims=True)
    dshift[...] = jnp.sum(dn, axis=0, keepdims=True)
    dz_out[...] = norm_back(dn, hat, inv, gain).astype(BF16)


def mlp_grads(normed, grad, w_in, b_in, w_out, act, gpre, db):
    pixels = grad.shape[0]
    for cut in hidden_chunks(w_in.shape[2]):
        bias = b_in[:, cut]
        bias_sum = None
        for block in pixel_blocks(pixels):
            pre = dot_nn(normed[block, :], w_in[0, :, cut]) + bias
            value, slope = gelu_parts(pre)
            act[block, cut] = value.astype(BF16)
            gradient = dot_nn(grad[block, :], w_out[0, :, cut]) * slope
            gpre[block, cut] = gradient.astype(BF16)
            part = jnp.sum(gradient, axis=0, keepdims=True)
            bias_sum = part if bias_sum is None else bias_sum + part
        db[:, cut] = bias_sum


def weight_grads(place, normed, grad, act, gpre, dw, per):
    hidden, channels = act.shape[1], grad.shape[1]
    size = min(n for n in range(128, hidden + 1, 128) if hidden % n == 0 and n % (2 * per) == 0 and n >= 256)
    for first in range(0, hidden, size):
        cut = slice(first, first + size)
        for i, (left, right) in enumerate(((gpre, normed), (act, grad))):
            value = dot_tn(left[:, cut], right[...]).astype(BF16)
            if len(dw) == 1:
                dw[0][i, cut, :] = value
                continue
            value = value.reshape(size // (2 * per), 2, per, channels)
            upper = place[4] == 1
            half = slice(first // 2, (first + size) // 2)
            dw[0][i, half, :] = jnp.where(upper, value[:, 0], value[:, 1]).reshape(-1, channels)
            dw[1][i, half, :] = jnp.where(upper, value[:, 1], value[:, 0]).reshape(-1, channels)


def fetch_layers(triples, arrived):
    copies = [
        pltpu.make_async_copy(source.at[pl.ds(layer, 1)], target, arrived.at[i])
        for i, (source, layer, target) in enumerate(triples)
    ]
    for copy in copies:
        copy.start()
    return copies


def edges_kernel(place, tile, copy, twin, other):
    width = twin.shape[0]
    odd = place[5] == 1
    copy[...] = tile[...]
    low, high = tile[:width].astype(F32), tile[tile.shape[0] - width :].astype(F32)
    twin[...] = jnp.where(odd, low, high).astype(BF16)
    other[...] = jnp.where(odd, high, low).astype(BF16)


def forward_kernel(
    place, xpad, taps, gains, shifts, w_in, w_out, b_in, mids, z_out,
    xs, zs, act, w_in0, w_out0, arrived,
):
    waits = fetch_layers(((w_in, 0, w_in0), (w_out, 0, w_out0)), arrived)
    groups, mid_rows, mid_cols = zs.shape[:3]
    rows, cols = z_out.shape[1:3]
    for g in range(groups):
        xs[g] = xpad[:, :, g * LANES : (g + 1) * LANES].astype(F32)
    conv_pass(xs, 0, 0, taps, 0, zs, mid_rows, mid_cols)
    z_out[...] = zs[:, HALO : HALO + rows, HALO : HALO + cols, :]
    strip = act.shape[0] // mid_cols
    for wait in waits:
        wait.wait()

    def one_strip(step, carry):
        top = step * strip
        hat, _ = norm_parts(joined(zs, pl.ds(top, strip)))
        normed = (hat * gains[0:1] + shifts[0:1]).astype(BF16)
        for cut in hidden_chunks(w_in0.shape[2]):
            pre = dot_nn(normed, w_in0[0, :, cut]) + b_in[0:1, cut]
            act[:, cut] = gelu_only(pre).astype(BF16)
        mixed = dot_nt(act[...], w_out0[0])
        row = lax.broadcasted_iota(jnp.int32, (strip, mid_cols, 1), 0) + (top - HALO) + place[0]
        col = lax.broadcasted_iota(jnp.int32, (strip, mid_cols, 1), 1) - HALO + place[1]
        real = (row >= 0) & (row < place[2]) & (col >= 0) & (col < place[3])
        real = jnp.where(real, 1.0, 0.0).reshape(strip * mid_cols, 1)
        base = joined(xs, pl.ds(top + HALO, strip), slice(HALO, HALO + mid_cols))
        mid = (base + mixed).astype(BF16).astype(F32) * real
        split_to(mids, pl.ds(top, strip), mid, (strip, mid_cols))
        return carry

    lax.fori_loop(0, mid_rows // strip, one_strip, 0, unroll=True)


def top_kernel(
    mids, grad, taps, gains, shifts, w_in, w_out, b_in,
    dz_out, normed, act, gpre, db, dgain, dshift, z, w_in1, w_out1, arrived,
):
    waits = fetch_layers(((w_in, 1, w_in1), (w_out, 1, w_out1)), arrived)
    conv_pass(mids, 0, 0, taps, 1, z, *z.shape[1:3])
    hat, inv = norm_parts(joined(z, slice(None)))
    normed[...] = (hat * gains[1:2] + shifts[1:2]).astype(BF16)
    for wait in waits:
        wait.wait()
    mlp_grads(normed, grad, w_in1, b_in.at[pl.ds(1, 1)], w_out1, act, gpre, db)
    dz_of(gpre, w_in1, hat, inv, gains[1:2], dz_out, dgain, dshift)


def again_kernel(z0, gains, shifts, w_in, b_in, hat_out, inv_out, normed, act, slope, w_in0, arrived):
    (wait,) = fetch_layers(((w_in, 0, w_in0),), arrived)
    hat, inv = norm_parts(joined(z0, slice(None)))
    hat_out[...] = hat
    inv_out[...] = jnp.broadcast_to(inv, inv_out.shape)
    normed[...] = (hat * gains[0:1] + shifts[0:1]).astype(BF16)
    wait.wait()
    hidden_forward(normed, w_in0, b_in.at[pl.ds(0, 1)], act, slope)


def low_kernel(
    per, place, dzpad, grad, hat, inv, normed, act, slope, taps, gains, w_in, w_out,
    gmid, dz_out, db, dgain, dshift, *rest,
):
    *dw, dzs, spread, gpre, w_in0, w_out0, arrived = rest
    waits = fetch_layers(((w_out, 0, w_out0), (w_in, 0, w_in0)), arrived)
    spread_pass(dzpad, dzs, taps, 1, spread)
    gmid[...] = (grad[...].astype(F32) + joined(spread, slice(None))).astype(BF16)
    for wait in waits:
        wait.wait()
    hidden_back(gmid, w_out0, slope, gpre, db)
    dz_of(gpre, w_in0, hat[...], inv[:, :1], gains[0:1], dz_out, dgain, dshift)
    weight_grads(place, normed, gmid, act, gpre, dw, per)


def weights_top_kernel(per, place, normed, act, gpre, grad, *dw):
    weight_grads(place, normed, grad, act, gpre, dw, per)


def spread_pass(dzpad, dzs, taps, layer, spread):
    for g in range(dzs.shape[0]):
        dzs[g] = dzpad[:, :, g * LANES : (g + 1) * LANES].astype(F32)
    conv_pass(dzs, 0, 0, taps, layer, spread, *spread.shape[1:3], back=True)


def last_kernel(dzpad, gmid, taps, out, dzs, spread):
    spread_pass(dzpad, dzs, taps, 0, spread)
    out[...] = (gmid[...].astype(F32) + joined(spread, slice(None))).astype(BF16)


def small_rows_of(values, row0, col0, dz, dzs, taps, db, dgain, dshift, sums):
    rows, cols = dzs.shape[1:3]
    channels = sums.shape[1]
    split_to(dzs, slice(None), dz[...].astype(F32), (rows, cols))
    count = db.shape[1] // channels
    for k in range(count):
        sums[k : k + 1, :] = db[:, k * channels : (k + 1) * channels]
    sums[count : count + 1, :] = dgain[...]
    sums[count + 1 : count + 2, :] = dshift[...]
    tap_pass(values, row0, col0, dzs, taps, rows, cols)
    for g in range(taps.shape[0]):
        sums[count + 2 : count + 51, g * LANES : (g + 1) * LANES] = taps[g]


def top_taps_kernel(mids, dz, db, dgain, dshift, sums, dzs, taps):
    sums[...] = jnp.zeros(sums.shape, F32)
    small_rows_of(mids, 0, 0, dz, dzs, taps, db, dgain, dshift, sums)


def taps_kernel(place, xpad, dz, db, dgain, dshift, sums1, send, keep, xs, dzs, taps, sums0):
    for g in range(dzs.shape[0]):
        xs[g] = xpad[:, :, g * LANES : (g + 1) * LANES].astype(F32)
    sums0[...] = jnp.zeros(sums0.shape, F32)
    small_rows_of(xs, HALO, HALO, dz, dzs, taps, db, dgain, dshift, sums0)
    upper = place[4] == 1
    send[...] = jnp.where(upper, sums0[...], sums1[...]).astype(BF16)
    keep[...] = jnp.where(upper, sums1[...], sums0[...]).astype(BF16)


def small_kernel(scale, place, mine, got, taps_out, gains, shifts, biases):
    upper = place[4] == 1
    own, came = mine[...].astype(F32) * scale, got[...].astype(F32) * scale
    channels = own.shape[1]
    count = biases.shape[1] // channels
    for layer, part in enumerate((jnp.where(upper, came, own), jnp.where(upper, own, came))):
        at = slice(layer, layer + 1)
        for k in range(count):
            biases[at, k * channels : (k + 1) * channels] = part[k : k + 1, :]
        gains[at, :] = part[count : count + 1, :]
        shifts[at, :] = part[count + 1 : count + 2, :]
        for tap in range(49):
            taps_out[tap, at, :] = part[count + 2 + tap : count + 3 + tap, :]


def weights_kernel(scale, keep0, got0, keep1, got1, out_in, out_out):
    for layer, (keep, got) in enumerate(((keep0, got0), (keep1, got1))):
        for i, out in enumerate((out_in, out_out)):
            out[layer] = (keep[i].astype(F32) + got[i].astype(F32)) * scale


def shape(*dims, dtype=F32):
    return jax.ShapeDtypeStruct(dims, dtype)


def run(kernel, outs, scratch, args, specs=None, fetched=0, name=None, room=46):
    vmem = pl.BlockSpec(memory_space=pltpu.VMEM)
    semaphores = [pltpu.SemaphoreType.DMA((fetched,))] if fetched else []
    return pl.pallas_call(
        kernel,
        out_shape=outs,
        in_specs=[
            vmem if s is None else pl.BlockSpec(memory_space=s) for s in (specs or [None] * len(args))
        ],
        out_specs=tuple(vmem for _ in outs),
        scratch_shapes=[pltpu.VMEM(s.shape, s.dtype) for s in scratch] + semaphores,
        compiler_params=pltpu.CompilerParams(vmem_limit_bytes=room * 1024 * 1024),
        name=name,
    )(*args)


def edges(tile, axis, width, odd):
    count = tile.shape[axis]
    low = lax.slice_in_dim(tile, 0, width, axis=axis)
    high = lax.slice_in_dim(tile, count - width, count, axis=axis)
    return jnp.where(odd, low, high), jnp.where(odd, high, low)


def to_twin(edge, axis):
    count = lax.axis_size(axis)
    return lax.ppermute(edge, axis, [(i, i ^ 1) for i in range(count) if i ^ 1 < count])


def to_other(edge, axis):
    n_rows, n_cols = lax.axis_size("rows"), lax.axis_size("cols")
    count = lax.axis_size(axis)
    pairs = []
    for r in range(n_rows):
        for c in range(n_cols):
            at = r if axis == "rows" else c
            partner = at + 1 if at % 2 else at - 1
            if 0 <= partner < count:
                there = (partner, c) if axis == "rows" else (r, partner)
            else:
                there = (r, c ^ 1) if axis == "rows" else (r ^ 1, c)
            pairs.append((r * n_cols + c, there[0] * n_cols + there[1]))
    return lax.ppermute(edge, ("rows", "cols"), pairs)


def rimmed(tile, from_twin, from_other, axis, odd, outer):
    from_other = jnp.where(outer, jnp.zeros_like(from_other), from_other)
    low = jnp.where(odd, from_twin, from_other)
    high = jnp.where(odd, from_other, from_twin)
    return jnp.concatenate([low, tile, high], axis=axis)


def flip_bit(value, *bits):
    flip = sum(1 << bit for bit in bits)
    both = ("rows", "cols")
    total = lax.axis_size("rows") * lax.axis_size("cols")
    return lax.ppermute(value, both, [(i, i ^ flip) for i in range(total)])


def halves(chunks, dim, mine):
    sizes = [1 if d == dim else n for d, n in enumerate(chunks.shape)]

    def one(bit):
        starts = [bit if d == dim else jnp.uint32(0) for d in range(chunks.ndim)]
        return lax.squeeze(lax.dynamic_slice(chunks, starts, sizes), (dim,))

    return one(mine[1]), one(mine[0])


def summed(own, *got):
    parts = [part.astype(F32) for part in (own,) + got]
    while len(parts) > 1:
        parts = [a + b for a, b in zip(parts[::2], parts[1::2])]
    return parts[0].astype(BF16)


def cut(chunks, order, bit, mine):
    spot = order.index(bit)
    per = chunks.shape[-2:]
    pair = chunks.reshape((-1, 2 ** spot, 2, 2 ** (len(order) - spot - 1)) + per)
    send, keep = halves(pair, 2, mine[bit])
    return send, keep, [b for b in order if b != bit]


def step(chunks, order, bit, mine):
    send, keep, left = cut(chunks, order, bit, mine)
    return keep, flip_bit(send, bit), left


def shards(activations, grad_out, kernels, norm_gains, norm_shifts, w_in, b_in, w_out):
    rows, cols, channels = activations.shape
    layers, _, hidden = w_in.shape
    groups = channels // LANES
    n_rows, n_cols = lax.axis_size("rows"), lax.axis_size("cols")
    total = n_rows * n_cols
    bits = total.bit_length() - 1
    col_bits = n_cols.bit_length() - 1
    me = (lax.axis_index("rows") * n_cols + lax.axis_index("cols")).astype(jnp.uint32)
    mine = [(((me >> k) & 1), 1 - ((me >> k) & 1)) for k in range(bits)]
    grad_scale = 1.0 / math.sqrt(rows * cols * total)
    pixels = rows * cols

    taps = kernels.transpose(1, 2, 0, 3).reshape(49, layers, channels)
    place = jnp.stack(
        [
            lax.axis_index("rows") * rows,
            lax.axis_index("cols") * cols,
            jnp.int32(rows * n_rows),
            jnp.int32(cols * n_cols),
            lax.axis_index("cols") & 1,
            lax.axis_index("rows") & 1,
        ]
    ).astype(jnp.int32)
    grad_flat = grad_out.reshape(pixels, channels)

    at_row, at_col = lax.axis_index("rows"), lax.axis_index("cols")
    odd_col, odd_row = (at_col & 1) == 1, (at_row & 1) == 1
    outer_col = (at_col == 0) | (at_col == n_cols - 1)
    outer_row = (at_row == 0) | (at_row == n_rows - 1)
    activations, place, mine, odd_col, odd_row, outer_col, outer_row = lax.optimization_barrier(
        (activations, place, mine, odd_col, odd_row, outer_col, outer_row)
    )

    def rim_cols(tile, width):
        twin, other = edges(tile, 1, width, odd_col)
        return rimmed(tile, to_twin(twin, "cols"), to_other(other, "cols"), 1, odd_col, outer_col)

    def filled(wide):
        return jnp.pad(wide, ((0, 0), (0, cols + 16 - wide.shape[1]), (0, 0)))

    mid_rows, mid_cols = rows + 2 * HALO, cols + 8
    strip = max(d for d in range(1, mid_rows + 1) if mid_rows % d == 0 and d * mid_cols <= 264)
    weights = [shape(1, channels, hidden, dtype=BF16)] * 2
    tile_z = shape(groups, rows, cols, LANES)
    tile_b = shape(pixels, channels, dtype=BF16)
    tile_h = shape(pixels, hidden, dtype=BF16)
    per = hidden // total
    split = 2 if per % 16 == 0 and col_bits == 2 else 1
    grads_b = (shape(2, hidden // split, channels, dtype=BF16),) * split
    small_outs = (shape(1, hidden), shape(1, channels), shape(1, channels))
    small_rows = -(-(hidden // channels + 51) // 8) * 8

    edge = shape(WIDE, cols, channels, dtype=BF16)
    tile, twin, other = run(
        edges_kernel,
        (shape(rows, cols, channels, dtype=BF16), edge, edge),
        [],
        (place, activations),
        [pltpu.SMEM, None],
        name="edges",
    )
    wide = rimmed(tile, to_twin(twin, "rows"), to_other(other, "rows"), 0, odd_row, outer_row)
    xpad = filled(rim_cols(wide, WIDE))
    mids, z0 = run(
        forward_kernel,
        (shape(groups, mid_rows, mid_cols, LANES), tile_z),
        [
            shape(groups, *xpad.shape[:2], LANES),
            shape(groups, mid_rows, mid_cols, LANES),
            shape(strip * mid_cols, hidden, dtype=BF16),
        ]
        + weights,
        (place, xpad, taps, norm_gains, norm_shifts, w_in, w_out, b_in),
        [pltpu.SMEM] + [None] * 4 + [pl.ANY] * 2 + [None],
        fetched=2,
        name="forward",
        room=50,
    )
    dz1, normed1, act1, gpre1, *small1 = run(
        top_kernel,
        (tile_b, tile_b, tile_h, tile_h) + small_outs,
        [tile_z] + weights,
        (mids, grad_flat, taps, norm_gains, norm_shifts, w_in, w_out, b_in),
        [None] * 5 + [pl.ANY] * 2 + [None],
        fetched=2,
        name="top",
        room=50,
    )

    sides = (col_bits - 1, col_bits)

    def fenced(*values):
        leaves, tree = jax.tree.flatten(values)
        arrays = [i for i, leaf in enumerate(leaves) if not isinstance(leaf, int)]
        for i, value in zip(arrays, lax.optimization_barrier(tuple(leaves[i] for i in arrays))):
            leaves[i] = value
        return jax.tree.unflatten(tree, leaves)

    def settled(flight):
        return summed(flight[0], flight[1]), flight[2]

    def start(dw):
        order = list(range(bits - 1, -1, -1))
        if split == 2:
            send, keep = (d.reshape(2, total // 2, per, channels) for d in dw)
            return keep, flip_bit(send, 0), order[:-1]
        chunks = dw[0].reshape(2, total, per, channels)
        for bit in range(col_bits - 2):
            chunks, order = settled(step(chunks, order, bit, mine))
        return step(chunks, order, col_bits - 2, mine)

    def fork(flight):
        chunks, order = settled(flight)
        return [step(chunks[i], order, sides[i], mine) for i in range(2)]

    def onward(parts, bit, *riders):
        kept, sent, lefts = [], [], []
        for chunks, order in parts:
            send, keep, left = cut(chunks, order, bit, mine)
            kept.append(keep)
            sent.append(send.reshape(-1, channels))
            lefts.append(left)
        got = flip_bit(jnp.concatenate(sent + list(riders), axis=0), bit)
        flights, first = [], 0
        for keep, send, left in zip(kept, sent, lefts):
            came = got[first : first + send.shape[0]].reshape(keep.shape)
            flights.append((keep, came, left))
            first += send.shape[0]
        return flights, [got[first:]] if riders else []

    def merged(flights):
        done = [settled(f) for f in flights]
        return jnp.stack([d[0].reshape(-1, per, channels) for d in done]), done[0][1]

    tile1 = dz1.reshape(rows, cols, channels)
    twin, other = edges(tile1, 0, HALO, odd_row)
    twin, other = to_twin(twin, "rows"), to_other(other, "rows")
    dw1 = run(
        functools.partial(weights_top_kernel, per),
        grads_b,
        [],
        (place, normed1, act1, gpre1, grad_flat),
        [pltpu.SMEM] + [None] * 4,
        name="weights_top",
    )
    run1 = start(dw1)
    tile_f = shape(pixels, channels)
    again = run(
        again_kernel,
        (tile_f, shape(pixels, LANES), tile_b, tile_h, shape(pixels, hidden)),
        weights[:1],
        (z0, norm_gains, norm_shifts, w_in, b_in),
        [None] * 3 + [pl.ANY, None],
        fetched=1,
        name="again",
    )
    tile1, twin, other, again = fenced(tile1, twin, other, again)
    wide1 = rimmed(tile1, twin, other, 0, odd_row, outer_row)
    twin, other = edges(wide1, 1, HALO, odd_col)
    twin, other = to_twin(twin, "cols"), to_other(other, "cols")
    run1, mids = fenced(run1, mids)
    pair1 = fork(run1)
    small_f = shape(small_rows, channels)
    (small1,) = run(
        top_taps_kernel,
        (small_f,),
        [tile_z, shape(groups, 49, LANES)],
        (mids, dz1, *small1),
        name="top_taps",
    )
    wide1, twin, other, small1 = fenced(wide1, twin, other, small1)
    dzpad1 = filled(rimmed(wide1, twin, other, 1, odd_col, outer_col))
    spread_scratch = [shape(groups, *dzpad1.shape[:2], LANES), tile_z]
    grad_mid, dz0, *rest = run(
        functools.partial(low_kernel, per),
        (tile_b, tile_b) + small_outs + grads_b,
        spread_scratch + [tile_h] + weights,
        (place, dzpad1, grad_flat, *again, taps, norm_gains, w_in, w_out),
        [pltpu.SMEM] + [None] * 9 + [pl.ANY] * 2,
        fetched=2,
        name="low",
    )
    small0, dw0 = rest[:3], rest[3:]
    dz0, dw0, pair1, small0 = fenced(dz0, dw0, pair1, small0)
    run0 = start(dw0)
    low_bit = col_bits + 1
    pair1, _ = onward([settled(f) for f in pair1], low_bit)
    small_b = shape(small_rows, channels, dtype=BF16)
    send, small = run(
        taps_kernel,
        (small_b, small_b),
        [shape(groups, *xpad.shape[:2], LANES), tile_z, shape(groups, 49, LANES), small_f],
        (place, xpad, dz0, *small0, small1),
        [pltpu.SMEM] + [None] * 6,
        name="taps",
    )
    small_got = flip_bit(send, 0)
    run0, dz0, small, small_got = fenced(run0, dz0, small, small_got)
    pair0 = fork(run0)
    tile0 = dz0.reshape(rows, cols, channels)
    twin, other = edges(tile0, 0, HALO, odd_row)
    twin, other = to_twin(twin, "rows"), to_other(other, "rows")
    small = summed(small, small_got)
    for bit in range(1, col_bits - 1):
        small = summed(small, flip_bit(small, bit))
    small_got = flip_bit(small, sides[0])
    pair0, pair1, tile0, twin, other, small, small_got = fenced(
        pair0, pair1, tile0, twin, other, small, small_got
    )
    small = summed(small, small_got)
    moved_in, (small_got,) = onward([settled(pair0[0]), settled(pair1[0])], sides[1], small)
    moved_out, _ = onward([settled(pair0[1]), settled(pair1[1])], sides[0])
    both = [moved_in, moved_out]
    wide0 = rimmed(tile0, twin, other, 0, odd_row, outer_row)
    twin, other = edges(wide0, 1, HALO, odd_col)
    twin, other = to_twin(twin, "cols"), to_other(other, "cols")
    both, wide0, twin, other, small, small_got = fenced(both, wide0, twin, other, small, small_got)
    small = summed(small, small_got)
    (run0,), (small_got,) = onward([merged([both[0][0], both[1][0]])], low_bit, small)
    part1, order1 = merged([both[0][1], both[1][1]])
    flight1 = (part1, jnp.zeros_like(part1), order1)
    if order1:
        (flight1,), _ = onward([(part1, order1)], order1[-1])
    (grad_in,) = run(
        last_kernel,
        (tile_b,),
        spread_scratch,
        (filled(rimmed(wide0, twin, other, 1, odd_col, outer_col)), grad_mid, taps),
        name="last",
    )
    while run0[2]:
        run0, flight1, small, small_got, grad_in = fenced(run0, flight1, small, small_got, grad_in)
        small = summed(small, small_got)
        (run0,), (small_got,) = onward([settled(run0)], run0[2][-1], small)
        if flight1[2]:
            (flight1,), _ = onward([settled(flight1)], flight1[2][-1])
    run0, flight1, small, small_got = fenced(run0, flight1, small, small_got)
    small = summed(small, small_got)
    small_got = flip_bit(small, 0)
    share = shape(layers, per, channels)
    grad_w_in, grad_w_out = run(
        functools.partial(weights_kernel, grad_scale),
        (share, share),
        [],
        [part.reshape(2, per, channels) for part in run0[:2] + flight1[:2]],
        name="weights",
    )
    grad_taps, grad_gains, grad_shifts, grad_b_in = run(
        functools.partial(small_kernel, grad_scale),
        (
            shape(49, layers, channels),
            shape(layers, channels),
            shape(layers, channels),
            shape(layers, hidden),
        ),
        [],
        (place, small, small_got),
        [pltpu.SMEM, None, None],
        name="small",
    )
    return (
        grad_in.reshape(rows, cols, channels),
        grad_taps.reshape(7, 7, layers, channels).transpose(2, 0, 1, 3),
        grad_gains,
        grad_shifts,
        grad_b_in,
        jnp.swapaxes(grad_w_in, 1, 2),
        jnp.swapaxes(grad_w_out, 1, 2),
    )


def solution(mesh):
    tile = P("rows", "cols", None)
    sliced = P(None, None, ("rows", "cols"))
    return jax.shard_map(
        shards,
        mesh=mesh,
        in_specs=(tile, tile, P(), P(), P(), P(), P(), P()),
        out_specs=(tile, P(), P(), P(), P(), sliced, sliced),
        check_vma=False,
    )
```

```python
import functools
import math

import jax
import jax.numpy as jnp
from jax import lax
from jax.experimental import pallas as pl
from jax.experimental.pallas import tpu as pltpu
from jax.sharding import PartitionSpec as P

EPSILON = 1e-06
INV_ROOT_TAU = 0.3989422804014327
HALF_LOG2E = 0.7213475204444817
ERFC_SLOPE = 0.4 * 0.7071067811865476
ERFC_TERMS = (
    0.23195388609975262,
    0.16163296978938874,
    0.4687286953098433,
    -0.3714470456115026,
    0.7094654203066808,
    -0.2003339536843631,
)
LANES = 128
HALO = 3
WIDE = 2 * HALO
F32 = jnp.float32
BF16 = jnp.bfloat16


def normal_parts(x):
    size = jnp.abs(x)
    bell = jnp.exp2(x * x * (-HALF_LOG2E))
    t = pl.reciprocal(1.0 + ERFC_SLOPE * size, approx=True)
    series = 0.5 * ERFC_TERMS[-1]
    for term in ERFC_TERMS[-2::-1]:
        series = series * t + 0.5 * term
    return size, series * t * bell, bell


def gelu_only(x):
    size, tail, _ = normal_parts(x)
    return jnp.maximum(x, 0.0) - size * tail


def gelu_parts(x):
    size, tail, bell = normal_parts(x)
    cdf = jnp.where(x >= 0, 1.0 - tail, tail)
    return jnp.maximum(x, 0.0) - size * tail, cdf + x * bell * INV_ROOT_TAU


def strip_rows(rows, cols):
    most = max(1, 288 // cols)
    return max(d for d in range(1, rows + 1) if rows % d == 0 and d <= most)


def conv_pass(source, row0, col0, taps, layer, target, rows, cols, back=False):
    strip = strip_rows(rows, cols)
    groups = source.shape[0]

    def one_strip(step, carry):
        g = step // (rows // strip)
        top = (step % (rows // strip)) * strip
        lanes = pl.ds(pl.multiple_of(g * LANES, LANES), LANES)
        sums = [jnp.zeros((cols, LANES), F32) for _ in range(strip)]
        for b in range(7):
            spots = [48 - 7 * a - b if back else 7 * a + b for a in range(7)]
            weights = [taps[spot, pl.ds(layer, 1), lanes] for spot in spots]
            for r in range(strip + 6):
                line = source[g, row0 + top + r, pl.ds(col0 + b, cols), :]
                for a in range(7):
                    if 0 <= r - a < strip:
                        sums[r - a] = sums[r - a] + weights[a] * line
        for i in range(strip):
            target[g, top + i] = sums[i]
        return carry

    lax.fori_loop(0, groups * (rows // strip), one_strip, 0)


def tap_pass(source, row0, col0, grad, target, rows, cols):
    def one_group(g, carry):
        lines = [grad[g, i] for i in range(rows)]
        for b in range(7):
            sums = [None] * 7
            for r in range(rows + 6):
                line = source[g, row0 + r, pl.ds(col0 + b, cols), :]
                for a in range(7):
                    if 0 <= r - a < rows:
                        part = lines[r - a] * line
                        sums[a] = part if sums[a] is None else sums[a] + part
            for a in range(7):
                total = jnp.sum(sums[a], axis=0, keepdims=True)
                target[g, pl.ds(7 * a + b, 1), :] = total
        return carry

    lax.fori_loop(0, source.shape[0], one_group, 0)


def joined(ref, rows, cols=slice(None)):
    parts = [ref[g, rows, cols, :] for g in range(ref.shape[0])]
    return jnp.concatenate([p.reshape(-1, LANES) for p in parts], axis=1)


def split_to(ref, rows, value, shape):
    for g in range(ref.shape[0]):
        ref[g, rows] = value[:, g * LANES : (g + 1) * LANES].reshape(*shape, LANES)


def norm_parts(z):
    center = z - jnp.mean(z, axis=-1, keepdims=True)
    inv = lax.rsqrt(jnp.mean(center * center, axis=-1, keepdims=True) + EPSILON)
    return center * inv, inv


def norm_back(dn, hat, inv, gain):
    scaled = dn * gain
    return inv * (
        scaled
        - jnp.mean(scaled, axis=-1, keepdims=True)
        - hat * jnp.mean(scaled * hat, axis=-1, keepdims=True)
    )


def dot_nn(a, b):
    return jnp.dot(a, b, preferred_element_type=F32)


def dot_nt(a, b):
    return lax.dot_general(a, b, (((1,), (1,)), ((), ())), preferred_element_type=F32)


def dot_tn(a, b):
    return lax.dot_general(a, b, (((0,), (0,)), ((), ())), preferred_element_type=F32)


def pixel_blocks(pixels):
    best = max(d for d in range(16, 257, 16) if pixels % d == 0)
    return [slice(start, start + best) for start in range(0, pixels, best)]


def hidden_chunks(hidden):
    size = 256 if hidden % 256 == 0 else hidden
    return [slice(start, start + size) for start in range(0, hidden, size)]


def hidden_forward(normed, w_in, bias, act, slope):
    for cut in hidden_chunks(w_in.shape[2]):
        for block in pixel_blocks(normed.shape[0]):
            value, factor = gelu_parts(dot_nn(normed[block, :], w_in[0, :, cut]) + bias[:, cut])
            act[block, cut] = value.astype(BF16)
            slope[block, cut] = factor


def hidden_back(grad, w_out, slope, gpre, db):
    for cut in hidden_chunks(w_out.shape[2]):
        bias_sum = None
        for block in pixel_blocks(grad.shape[0]):
            gradient = dot_nn(grad[block, :], w_out[0, :, cut]) * slope[block, cut]
            gpre[block, cut] = gradient.astype(BF16)
            part = jnp.sum(gradient, axis=0, keepdims=True)
            bias_sum = part if bias_sum is None else bias_sum + part
        db[:, cut] = bias_sum


def dz_of(gpre, w_in, hat, inv, gain, dz_out, dgain, dshift):
    dn = dot_nt(gpre[...], w_in[0])
    dgain[...] = jnp.sum(dn * hat, axis=0, keepdims=True)
    dshift[...] = jnp.sum(dn, axis=0, keepdims=True)
    dz_out[...] = norm_back(dn, hat, inv, gain).astype(BF16)


def mlp_grads(normed, grad, w_in, b_in, w_out, act, gpre, db):
    pixels = grad.shape[0]
    for cut in hidden_chunks(w_in.shape[2]):
        bias = b_in[:, cut]
        bias_sum = None
        for block in pixel_blocks(pixels):
            pre = dot_nn(normed[block, :], w_in[0, :, cut]) + bias
            value, slope = gelu_parts(pre)
            act[block, cut] = value.astype(BF16)
            gradient = dot_nn(grad[block, :], w_out[0, :, cut]) * slope
            gpre[block, cut] = gradient.astype(BF16)
            part = jnp.sum(gradient, axis=0, keepdims=True)
            bias_sum = part if bias_sum is None else bias_sum + part
        db[:, cut] = bias_sum


def weight_grads(place, normed, grad, act, gpre, dw, per):
    hidden, channels = act.shape[1], grad.shape[1]
    size = min(n for n in range(128, hidden + 1, 128) if hidden % n == 0 and n % (2 * per) == 0 and n >= 256)
    for first in range(0, hidden, size):
        cut = slice(first, first + size)
        for i, (left, right) in enumerate(((gpre, normed), (act, grad))):
            value = dot_tn(left[:, cut], right[...]).astype(BF16)
            if len(dw) == 1:
                dw[0][i, cut, :] = value
                continue
            value = value.reshape(size // (2 * per), 2, per, channels)
            upper = place[4] == 1
            half = slice(first // 2, (first + size) // 2)
            dw[0][i, half, :] = jnp.where(upper, value[:, 0], value[:, 1]).reshape(-1, channels)
            dw[1][i, half, :] = jnp.where(upper, value[:, 1], value[:, 0]).reshape(-1, channels)


def fetch_layers(triples, arrived):
    copies = [
        pltpu.make_async_copy(source.at[pl.ds(layer, 1)], target, arrived.at[i])
        for i, (source, layer, target) in enumerate(triples)
    ]
    for copy in copies:
        copy.start()
    return copies


def edges_kernel(place, tile, copy, twin, other):
    width = twin.shape[0]
    odd = place[5] == 1
    copy[...] = tile[...]
    low, high = tile[:width].astype(F32), tile[tile.shape[0] - width :].astype(F32)
    twin[...] = jnp.where(odd, low, high).astype(BF16)
    other[...] = jnp.where(odd, high, low).astype(BF16)


def forward_kernel(
    place, xpad, taps, gains, shifts, w_in, w_out, b_in, mids, z_out,
    xs, zs, act, w_in0, w_out0, arrived,
):
    waits = fetch_layers(((w_in, 0, w_in0), (w_out, 0, w_out0)), arrived)
    groups, mid_rows, mid_cols = zs.shape[:3]
    rows, cols = z_out.shape[1:3]
    for g in range(groups):
        xs[g] = xpad[:, :, g * LANES : (g + 1) * LANES].astype(F32)
    conv_pass(xs, 0, 0, taps, 0, zs, mid_rows, mid_cols)
    z_out[...] = zs[:, HALO : HALO + rows, HALO : HALO + cols, :]
    strip = act.shape[0] // mid_cols
    for wait in waits:
        wait.wait()

    def one_strip(step, carry):
        top = step * strip
        hat, _ = norm_parts(joined(zs, pl.ds(top, strip)))
        normed = (hat * gains[0:1] + shifts[0:1]).astype(BF16)
        for cut in hidden_chunks(w_in0.shape[2]):
            pre = dot_nn(normed, w_in0[0, :, cut]) + b_in[0:1, cut]
            act[:, cut] = gelu_only(pre).astype(BF16)
        mixed = dot_nt(act[...], w_out0[0])
        row = lax.broadcasted_iota(jnp.int32, (strip, mid_cols, 1), 0) + (top - HALO) + place[0]
        col = lax.broadcasted_iota(jnp.int32, (strip, mid_cols, 1), 1) - HALO + place[1]
        real = (row >= 0) & (row < place[2]) & (col >= 0) & (col < place[3])
        real = jnp.where(real, 1.0, 0.0).reshape(strip * mid_cols, 1)
        base = joined(xs, pl.ds(top + HALO, strip), slice(HALO, HALO + mid_cols))
        mid = (base + mixed).astype(BF16).astype(F32) * real
        split_to(mids, pl.ds(top, strip), mid, (strip, mid_cols))
        return carry

    lax.fori_loop(0, mid_rows // strip, one_strip, 0, unroll=True)


def top_kernel(
    mids, grad, taps, gains, shifts, w_in, w_out, b_in,
    dz_out, normed, act, gpre, db, dgain, dshift, z, w_in1, w_out1, arrived,
):
    waits = fetch_layers(((w_in, 1, w_in1), (w_out, 1, w_out1)), arrived)
    conv_pass(mids, 0, 0, taps, 1, z, *z.shape[1:3])
    hat, inv = norm_parts(joined(z, slice(None)))
    normed[...] = (hat * gains[1:2] + shifts[1:2]).astype(BF16)
    for wait in waits:
        wait.wait()
    mlp_grads(normed, grad, w_in1, b_in.at[pl.ds(1, 1)], w_out1, act, gpre, db)
    dz_of(gpre, w_in1, hat, inv, gains[1:2], dz_out, dgain, dshift)


def again_kernel(z0, gains, shifts, w_in, b_in, hat_out, inv_out, normed, act, slope, w_in0, arrived):
    (wait,) = fetch_layers(((w_in, 0, w_in0),), arrived)
    hat, inv = norm_parts(joined(z0, slice(None)))
    hat_out[...] = hat
    inv_out[...] = jnp.broadcast_to(inv, inv_out.shape)
    normed[...] = (hat * gains[0:1] + shifts[0:1]).astype(BF16)
    wait.wait()
    hidden_forward(normed, w_in0, b_in.at[pl.ds(0, 1)], act, slope)


def low_kernel(
    per, place, dzpad, grad, hat, inv, normed, act, slope, taps, gains, w_in, w_out,
    gmid, dz_out, db, dgain, dshift, *rest,
):
    *dw, dzs, spread, gpre, w_in0, w_out0, arrived = rest
    waits = fetch_layers(((w_out, 0, w_out0), (w_in, 0, w_in0)), arrived)
    spread_pass(dzpad, dzs, taps, 1, spread)
    gmid[...] = (grad[...].astype(F32) + joined(spread, slice(None))).astype(BF16)
    for wait in waits:
        wait.wait()
    hidden_back(gmid, w_out0, slope, gpre, db)
    dz_of(gpre, w_in0, hat[...], inv[:, :1], gains[0:1], dz_out, dgain, dshift)
    weight_grads(place, normed, gmid, act, gpre, dw, per)


def weights_top_kernel(per, place, normed, act, gpre, grad, *dw):
    weight_grads(place, normed, grad, act, gpre, dw, per)


def spread_pass(dzpad, dzs, taps, layer, spread):
    for g in range(dzs.shape[0]):
        dzs[g] = dzpad[:, :, g * LANES : (g + 1) * LANES].astype(F32)
    conv_pass(dzs, 0, 0, taps, layer, spread, *spread.shape[1:3], back=True)


def last_kernel(dzpad, gmid, taps, out, dzs, spread):
    spread_pass(dzpad, dzs, taps, 0, spread)
    out[...] = (gmid[...].astype(F32) + joined(spread, slice(None))).astype(BF16)


def small_rows_of(values, row0, col0, dz, dzs, taps, db, dgain, dshift, sums):
    rows, cols = dzs.shape[1:3]
    channels = sums.shape[1]
    split_to(dzs, slice(None), dz[...].astype(F32), (rows, cols))
    count = db.shape[1] // channels
    for k in range(count):
        sums[k : k + 1, :] = db[:, k * channels : (k + 1) * channels]
    sums[count : count + 1, :] = dgain[...]
    sums[count + 1 : count + 2, :] = dshift[...]
    tap_pass(values, row0, col0, dzs, taps, rows, cols)
    for g in range(taps.shape[0]):
        sums[count + 2 : count + 51, g * LANES : (g + 1) * LANES] = taps[g]


def top_taps_kernel(mids, dz, db, dgain, dshift, sums, dzs, taps):
    sums[...] = jnp.zeros(sums.shape, F32)
    small_rows_of(mids, 0, 0, dz, dzs, taps, db, dgain, dshift, sums)


def taps_kernel(place, xpad, dz, db, dgain, dshift, sums1, send, keep, xs, dzs, taps, sums0):
    for g in range(dzs.shape[0]):
        xs[g] = xpad[:, :, g * LANES : (g + 1) * LANES].astype(F32)
    sums0[...] = jnp.zeros(sums0.shape, F32)
    small_rows_of(xs, HALO, HALO, dz, dzs, taps, db, dgain, dshift, sums0)
    upper = place[4] == 1
    send[...] = jnp.where(upper, sums0[...], sums1[...]).astype(BF16)
    keep[...] = jnp.where(upper, sums1[...], sums0[...]).astype(BF16)


def small_kernel(scale, place, mine, got, taps_out, gains, shifts, biases):
    upper = place[4] == 1
    own, came = mine[...].astype(F32) * scale, got[...].astype(F32) * scale
    channels = own.shape[1]
    count = biases.shape[1] // channels
    for layer, part in enumerate((jnp.where(upper, came, own), jnp.where(upper, own, came))):
        at = slice(layer, layer + 1)
        for k in range(count):
            biases[at, k * channels : (k + 1) * channels] = part[k : k + 1, :]
        gains[at, :] = part[count : count + 1, :]
        shifts[at, :] = part[count + 1 : count + 2, :]
        for tap in range(49):
            taps_out[tap, at, :] = part[count + 2 + tap : count + 3 + tap, :]


def weights_kernel(scale, keep0, got0, keep1, got1, out_in, out_out):
    for layer, (keep, got) in enumerate(((keep0, got0), (keep1, got1))):
        for i, out in enumerate((out_in, out_out)):
            out[layer] = (keep[i].astype(F32) + got[i].astype(F32)) * scale


def shape(*dims, dtype=F32):
    return jax.ShapeDtypeStruct(dims, dtype)


def run(kernel, outs, scratch, args, specs=None, fetched=0, name=None, room=46):
    vmem = pl.BlockSpec(memory_space=pltpu.VMEM)
    semaphores = [pltpu.SemaphoreType.DMA((fetched,))] if fetched else []
    return pl.pallas_call(
        kernel,
        out_shape=outs,
        in_specs=[
            vmem if s is None else pl.BlockSpec(memory_space=s) for s in (specs or [None] * len(args))
        ],
        out_specs=tuple(vmem for _ in outs),
        scratch_shapes=[pltpu.VMEM(s.shape, s.dtype) for s in scratch] + semaphores,
        compiler_params=pltpu.CompilerParams(vmem_limit_bytes=room * 1024 * 1024),
        name=name,
    )(*args)


def edges(tile, axis, width, odd):
    count = tile.shape[axis]
    low = lax.slice_in_dim(tile, 0, width, axis=axis)
    high = lax.slice_in_dim(tile, count - width, count, axis=axis)
    return jnp.where(odd, low, high), jnp.where(odd, high, low)


def to_twin(edge, axis):
    count = lax.axis_size(axis)
    return lax.ppermute(edge, axis, [(i, i ^ 1) for i in range(count) if i ^ 1 < count])


def to_other(edge, axis):
    n_rows, n_cols = lax.axis_size("rows"), lax.axis_size("cols")
    count = lax.axis_size(axis)
    pairs = []
    for r in range(n_rows):
        for c in range(n_cols):
            at = r if axis == "rows" else c
            partner = at + 1 if at % 2 else at - 1
            if 0 <= partner < count:
                there = (partner, c) if axis == "rows" else (r, partner)
            else:
                there = (r, c ^ 1) if axis == "rows" else (r ^ 1, c)
            pairs.append((r * n_cols + c, there[0] * n_cols + there[1]))
    return lax.ppermute(edge, ("rows", "cols"), pairs)


def rimmed(tile, from_twin, from_other, axis, odd, outer):
    from_other = jnp.where(outer, jnp.zeros_like(from_other), from_other)
    low = jnp.where(odd, from_twin, from_other)
    high = jnp.where(odd, from_other, from_twin)
    return jnp.concatenate([low, tile, high], axis=axis)


def flip_bit(value, *bits):
    flip = sum(1 << bit for bit in bits)
    both = ("rows", "cols")
    total = lax.axis_size("rows") * lax.axis_size("cols")
    return lax.ppermute(value, both, [(i, i ^ flip) for i in range(total)])


def halves(chunks, dim, mine):
    sizes = [1 if d == dim else n for d, n in enumerate(chunks.shape)]

    def one(bit):
        starts = [bit if d == dim else jnp.uint32(0) for d in range(chunks.ndim)]
        return lax.squeeze(lax.dynamic_slice(chunks, starts, sizes), (dim,))

    return one(mine[1]), one(mine[0])


def summed(own, *got):
    parts = [part.astype(F32) for part in (own,) + got]
    while len(parts) > 1:
        parts = [a + b for a, b in zip(parts[::2], parts[1::2])]
    return parts[0].astype(BF16)


def cut(chunks, order, bit, mine):
    spot = order.index(bit)
    per = chunks.shape[-2:]
    pair = chunks.reshape((-1, 2 ** spot, 2, 2 ** (len(order) - spot - 1)) + per)
    send, keep = halves(pair, 2, mine[bit])
    return send, keep, [b for b in order if b != bit]


def step(chunks, order, bit, mine):
    send, keep, left = cut(chunks, order, bit, mine)
    return keep, flip_bit(send, bit), left


def shards(activations, grad_out, kernels, norm_gains, norm_shifts, w_in, b_in, w_out):
    rows, cols, channels = activations.shape
    layers, _, hidden = w_in.shape
    groups = channels // LANES
    n_rows, n_cols = lax.axis_size("rows"), lax.axis_size("cols")
    total = n_rows * n_cols
    bits = total.bit_length() - 1
    col_bits = n_cols.bit_length() - 1
    me = (lax.axis_index("rows") * n_cols + lax.axis_index("cols")).astype(jnp.uint32)
    mine = [(((me >> k) & 1), 1 - ((me >> k) & 1)) for k in range(bits)]
    grad_scale = 1.0 / math.sqrt(rows * cols * total)
    pixels = rows * cols

    taps = kernels.transpose(1, 2, 0, 3).reshape(49, layers, channels)
    place = jnp.stack(
        [
            lax.axis_index("rows") * rows,
            lax.axis_index("cols") * cols,
            jnp.int32(rows * n_rows),
            jnp.int32(cols * n_cols),
            lax.axis_index("cols") & 1,
            lax.axis_index("rows") & 1,
        ]
    ).astype(jnp.int32)
    grad_flat = grad_out.reshape(pixels, channels)

    at_row, at_col = lax.axis_index("rows"), lax.axis_index("cols")
    odd_col, odd_row = (at_col & 1) == 1, (at_row & 1) == 1
    outer_col = (at_col == 0) | (at_col == n_cols - 1)
    outer_row = (at_row == 0) | (at_row == n_rows - 1)
    activations, place, mine, odd_col, odd_row, outer_col, outer_row = lax.optimization_barrier(
        (activations, place, mine, odd_col, odd_row, outer_col, outer_row)
    )

    def rim_cols(tile, width):
        twin, other = edges(tile, 1, width, odd_col)
        return rimmed(tile, to_twin(twin, "cols"), to_other(other, "cols"), 1, odd_col, outer_col)

    def filled(wide):
        return jnp.pad(wide, ((0, 0), (0, cols + 16 - wide.shape[1]), (0, 0)))

    mid_rows, mid_cols = rows + 2 * HALO, cols + 8
    strip = max(d for d in range(1, mid_rows + 1) if mid_rows % d == 0 and d * mid_cols <= 264)
    weights = [shape(1, channels, hidden, dtype=BF16)] * 2
    tile_z = shape(groups, rows, cols, LANES)
    tile_b = shape(pixels, channels, dtype=BF16)
    tile_h = shape(pixels, hidden, dtype=BF16)
    per = hidden // total
    split = 2 if per % 16 == 0 and col_bits == 2 else 1
    grads_b = (shape(2, hidden // split, channels, dtype=BF16),) * split
    small_outs = (shape(1, hidden), shape(1, channels), shape(1, channels))
    small_rows = -(-(hidden // channels + 51) // 8) * 8

    edge = shape(WIDE, cols, channels, dtype=BF16)
    tile, twin, other = run(
        edges_kernel,
        (shape(rows, cols, channels, dtype=BF16), edge, edge),
        [],
        (place, activations),
        [pltpu.SMEM, None],
        name="edges",
    )
    wide = rimmed(tile, to_twin(twin, "rows"), to_other(other, "rows"), 0, odd_row, outer_row)
    xpad = filled(rim_cols(wide, WIDE))
    mids, z0 = run(
        forward_kernel,
        (shape(groups, mid_rows, mid_cols, LANES), tile_z),
        [
            shape(groups, *xpad.shape[:2], LANES),
            shape(groups, mid_rows, mid_cols, LANES),
            shape(strip * mid_cols, hidden, dtype=BF16),
        ]
        + weights,
        (place, xpad, taps, norm_gains, norm_shifts, w_in, w_out, b_in),
        [pltpu.SMEM] + [None] * 4 + [pl.ANY] * 2 + [None],
        fetched=2,
        name="forward",
        room=50,
    )
    dz1, normed1, act1, gpre1, *small1 = run(
        top_kernel,
        (tile_b, tile_b, tile_h, tile_h) + small_outs,
        [tile_z] + weights,
        (mids, grad_flat, taps, norm_gains, norm_shifts, w_in, w_out, b_in),
        [None] * 5 + [pl.ANY] * 2 + [None],
        fetched=2,
        name="top",
        room=50,
    )

    sides = (col_bits - 1, col_bits)

    def fenced(*values):
        leaves, tree = jax.tree.flatten(values)
        arrays = [i for i, leaf in enumerate(leaves) if not isinstance(leaf, int)]
        for i, value in zip(arrays, lax.optimization_barrier(tuple(leaves[i] for i in arrays))):
            leaves[i] = value
        return jax.tree.unflatten(tree, leaves)

    def settled(flight):
        return summed(flight[0], flight[1]), flight[2]

    def start(dw):
        order = list(range(bits - 1, -1, -1))
        if split == 2:
            send, keep = (d.reshape(2, total // 2, per, channels) for d in dw)
            return keep, flip_bit(send, 0), order[:-1]
        chunks = dw[0].reshape(2, total, per, channels)
        for bit in range(col_bits - 2):
            chunks, order = settled(step(chunks, order, bit, mine))
        return step(chunks, order, col_bits - 2, mine)

    def fork(flight):
        chunks, order = settled(flight)
        return [step(chunks[i], order, sides[i], mine) for i in range(2)]

    def onward(parts, bit, *riders):
        kept, sent, lefts = [], [], []
        for chunks, order in parts:
            send, keep, left = cut(chunks, order, bit, mine)
            kept.append(keep)
            sent.append(send.reshape(-1, channels))
            lefts.append(left)
        got = flip_bit(jnp.concatenate(sent + list(riders), axis=0), bit)
        flights, first = [], 0
        for keep, send, left in zip(kept, sent, lefts):
            came = got[first : first + send.shape[0]].reshape(keep.shape)
            flights.append((keep, came, left))
            first += send.shape[0]
        return flights, [got[first:]] if riders else []

    def merged(flights):
        done = [settled(f) for f in flights]
        return jnp.stack([d[0].reshape(-1, per, channels) for d in done]), done[0][1]

    tile1 = dz1.reshape(rows, cols, channels)
    twin, other = edges(tile1, 0, HALO, odd_row)
    twin, other = to_twin(twin, "rows"), to_other(other, "rows")
    dw1 = run(
        functools.partial(weights_top_kernel, per),
        grads_b,
        [],
        (place, normed1, act1, gpre1, grad_flat),
        [pltpu.SMEM] + [None] * 4,
        name="weights_top",
    )
    run1 = start(dw1)
    tile_f = shape(pixels, channels)
    again = run(
        again_kernel,
        (tile_f, shape(pixels, LANES), tile_b, tile_h, shape(pixels, hidden)),
        weights[:1],
        (z0, norm_gains, norm_shifts, w_in, b_in),
        [None] * 3 + [pl.ANY, None],
        fetched=1,
        name="again",
    )
    tile1, twin, other, again = fenced(tile1, twin, other, again)
    wide1 = rimmed(tile1, twin, other, 0, odd_row, outer_row)
    twin, other = edges(wide1, 1, HALO, odd_col)
    twin, other = to_twin(twin, "cols"), to_other(other, "cols")
    run1, mids = fenced(run1, mids)
    pair1 = fork(run1)
    small_f = shape(small_rows, channels)
    (small1,) = run(
        top_taps_kernel,
        (small_f,),
        [tile_z, shape(groups, 49, LANES)],
        (mids, dz1, *small1),
        name="top_taps",
    )
    wide1, twin, other, small1 = fenced(wide1, twin, other, small1)
    dzpad1 = filled(rimmed(wide1, twin, other, 1, odd_col, outer_col))
    spread_scratch = [shape(groups, *dzpad1.shape[:2], LANES), tile_z]
    grad_mid, dz0, *rest = run(
        functools.partial(low_kernel, per),
        (tile_b, tile_b) + small_outs + grads_b,
        spread_scratch + [tile_h] + weights,
        (place, dzpad1, grad_flat, *again, taps, norm_gains, w_in, w_out),
        [pltpu.SMEM] + [None] * 9 + [pl.ANY] * 2,
        fetched=2,
        name="low",
    )
    small0, dw0 = rest[:3], rest[3:]
    dz0, dw0, pair1, small0 = fenced(dz0, dw0, pair1, small0)
    run0 = start(dw0)
    low_bit = col_bits + 1
    pair1, _ = onward([settled(f) for f in pair1], low_bit)
    small_b = shape(small_rows, channels, dtype=BF16)
    send, small = run(
        taps_kernel,
        (small_b, small_b),
        [shape(groups, *xpad.shape[:2], LANES), tile_z, shape(groups, 49, LANES), small_f],
        (place, xpad, dz0, *small0, small1),
        [pltpu.SMEM] + [None] * 6,
        name="taps",
    )
    small_got = flip_bit(send, 0)
    run0, dz0, small, small_got = fenced(run0, dz0, small, small_got)
    pair0 = fork(run0)
    small = summed(small, small_got)
    for bit in range(1, col_bits - 1):
        small = summed(small, flip_bit(small, bit))
    small_by = [flip_bit(small, sides[1]), flip_bit(small, sides[0]), flip_bit(small, *sides)]
    pair0, pair1, dz0, small, small_by = fenced(pair0, pair1, dz0, small, small_by)
    both = [onward([settled(pair0[i]), settled(pair1[i])], sides[1 - i])[0] for i in range(2)]
    small = summed(small, *small_by)
    small_got = flip_bit(small, low_bit)
    tile0 = dz0.reshape(rows, cols, channels)
    twin, other = edges(tile0, 0, HALO, odd_row)
    twin, other = to_twin(twin, "rows"), to_other(other, "rows")
    both, tile0, twin, other, small, small_got = fenced(both, tile0, twin, other, small, small_got)
    (run0,), _ = onward([merged([both[0][0], both[1][0]])], low_bit)
    small = summed(small, small_got)
    (flight1,), (small_got,) = onward([merged([both[0][1], both[1][1]])], low_bit + 1, small)
    wide0 = rimmed(tile0, twin, other, 0, odd_row, outer_row)
    twin, other = edges(wide0, 1, HALO, odd_col)
    twin, other = to_twin(twin, "cols"), to_other(other, "cols")
    outs = None
    while run0[2]:
        run0, flight1, small, small_got, wide0, twin, other = fenced(
            run0, flight1, small, small_got, wide0, twin, other
        )
        (run0,), _ = onward([settled(run0)], run0[2][-1])
        if small_got is not None:
            small = summed(small, small_got)
            small_got = None
        if flight1[2]:
            (flight1,), (small_got,) = onward([settled(flight1)], flight1[2][-1], small)
        elif outs is None:
            (grad_in,) = run(
                last_kernel,
                (tile_b,),
                spread_scratch,
                (filled(rimmed(wide0, twin, other, 1, odd_col, outer_col)), grad_mid, taps),
                name="last",
            )
            outs = run(
                functools.partial(small_kernel, grad_scale),
                (
                    shape(49, layers, channels),
                    shape(layers, channels),
                    shape(layers, channels),
                    shape(layers, hidden),
                ),
                [],
                (place, small, flip_bit(small, 0)),
                [pltpu.SMEM, None, None],
                name="small",
            )
    run0, flight1, grad_in, outs = fenced(run0, flight1, grad_in, outs)
    grad_taps, grad_gains, grad_shifts, grad_b_in = outs
    share = shape(layers, per, channels)
    grad_w_in, grad_w_out = run(
        functools.partial(weights_kernel, grad_scale),
        (share, share),
        [],
        [part.reshape(2, per, channels) for part in run0[:2] + flight1[:2]],
        name="weights",
    )
    return (
        grad_in.reshape(rows, cols, channels),
        grad_taps.reshape(7, 7, layers, channels).transpose(2, 0, 1, 3),
        grad_gains,
        grad_shifts,
        grad_b_in,
        jnp.swapaxes(grad_w_in, 1, 2),
        jnp.swapaxes(grad_w_out, 1, 2),
    )


def solution(mesh):
    tile = P("rows", "cols", None)
    sliced = P(None, None, ("rows", "cols"))
    return jax.shard_map(
        shards,
        mesh=mesh,
        in_specs=(tile, tile, P(), P(), P(), P(), P(), P()),
        out_specs=(tile, P(), P(), P(), P(), sliced, sliced),
        check_vma=False,
    )
```

```python
import functools
import math

import jax
import jax.numpy as jnp
from jax import lax
from jax.experimental import pallas as pl
from jax.experimental.pallas import tpu as pltpu
from jax.sharding import PartitionSpec as P

EPSILON = 1e-06
INV_ROOT_TAU = 0.3989422804014327
HALF_LOG2E = 0.7213475204444817
ERFC_SLOPE = 0.4 * 0.7071067811865476
ERFC_TERMS = (
    0.23195388609975262,
    0.16163296978938874,
    0.4687286953098433,
    -0.3714470456115026,
    0.7094654203066808,
    -0.2003339536843631,
)
LANES = 128
HALO = 3
WIDE = 2 * HALO
F32 = jnp.float32
BF16 = jnp.bfloat16


def normal_parts(x):
    size = jnp.abs(x)
    bell = jnp.exp2(x * x * (-HALF_LOG2E))
    t = pl.reciprocal(1.0 + ERFC_SLOPE * size, approx=True)
    series = 0.5 * ERFC_TERMS[-1]
    for term in ERFC_TERMS[-2::-1]:
        series = series * t + 0.5 * term
    return size, series * t * bell, bell


def gelu_only(x):
    size, tail, _ = normal_parts(x)
    return jnp.maximum(x, 0.0) - size * tail


def gelu_parts(x):
    size, tail, bell = normal_parts(x)
    cdf = jnp.where(x >= 0, 1.0 - tail, tail)
    return jnp.maximum(x, 0.0) - size * tail, cdf + x * bell * INV_ROOT_TAU


def strip_rows(rows, cols):
    most = max(1, 288 // cols)
    return max(d for d in range(1, rows + 1) if rows % d == 0 and d <= most)


def conv_pass(source, row0, col0, taps, layer, target, rows, cols, back=False):
    strip = strip_rows(rows, cols)
    groups = source.shape[0]

    def one_strip(step, carry):
        g = step // (rows // strip)
        top = (step % (rows // strip)) * strip
        lanes = pl.ds(pl.multiple_of(g * LANES, LANES), LANES)
        sums = [jnp.zeros((cols, LANES), F32) for _ in range(strip)]
        for b in range(7):
            spots = [48 - 7 * a - b if back else 7 * a + b for a in range(7)]
            weights = [taps[spot, pl.ds(layer, 1), lanes] for spot in spots]
            for r in range(strip + 6):
                line = source[g, row0 + top + r, pl.ds(col0 + b, cols), :]
                for a in range(7):
                    if 0 <= r - a < strip:
                        sums[r - a] = sums[r - a] + weights[a] * line
        for i in range(strip):
            target[g, top + i] = sums[i]
        return carry

    lax.fori_loop(0, groups * (rows // strip), one_strip, 0)


def tap_pass(source, row0, col0, grad, target, rows, cols):
    def one_group(g, carry):
        lines = [grad[g, i] for i in range(rows)]
        for b in range(7):
            sums = [None] * 7
            for r in range(rows + 6):
                line = source[g, row0 + r, pl.ds(col0 + b, cols), :]
                for a in range(7):
                    if 0 <= r - a < rows:
                        part = lines[r - a] * line
                        sums[a] = part if sums[a] is None else sums[a] + part
            for a in range(7):
                total = jnp.sum(sums[a], axis=0, keepdims=True)
                target[g, pl.ds(7 * a + b, 1), :] = total
        return carry

    lax.fori_loop(0, source.shape[0], one_group, 0)


def joined(ref, rows, cols=slice(None)):
    parts = [ref[g, rows, cols, :] for g in range(ref.shape[0])]
    return jnp.concatenate([p.reshape(-1, LANES) for p in parts], axis=1)


def split_to(ref, rows, value, shape):
    for g in range(ref.shape[0]):
        ref[g, rows] = value[:, g * LANES : (g + 1) * LANES].reshape(*shape, LANES)


def norm_parts(z):
    center = z - jnp.mean(z, axis=-1, keepdims=True)
    inv = lax.rsqrt(jnp.mean(center * center, axis=-1, keepdims=True) + EPSILON)
    return center * inv, inv


def norm_back(dn, hat, inv, gain):
    scaled = dn * gain
    return inv * (
        scaled
        - jnp.mean(scaled, axis=-1, keepdims=True)
        - hat * jnp.mean(scaled * hat, axis=-1, keepdims=True)
    )


def dot_nn(a, b):
    return jnp.dot(a, b, preferred_element_type=F32)


def dot_nt(a, b):
    return lax.dot_general(a, b, (((1,), (1,)), ((), ())), preferred_element_type=F32)


def dot_tn(a, b):
    return lax.dot_general(a, b, (((0,), (0,)), ((), ())), preferred_element_type=F32)


def pixel_blocks(pixels):
    best = max(d for d in range(16, 129, 16) if pixels % d == 0)
    return [slice(start, start + best) for start in range(0, pixels, best)]


def hidden_chunks(hidden):
    size = 256 if hidden % 256 == 0 else hidden
    return [slice(start, start + size) for start in range(0, hidden, size)]


def hidden_forward(normed, w_in, bias, act, slope):
    for cut in hidden_chunks(w_in.shape[2]):
        for block in pixel_blocks(normed.shape[0]):
            value, factor = gelu_parts(dot_nn(normed[block, :], w_in[0, :, cut]) + bias[:, cut])
            act[block, cut] = value.astype(BF16)
            slope[block, cut] = factor


def hidden_back(grad, w_out, slope, gpre, db):
    for cut in hidden_chunks(w_out.shape[2]):
        bias_sum = None
        for block in pixel_blocks(grad.shape[0]):
            gradient = dot_nn(grad[block, :], w_out[0, :, cut]) * slope[block, cut]
            gpre[block, cut] = gradient.astype(BF16)
            part = jnp.sum(gradient, axis=0, keepdims=True)
            bias_sum = part if bias_sum is None else bias_sum + part
        db[:, cut] = bias_sum


def dz_of(gpre, w_in, hat, inv, gain, dz_out, dgain, dshift):
    dn = dot_nt(gpre[...], w_in[0])
    dgain[...] = jnp.sum(dn * hat, axis=0, keepdims=True)
    dshift[...] = jnp.sum(dn, axis=0, keepdims=True)
    dz_out[...] = norm_back(dn, hat, inv, gain).astype(BF16)


def mlp_grads(normed, grad, w_in, b_in, w_out, act, gpre, db):
    pixels = grad.shape[0]
    for cut in hidden_chunks(w_in.shape[2]):
        bias = b_in[:, cut]
        bias_sum = None
        for block in pixel_blocks(pixels):
            pre = dot_nn(normed[block, :], w_in[0, :, cut]) + bias
            value, slope = gelu_parts(pre)
            act[block, cut] = value.astype(BF16)
            gradient = dot_nn(grad[block, :], w_out[0, :, cut]) * slope
            gpre[block, cut] = gradient.astype(BF16)
            part = jnp.sum(gradient, axis=0, keepdims=True)
            bias_sum = part if bias_sum is None else bias_sum + part
        db[:, cut] = bias_sum


def weight_grads(place, normed, grad, act, gpre, dw, per):
    hidden, channels = act.shape[1], grad.shape[1]
    size = min(n for n in range(128, hidden + 1, 128) if hidden % n == 0 and n % (2 * per) == 0 and n >= 256)
    for first in range(0, hidden, size):
        cut = slice(first, first + size)
        for i, (left, right) in enumerate(((gpre, normed), (act, grad))):
            value = dot_tn(left[:, cut], right[...]).astype(BF16)
            if len(dw) == 1:
                dw[0][i, cut, :] = value
                continue
            value = value.reshape(size // (2 * per), 2, per, channels)
            upper = place[4] == 1
            half = slice(first // 2, (first + size) // 2)
            dw[0][i, half, :] = jnp.where(upper, value[:, 0], value[:, 1]).reshape(-1, channels)
            dw[1][i, half, :] = jnp.where(upper, value[:, 1], value[:, 0]).reshape(-1, channels)


def fetch_layers(triples, arrived):
    copies = [
        pltpu.make_async_copy(source.at[pl.ds(layer, 1)], target, arrived.at[i])
        for i, (source, layer, target) in enumerate(triples)
    ]
    for copy in copies:
        copy.start()
    return copies


def edges_kernel(place, tile, copy, twin, other):
    width = twin.shape[0]
    odd = place[5] == 1
    copy[...] = tile[...]
    low, high = tile[:width].astype(F32), tile[tile.shape[0] - width :].astype(F32)
    twin[...] = jnp.where(odd, low, high).astype(BF16)
    other[...] = jnp.where(odd, high, low).astype(BF16)


def forward_kernel(
    place, xpad, taps, gains, shifts, w_in, w_out, b_in, mids, z_out,
    xs, zs, act, w_in0, w_out0, arrived,
):
    waits = fetch_layers(((w_in, 0, w_in0), (w_out, 0, w_out0)), arrived)
    groups, mid_rows, mid_cols = zs.shape[:3]
    rows, cols = z_out.shape[1:3]
    for g in range(groups):
        xs[g] = xpad[:, :, g * LANES : (g + 1) * LANES].astype(F32)
    conv_pass(xs, 0, 0, taps, 0, zs, mid_rows, mid_cols)
    z_out[...] = zs[:, HALO : HALO + rows, HALO : HALO + cols, :]
    strip = act.shape[0] // mid_cols
    for wait in waits:
        wait.wait()

    def one_strip(step, carry):
        top = step * strip
        hat, _ = norm_parts(joined(zs, pl.ds(top, strip)))
        normed = (hat * gains[0:1] + shifts[0:1]).astype(BF16)
        for cut in hidden_chunks(w_in0.shape[2]):
            pre = dot_nn(normed, w_in0[0, :, cut]) + b_in[0:1, cut]
            act[:, cut] = gelu_only(pre).astype(BF16)
        mixed = dot_nt(act[...], w_out0[0])
        row = lax.broadcasted_iota(jnp.int32, (strip, mid_cols, 1), 0) + (top - HALO) + place[0]
        col = lax.broadcasted_iota(jnp.int32, (strip, mid_cols, 1), 1) - HALO + place[1]
        real = (row >= 0) & (row < place[2]) & (col >= 0) & (col < place[3])
        real = jnp.where(real, 1.0, 0.0).reshape(strip * mid_cols, 1)
        base = joined(xs, pl.ds(top + HALO, strip), slice(HALO, HALO + mid_cols))
        mid = (base + mixed).astype(BF16).astype(F32) * real
        split_to(mids, pl.ds(top, strip), mid, (strip, mid_cols))
        return carry

    lax.fori_loop(0, mid_rows // strip, one_strip, 0, unroll=True)


def top_kernel(
    mids, grad, taps, gains, shifts, w_in, w_out, b_in,
    dz_out, normed, act, gpre, db, dgain, dshift, z, w_in1, w_out1, arrived,
):
    waits = fetch_layers(((w_in, 1, w_in1), (w_out, 1, w_out1)), arrived)
    conv_pass(mids, 0, 0, taps, 1, z, *z.shape[1:3])
    hat, inv = norm_parts(joined(z, slice(None)))
    normed[...] = (hat * gains[1:2] + shifts[1:2]).astype(BF16)
    for wait in waits:
        wait.wait()
    mlp_grads(normed, grad, w_in1, b_in.at[pl.ds(1, 1)], w_out1, act, gpre, db)
    dz_of(gpre, w_in1, hat, inv, gains[1:2], dz_out, dgain, dshift)


def again_kernel(z0, gains, shifts, w_in, b_in, hat_out, inv_out, normed, act, slope, w_in0, arrived):
    (wait,) = fetch_layers(((w_in, 0, w_in0),), arrived)
    hat, inv = norm_parts(joined(z0, slice(None)))
    hat_out[...] = hat
    inv_out[...] = jnp.broadcast_to(inv, inv_out.shape)
    normed[...] = (hat * gains[0:1] + shifts[0:1]).astype(BF16)
    wait.wait()
    hidden_forward(normed, w_in0, b_in.at[pl.ds(0, 1)], act, slope)


def low_kernel(
    per, place, dzpad, grad, hat, inv, normed, act, slope, taps, gains, w_in, w_out,
    gmid, dz_out, db, dgain, dshift, *rest,
):
    *dw, dzs, spread, gpre, w_in0, w_out0, arrived = rest
    waits = fetch_layers(((w_out, 0, w_out0), (w_in, 0, w_in0)), arrived)
    spread_pass(dzpad, dzs, taps, 1, spread)
    gmid[...] = (grad[...].astype(F32) + joined(spread, slice(None))).astype(BF16)
    for wait in waits:
        wait.wait()
    hidden_back(gmid, w_out0, slope, gpre, db)
    dz_of(gpre, w_in0, hat[...], inv[:, :1], gains[0:1], dz_out, dgain, dshift)
    weight_grads(place, normed, gmid, act, gpre, dw, per)


def weights_top_kernel(per, place, normed, act, gpre, grad, *dw):
    weight_grads(place, normed, grad, act, gpre, dw, per)


def spread_pass(dzpad, dzs, taps, layer, spread):
    for g in range(dzs.shape[0]):
        dzs[g] = dzpad[:, :, g * LANES : (g + 1) * LANES].astype(F32)
    conv_pass(dzs, 0, 0, taps, layer, spread, *spread.shape[1:3], back=True)


def last_kernel(dzpad, gmid, taps, out, dzs, spread):
    spread_pass(dzpad, dzs, taps, 0, spread)
    out[...] = (gmid[...].astype(F32) + joined(spread, slice(None))).astype(BF16)


def small_rows_of(values, row0, col0, dz, dzs, taps, db, dgain, dshift, sums):
    rows, cols = dzs.shape[1:3]
    channels = sums.shape[1]
    split_to(dzs, slice(None), dz[...].astype(F32), (rows, cols))
    count = db.shape[1] // channels
    for k in range(count):
        sums[k : k + 1, :] = db[:, k * channels : (k + 1) * channels]
    sums[count : count + 1, :] = dgain[...]
    sums[count + 1 : count + 2, :] = dshift[...]
    tap_pass(values, row0, col0, dzs, taps, rows, cols)
    for g in range(taps.shape[0]):
        sums[count + 2 : count + 51, g * LANES : (g + 1) * LANES] = taps[g]


def top_taps_kernel(mids, dz, db, dgain, dshift, sums, dzs, taps):
    sums[...] = jnp.zeros(sums.shape, F32)
    small_rows_of(mids, 0, 0, dz, dzs, taps, db, dgain, dshift, sums)


def taps_kernel(place, xpad, dz, db, dgain, dshift, sums1, send, keep, xs, dzs, taps, sums0):
    for g in range(dzs.shape[0]):
        xs[g] = xpad[:, :, g * LANES : (g + 1) * LANES].astype(F32)
    sums0[...] = jnp.zeros(sums0.shape, F32)
    small_rows_of(xs, HALO, HALO, dz, dzs, taps, db, dgain, dshift, sums0)
    upper = place[4] == 1
    send[...] = jnp.where(upper, sums0[...], sums1[...]).astype(BF16)
    keep[...] = jnp.where(upper, sums1[...], sums0[...]).astype(BF16)


def small_kernel(scale, place, mine, got, taps_out, gains, shifts, biases):
    upper = place[4] == 1
    own, came = mine[...].astype(F32) * scale, got[...].astype(F32) * scale
    channels = own.shape[1]
    count = biases.shape[1] // channels
    for layer, part in enumerate((jnp.where(upper, came, own), jnp.where(upper, own, came))):
        at = slice(layer, layer + 1)
        for k in range(count):
            biases[at, k * channels : (k + 1) * channels] = part[k : k + 1, :]
        gains[at, :] = part[count : count + 1, :]
        shifts[at, :] = part[count + 1 : count + 2, :]
        for tap in range(49):
            taps_out[tap, at, :] = part[count + 2 + tap : count + 3 + tap, :]


def weights_kernel(scale, keep0, got0, keep1, got1, out_in, out_out):
    for layer, (keep, got) in enumerate(((keep0, got0), (keep1, got1))):
        for i, out in enumerate((out_in, out_out)):
            out[layer] = (keep[i].astype(F32) + got[i].astype(F32)) * scale


def shape(*dims, dtype=F32):
    return jax.ShapeDtypeStruct(dims, dtype)


def run(kernel, outs, scratch, args, specs=None, fetched=0, name=None, room=46):
    vmem = pl.BlockSpec(memory_space=pltpu.VMEM)
    semaphores = [pltpu.SemaphoreType.DMA((fetched,))] if fetched else []
    return pl.pallas_call(
        kernel,
        out_shape=outs,
        in_specs=[
            vmem if s is None else pl.BlockSpec(memory_space=s) for s in (specs or [None] * len(args))
        ],
        out_specs=tuple(vmem for _ in outs),
        scratch_shapes=[pltpu.VMEM(s.shape, s.dtype) for s in scratch] + semaphores,
        compiler_params=pltpu.CompilerParams(vmem_limit_bytes=room * 1024 * 1024),
        name=name,
    )(*args)


def edges(tile, axis, width, odd):
    count = tile.shape[axis]
    low = lax.slice_in_dim(tile, 0, width, axis=axis)
    high = lax.slice_in_dim(tile, count - width, count, axis=axis)
    return jnp.where(odd, low, high), jnp.where(odd, high, low)


def to_twin(edge, axis):
    count = lax.axis_size(axis)
    return lax.ppermute(edge, axis, [(i, i ^ 1) for i in range(count) if i ^ 1 < count])


def to_other(edge, axis):
    n_rows, n_cols = lax.axis_size("rows"), lax.axis_size("cols")
    count = lax.axis_size(axis)
    pairs = []
    for r in range(n_rows):
        for c in range(n_cols):
            at = r if axis == "rows" else c
            partner = at + 1 if at % 2 else at - 1
            if 0 <= partner < count:
                there = (partner, c) if axis == "rows" else (r, partner)
            else:
                there = (r, c ^ 1) if axis == "rows" else (r ^ 1, c)
            pairs.append((r * n_cols + c, there[0] * n_cols + there[1]))
    return lax.ppermute(edge, ("rows", "cols"), pairs)


def rimmed(tile, from_twin, from_other, axis, odd, outer):
    from_other = jnp.where(outer, jnp.zeros_like(from_other), from_other)
    low = jnp.where(odd, from_twin, from_other)
    high = jnp.where(odd, from_other, from_twin)
    return jnp.concatenate([low, tile, high], axis=axis)


def flip_bit(value, *bits):
    flip = sum(1 << bit for bit in bits)
    both = ("rows", "cols")
    total = lax.axis_size("rows") * lax.axis_size("cols")
    return lax.ppermute(value, both, [(i, i ^ flip) for i in range(total)])


def halves(chunks, dim, mine):
    sizes = [1 if d == dim else n for d, n in enumerate(chunks.shape)]

    def one(bit):
        starts = [bit if d == dim else jnp.uint32(0) for d in range(chunks.ndim)]
        return lax.squeeze(lax.dynamic_slice(chunks, starts, sizes), (dim,))

    return one(mine[1]), one(mine[0])


def summed(own, *got):
    parts = [part.astype(F32) for part in (own,) + got]
    while len(parts) > 1:
        parts = [a + b for a, b in zip(parts[::2], parts[1::2])]
    return parts[0].astype(BF16)


def cut(chunks, order, bit, mine):
    spot = order.index(bit)
    per = chunks.shape[-2:]
    pair = chunks.reshape((-1, 2 ** spot, 2, 2 ** (len(order) - spot - 1)) + per)
    send, keep = halves(pair, 2, mine[bit])
    return send, keep, [b for b in order if b != bit]


def step(chunks, order, bit, mine):
    send, keep, left = cut(chunks, order, bit, mine)
    return keep, flip_bit(send, bit), left


def shards(activations, grad_out, kernels, norm_gains, norm_shifts, w_in, b_in, w_out):
    rows, cols, channels = activations.shape
    layers, _, hidden = w_in.shape
    groups = channels // LANES
    n_rows, n_cols = lax.axis_size("rows"), lax.axis_size("cols")
    total = n_rows * n_cols
    bits = total.bit_length() - 1
    col_bits = n_cols.bit_length() - 1
    me = (lax.axis_index("rows") * n_cols + lax.axis_index("cols")).astype(jnp.uint32)
    mine = [(((me >> k) & 1), 1 - ((me >> k) & 1)) for k in range(bits)]
    grad_scale = 1.0 / math.sqrt(rows * cols * total)
    pixels = rows * cols

    taps = kernels.transpose(1, 2, 0, 3).reshape(49, layers, channels)
    place = jnp.stack(
        [
            lax.axis_index("rows") * rows,
            lax.axis_index("cols") * cols,
            jnp.int32(rows * n_rows),
            jnp.int32(cols * n_cols),
            lax.axis_index("cols") & 1,
            lax.axis_index("rows") & 1,
        ]
    ).astype(jnp.int32)
    grad_flat = grad_out.reshape(pixels, channels)

    at_row, at_col = lax.axis_index("rows"), lax.axis_index("cols")
    odd_col, odd_row = (at_col & 1) == 1, (at_row & 1) == 1
    outer_col = (at_col == 0) | (at_col == n_cols - 1)
    outer_row = (at_row == 0) | (at_row == n_rows - 1)
    activations, place, mine, odd_col, odd_row, outer_col, outer_row = lax.optimization_barrier(
        (activations, place, mine, odd_col, odd_row, outer_col, outer_row)
    )

    def rim_cols(tile, width):
        twin, other = edges(tile, 1, width, odd_col)
        return rimmed(tile, to_twin(twin, "cols"), to_other(other, "cols"), 1, odd_col, outer_col)

    def filled(wide):
        return jnp.pad(wide, ((0, 0), (0, cols + 16 - wide.shape[1]), (0, 0)))

    mid_rows, mid_cols = rows + 2 * HALO, cols + 8
    strip = max(d for d in range(1, mid_rows + 1) if mid_rows % d == 0 and d * mid_cols <= 264)
    weights = [shape(1, channels, hidden, dtype=BF16)] * 2
    tile_z = shape(groups, rows, cols, LANES)
    tile_b = shape(pixels, channels, dtype=BF16)
    tile_h = shape(pixels, hidden, dtype=BF16)
    per = hidden // total
    split = 2 if per % 16 == 0 and col_bits == 2 else 1
    grads_b = (shape(2, hidden // split, channels, dtype=BF16),) * split
    small_outs = (shape(1, hidden), shape(1, channels), shape(1, channels))
    small_rows = -(-(hidden // channels + 51) // 8) * 8

    edge = shape(WIDE, cols, channels, dtype=BF16)
    tile, twin, other = run(
        edges_kernel,
        (shape(rows, cols, channels, dtype=BF16), edge, edge),
        [],
        (place, activations),
        [pltpu.SMEM, None],
        name="edges",
    )
    wide = rimmed(tile, to_twin(twin, "rows"), to_other(other, "rows"), 0, odd_row, outer_row)
    xpad = filled(rim_cols(wide, WIDE))
    mids, z0 = run(
        forward_kernel,
        (shape(groups, mid_rows, mid_cols, LANES), tile_z),
        [
            shape(groups, *xpad.shape[:2], LANES),
            shape(groups, mid_rows, mid_cols, LANES),
            shape(strip * mid_cols, hidden, dtype=BF16),
        ]
        + weights,
        (place, xpad, taps, norm_gains, norm_shifts, w_in, w_out, b_in),
        [pltpu.SMEM] + [None] * 4 + [pl.ANY] * 2 + [None],
        fetched=2,
        name="forward",
        room=50,
    )
    dz1, normed1, act1, gpre1, *small1 = run(
        top_kernel,
        (tile_b, tile_b, tile_h, tile_h) + small_outs,
        [tile_z] + weights,
        (mids, grad_flat, taps, norm_gains, norm_shifts, w_in, w_out, b_in),
        [None] * 5 + [pl.ANY] * 2 + [None],
        fetched=2,
        name="top",
        room=50,
    )

    sides = (col_bits - 1, col_bits)

    def fenced(*values):
        leaves, tree = jax.tree.flatten(values)
        arrays = [i for i, leaf in enumerate(leaves) if not isinstance(leaf, int)]
        for i, value in zip(arrays, lax.optimization_barrier(tuple(leaves[i] for i in arrays))):
            leaves[i] = value
        return jax.tree.unflatten(tree, leaves)

    def settled(flight):
        return summed(flight[0], flight[1]), flight[2]

    def start(dw):
        order = list(range(bits - 1, -1, -1))
        if split == 2:
            send, keep = (d.reshape(2, total // 2, per, channels) for d in dw)
            return keep, flip_bit(send, 0), order[:-1]
        chunks = dw[0].reshape(2, total, per, channels)
        for bit in range(col_bits - 2):
            chunks, order = settled(step(chunks, order, bit, mine))
        return step(chunks, order, col_bits - 2, mine)

    def fork(flight):
        chunks, order = settled(flight)
        return [step(chunks[i], order, sides[i], mine) for i in range(2)]

    def onward(parts, bit, *riders):
        kept, sent, lefts = [], [], []
        for chunks, order in parts:
            send, keep, left = cut(chunks, order, bit, mine)
            kept.append(keep)
            sent.append(send.reshape(-1, channels))
            lefts.append(left)
        got = flip_bit(jnp.concatenate(sent + list(riders), axis=0), bit)
        flights, first = [], 0
        for keep, send, left in zip(kept, sent, lefts):
            came = got[first : first + send.shape[0]].reshape(keep.shape)
            flights.append((keep, came, left))
            first += send.shape[0]
        return flights, [got[first:]] if riders else []

    def merged(flights):
        done = [settled(f) for f in flights]
        return jnp.stack([d[0].reshape(-1, per, channels) for d in done]), done[0][1]

    tile1 = dz1.reshape(rows, cols, channels)
    twin, other = edges(tile1, 0, HALO, odd_row)
    twin, other = to_twin(twin, "rows"), to_other(other, "rows")
    dw1 = run(
        functools.partial(weights_top_kernel, per),
        grads_b,
        [],
        (place, normed1, act1, gpre1, grad_flat),
        [pltpu.SMEM] + [None] * 4,
        name="weights_top",
    )
    run1 = start(dw1)
    tile_f = shape(pixels, channels)
    again = run(
        again_kernel,
        (tile_f, shape(pixels, LANES), tile_b, tile_h, shape(pixels, hidden)),
        weights[:1],
        (z0, norm_gains, norm_shifts, w_in, b_in),
        [None] * 3 + [pl.ANY, None],
        fetched=1,
        name="again",
    )
    tile1, twin, other, again = fenced(tile1, twin, other, again)
    wide1 = rimmed(tile1, twin, other, 0, odd_row, outer_row)
    twin, other = edges(wide1, 1, HALO, odd_col)
    twin, other = to_twin(twin, "cols"), to_other(other, "cols")
    run1, mids = fenced(run1, mids)
    pair1 = fork(run1)
    small_f = shape(small_rows, channels)
    (small1,) = run(
        top_taps_kernel,
        (small_f,),
        [tile_z, shape(groups, 49, LANES)],
        (mids, dz1, *small1),
        name="top_taps",
    )
    wide1, twin, other, small1 = fenced(wide1, twin, other, small1)
    dzpad1 = filled(rimmed(wide1, twin, other, 1, odd_col, outer_col))
    spread_scratch = [shape(groups, *dzpad1.shape[:2], LANES), tile_z]
    grad_mid, dz0, *rest = run(
        functools.partial(low_kernel, per),
        (tile_b, tile_b) + small_outs + grads_b,
        spread_scratch + [tile_h] + weights,
        (place, dzpad1, grad_flat, *again, taps, norm_gains, w_in, w_out),
        [pltpu.SMEM] + [None] * 9 + [pl.ANY] * 2,
        fetched=2,
        name="low",
    )
    small0, dw0 = rest[:3], rest[3:]
    dz0, dw0, pair1, small0 = fenced(dz0, dw0, pair1, small0)
    run0 = start(dw0)
    low_bit = col_bits + 1
    pair1, _ = onward([settled(f) for f in pair1], low_bit)
    small_b = shape(small_rows, channels, dtype=BF16)
    send, small = run(
        taps_kernel,
        (small_b, small_b),
        [shape(groups, *xpad.shape[:2], LANES), tile_z, shape(groups, 49, LANES), small_f],
        (place, xpad, dz0, *small0, small1),
        [pltpu.SMEM] + [None] * 6,
        name="taps",
    )
    small_got = flip_bit(send, 0)
    run0, dz0, small, small_got = fenced(run0, dz0, small, small_got)
    pair0 = fork(run0)
    small = summed(small, small_got)
    for bit in range(1, col_bits - 1):
        small = summed(small, flip_bit(small, bit))
    small_by = [flip_bit(small, sides[1]), flip_bit(small, sides[0]), flip_bit(small, *sides)]
    pair0, pair1, dz0, small, small_by = fenced(pair0, pair1, dz0, small, small_by)
    both = [onward([settled(pair0[i]), settled(pair1[i])], sides[1 - i])[0] for i in range(2)]
    small = summed(small, *small_by)
    small_got = flip_bit(small, low_bit)
    tile0 = dz0.reshape(rows, cols, channels)
    twin, other = edges(tile0, 0, HALO, odd_row)
    twin, other = to_twin(twin, "rows"), to_other(other, "rows")
    both, tile0, twin, other, small, small_got = fenced(both, tile0, twin, other, small, small_got)
    (run0,), _ = onward([merged([both[0][0], both[1][0]])], low_bit)
    small = summed(small, small_got)
    (flight1,), (small_got,) = onward([merged([both[0][1], both[1][1]])], low_bit + 1, small)
    wide0 = rimmed(tile0, twin, other, 0, odd_row, outer_row)
    twin, other = edges(wide0, 1, HALO, odd_col)
    twin, other = to_twin(twin, "cols"), to_other(other, "cols")
    outs = None
    while run0[2]:
        run0, flight1, small, small_got, wide0, twin, other = fenced(
            run0, flight1, small, small_got, wide0, twin, other
        )
        (run0,), _ = onward([settled(run0)], run0[2][-1])
        if small_got is not None:
            small = summed(small, small_got)
            small_got = None
        if flight1[2]:
            (flight1,), (small_got,) = onward([settled(flight1)], flight1[2][-1], small)
        elif outs is None:
            (grad_in,) = run(
                last_kernel,
                (tile_b,),
                spread_scratch,
                (filled(rimmed(wide0, twin, other, 1, odd_col, outer_col)), grad_mid, taps),
                name="last",
            )
            outs = run(
                functools.partial(small_kernel, grad_scale),
                (
                    shape(49, layers, channels),
                    shape(layers, channels),
                    shape(layers, channels),
                    shape(layers, hidden),
                ),
                [],
                (place, small, flip_bit(small, 0)),
                [pltpu.SMEM, None, None],
                name="small",
            )
    run0, flight1, grad_in, outs = fenced(run0, flight1, grad_in, outs)
    grad_taps, grad_gains, grad_shifts, grad_b_in = outs
    share = shape(layers, per, channels)
    grad_w_in, grad_w_out = run(
        functools.partial(weights_kernel, grad_scale),
        (share, share),
        [],
        [part.reshape(2, per, channels) for part in run0[:2] + flight1[:2]],
        name="weights",
    )
    return (
        grad_in.reshape(rows, cols, channels),
        grad_taps.reshape(7, 7, layers, channels).transpose(2, 0, 1, 3),
        grad_gains,
        grad_shifts,
        grad_b_in,
        jnp.swapaxes(grad_w_in, 1, 2),
        jnp.swapaxes(grad_w_out, 1, 2),
    )


def solution(mesh):
    tile = P("rows", "cols", None)
    sliced = P(None, None, ("rows", "cols"))
    return jax.shard_map(
        shards,
        mesh=mesh,
        in_specs=(tile, tile, P(), P(), P(), P(), P(), P()),
        out_specs=(tile, P(), P(), P(), P(), sliced, sliced),
        check_vma=False,
    )
```
